32 devices in a mesh: seq: 8 (over z, y), mp: 4 (over x, core).
Axes of the slice: x: 2, y: 2, z: 4, core: 2. Of those that a mesh axis runs over, the one named last changes fastest.
Arguments:
- queries: bfloat16 [2048, 2048], P('seq', 'mp'), may hold values from -120 to 120
- keys: bfloat16 [2048, 2048], P('seq', 'mp'), may hold values from -8 to 8
- values: bfloat16 [2048, 2048], P('seq', 'mp'), may hold values from -7 to 7
- out_weight: bfloat16 [2048, 2048], P('mp'), may hold values from -0.125 to 0.125
- out_grad: bfloat16 [2048, 2048], P(('seq', 'mp')), may hold values from -6 to 6
Outputs:
- mixed: bfloat16 [2048, 2048], P(('seq', 'mp'))
- query_grad: bfloat16 [2048, 2048], P('seq', 'mp')
- key_grad: bfloat16 [2048, 2048], P('seq', 'mp')
- value_grad: bfloat16 [2048, 2048], P('seq', 'mp')
The draws below stay inside these ranges and needn't reach their ends.
All inputs are finite; a program needn't handle non-finite values.
Results may differ from the reference program's by a relative error of at most 0.012.
The reference program's roundings to bfloat16 on the way (of `pooled`, `prob`, `attended`, `grad_attended` and `shift`) count: a program that leaves them out, or rounds other values in their place, can miss the bound.
Values may be sent and summed in bfloat16 or wider, within the bound.
No kernel may reach another device: no remote copies, remote signals or barrier semaphores. Data moves between devices by JAX's collectives and lax.ppermute only.
A program may use at most 64 MiB of HBM per device.

```python
import jax
import jax.numpy as jnp
from jax import lax

HEADS = 16
HEAD_DIM = 128
BLOCK = 256
LEVELS = 2
D = 2048
TOKENS = 2048
N_MP = 4


def shared_keys(key):
    return 1.25 * jax.random.truncated_normal(key, -5.0, 5.0, (TOKENS, D), jnp.float32)


def draw_keys(key, part):
    base = shared_keys(key)
    return base.astype(jnp.bfloat16)


def draw_queries(key, part):
    key = jax.random.fold_in(key, 5)
    rough = 1.25 * jax.random.truncated_normal(key, -5.0, 5.0, (TOKENS, D), jnp.float32)
    return rough.astype(jnp.bfloat16)


def draw_values(key, part):
    key = jax.random.fold_in(key, 7)
    first, second, third = jax.random.split(key, 3)
    cycles = jax.random.randint(first, (D,), 1, 9).astype(jnp.float32)
    phase = jax.random.uniform(second, (D,), jnp.float32, -3.14159, 3.14159)
    position = jnp.arange(TOKENS, dtype=jnp.int32).astype(jnp.float32) / TOKENS
    smooth = jnp.sin(6.2831853 * position[:, None] * cycles[None, :] + phase[None, :])
    rough = jax.random.truncated_normal(third, -5.0, 5.0, (TOKENS, D), jnp.float32)
    field = rough + smooth
    return field.astype(jnp.bfloat16)


def block_levels(rng, dims, shards, smallest, largest):
    factor_of = 1.0
    for axis_at, blocks in shards:
        steps = jax.random.uniform(jax.random.fold_in(jax.random.fold_in(rng, 6), axis_at), (blocks,), jnp.float32, smallest / len(shards), largest / len(shards))
        factor_of = factor_of * jnp.repeat(jnp.exp(steps), dims[axis_at] // blocks).reshape((-1,) + (1,) * (len(dims) - 1 - axis_at))
    return factor_of


def noise(stream_key, shape, spread, most, cuts=(), kind=jnp.bfloat16):
    array = jax.random.normal(stream_key, shape, jnp.float32) * spread
    if len(cuts) > 0:
        array = block_levels(stream_key, shape, cuts, -0.22, 0.18) * array
    return jnp.clip(array, min=-most, max=most).astype(kind)


def setup_inputs(seed: int = 0) -> dict:
    key_of = jax.random.split(jax.random.key(seed), 6)
    return {
        "queries": draw_queries(jax.random.fold_in(key_of[5], 71), 0),
        "keys": draw_keys(jax.random.fold_in(key_of[5], 71), 0),
        "values": draw_values(jax.random.fold_in(key_of[5], 71), 0),
        "out_weight": noise(key_of[3], (D, D), D ** -0.5, 0.125, ((0, 4),)),
        "out_grad": noise(key_of[4], (TOKENS, D), 1.0, 6.0, ((0, 32),)),
    }


def pool_rows(rows):
    pairs = rows.astype(jnp.float32).reshape(rows.shape[0] // 2, 2, rows.shape[1])
    return ((pairs[:, 0] + pairs[:, 1]) * 0.5).astype(jnp.bfloat16)


def split_heads(rows):
    return rows.astype(jnp.float32).reshape(rows.shape[0], HEADS, HEAD_DIM)


def rounded(numbers):
    return lax.optimization_barrier(numbers.astype(jnp.bfloat16)).astype(jnp.float32)


def block_terms(index, queries, padded_keys, padded_values, pooled):
    scale = HEAD_DIM ** -0.5
    start = (index * BLOCK).astype(jnp.int32)
    fine_queries = split_heads(lax.dynamic_slice_in_dim(queries, start, BLOCK, 0))
    near_keys = split_heads(lax.dynamic_slice_in_dim(padded_keys, start, 3 * BLOCK, 0))
    near_values = split_heads(lax.dynamic_slice_in_dim(padded_values, start, 3 * BLOCK, 0))
    beside = index - 1 + jnp.arange(3 * BLOCK, dtype=jnp.int32) // BLOCK
    present = (beside >= 0) & (beside < TOKENS // BLOCK)
    near_scores = scale * jnp.einsum("thd,shd->hts", fine_queries, near_keys)
    near_scores = jnp.where(present[None, None, :], near_scores, -jnp.inf)
    entries = [(near_scores, fine_queries, near_keys, near_values, start, start, 1.0)]
    for level in range(1, LEVELS + 1):
        pooled_queries, pooled_keys, pooled_values = pooled[level - 1]
        level_rows = ((start + jnp.arange(BLOCK, dtype=jnp.int32)) >> level).astype(jnp.int32)
        sibling_start = (((index >> level) ^ 1) * BLOCK).astype(jnp.int32)
        coarse_queries = split_heads(jnp.take(pooled_queries, level_rows, axis=0))
        coarse_keys = split_heads(lax.dynamic_slice_in_dim(pooled_keys, sibling_start, BLOCK, 0))
        coarse_values = split_heads(lax.dynamic_slice_in_dim(pooled_values, sibling_start, BLOCK, 0))
        scores = scale * jnp.einsum("thd,shd->hts", coarse_queries, coarse_keys)
        entries.append((scores, coarse_queries, coarse_keys, coarse_values, level_rows, sibling_start, 2.0 ** level))
    top = entries[0][0].max(-1)
    for entry in entries[1:]:
        top = jnp.maximum(top, entry[0].max(-1))
    weights = [entry[6] * jnp.exp(entry[0] - top[..., None]) for entry in entries]
    total = weights[0].sum(-1)
    for weight in weights[1:]:
        total = total + weight.sum(-1)
    probs = [rounded(weight / total[..., None]) for weight in weights]
    return entries, probs


def reference(queries, keys, values, out_weight, out_grad):
    scale = HEAD_DIM ** -0.5
    pooled = []
    level_q, level_k, level_v = queries, keys, values
    for level in range(LEVELS):
        level_q, level_k, level_v = pool_rows(level_q), pool_rows(level_k), pool_rows(level_v)
        pooled.append((level_q, level_k, level_v))
    padding = jnp.zeros((BLOCK, D), keys.dtype)
    padded_keys = jnp.concatenate([padding, keys, padding], 0)
    padded_values = jnp.concatenate([padding, values, padding], 0)
    indices = jnp.arange(TOKENS // BLOCK, dtype=jnp.int32)

    def forward(index):
        entries, probs = block_terms(index, queries, padded_keys, padded_values, pooled)
        context = jnp.zeros((BLOCK, HEADS, HEAD_DIM), jnp.float32)
        for entry, prob in zip(entries, probs):
            context = context + jnp.einsum("hts,shd->thd", prob, entry[3])
        return context.reshape(BLOCK, D).astype(jnp.bfloat16)

    attended = lax.map(forward, indices).reshape(TOKENS, D)
    group = D // N_MP
    summed = jnp.zeros((TOKENS, D), jnp.float32)
    for part_index in range(N_MP):
        partial_sum = jnp.dot(attended[:, part_index * group:(part_index + 1) * group],
                              out_weight[part_index * group:(part_index + 1) * group],
                              preferred_element_type=jnp.float32)
        summed = summed + rounded(partial_sum)
    mixed = summed.astype(jnp.bfloat16)
    grad_attended = jnp.dot(out_grad, out_weight.T, preferred_element_type=jnp.float32).astype(jnp.bfloat16)

    def backward(carry, index):
        near_sums, coarse_sums = carry
        entries, probs = block_terms(index, queries, padded_keys, padded_values, pooled)
        grad_rows = split_heads(lax.dynamic_slice_in_dim(grad_attended, (index * BLOCK).astype(jnp.int32), BLOCK, 0))
        slopes = [jnp.einsum("thd,shd->hts", grad_rows, entry[3]) for entry in entries]
        delta = (probs[0] * slopes[0]).sum(-1)
        for prob, slope in zip(probs[1:], slopes[1:]):
            delta = delta + (prob * slope).sum(-1)
        shifts = [rounded(prob * (slope - delta[..., None])) for prob, slope in zip(probs, slopes)]
        near_entry = entries[0]
        query_rows = scale * jnp.einsum("hts,shd->thd", shifts[0], near_entry[2])
        key_part = scale * jnp.einsum("hts,thd->shd", shifts[0], near_entry[1])
        value_part = jnp.einsum("hts,thd->shd", probs[0], grad_rows)
        window = jnp.concatenate([key_part.reshape(3 * BLOCK, D), value_part.reshape(3 * BLOCK, D)], 1)
        start = near_entry[4]
        near_sums = lax.dynamic_update_slice_in_dim(
            near_sums, lax.dynamic_slice_in_dim(near_sums, start, 3 * BLOCK, 0) + window, start, 0)
        updated = []
        for entry, prob, shift, sums in zip(entries[1:], probs[1:], shifts[1:], coarse_sums):
            query_sums, pair_sums = sums
            coarse_rows = scale * jnp.einsum("hts,shd->thd", shift, entry[2]).reshape(BLOCK, D)
            query_sums = query_sums.at[entry[4]].add(coarse_rows)
            key_coarse = scale * jnp.einsum("hts,thd->shd", shift, entry[1]).reshape(BLOCK, D)
            value_coarse = jnp.einsum("hts,thd->shd", prob, grad_rows).reshape(BLOCK, D)
            pair = jnp.concatenate([key_coarse, value_coarse], 1)
            pair_sums = lax.dynamic_update_slice_in_dim(
                pair_sums, lax.dynamic_slice_in_dim(pair_sums, entry[5], BLOCK, 0) + pair, entry[5], 0)
            updated.append((query_sums, pair_sums))
        return (near_sums, updated), query_rows.reshape(BLOCK, D)

    initial = (jnp.zeros((TOKENS + 2 * BLOCK, 2 * D), jnp.float32),
               [(jnp.zeros((TOKENS >> level, D), jnp.float32), jnp.zeros((TOKENS >> level, 2 * D), jnp.float32))
                for level in range(1, LEVELS + 1)])
    (near_sums, coarse_sums), near_query = lax.scan(backward, initial, indices)
    query_total = near_query.reshape(TOKENS, D)
    pair_total = near_sums[BLOCK:BLOCK + TOKENS]
    for level in range(1, LEVELS + 1):
        query_sums, pair_sums = coarse_sums[level - 1]
        query_total = query_total + jnp.repeat(query_sums, 2 ** level, axis=0) / (2.0 ** level)
        pair_total = pair_total + jnp.repeat(pair_sums, 2 ** level, axis=0) / (2.0 ** level)
    return (mixed, query_total.astype(jnp.bfloat16), pair_total[:, :D].astype(jnp.bfloat16),
            pair_total[:, D:].astype(jnp.bfloat16))
```

```python
import functools

import jax
import jax.numpy as jnp
from jax import lax
from jax.experimental import pallas as pl
from jax.experimental.pallas import tpu as pltpu
from jax.sharding import PartitionSpec as P

HEAD_DIM = 128
BLOCK = 256
LEVELS = 2
GROUP = 4
SCALE = HEAD_DIM**-0.5
LOG2E = 1.4426950408889634
BF16 = jnp.bfloat16
F32 = jnp.float32


def dot(a, b):
    return lax.dot_general(a, b, (((1,), (0,)), ((), ())), preferred_element_type=F32)


def dot_nt(a, b):
    return lax.dot_general(a, b, (((1,), (1,)), ((), ())), preferred_element_type=F32)


def shape(*dims, dtype=BF16):
    return jax.ShapeDtypeStruct(dims, dtype)


def call(kernel, out_shape, args, scratch=(), flops=0, limit=32):
    whole = pl.BlockSpec(memory_space=pltpu.VMEM)
    moved = sum(x.size * x.dtype.itemsize for x in (*args, *out_shape))
    return pl.pallas_call(
        kernel,
        out_shape=out_shape,
        in_specs=[whole] * len(args),
        out_specs=[whole] * len(out_shape),
        scratch_shapes=scratch,
        compiler_params=pltpu.CompilerParams(vmem_limit_bytes=limit << 20),
        cost_estimate=pl.CostEstimate(flops=flops, bytes_accessed=moved, transcendentals=0),
    )(*args)


def member():
    return lax.rem(lax.axis_index("seq"), GROUP)


def columns(index):
    return pl.ds(pl.multiple_of(index * HEAD_DIM, HEAD_DIM), HEAD_DIM)


def span(index, size):
    return pl.ds(pl.multiple_of(index * size, size), size)


def iota(dims, axis):
    return lax.broadcasted_iota(jnp.int32, dims, axis)


def averaging(level):
    dims = (BLOCK, BLOCK)
    same = (iota(dims, 0) >> level) == (iota(dims, 1) >> level)
    return jnp.where(same, 2.0**-level, 0.0).astype(BF16)


def pooling():
    dims = (BLOCK // 2, BLOCK)
    return jnp.where(iota(dims, 0) == (iota(dims, 1) >> 1), 0.5, 0.0).astype(BF16)


def spreading(level):
    dims = (BLOCK, BLOCK >> level)
    return jnp.where((iota(dims, 0) >> level) == iota(dims, 1), 2.0**-level, 0.0).astype(BF16)


def halves(x):
    high = x.astype(BF16)
    return high, (x - high.astype(F32)).astype(BF16)


def pack_kernel(q, k, v, *outs):
    me = member()
    for step, out in enumerate(outs):
        for part, source in enumerate((q, k, v)):
            out[part] = source[:, columns(me ^ step)]


def gather_kernel(nb, groups, *refs):
    chunks, (full, spread_q, level_1, level_2, sent) = refs[:GROUP], refs[GROUP:]
    me = member()
    rows = chunks[0].shape[1]
    for step, chunk in enumerate(chunks):
        full[:, span(me ^ step, rows), :] = chunk[...]
    pool, even_1, even_2 = pooling(), averaging(1), averaging(2)
    for b in range(nb):
        at = slice(b * BLOCK, (b + 1) * BLOCK)
        once = dot(even_1, full[0, at]).astype(BF16)
        spread_q[0, at] = once
        spread_q[1, at] = dot(even_2, once).astype(BF16)
        for part in range(2):
            half = BLOCK // 2
            level_1[part, b * half : (b + 1) * half] = dot(pool, full[part + 1, at]).astype(BF16)
    for b in range(nb // 2):
        half = BLOCK // 2
        for part in range(2):
            block = level_1[part, b * BLOCK : (b + 1) * BLOCK]
            level_2[part, b * half : (b + 1) * half] = dot(pool, block).astype(BF16)
    upper = lax.axis_index("seq") >= GROUP
    for part in range(2):
        sent[part] = level_2[part]
        low, high = full[part + 1, :BLOCK], full[part + 1, (nb - 1) * BLOCK :]
        if groups == 2:
            sent[2 + part] = jnp.where(upper, low, high)
        else:
            sent[2 + part] = high
            sent[4 + part] = low


def sibling(b):
    return (b >> 1) ^ 1


def rim_present(groups):
    group = lax.axis_index("seq") // GROUP
    return group > 0, group < groups - 1


def forward_kernel(nb, groups, *refs):
    full, spread_q, level_1, level_2, rim_low, rim_high, prob, *outs, keys, v_t, v1_t, v2_t = refs
    rows = outs[0].shape[0]
    tokens = nb * BLOCK
    me = member()
    present = rim_present(groups)
    keys[:BLOCK] = rim_low[0]
    keys[BLOCK : BLOCK + tokens] = full[1]
    keys[BLOCK + tokens :] = rim_high[0]
    v_t[:, :BLOCK] = rim_low[1].T
    v_t[:, BLOCK + tokens :] = rim_high[1].T
    for b in range(nb):
        v_t[:, (b + 1) * BLOCK : (b + 2) * BLOCK] = full[2, b * BLOCK : (b + 1) * BLOCK].T
    for b in range(level_1.shape[1] // BLOCK):
        v1_t[:, b * BLOCK : (b + 1) * BLOCK] = level_1[1, b * BLOCK : (b + 1) * BLOCK].T
    for b in range(level_2.shape[1] // BLOCK):
        v2_t[:, b * BLOCK : (b + 1) * BLOCK] = level_2[1, b * BLOCK : (b + 1) * BLOCK].T
    for b in range(nb):
        at = slice(b * BLOCK, (b + 1) * BLOCK)
        at_1 = slice(sibling(b) * BLOCK, (sibling(b) + 1) * BLOCK)
        at_2 = slice(0, BLOCK)
        query = full[0, at]
        scores = []
        for near in range(3):
            score = dot_nt(keys[(b + near) * BLOCK : (b + near + 1) * BLOCK], query)
            score = score * (SCALE * LOG2E)
            if b + near == 0:
                score = jnp.where(present[0], score, -jnp.inf)
            if b + near == nb + 1:
                score = jnp.where(present[1], score, -jnp.inf)
            scores.append(score)
        scores.append(dot_nt(level_1[0, at_1], spread_q[0, at]) * (SCALE * LOG2E))
        scores.append(dot_nt(level_2[0, at_2], spread_q[1, at]) * (SCALE * LOG2E))
        top = scores[0].max(0, keepdims=True)
        for score in scores[1:]:
            top = jnp.maximum(top, score.max(0, keepdims=True))
        weights = [jnp.exp2(score - top) for score in scores[:3]]
        weights.append(2.0 * jnp.exp2(scores[3] - top))
        weights.append(4.0 * jnp.exp2(scores[4] - top))
        total = weights[0].sum(0, keepdims=True)
        for weight in weights[1:]:
            total = total + weight.sum(0, keepdims=True)
        inverse = 1.0 / total
        for part, weight in enumerate(weights):
            prob[b, part * BLOCK : (part + 1) * BLOCK] = (weight * inverse).astype(BF16)
        context = dot(v_t[:, b * BLOCK : (b + 3) * BLOCK], prob[b, : 3 * BLOCK])
        context = context + dot(v1_t[:, at_1], prob[b, 3 * BLOCK : 4 * BLOCK])
        context = context + dot(v2_t[:, at_2], prob[b, 4 * BLOCK :])
        attended = context.T.astype(BF16)
        per = rows // BLOCK
        for step, out in enumerate(outs):

            @pl.when(me ^ step == b // per)
            def _():
                out[(b % per) * BLOCK : (b % per + 1) * BLOCK] = attended


def backward_kernel(nb, groups, *refs):
    full, spread_q, level_1, level_2, rim_low, rim_high, prob = refs[:7]
    chunks = refs[7 : 7 + GROUP]
    grad_q, grad_kv, sent, grads, values, k_t, k1_t, k2_t, sums, sums_1, sums_2 = refs[7 + GROUP :]
    rows = chunks[0].shape[0]
    tokens = nb * BLOCK
    me = member()
    for step, chunk in enumerate(chunks):
        grads[span(me ^ step, rows), :] = chunk[...]
    values[:BLOCK] = rim_low[1]
    values[BLOCK : BLOCK + tokens] = full[2]
    values[BLOCK + tokens :] = rim_high[1]
    k_t[:, :BLOCK] = rim_low[0].T
    k_t[:, BLOCK + tokens :] = rim_high[0].T
    for b in range(nb):
        k_t[:, (b + 1) * BLOCK : (b + 2) * BLOCK] = full[1, b * BLOCK : (b + 1) * BLOCK].T
    for b in range(level_1.shape[1] // BLOCK):
        k1_t[:, b * BLOCK : (b + 1) * BLOCK] = level_1[0, b * BLOCK : (b + 1) * BLOCK].T
    for b in range(level_2.shape[1] // BLOCK):
        k2_t[:, b * BLOCK : (b + 1) * BLOCK] = level_2[0, b * BLOCK : (b + 1) * BLOCK].T
    even_1, even_2 = averaging(1), averaging(2)
    sums[...] = jnp.zeros_like(sums)
    sums_1[...] = jnp.zeros_like(sums_1)
    sums_2[...] = jnp.zeros_like(sums_2)
    for b in range(nb):
        at = slice(b * BLOCK, (b + 1) * BLOCK)
        window = slice(b * BLOCK, (b + 3) * BLOCK)
        at_1 = slice(sibling(b) * BLOCK, (sibling(b) + 1) * BLOCK)
        at_2 = slice(0, BLOCK)
        grad = grads[at]
        slope = [
            dot_nt(values[window], grad),
            dot_nt(level_1[1, at_1], grad),
            dot_nt(level_2[1, at_2], grad),
        ]
        parts = (slice(0, 3 * BLOCK), slice(3 * BLOCK, 4 * BLOCK), slice(4 * BLOCK, 5 * BLOCK))
        delta = 0.0
        for part, s in zip(parts, slope):
            delta = delta + (prob[b, part].astype(F32) * s).sum(0, keepdims=True)
        shift = [
            (prob[b, part].astype(F32) * (s - delta)).astype(BF16) for part, s in zip(parts, slope)
        ]
        grad_t = dot(k_t[:, window], shift[0])
        for spread, key_t, s in ((even_1, k1_t[:, at_1], shift[1]), (even_2, k2_t[:, at_2], shift[2])):
            high, low = halves(dot(key_t, s))
            grad_t = grad_t + (dot(high, spread) + dot(low, spread))
        grad_q[at] = (SCALE * grad_t).T.astype(BF16)
        sums[0, window] += dot(shift[0], full[0, at])
        sums[1, window] += dot(prob[b, parts[0]], grad)
        sums_1[0, at_1] += dot(shift[1], spread_q[0, at])
        sums_1[1, at_1] += dot(prob[b, parts[1]], grad)
        sums_2[0, at_2] += dot(shift[2], spread_q[1, at])
        sums_2[1, at_2] += dot(prob[b, parts[2]], grad)
    upper = lax.axis_index("seq") >= GROUP
    for part, factor in enumerate((SCALE, 1.0)):
        spread = spreading(1)
        half = BLOCK // 2
        for b in range(nb):
            total = sums[part, (b + 1) * BLOCK : (b + 2) * BLOCK]
            high, low = halves(sums_1[part, b * half : (b + 1) * half])
            total = total + (dot(spread, high) + dot(spread, low))
            grad_kv[part, b * BLOCK : (b + 1) * BLOCK] = factor * total
        low, high = sums[part, :BLOCK], sums[part, BLOCK + tokens :]
        sent[part] = (factor * sums_2[part]).astype(BF16)
        if groups == 2:
            sent[2 + part] = (factor * jnp.where(upper, low, high)).astype(BF16)
        else:
            sent[2 + part] = (factor * high).astype(BF16)
            sent[4 + part] = (factor * low).astype(BF16)


def combine_kernel(nb, groups, *refs):
    grad_q, grad_kv, got_2, got_low, got_high = refs[:5]
    outs, (final,) = refs[5 : 5 + GROUP], refs[5 + GROUP :]
    rows = outs[0].shape[1]
    me = member()
    present = rim_present(groups)
    spread = spreading(2)
    for part in range(2):
        for b in range(nb):
            total = grad_kv[part, b * BLOCK : (b + 1) * BLOCK]
            quarter = BLOCK // 4
            total = total + dot(spread, got_2[part, b * quarter : (b + 1) * quarter])
            if b == 0:
                total = total + jnp.where(present[0], got_low[part].astype(F32), 0.0)
            if b == nb - 1:
                total = total + jnp.where(present[1], got_high[part].astype(F32), 0.0)
            final[part, b * BLOCK : (b + 1) * BLOCK] = total.astype(BF16)
    for step, out in enumerate(outs):
        at = span(me ^ step, rows)
        out[0] = grad_q[at, :]
        out[1] = final[0, at, :]
        out[2] = final[1, at, :]


def unpack_kernel(*refs):
    chunks, outs = refs[:GROUP], refs[GROUP:]
    me = member()
    for step, chunk in enumerate(chunks):
        for part, out in enumerate(outs):
            out[:, columns(me ^ step)] = chunk[part]


def grad_kernel(out_grad, out_weight, *outs):
    me = member()
    for step, out in enumerate(outs):
        weight = out_weight[span(me ^ step, HEAD_DIM), :]
        out[...] = dot_nt(out_grad[...], weight).astype(BF16)


def project_kernel(*refs):
    chunks, (out_weight, out, attended) = refs[:GROUP], refs[GROUP:]
    me = member()
    for step, chunk in enumerate(chunks):
        attended[:, columns(me ^ step)] = chunk[...]
    out[...] = dot(attended[...], out_weight[...]).astype(BF16)


def moved(x, pairs):
    return lax.ppermute(x, "seq", pairs)


def exchanged(chunks, count):
    got = [chunks[0]]
    for step in range(1, GROUP):
        got.append(moved(chunks[step], [(i, i ^ step) for i in range(count)]))
    return got


def crossed(sent, count):
    across = [(i, i ^ GROUP) for i in range(count)]
    if count == 2 * GROUP:
        got = moved(sent, across)
        return got[:2], got[2:], got[2:]
    up = [(i, i + GROUP) for i in range(count - GROUP)]
    down = [(j, i) for i, j in up]
    return moved(sent[:2], across), moved(sent[2:4], up), moved(sent[4:], down)


def per_device(queries, keys, values, out_weight, out_grad):
    rows, width = queries.shape
    assert width == GROUP * HEAD_DIM and rows == BLOCK
    count = lax.axis_size("seq")
    groups = count // GROUP
    nb = GROUP
    tokens = GROUP * rows
    assert count % (2 * GROUP) == 0

    whole_grad = lax.all_gather(out_grad, "mp", axis=0, tiled=True)
    packed = call(pack_kernel, [shape(3, rows, HEAD_DIM)] * GROUP, (queries, keys, values))
    chunks = exchanged(packed, count)
    full, spread_q, level_1, level_2, sent = call(
        functools.partial(gather_kernel, nb, groups),
        [
            shape(3, tokens, HEAD_DIM),
            shape(2, tokens, HEAD_DIM),
            shape(2, tokens // 2, HEAD_DIM),
            shape(2, tokens // 4, HEAD_DIM),
            shape(4 if groups == 2 else 6, BLOCK, HEAD_DIM),
        ],
        chunks,
    )
    other_2, rim_low, rim_high = crossed(sent, count)
    score_flops = 2 * tokens * 5 * BLOCK * HEAD_DIM
    prob, *attended = call(
        functools.partial(forward_kernel, nb, groups),
        [shape(nb, 5 * BLOCK, BLOCK)] + [shape(rows, HEAD_DIM)] * GROUP,
        (full, spread_q, level_1, other_2, rim_low, rim_high),
        scratch=[
            pltpu.VMEM((tokens + 2 * BLOCK, HEAD_DIM), BF16),
            pltpu.VMEM((HEAD_DIM, tokens + 2 * BLOCK), BF16),
            pltpu.VMEM((HEAD_DIM, tokens // 2), BF16),
            pltpu.VMEM((HEAD_DIM, tokens // 4), BF16),
        ],
        flops=2 * score_flops,
    )
    grad_chunks = call(
        grad_kernel,
        [shape(rows, HEAD_DIM)] * GROUP,
        (whole_grad, out_weight),
        flops=2 * rows * out_weight.size,
    )
    grad_chunks = exchanged(grad_chunks, count)
    attended = exchanged(attended, count)
    (partial_mixed,) = call(
        project_kernel,
        [shape(rows, out_weight.shape[1])],
        (*attended, out_weight),
        scratch=[pltpu.VMEM((rows, width), BF16)],
        flops=2 * rows * out_weight.size,
    )
    mixed = lax.psum_scatter(partial_mixed, "mp", scatter_dimension=0, tiled=True)
    grad_q, grad_kv, sent = call(
        functools.partial(backward_kernel, nb, groups),
        [
            shape(tokens, HEAD_DIM),
            shape(2, tokens, HEAD_DIM, dtype=F32),
            shape(4 if groups == 2 else 6, BLOCK, HEAD_DIM),
        ],
        (full, spread_q, level_1, other_2, rim_low, rim_high, prob, *grad_chunks),
        scratch=[
            pltpu.VMEM((tokens, HEAD_DIM), BF16),
            pltpu.VMEM((tokens + 2 * BLOCK, HEAD_DIM), BF16),
            pltpu.VMEM((HEAD_DIM, tokens + 2 * BLOCK), BF16),
            pltpu.VMEM((HEAD_DIM, tokens // 2), BF16),
            pltpu.VMEM((HEAD_DIM, tokens // 4), BF16),
            pltpu.VMEM((2, tokens + 2 * BLOCK, HEAD_DIM), F32),
            pltpu.VMEM((2, tokens // 2, HEAD_DIM), F32),
            pltpu.VMEM((2, tokens // 4, HEAD_DIM), F32),
        ],
        flops=4 * score_flops,
    )
    got_2, got_low, got_high = crossed(sent, count)
    final = call(
        functools.partial(combine_kernel, nb, groups),
        [shape(3, rows, HEAD_DIM)] * GROUP,
        (grad_q, grad_kv, got_2, got_low, got_high),
        scratch=[pltpu.VMEM((2, tokens, HEAD_DIM), BF16)],
    )
    grads = call(unpack_kernel, [shape(rows, width)] * 3, exchanged(final, count))
    return (mixed, *grads)


def solution(mesh):
    return jax.shard_map(
        per_device,
        mesh=mesh,
        in_specs=(
            P("seq", "mp"),
            P("seq", "mp"),
            P("seq", "mp"),
            P("mp", None),
            P(("seq", "mp"), None),
        ),
        out_specs=(P(("seq", "mp"), None), P("seq", "mp"), P("seq", "mp"), P("seq", "mp")),
        check_vma=False,
    )
```

```python
import functools

import jax
import jax.numpy as jnp
from jax import lax
from jax.experimental import pallas as pl
from jax.experimental.pallas import tpu as pltpu
from jax.sharding import PartitionSpec as P

HEAD_DIM = 128
BLOCK = 256
LEVELS = 2
GROUP = 4
N_MP = 4
SCALE = HEAD_DIM**-0.5
LOG2E = 1.4426950408889634
BF16 = jnp.bfloat16
F32 = jnp.float32


def dot(a, b):
    return lax.dot_general(a, b, (((1,), (0,)), ((), ())), preferred_element_type=F32)


def dot_nt(a, b):
    return lax.dot_general(a, b, (((1,), (1,)), ((), ())), preferred_element_type=F32)


def shape(*dims, dtype=BF16):
    return jax.ShapeDtypeStruct(dims, dtype)


def call(kernel, out_shape, args, scratch=(), flops=0, limit=32, space=pltpu.VMEM):
    whole = pl.BlockSpec(memory_space=pltpu.VMEM)
    moved = sum(x.size * x.dtype.itemsize for x in (*args, *out_shape))
    return pl.pallas_call(
        kernel,
        out_shape=out_shape,
        in_specs=[pl.BlockSpec(memory_space=space)] * len(args),
        out_specs=[whole] * len(out_shape),
        scratch_shapes=scratch,
        compiler_params=pltpu.CompilerParams(vmem_limit_bytes=limit << 20),
        cost_estimate=pl.CostEstimate(flops=flops, bytes_accessed=moved, transcendentals=0),
    )(*args)


def member():
    return lax.rem(lax.axis_index("seq"), GROUP)


def columns(index):
    return pl.ds(pl.multiple_of(index * HEAD_DIM, HEAD_DIM), HEAD_DIM)


def span(index, size):
    return pl.ds(pl.multiple_of(index * size, size), size)


def iota(dims, axis):
    return lax.broadcasted_iota(jnp.int32, dims, axis)


def averaging(level):
    dims = (BLOCK, BLOCK)
    same = (iota(dims, 0) >> level) == (iota(dims, 1) >> level)
    return jnp.where(same, 2.0**-level, 0.0).astype(BF16)


def pooling():
    dims = (BLOCK // 2, BLOCK)
    return jnp.where(iota(dims, 0) == (iota(dims, 1) >> 1), 0.5, 0.0).astype(BF16)


def spreading(level):
    dims = (BLOCK, BLOCK >> level)
    return jnp.where((iota(dims, 0) >> level) == iota(dims, 1), 2.0**-level, 0.0).astype(BF16)


def halves(x):
    high = x.astype(BF16)
    return high, (x - high.astype(F32)).astype(BF16)


def pack_kernel(q, k, v, *refs):
    chunks, rims, tops = refs[:GROUP], refs[GROUP : 2 * GROUP], refs[2 * GROUP : 3 * GROUP]
    held, sems = refs[3 * GROUP :]
    me = member()
    copies = [
        pltpu.make_async_copy(source, held.at[part], sems.at[part])
        for part, source in enumerate((q, k, v))
    ]
    for copy in copies:
        copy.start()
    pool = pooling()
    half = BLOCK // 2
    for part, copy in enumerate(copies):
        copy.wait()
        for step in range(GROUP):
            chunks[step][part] = held[part, :, columns(me ^ step)]
            if part:
                rims[step][part - 1] = held[part, :, columns(me ^ step)]
        if part:
            once = dot(pool, held[part]).astype(BF16)
            held[part, :half] = once
            held[part, half : half + half // 2] = dot(pool[: half // 2, :half], once).astype(BF16)
            for step in range(GROUP):
                tops[step][part - 1] = held[part, half : half + half // 2, columns(me ^ step)]


def sibling(b):
    return (b >> 1) ^ 1


def rim_present(groups):
    group = lax.axis_index("seq") // GROUP
    return group > 0, group < groups - 1


def picked(out, index, refs):
    for step, ref in enumerate(refs):

        @pl.when(index == step)
        def _():
            out[...] = ref[...]


def forward_kernel(nb, groups, *refs):
    chunks, tops, refs = refs[:GROUP], refs[GROUP : 2 * GROUP], refs[2 * GROUP :]
    lows, refs = refs[:GROUP], refs[GROUP:]
    highs = lows
    if groups > 2:
        highs, refs = refs[:GROUP], refs[GROUP:]
    query, near, level_1, level_2, prob, *outs, rim_low, rim_high, v_t, v1_t, v2_t = refs
    tokens = nb * BLOCK
    me = member()
    present = rim_present(groups)
    for step, chunk in enumerate(chunks):
        query[0, span(me ^ step, BLOCK), :] = chunk[0]
        near[:, pl.ds(pl.multiple_of((me ^ step) * BLOCK + BLOCK, BLOCK), BLOCK), :] = chunk[1:]
    quarter = BLOCK // 4
    for step, chunk in enumerate(tops):
        level_2[:, span(me ^ step, quarter), :] = chunk[...]
    if groups > 2:
        picked(rim_low, me ^ 3, lows)
        picked(rim_high, me, highs)
    else:
        picked(rim_low, jnp.where(present[0], me ^ 3, me), lows)
        rim_high = rim_low
    near[:, :BLOCK] = rim_low[...]
    near[:, BLOCK + tokens :] = rim_high[...]
    pool, even_1, even_2 = pooling(), averaging(1), averaging(2)
    half = BLOCK // 2
    for b in range(nb):
        at = slice(b * BLOCK, (b + 1) * BLOCK)
        once = dot(even_1, query[0, at]).astype(BF16)
        query[1, at] = once
        query[2, at] = dot(even_2, once).astype(BF16)
        for part in range(2):
            block = near[part, (b + 1) * BLOCK : (b + 2) * BLOCK]
            level_1[part, b * half : (b + 1) * half] = dot(pool, block).astype(BF16)
    for b in range(nb + 2):
        v_t[:, b * BLOCK : (b + 1) * BLOCK] = near[1, b * BLOCK : (b + 1) * BLOCK].T
    for b in range(nb // 2):
        v1_t[:, b * BLOCK : (b + 1) * BLOCK] = level_1[1, b * BLOCK : (b + 1) * BLOCK].T
    v2_t[...] = level_2[1].T
    for b in range(nb):
        at = slice(b * BLOCK, (b + 1) * BLOCK)
        at_1 = slice(sibling(b) * BLOCK, (sibling(b) + 1) * BLOCK)
        scores = []
        for side in range(3):
            score = dot_nt(near[0, (b + side) * BLOCK : (b + side + 1) * BLOCK], query[0, at])
            score = score * (SCALE * LOG2E)
            if b + side == 0:
                score = jnp.where(present[0], score, -jnp.inf)
            if b + side == nb + 1:
                score = jnp.where(present[1], score, -jnp.inf)
            scores.append(score)
        scores.append(dot_nt(level_1[0, at_1], query[1, at]) * (SCALE * LOG2E))
        scores.append(dot_nt(level_2[0], query[2, at]) * (SCALE * LOG2E))
        top = scores[0].max(0, keepdims=True)
        for score in scores[1:]:
            top = jnp.maximum(top, score.max(0, keepdims=True))
        weights = [jnp.exp2(score - top) for score in scores[:3]]
        weights.append(2.0 * jnp.exp2(scores[3] - top))
        weights.append(4.0 * jnp.exp2(scores[4] - top))
        total = weights[0].sum(0, keepdims=True)
        for weight in weights[1:]:
            total = total + weight.sum(0, keepdims=True)
        inverse = 1.0 / total
        for part, weight in enumerate(weights):
            prob[b, part * BLOCK : (part + 1) * BLOCK] = (weight * inverse).astype(BF16)
        context = dot(v_t[:, b * BLOCK : (b + 3) * BLOCK], prob[b, : 3 * BLOCK])
        context = context + dot(v1_t[:, at_1], prob[b, 3 * BLOCK : 4 * BLOCK])
        context = context + dot(v2_t[...], prob[b, 4 * BLOCK :])
        attended = context.T.astype(BF16)
        for step, out in enumerate(outs):

            @pl.when(me ^ step == b)
            def _():
                out[...] = attended


def backward_kernel(nb, groups, *refs):
    (query, near, level_1, level_2, prob), refs = refs[:5], refs[5:]
    chunks, refs = refs[:GROUP], refs[GROUP:]
    outs, tops, refs = refs[:GROUP], refs[GROUP : 2 * GROUP], refs[2 * GROUP :]
    rims, refs = refs[: 1 if groups == 2 else 2], refs[1 if groups == 2 else 2 :]
    grads, k_t, k1_t, k2_t, sums, sums_1, sums_2 = refs
    tokens = nb * BLOCK
    me = member()
    for step, chunk in enumerate(chunks):
        grads[span(me ^ step, BLOCK), :] = chunk[...]
    for b in range(nb + 2):
        k_t[:, b * BLOCK : (b + 1) * BLOCK] = near[0, b * BLOCK : (b + 1) * BLOCK].T
    for b in range(nb // 2):
        k1_t[:, b * BLOCK : (b + 1) * BLOCK] = level_1[0, b * BLOCK : (b + 1) * BLOCK].T
    k2_t[...] = level_2[0].T
    even_1, even_2 = averaging(1), averaging(2)
    sums[...] = jnp.zeros_like(sums)
    sums_1[...] = jnp.zeros_like(sums_1)
    sums_2[...] = jnp.zeros_like(sums_2)
    for b in range(nb):
        at = slice(b * BLOCK, (b + 1) * BLOCK)
        window = slice(b * BLOCK, (b + 3) * BLOCK)
        at_1 = slice(sibling(b) * BLOCK, (sibling(b) + 1) * BLOCK)
        grad = grads[at]
        slope = [
            dot_nt(near[1, window], grad),
            dot_nt(level_1[1, at_1], grad),
            dot_nt(level_2[1], grad),
        ]
        parts = (slice(0, 3 * BLOCK), slice(3 * BLOCK, 4 * BLOCK), slice(4 * BLOCK, 5 * BLOCK))
        delta = 0.0
        for part, s in zip(parts, slope):
            delta = delta + (prob[b, part].astype(F32) * s).sum(0, keepdims=True)
        shift = [
            (prob[b, part].astype(F32) * (s - delta)).astype(BF16) for part, s in zip(parts, slope)
        ]
        grad_t = dot(k_t[:, window], shift[0])
        for spread, key_t, s in ((even_1, k1_t[:, at_1], shift[1]), (even_2, k2_t[...], shift[2])):
            high, low = halves(dot(key_t, s))
            grad_t = grad_t + (dot(high, spread) + dot(low, spread))
        grad_q = (SCALE * grad_t).T.astype(BF16)
        for step, out in enumerate(outs):

            @pl.when(me ^ step == b)
            def _():
                out[0] = grad_q

        sums[0, window] += dot(shift[0], query[0, at])
        sums[1, window] += dot(prob[b, parts[0]], grad)
        sums_1[0, at_1] += dot(shift[1], query[1, at])
        sums_1[1, at_1] += dot(prob[b, parts[1]], grad)
        sums_2[0] += dot(shift[2], query[2, at])
        sums_2[1] += dot(prob[b, parts[2]], grad)
    upper = lax.axis_index("seq") >= GROUP
    spread = spreading(1)
    half, quarter = BLOCK // 2, BLOCK // 4
    for part, factor in enumerate((SCALE, 1.0)):
        for b in range(nb):
            total = sums[part, (b + 1) * BLOCK : (b + 2) * BLOCK]
            high, low = halves(sums_1[part, b * half : (b + 1) * half])
            total = total + (dot(spread, high) + dot(spread, low))
            total = (factor * total).astype(BF16)
            for step, out in enumerate(outs):

                @pl.when(me ^ step == b)
                def _():
                    out[1 + part] = total

        for step, out in enumerate(tops):
            out[part] = (factor * sums_2[part, span(me ^ step, quarter), :]).astype(BF16)
        low, high = sums[part, :BLOCK], sums[part, BLOCK + tokens :]
        if groups == 2:
            rims[0][part] = (factor * jnp.where(upper, low, high)).astype(BF16)
        else:
            rims[0][part] = (factor * low).astype(BF16)
            rims[1][part] = (factor * high).astype(BF16)


def unpack_kernel(groups, *refs):
    chunks, tops, refs = refs[:GROUP], refs[GROUP : 2 * GROUP], refs[2 * GROUP :]
    rims, outs = refs[:-3], refs[-3:]
    me = member()
    spread = spreading(2)
    for step, chunk in enumerate(chunks):
        at = columns(me ^ step)
        outs[0][:, at] = chunk[0]
        for part in range(2):
            total = chunk[1 + part].astype(F32) + dot(spread, tops[step][part])
            for rim in rims[step::GROUP]:
                total = total + rim[part].astype(F32)
            outs[1 + part][:, at] = total.astype(BF16)


def share():
    return lax.axis_index("mp")


def grad_kernel(*refs):
    pieces, out_weight, outs, whole = refs[:N_MP], refs[N_MP], refs[N_MP + 1 : -1], refs[-1]
    me = member()
    for step, piece in enumerate(pieces):
        whole[span(share() ^ step, piece.shape[0]), :] = piece[...]
    for step, out in enumerate(outs):
        weight = out_weight[span(me ^ step, HEAD_DIM), :]
        out[...] = dot_nt(whole[...], weight).astype(BF16)


def project_kernel(*refs):
    chunks, out_weight, outs, (attended, whole) = refs[:GROUP], refs[GROUP], refs[GROUP + 1 : -2], refs[-2:]
    me = member()
    for step, chunk in enumerate(chunks):
        attended[:, columns(me ^ step)] = chunk[...]
    whole[...] = dot(attended[...], out_weight[...]).astype(BF16)
    for step, out in enumerate(outs):
        out[...] = whole[span(share() ^ step, out.shape[0]), :]


def swapped(x, axis, step):
    return lax.ppermute(x, axis, [(i, i ^ step) for i in range(lax.axis_size(axis))])


def exchanged(chunks):
    return [chunks[0]] + [swapped(chunks[step], "seq", step) for step in range(1, GROUP)]


def rim_pairs(step, count):
    last = GROUP - 1
    up = [(i + last, i + GROUP + (last ^ step)) for i in range(0, count - GROUP, GROUP)]
    down = [(i, i - GROUP + step) for i in range(GROUP, count, GROUP)]
    return [up + down] if count == 2 * GROUP else [up, down]


def per_device(queries, keys, values, out_weight, out_grad):
    rows, width = queries.shape
    assert width == GROUP * HEAD_DIM and rows == BLOCK and lax.axis_size("mp") == N_MP
    count = lax.axis_size("seq")
    groups = count // GROUP
    nb = GROUP
    tokens = GROUP * rows
    assert count % (2 * GROUP) == 0
    quarter = rows // 4
    model = out_weight.shape[1]
    local = rows // N_MP

    chunk_shapes = [shape(3, rows, HEAD_DIM)] * GROUP
    rim_shapes = [shape(2, rows, HEAD_DIM)] * GROUP
    top_shapes = [shape(2, quarter, HEAD_DIM)] * GROUP
    packed = call(
        pack_kernel,
        chunk_shapes + rim_shapes + top_shapes,
        (queries, keys, values),
        scratch=[pltpu.VMEM((3, rows, width), BF16), pltpu.SemaphoreType.DMA((3,))],
        space=pltpu.HBM,
    )
    chunks, rims, tops = packed[:GROUP], packed[GROUP : 2 * GROUP], packed[2 * GROUP :]
    far = swapped(out_grad, "mp", 2)
    rims = [
        lax.ppermute(rims[step], "seq", pairs)
        for side in range(1 if groups == 2 else 2)
        for step in range(GROUP)
        for pairs in [rim_pairs(step, count)[side]]
    ]
    tops = [swapped(tops[step], "seq", GROUP + step) for step in range(GROUP)]
    chunks = exchanged(chunks)
    pieces = [out_grad, swapped(out_grad, "mp", 1), far, swapped(far, "mp", 1)]
    grad_chunks = call(
        grad_kernel,
        [shape(rows, HEAD_DIM)] * GROUP,
        (*pieces, out_weight),
        scratch=[pltpu.VMEM((rows, model), BF16)],
        flops=2 * rows * out_weight.size,
    )
    grad_chunks = exchanged(grad_chunks)
    score_flops = 2 * tokens * 5 * BLOCK * HEAD_DIM
    *kept, attended_0, attended_1, attended_2, attended_3 = call(
        functools.partial(forward_kernel, nb, groups),
        [
            shape(3, tokens, HEAD_DIM),
            shape(2, tokens + 2 * BLOCK, HEAD_DIM),
            shape(2, tokens // 2, HEAD_DIM),
            shape(2, tokens // 4, HEAD_DIM),
            shape(nb, 5 * BLOCK, BLOCK),
        ]
        + [shape(rows, HEAD_DIM)] * GROUP,
        (*chunks, *tops, *rims),
        scratch=[
            pltpu.VMEM((2, BLOCK, HEAD_DIM), BF16),
            pltpu.VMEM((2, BLOCK, HEAD_DIM), BF16),
            pltpu.VMEM((HEAD_DIM, tokens + 2 * BLOCK), BF16),
            pltpu.VMEM((HEAD_DIM, tokens // 2), BF16),
            pltpu.VMEM((HEAD_DIM, tokens // 4), BF16),
        ],
        flops=2 * score_flops,
    )
    attended = exchanged([attended_0, attended_1, attended_2, attended_3])
    mixed = call(
        project_kernel,
        [shape(local, model)] * N_MP,
        (*attended, out_weight),
        scratch=[pltpu.VMEM((rows, width), BF16), pltpu.VMEM((rows, model), BF16)],
        flops=2 * rows * out_weight.size,
    )
    across = (mixed[2].astype(F32) + swapped(mixed[3], "mp", 1).astype(F32)).astype(BF16)
    here = mixed[0].astype(F32) + swapped(mixed[1], "mp", 1).astype(F32)
    mixed = (here + swapped(across, "mp", 2).astype(F32)).astype(BF16)
    grads = call(
        functools.partial(backward_kernel, nb, groups),
        chunk_shapes + top_shapes + rim_shapes[: 1 if groups == 2 else 2],
        (*kept, *grad_chunks),
        scratch=[
            pltpu.VMEM((tokens, HEAD_DIM), BF16),
            pltpu.VMEM((HEAD_DIM, tokens + 2 * BLOCK), BF16),
            pltpu.VMEM((HEAD_DIM, tokens // 2), BF16),
            pltpu.VMEM((HEAD_DIM, tokens // 4), BF16),
            pltpu.VMEM((2, tokens + 2 * BLOCK, HEAD_DIM), F32),
            pltpu.VMEM((2, tokens // 2, HEAD_DIM), F32),
            pltpu.VMEM((2, tokens // 4, HEAD_DIM), F32),
        ],
        flops=4 * score_flops,
    )
    chunks, tops, rims = grads[:GROUP], grads[GROUP : 2 * GROUP], grads[2 * GROUP :]
    rims = [
        lax.ppermute(rims[side], "seq", [(j, i) for i, j in rim_pairs(step, count)[side]])
        for side in range(len(rims))
        for step in range(GROUP)
    ]
    tops = [swapped(tops[step], "seq", GROUP + step) for step in range(GROUP)]
    chunks = exchanged(chunks)
    grads = call(
        functools.partial(unpack_kernel, groups), [shape(rows, width)] * 3, (*chunks, *tops, *rims)
    )
    return (mixed, *grads)


def solution(mesh):
    return jax.shard_map(
        per_device,
        mesh=mesh,
        in_specs=(
            P("seq", "mp"),
            P("seq", "mp"),
            P("seq", "mp"),
            P("mp", None),
            P(("seq", "mp"), None),
        ),
        out_specs=(P(("seq", "mp"), None), P("seq", "mp"), P("seq", "mp"), P("seq", "mp")),
        check_vma=False,
    )
```

```python
import functools

import jax
import jax.numpy as jnp
from jax import lax
from jax.experimental import pallas as pl
from jax.experimental.pallas import tpu as pltpu
from jax.sharding import PartitionSpec as P

HEAD_DIM = 128
BLOCK = 256
LEVELS = 2
GROUP = 4
N_MP = 4
SCALE = HEAD_DIM**-0.5
LOG2E = 1.4426950408889634
BF16 = jnp.bfloat16
F32 = jnp.float32


def dot(a, b):
    return lax.dot_general(a, b, (((1,), (0,)), ((), ())), preferred_element_type=F32)


def dot_nt(a, b):
    return lax.dot_general(a, b, (((1,), (1,)), ((), ())), preferred_element_type=F32)


def shape(*dims, dtype=BF16):
    return jax.ShapeDtypeStruct(dims, dtype)


def call(kernel, out_shape, args, scratch=(), flops=0, limit=32, space=pltpu.VMEM):
    whole = pl.BlockSpec(memory_space=pltpu.VMEM)
    moved = sum(x.size * x.dtype.itemsize for x in (*args, *out_shape))
    return pl.pallas_call(
        kernel,
        out_shape=out_shape,
        in_specs=[pl.BlockSpec(memory_space=space)] * len(args),
        out_specs=[whole] * len(out_shape),
        scratch_shapes=scratch,
        compiler_params=pltpu.CompilerParams(vmem_limit_bytes=limit << 20),
        cost_estimate=pl.CostEstimate(flops=flops, bytes_accessed=moved, transcendentals=0),
    )(*args)


def columns(index):
    return pl.ds(pl.multiple_of(index * HEAD_DIM, HEAD_DIM), HEAD_DIM)


def span(index, size):
    return pl.ds(pl.multiple_of(index * size, size), size)


def iota(dims, axis):
    return lax.broadcasted_iota(jnp.int32, dims, axis)


def averaging(level):
    dims = (BLOCK, BLOCK)
    same = (iota(dims, 0) >> level) == (iota(dims, 1) >> level)
    return jnp.where(same, 2.0**-level, 0.0).astype(BF16)


def pooling():
    dims = (BLOCK // 2, BLOCK)
    return jnp.where(iota(dims, 0) == (iota(dims, 1) >> 1), 0.5, 0.0).astype(BF16)


def spreading(level):
    dims = (BLOCK, BLOCK >> level)
    return jnp.where((iota(dims, 0) >> level) == iota(dims, 1), 2.0**-level, 0.0).astype(BF16)


def halves(x):
    high = x.astype(BF16)
    return high, (x - high.astype(F32)).astype(BF16)


def at_block(b):
    return slice(b * BLOCK, (b + 1) * BLOCK)


def sibling(b):
    return (b >> 1) ^ 1


def rim_present(groups):
    group = lax.axis_index("seq") // GROUP
    return group > 0, group < groups - 1


def pack_kernel(q, k, v, chunks, tops, held, sems):
    copies = [
        pltpu.make_async_copy(source, held.at[part], sems.at[part])
        for part, source in enumerate((k, v, q))
    ]
    for copy in copies:
        copy.start()
    pool = pooling()
    half = BLOCK // 2
    for part, copy in enumerate(copies):
        copy.wait()
        for head in range(GROUP):
            at = slice(head * HEAD_DIM, (head + 1) * HEAD_DIM)
            chunks[head, part] = held[part, :, at]
        if part < 2:
            once = dot(pool, held[part]).astype(BF16)
            twice = dot(pool[: half // 2, :half], once).astype(BF16)
            for head in range(GROUP):
                tops[head, part] = twice[:, head * HEAD_DIM : (head + 1) * HEAD_DIM]


def rim_kernel(groups, full, *outs):
    last = full.shape[0] - 1
    if groups == 2:
        upper = lax.axis_index("seq") >= GROUP
        outs[0][...] = jnp.where(upper, full[0, :2], full[last, :2])
    else:
        outs[0][...] = full[last, :2]
        outs[1][...] = full[0, :2]


def near_sides(b, nb):
    return [side for side in range(3) if 0 <= b + side - 1 < nb]


def local_kernel(nb, full, spread_q, level_1, k_t, v_t, k1_t, v1_t, weights, stats):
    pool, even_1, even_2 = pooling(), averaging(1), averaging(2)
    half = BLOCK // 2
    for b in range(nb):
        once = dot(even_1, full[b, 2]).astype(BF16)
        spread_q[0, b] = once
        spread_q[1, b] = dot(even_2, once).astype(BF16)
        for part, transposed in enumerate((k_t, v_t)):
            level_1[part, b * half : (b + 1) * half] = dot(pool, full[b, part]).astype(BF16)
            transposed[:, at_block(b)] = full[b, part].T
    for c in range(nb // 2):
        for part, transposed in enumerate((k1_t, v1_t)):
            transposed[:, at_block(c)] = level_1[part, at_block(c)].T
    for b in range(nb):
        sides = near_sides(b, nb)
        scores = [dot_nt(full[b + side - 1, 0], full[b, 2]) * (SCALE * LOG2E) for side in sides]
        coarse = dot_nt(level_1[0, at_block(sibling(b))], spread_q[0, b]) * (SCALE * LOG2E)
        top = coarse.max(0, keepdims=True)
        for score in scores:
            top = jnp.maximum(top, score.max(0, keepdims=True))
        weight = 2.0 * jnp.exp2(coarse - top)
        weights[b, 3] = weight
        total = weight.sum(0, keepdims=True)
        for side, score in zip(sides, scores):
            weight = jnp.exp2(score - top)
            weights[b, side] = weight
            total = total + weight.sum(0, keepdims=True)
        stats[b, :1] = top
        stats[b, 1:2] = total


def rim_sides(b, nb):
    return [side for side in range(3) if not 0 <= b + side - 1 < nb]


def forward_kernel(nb, groups, *refs):
    full, spread_q, v_t, v1_t, weights, stats, tops, rim_low, rim_high, prob, attended, level_2 = refs
    present = rim_present(groups)
    quarter = BLOCK // 4
    for step in range(GROUP):
        level_2[:, step * quarter : (step + 1) * quarter] = tops[step]
    v2_t = level_2[1].T
    for b in range(nb):
        sides = rim_sides(b, nb)
        scores = []
        for side in sides:
            score = dot_nt((rim_high if side else rim_low)[0], full[b, 2]) * (SCALE * LOG2E)
            scores.append(jnp.where(present[side // 2], score, -jnp.inf))
        coarse = dot_nt(level_2[0], spread_q[1, b]) * (SCALE * LOG2E)
        old = stats[b, :1]
        top = jnp.maximum(old, coarse.max(0, keepdims=True))
        for score in scores:
            top = jnp.maximum(top, score.max(0, keepdims=True))
        shrink = jnp.exp2(old - top)
        far = 4.0 * jnp.exp2(coarse - top)
        total = shrink * stats[b, 1:2] + far.sum(0, keepdims=True)
        fresh = []
        for score in scores:
            fresh.append(jnp.exp2(score - top))
            total = total + fresh[-1].sum(0, keepdims=True)
        inverse = 1.0 / total
        shrink = shrink * inverse
        prob[b, 4] = (far * inverse).astype(BF16)
        prob[b, 3] = (weights[b, 3] * shrink).astype(BF16)
        context = dot(v2_t, prob[b, 4]) + dot(v1_t[:, at_block(sibling(b))], prob[b, 3])
        for side in near_sides(b, nb):
            prob[b, side] = (weights[b, side] * shrink).astype(BF16)
            context = context + dot(v_t[:, at_block(b + side - 1)], prob[b, side])
        for side, weight in zip(sides, fresh):
            prob[b, side] = (weight * inverse).astype(BF16)
            context = context + dot((rim_high if side else rim_low)[1].T, prob[b, side])
        attended[b] = context.T.astype(BF16)


def slope_kernel(nb, groups, *refs):
    full, spread_q, level_1, tops, rim_low, rim_high, prob, grads, shift, top_out = refs[:10]
    rim_outs, level_2, sums, rim_sums = refs[10:-3], refs[-3], refs[-2], refs[-1]
    quarter = BLOCK // 4
    for step in range(GROUP):
        level_2[:, step * quarter : (step + 1) * quarter] = tops[step]
    for b in range(nb):
        grad = grads[b]
        slopes = []
        for side in range(3):
            if side in near_sides(b, nb):
                value = full[b + side - 1, 1]
            else:
                value = (rim_high if side else rim_low)[1]
            slopes.append(dot_nt(value, grad))
        slopes.append(dot_nt(level_1[1, at_block(sibling(b))], grad))
        slopes.append(dot_nt(level_2[1], grad))
        delta = 0.0
        for part, slope in enumerate(slopes):
            delta = delta + (prob[b, part].astype(F32) * slope).sum(0, keepdims=True)
        for part, slope in enumerate(slopes):
            shift[b, part] = (prob[b, part].astype(F32) * (slope - delta)).astype(BF16)
        for side in rim_sides(b, nb):
            rim_sums[side // 2, 0] = SCALE * dot(shift[b, side], full[b, 2])
            rim_sums[side // 2, 1] = dot(prob[b, side], grad)
        key, value = SCALE * dot(shift[b, 4], spread_q[1, b]), dot(prob[b, 4], grad)
        if b:
            key, value = key + sums[0], value + sums[1]
        if b < nb - 1:
            sums[0], sums[1] = key, value
        else:
            top_out[0], top_out[1] = key.astype(BF16), value.astype(BF16)
    low, high = rim_sums[0], rim_sums[1]
    if groups == 2:
        upper = lax.axis_index("seq") >= GROUP
        rim_outs[0][...] = jnp.where(upper, low, high).astype(BF16)
    else:
        rim_outs[0][...] = high.astype(BF16)
        rim_outs[1][...] = low.astype(BF16)


def backward_kernel(nb, full, spread_q, k_t, k1_t, tops, rim_low, rim_high, prob, shift, grads, *refs):
    grad_q, grad_kv, k2_t, sums_1 = refs
    quarter = BLOCK // 4
    for step in range(GROUP):
        k2_t[:, step * quarter : (step + 1) * quarter] = tops[step, 0].T
    even_1, even_2 = averaging(1), averaging(2)
    for b in range(nb):
        grad_t = 0.0
        for side in range(3):
            if side in near_sides(b, nb):
                key_t = k_t[:, at_block(b + side - 1)]
            else:
                key_t = (rim_high if side else rim_low)[0].T
            grad_t = grad_t + dot(key_t, shift[b, side])
        for spread, key_t, part in ((even_1, k1_t[:, at_block(sibling(b))], 3), (even_2, k2_t[...], 4)):
            high, low = halves(dot(key_t, shift[b, part]))
            grad_t = grad_t + (dot(high, spread) + dot(low, spread))
        grad_q[b] = (SCALE * grad_t).T.astype(BF16)
    for c in range(nb // 2):
        users = [b for b in range(nb) if sibling(b) == c]
        sums_1[0, at_block(c)] = SCALE * sum(dot(shift[b, 3], spread_q[0, b]) for b in users)
        sums_1[1, at_block(c)] = sum(dot(prob[b, 3], grads[b]) for b in users)
    spread = spreading(1)
    half = BLOCK // 2
    for s in range(nb):
        users = [(s + 1 - side, side) for side in range(3) if 0 <= s + 1 - side < nb]
        key = SCALE * sum(dot(shift[b, side], full[b, 2]) for b, side in users)
        value = sum(dot(prob[b, side], grads[b]) for b, side in users)
        for part, total in enumerate((key, value)):
            high, low = halves(sums_1[part, s * half : (s + 1) * half])
            grad_kv[part, s] = total + (dot(spread, high) + dot(spread, low))


def combine_kernel(nb, groups, grad_kv, got_top, got_low, got_high, out):
    present = rim_present(groups)
    spread = spreading(2)
    quarter = BLOCK // 4
    for b in range(nb):
        for part in range(2):
            total = grad_kv[part, b] + dot(spread, got_top[part, b * quarter : (b + 1) * quarter])
            if b == 0:
                total = total + jnp.where(present[0], got_low[part].astype(F32), 0.0)
            if b == nb - 1:
                total = total + jnp.where(present[1], got_high[part].astype(F32), 0.0)
            out[b, part] = total.astype(BF16)


def unpack_kernel(grad_q, grad_kv, *outs):
    for head in range(GROUP):
        at = slice(head * HEAD_DIM, (head + 1) * HEAD_DIM)
        outs[0][:, at] = grad_q[head]
        outs[1][:, at] = grad_kv[head, 0]
        outs[2][:, at] = grad_kv[head, 1]


def share():
    return lax.axis_index("mp")


def grad_kernel(*refs):
    pieces, (out_weight, out, whole) = refs[:N_MP], refs[N_MP:]
    for step, piece in enumerate(pieces):
        whole[span(share() ^ step, piece.shape[0]), :] = piece[...]
    rows = dot_nt(whole[...], out_weight[...]).astype(BF16)
    for head in range(GROUP):
        out[head] = rows[:, head * HEAD_DIM : (head + 1) * HEAD_DIM]


def project_kernel(chunks, out_weight, *refs):
    outs, (attended, whole) = refs[:-2], refs[-2:]
    for head in range(GROUP):
        attended[:, head * HEAD_DIM : (head + 1) * HEAD_DIM] = chunks[head]
    whole[...] = dot(attended[...], out_weight[...]).astype(BF16)
    for step, out in enumerate(outs):
        out[...] = whole[span(share() ^ step, out.shape[0]), :]


def swapped(x, axis, step):
    return lax.ppermute(x, axis, [(i, i ^ step) for i in range(lax.axis_size(axis))])


def regrouped(x):
    count = lax.axis_size("seq")
    members = [list(range(i, i + GROUP)) for i in range(0, count, GROUP)]
    return lax.all_to_all(x, "seq", 0, 0, axis_index_groups=members)


def beside(arrays):
    count = lax.axis_size("seq")
    if len(arrays) == 1:
        got = swapped(arrays[0], "seq", GROUP)
        return got, got
    up = [(i, i + GROUP) for i in range(count - GROUP)]
    return (
        lax.ppermute(arrays[0], "seq", up),
        lax.ppermute(arrays[1], "seq", [(j, i) for i, j in up]),
    )


def per_device(queries, keys, values, out_weight, out_grad):
    rows, width = queries.shape
    assert width == GROUP * HEAD_DIM and rows == BLOCK and lax.axis_size("mp") == N_MP
    count = lax.axis_size("seq")
    assert count % (2 * GROUP) == 0
    groups = count // GROUP
    nb = GROUP
    tokens = nb * rows
    half, quarter = rows // 2, rows // 4
    model = out_weight.shape[1]
    block = shape(2, rows, HEAD_DIM)
    rims = [block] * (1 if groups == 2 else 2)
    score_flops = 2 * tokens * 5 * BLOCK * HEAD_DIM
    weight_flops = 2 * rows * out_weight.size

    chunks, tops = call(
        pack_kernel,
        [shape(GROUP, 3, rows, HEAD_DIM), shape(GROUP, 2, quarter, HEAD_DIM)],
        (queries, keys, values),
        scratch=[pltpu.VMEM((3, rows, width), BF16), pltpu.SemaphoreType.DMA((3,))],
        space=pltpu.HBM,
    )
    tops = swapped(tops, "seq", GROUP)
    far = swapped(out_grad, "mp", 2)
    pieces = [out_grad, swapped(out_grad, "mp", 1), far, swapped(far, "mp", 1)]
    full = regrouped(chunks)
    rim_low, rim_high = beside(call(functools.partial(rim_kernel, groups), rims, (full,)))
    tops = regrouped(tops)
    (grads,) = call(
        grad_kernel,
        [shape(GROUP, rows, HEAD_DIM)],
        (*pieces, out_weight),
        scratch=[pltpu.VMEM((rows, model), BF16)],
        flops=weight_flops,
    )
    grads = regrouped(grads)
    spread_q, level_1, k_t, v_t, k1_t, v1_t, weights, stats = call(
        functools.partial(local_kernel, nb),
        [
            shape(2, nb, rows, HEAD_DIM),
            shape(2, tokens // 2, HEAD_DIM),
            shape(HEAD_DIM, tokens),
            shape(HEAD_DIM, tokens),
            shape(HEAD_DIM, tokens // 2),
            shape(HEAD_DIM, tokens // 2),
            shape(nb, 4, BLOCK, BLOCK, dtype=F32),
            shape(nb, 8, BLOCK, dtype=F32),
        ],
        (full,),
        flops=score_flops,
    )
    prob, attended = call(
        functools.partial(forward_kernel, nb, groups),
        [shape(nb, 5, BLOCK, BLOCK), shape(nb, rows, HEAD_DIM)],
        (full, spread_q, v_t, v1_t, weights, stats, tops, rim_low, rim_high),
        scratch=[pltpu.VMEM((2, BLOCK, HEAD_DIM), BF16)],
        flops=score_flops,
    )
    attended = regrouped(attended)
    mixed = call(
        project_kernel,
        [shape(rows // N_MP, model)] * N_MP,
        (attended, out_weight),
        scratch=[pltpu.VMEM((rows, width), BF16), pltpu.VMEM((rows, model), BF16)],
        flops=weight_flops,
    )
    across = (mixed[2].astype(F32) + swapped(mixed[3], "mp", 1).astype(F32)).astype(BF16)
    here = mixed[0].astype(F32) + swapped(mixed[1], "mp", 1).astype(F32)
    mixed = (here + swapped(across, "mp", 2).astype(F32)).astype(BF16)
    shift, top_grads, *rim_grads = call(
        functools.partial(slope_kernel, nb, groups),
        [shape(nb, 5, BLOCK, BLOCK), block] + rims,
        (full, spread_q, level_1, tops, rim_low, rim_high, prob, grads),
        scratch=[
            pltpu.VMEM((2, BLOCK, HEAD_DIM), BF16),
            pltpu.VMEM((2, BLOCK, HEAD_DIM), F32),
            pltpu.VMEM((2, 2, BLOCK, HEAD_DIM), F32),
        ],
        flops=score_flops,
    )
    top_grads = swapped(top_grads, "seq", GROUP)
    got_low, got_high = beside(rim_grads)
    grad_q, grad_kv = call(
        functools.partial(backward_kernel, nb),
        [shape(nb, rows, HEAD_DIM), shape(2, nb, rows, HEAD_DIM, dtype=F32)],
        (full, spread_q, k_t, k1_t, tops, rim_low, rim_high, prob, shift, grads),
        scratch=[pltpu.VMEM((HEAD_DIM, BLOCK), BF16), pltpu.VMEM((2, tokens // 2, HEAD_DIM), F32)],
        flops=3 * score_flops,
    )
    grad_q = regrouped(grad_q)
    (grad_kv,) = call(
        functools.partial(combine_kernel, nb, groups),
        [shape(nb, 2, rows, HEAD_DIM)],
        (grad_kv, top_grads, got_low, got_high),
    )
    grads = call(unpack_kernel, [shape(rows, width)] * 3, (grad_q, regrouped(grad_kv)))
    return (mixed, *grads)


def solution(mesh):
    return jax.shard_map(
        per_device,
        mesh=mesh,
        in_specs=(
            P("seq", "mp"),
            P("seq", "mp"),
            P("seq", "mp"),
            P("mp", None),
            P(("seq", "mp"), None),
        ),
        out_specs=(P(("seq", "mp"), None), P("seq", "mp"), P("seq", "mp"), P("seq", "mp")),
        check_vma=False,
    )
```

```python
import functools

import jax
import jax.numpy as jnp
from jax import lax
from jax.experimental import pallas as pl
from jax.experimental.pallas import tpu as pltpu
from jax.sharding import PartitionSpec as P

HEAD_DIM = 128
BLOCK = 256
LEVELS = 2
GROUP = 4
N_MP = 4
SCALE = HEAD_DIM**-0.5
LOG2E = 1.4426950408889634
BF16 = jnp.bfloat16
F32 = jnp.float32


def dot(a, b):
    return lax.dot_general(a, b, (((1,), (0,)), ((), ())), preferred_element_type=F32)


def dot_nt(a, b):
    return lax.dot_general(a, b, (((1,), (1,)), ((), ())), preferred_element_type=F32)


def shape(*dims, dtype=BF16):
    return jax.ShapeDtypeStruct(dims, dtype)


def call(kernel, out_shape, args, scratch=(), flops=0, limit=32, space=pltpu.VMEM):
    whole = pl.BlockSpec(memory_space=pltpu.VMEM)
    moved = sum(x.size * x.dtype.itemsize for x in (*args, *out_shape))
    return pl.pallas_call(
        kernel,
        out_shape=out_shape,
        in_specs=[pl.BlockSpec(memory_space=space)] * len(args),
        out_specs=[whole] * len(out_shape),
        scratch_shapes=scratch,
        compiler_params=pltpu.CompilerParams(vmem_limit_bytes=limit << 20),
        cost_estimate=pl.CostEstimate(flops=flops, bytes_accessed=moved if flops else 0, transcendentals=0),
    )(*args)


def columns(index):
    return pl.ds(pl.multiple_of(index * HEAD_DIM, HEAD_DIM), HEAD_DIM)


def span(index, size):
    return pl.ds(pl.multiple_of(index * size, size), size)


def iota(dims, axis):
    return lax.broadcasted_iota(jnp.int32, dims, axis)


def averaging(level):
    dims = (BLOCK, BLOCK)
    same = (iota(dims, 0) >> level) == (iota(dims, 1) >> level)
    return jnp.where(same, 2.0**-level, 0.0).astype(BF16)


def pooling():
    dims = (BLOCK // 2, BLOCK)
    return jnp.where(iota(dims, 0) == (iota(dims, 1) >> 1), 0.5, 0.0).astype(BF16)


def spreading(level):
    dims = (BLOCK, BLOCK >> level)
    return jnp.where((iota(dims, 0) >> level) == iota(dims, 1), 2.0**-level, 0.0).astype(BF16)


def halves(x):
    high = x.astype(BF16)
    return high, (x - high.astype(F32)).astype(BF16)


def at_block(b):
    return slice(b * BLOCK, (b + 1) * BLOCK)


def sibling(b):
    return (b >> 1) ^ 1


def rim_present(groups):
    group = lax.axis_index("seq") // GROUP
    return group > 0, group < groups - 1


def member():
    return lax.rem(lax.axis_index("seq"), GROUP)


def columns(index):
    return pl.ds(pl.multiple_of(index * HEAD_DIM, HEAD_DIM), HEAD_DIM)


def pack_kernel(k, v, *outs):
    me = member()
    for step, out in enumerate(outs):
        for part, source in enumerate((k, v)):
            out[part] = source[:, columns(me ^ step)]


def gather_kernel(nb, groups, q, far, *refs):
    chunks, (near, level_1, far_out, *refs) = refs[:GROUP], refs[GROUP:]
    far_out[...] = far[...]
    rims, queries = refs[:-GROUP], refs[-GROUP:]
    me = member()
    for step, chunk in enumerate(chunks):
        near[me ^ step] = chunk[...]
        queries[step][...] = q[:, columns(me ^ step)]
    pool = pooling()
    half = BLOCK // 2
    for part in range(2):
        for b in range(nb):
            level_1[part, b * half : (b + 1) * half] = dot(pool, near[b, part]).astype(BF16)
        for c in range(nb // 2):
            block = dot(pool, level_1[part, at_block(c)]).astype(BF16)
            rims[0][part, c * half : (c + 1) * half] = block
    if groups == 2:
        upper = lax.axis_index("seq") >= GROUP
        rims[0][2:] = jnp.where(upper, near[0], near[nb - 1])
    else:
        rims[1][...] = near[nb - 1]
        rims[2][...] = near[0]


def from_others(groups, refs):
    if groups == 2:
        return (refs[0].at[:2], refs[0].at[2:], refs[0].at[2:]), refs[1:]
    return refs[:3], refs[3:]


def near_sides(b, nb):
    return [side for side in range(3) if 0 <= b + side - 1 < nb]


def local_kernel(nb, near, level_1, *refs):
    chunks, _, (query, k_t, v_t, k1_t, v1_t, weights, stats) = refs[:GROUP], refs[GROUP], refs[GROUP + 1 :]
    me = member()
    for step, chunk in enumerate(chunks):
        query[0, me ^ step] = chunk[...]
    even_1, even_2 = averaging(1), averaging(2)
    for b in range(nb):
        once = dot(even_1, query[0, b]).astype(BF16)
        query[1, b] = once
        query[2, b] = dot(even_2, once).astype(BF16)
        for part, transposed in enumerate((k_t, v_t)):
            transposed[:, at_block(b)] = near[b, part].T
    for c in range(nb // 2):
        for part, transposed in enumerate((k1_t, v1_t)):
            transposed[:, at_block(c)] = level_1[part, at_block(c)].T
    for b in range(nb):
        sides = near_sides(b, nb)
        scores = [dot_nt(near[b + side - 1, 0], query[0, b]) * (SCALE * LOG2E) for side in sides]
        coarse = dot_nt(level_1[0, at_block(sibling(b))], query[1, b]) * (SCALE * LOG2E)
        top = coarse.max(0, keepdims=True)
        for score in scores:
            top = jnp.maximum(top, score.max(0, keepdims=True))
        weight = 2.0 * jnp.exp2(coarse - top)
        weights[b, 3] = weight
        total = weight.sum(0, keepdims=True)
        for side, score in zip(sides, scores):
            weight = jnp.exp2(score - top)
            weights[b, side] = weight
            total = total + weight.sum(0, keepdims=True)
        stats[b, :1] = top
        stats[b, 1:2] = total


def rim_sides(b, nb):
    return [side for side in range(3) if not 0 <= b + side - 1 < nb]


def forward_kernel(nb, groups, *refs):
    (query, v_t, v1_t, weights, stats), refs = refs[:5], refs[5:]
    (top_2, rim_low, rim_high), refs = from_others(groups, refs)
    prob, *outs, attended = refs[GROUP:]
    present = rim_present(groups)
    v2_t = top_2[1].T
    for b in range(nb):
        sides = rim_sides(b, nb)
        scores = []
        for side in sides:
            score = dot_nt((rim_high if side else rim_low)[0], query[0, b]) * (SCALE * LOG2E)
            scores.append(jnp.where(present[side // 2], score, -jnp.inf))
        coarse = dot_nt(top_2[0], query[2, b]) * (SCALE * LOG2E)
        old = stats[b, :1]
        top = jnp.maximum(old, coarse.max(0, keepdims=True))
        for score in scores:
            top = jnp.maximum(top, score.max(0, keepdims=True))
        shrink = jnp.exp2(old - top)
        far = 4.0 * jnp.exp2(coarse - top)
        total = shrink * stats[b, 1:2] + far.sum(0, keepdims=True)
        fresh = []
        for score in scores:
            fresh.append(jnp.exp2(score - top))
            total = total + fresh[-1].sum(0, keepdims=True)
        inverse = 1.0 / total
        shrink = shrink * inverse
        prob[b, 4] = (far * inverse).astype(BF16)
        prob[b, 3] = (weights[b, 3] * shrink).astype(BF16)
        context = dot(v2_t, prob[b, 4]) + dot(v1_t[:, at_block(sibling(b))], prob[b, 3])
        for side in near_sides(b, nb):
            prob[b, side] = (weights[b, side] * shrink).astype(BF16)
            context = context + dot(v_t[:, at_block(b + side - 1)], prob[b, side])
        for side, weight in zip(sides, fresh):
            prob[b, side] = (weight * inverse).astype(BF16)
            context = context + dot((rim_high if side else rim_low)[1].T, prob[b, side])
        attended[b] = context.T.astype(BF16)
    me = member()
    for step, out in enumerate(outs):
        out[...] = attended[me ^ step]


def slope_kernel(nb, groups, *refs):
    (query, near, level_1, prob), refs = refs[:4], refs[4:]
    (top_2, rim_low, rim_high), refs = from_others(groups, refs)
    chunks, (grads, shift, *rim_outs, sums, rim_sums) = refs[:GROUP], refs[GROUP:]
    me = member()
    for step, chunk in enumerate(chunks):
        grads[me ^ step] = chunk[...]
    for b in range(nb):
        grad = grads[b]
        slopes = []
        for side in range(3):
            if side in near_sides(b, nb):
                value = near[b + side - 1, 1]
            else:
                value = (rim_high if side else rim_low)[1]
            slopes.append(dot_nt(value, grad))
        slopes.append(dot_nt(level_1[1, at_block(sibling(b))], grad))
        slopes.append(dot_nt(top_2[1], grad))
        delta = 0.0
        for part, slope in enumerate(slopes):
            delta = delta + (prob[b, part].astype(F32) * slope).sum(0, keepdims=True)
        for part, slope in enumerate(slopes):
            shift[b, part] = (prob[b, part].astype(F32) * (slope - delta)).astype(BF16)
        for side in rim_sides(b, nb):
            rim_sums[side // 2, 0] = SCALE * dot(shift[b, side], query[0, b])
            rim_sums[side // 2, 1] = dot(prob[b, side], grad)
        key, value = SCALE * dot(shift[b, 4], query[2, b]), dot(prob[b, 4], grad)
        if b:
            key, value = key + sums[0], value + sums[1]
        if b < nb - 1:
            sums[0], sums[1] = key, value
        else:
            rim_outs[0][0], rim_outs[0][1] = key.astype(BF16), value.astype(BF16)
    low, high = rim_sums[0], rim_sums[1]
    if groups == 2:
        upper = lax.axis_index("seq") >= GROUP
        rim_outs[0][2:] = jnp.where(upper, low, high).astype(BF16)
    else:
        rim_outs[1][...] = high.astype(BF16)
        rim_outs[2][...] = low.astype(BF16)


def backward_kernel(nb, groups, *refs):
    (query, k_t, k1_t, prob, shift, grads), refs = refs[:6], refs[6:]
    (top_2, rim_low, rim_high), refs = from_others(groups, refs)
    *outs, grad_kv, grad_q, sums_1 = refs
    k2_t = top_2[0].T
    even_1, even_2 = averaging(1), averaging(2)
    for b in range(nb):
        grad_t = 0.0
        for side in range(3):
            if side in near_sides(b, nb):
                key_t = k_t[:, at_block(b + side - 1)]
            else:
                key_t = (rim_high if side else rim_low)[0].T
            grad_t = grad_t + dot(key_t, shift[b, side])
        for spread, key_t, part in ((even_1, k1_t[:, at_block(sibling(b))], 3), (even_2, k2_t, 4)):
            high, low = halves(dot(key_t, shift[b, part]))
            grad_t = grad_t + (dot(high, spread) + dot(low, spread))
        grad_q[b] = (SCALE * grad_t).T.astype(BF16)
    me = member()
    for step, out in enumerate(outs):
        out[...] = grad_q[me ^ step]
    for c in range(nb // 2):
        users = [b for b in range(nb) if sibling(b) == c]
        sums_1[0, at_block(c)] = SCALE * sum(dot(shift[b, 3], query[1, b]) for b in users)
        sums_1[1, at_block(c)] = sum(dot(prob[b, 3], grads[b]) for b in users)
    spread = spreading(1)
    half = BLOCK // 2
    for s in range(nb):
        users = [(s + 1 - side, side) for side in range(3) if 0 <= s + 1 - side < nb]
        key = SCALE * sum(dot(shift[b, side], query[0, b]) for b, side in users)
        value = sum(dot(prob[b, side], grads[b]) for b, side in users)
        for part, total in enumerate((key, value)):
            high, low = halves(sums_1[part, s * half : (s + 1) * half])
            grad_kv[part, s] = total + (dot(spread, high) + dot(spread, low))


def share_kernel(kept, got, _, across, here):
    across[...] = (kept[1].astype(F32) + got[1].astype(F32)).astype(BF16)
    here[...] = kept[0].astype(F32) + got[0].astype(F32)


def combine_kernel(nb, groups, grad_kv, *refs):
    (got_top, got_low, got_high), refs = from_others(groups, refs)
    chunks, (grad_q, *outs, out) = refs[:GROUP], refs[GROUP:]
    me = member()
    for step, chunk in enumerate(chunks):
        grad_q[:, columns(me ^ step)] = chunk[...]
    present = rim_present(groups)
    spread = spreading(2)
    quarter = BLOCK // 4
    for b in range(nb):
        for part in range(2):
            total = grad_kv[part, b] + dot(spread, got_top[part, b * quarter : (b + 1) * quarter])
            if b == 0:
                total = total + jnp.where(present[0], got_low[part].astype(F32), 0.0)
            if b == nb - 1:
                total = total + jnp.where(present[1], got_high[part].astype(F32), 0.0)
            out[b, part] = total.astype(BF16)
    for step, chunk in enumerate(outs):
        chunk[...] = out[me ^ step]


def unpack_kernel(*refs):
    here, across, *refs = refs
    grad_kv, outs = refs[:GROUP], refs[GROUP:]
    outs[2][...] = (here[...] + across[...].astype(F32)).astype(BF16)
    me = member()
    for step in range(GROUP):
        at = columns(me ^ step)
        outs[0][:, at] = grad_kv[step][0]
        outs[1][:, at] = grad_kv[step][1]


def share():
    return lax.axis_index("mp")


def grad_kernel(*refs):
    pieces, out_weight, outs, (whole, heads) = refs[:N_MP], refs[N_MP], refs[N_MP + 1 : -2], refs[-2:]
    me = member()
    for step, piece in enumerate(pieces):
        whole[span(share() ^ step, piece.shape[0]), :] = piece[...]
    heads[...] = dot_nt(whole[...], out_weight[...]).astype(BF16)
    for step, out in enumerate(outs):
        out[...] = heads[:, columns(me ^ step)]


def project_kernel(*refs):
    chunks, out_weight, (kept, sent, attended, whole) = refs[:GROUP], refs[GROUP], refs[-4:]
    me = member()
    for step, chunk in enumerate(chunks):
        attended[:, columns(me ^ step)] = chunk[...]
    whole[...] = dot(attended[...], out_weight[...]).astype(BF16)
    rows = kept.shape[1]
    for far in range(2):
        kept[far] = whole[span(share() ^ (2 * far), rows), :]
        sent[far] = whole[span(share() ^ (2 * far + 1), rows), :]


def swapped(x, axis, step):
    return lax.ppermute(x, axis, [(i, i ^ step) for i in range(lax.axis_size(axis))])


def exchanged(chunks):
    got = {step: swapped(chunks[step], "seq", step) for step in (3, 1, 2)}
    return [chunks[0]] + [got[step] for step in range(1, GROUP)]


def crossed(arrays):
    count = lax.axis_size("seq")
    across = swapped(arrays[0], "seq", GROUP)
    if len(arrays) == 1:
        return [across]
    up = [(i, i + GROUP) for i in range(count - GROUP)]
    down = [(j, i) for i, j in up]
    return [across, lax.ppermute(arrays[1], "seq", up), lax.ppermute(arrays[2], "seq", down)]


def per_device(queries, keys, values, out_weight, out_grad):
    rows, width = queries.shape
    assert width == GROUP * HEAD_DIM and rows == BLOCK and lax.axis_size("mp") == N_MP
    count = lax.axis_size("seq")
    assert count % (2 * GROUP) == 0
    groups = count // GROUP
    nb = GROUP
    tokens = nb * rows
    half, quarter = rows // 2, rows // 4
    model = out_weight.shape[1]
    block = shape(2, rows, HEAD_DIM)
    sent = [shape(4, rows, HEAD_DIM)] if groups == 2 else [block] * 3
    score_flops = 2 * tokens * 5 * BLOCK * HEAD_DIM
    weight_flops = 2 * rows * out_weight.size

    chunk = shape(rows, HEAD_DIM)
    pairs = call(pack_kernel, [block] * GROUP, (keys, values))
    far = swapped(out_grad, "mp", 2)
    beside_1 = swapped(out_grad, "mp", 1)
    pairs = exchanged(pairs)
    near, level_1, far, *refs = call(
        functools.partial(gather_kernel, nb, groups),
        [shape(nb, 2, rows, HEAD_DIM), shape(2, tokens // 2, HEAD_DIM), shape(*far.shape)]
        + sent
        + [chunk] * GROUP,
        (queries, far, *pairs),
    )
    others = crossed(refs[:-GROUP])
    query_chunks = exchanged(refs[-GROUP:])
    pieces = [out_grad, beside_1, far, swapped(far, "mp", 1)]
    grad_chunks = call(
        grad_kernel,
        [chunk] * GROUP,
        (*pieces, out_weight),
        scratch=[pltpu.VMEM((rows, model), BF16), pltpu.VMEM((rows, width), BF16)],
        flops=weight_flops,
    )
    query, k_t, v_t, k1_t, v1_t, weights, stats = call(
        functools.partial(local_kernel, nb),
        [
            shape(3, nb, rows, HEAD_DIM),
            shape(HEAD_DIM, tokens),
            shape(HEAD_DIM, tokens),
            shape(HEAD_DIM, tokens // 2),
            shape(HEAD_DIM, tokens // 2),
            shape(nb, 4, BLOCK, BLOCK, dtype=F32),
            shape(nb, 8, BLOCK, dtype=F32),
        ],
        (near, level_1, *query_chunks, grad_chunks[0]),
        flops=score_flops,
    )
    grad_chunks = exchanged(grad_chunks)
    prob, *attended = call(
        functools.partial(forward_kernel, nb, groups),
        [shape(nb, 5, BLOCK, BLOCK)] + [chunk] * GROUP,
        (query, v_t, v1_t, weights, stats, *others, *grad_chunks),
        scratch=[pltpu.VMEM((nb, rows, HEAD_DIM), BF16)],
        flops=score_flops,
    )
    attended = exchanged(attended)
    grads, shift, *rim_grads = call(
        functools.partial(slope_kernel, nb, groups),
        [shape(nb, rows, HEAD_DIM), shape(nb, 5, BLOCK, BLOCK)] + sent,
        (query, near, level_1, prob, *others, *grad_chunks),
        scratch=[pltpu.VMEM((2, BLOCK, HEAD_DIM), F32), pltpu.VMEM((2, 2, BLOCK, HEAD_DIM), F32)],
        flops=score_flops,
    )
    other_grads = crossed(rim_grads)
    *grad_q, grad_kv = call(
        functools.partial(backward_kernel, nb, groups),
        [chunk] * GROUP + [shape(2, nb, rows, HEAD_DIM, dtype=F32)],
        (query, k_t, k1_t, prob, shift, grads, *others),
        scratch=[
            pltpu.VMEM((nb, rows, HEAD_DIM), BF16),
            pltpu.VMEM((2, tokens // 2, HEAD_DIM), F32),
        ],
        flops=1,
    )
    grad_q = exchanged(grad_q)
    local = rows // N_MP
    shares = shape(2, local, model)
    kept, given = call(
        project_kernel,
        [shares] * 2,
        (*attended, out_weight, grads),
        scratch=[pltpu.VMEM((rows, width), BF16), pltpu.VMEM((rows, model), BF16)],
        flops=weight_flops,
    )
    grad_q, *grad_kv = call(
        functools.partial(combine_kernel, nb, groups),
        [shape(rows, width)] + [block] * GROUP,
        (grad_kv, *other_grads, *grad_q),
        scratch=[pltpu.VMEM((nb, 2, rows, HEAD_DIM), BF16)],
        flops=20 * score_flops,
    )
    across, here = call(
        share_kernel,
        [shape(local, model), shape(local, model, dtype=F32)],
        (kept, swapped(given, "mp", 1), grad_kv[0]),
    )
    grad_kv = exchanged(grad_kv)
    across = swapped(across, "mp", 2)
    grad_k, grad_v, mixed = call(
        unpack_kernel,
        [shape(rows, width)] * 2 + [shape(local, model)],
        (here, across, *grad_kv),
    )
    return mixed, grad_q, grad_k, grad_v


def solution(mesh):
    return jax.shard_map(
        per_device,
        mesh=mesh,
        in_specs=(
            P("seq", "mp"),
            P("seq", "mp"),
            P("seq", "mp"),
            P("mp", None),
            P(("seq", "mp"), None),
        ),
        out_specs=(P(("seq", "mp"), None), P("seq", "mp"), P("seq", "mp"), P("seq", "mp")),
        check_vma=False,
    )
```

```python
import functools

import jax
import jax.numpy as jnp
from jax import lax
from jax.experimental import pallas as pl
from jax.experimental.pallas import tpu as pltpu
from jax.sharding import PartitionSpec as P

HEAD_DIM = 128
BLOCK = 256
LEVELS = 2
GROUP = 4
N_MP = 4
SCALE = HEAD_DIM**-0.5
LOG2E = 1.4426950408889634
BF16 = jnp.bfloat16
F32 = jnp.float32


def dot(a, b):
    return lax.dot_general(a, b, (((1,), (0,)), ((), ())), preferred_element_type=F32)


def dot_nt(a, b):
    return lax.dot_general(a, b, (((1,), (1,)), ((), ())), preferred_element_type=F32)


def shape(*dims, dtype=BF16):
    return jax.ShapeDtypeStruct(dims, dtype)


def call(kernel, out_shape, args, scratch=(), flops=0, limit=32, space=pltpu.VMEM):
    whole = pl.BlockSpec(memory_space=pltpu.VMEM)
    moved = sum(x.size * x.dtype.itemsize for x in (*args, *out_shape))
    return pl.pallas_call(
        kernel,
        out_shape=out_shape,
        in_specs=[pl.BlockSpec(memory_space=space)] * len(args),
        out_specs=[whole] * len(out_shape),
        scratch_shapes=scratch,
        compiler_params=pltpu.CompilerParams(vmem_limit_bytes=limit << 20),
        cost_estimate=pl.CostEstimate(flops=flops, bytes_accessed=moved if flops else 0, transcendentals=0),
    )(*args)


def columns(index):
    return pl.ds(pl.multiple_of(index * HEAD_DIM, HEAD_DIM), HEAD_DIM)


def span(index, size):
    return pl.ds(pl.multiple_of(index * size, size), size)


def iota(dims, axis):
    return lax.broadcasted_iota(jnp.int32, dims, axis)


def averaging(level):
    dims = (BLOCK, BLOCK)
    same = (iota(dims, 0) >> level) == (iota(dims, 1) >> level)
    return jnp.where(same, 2.0**-level, 0.0).astype(BF16)


def pooling():
    dims = (BLOCK // 2, BLOCK)
    return jnp.where(iota(dims, 0) == (iota(dims, 1) >> 1), 0.5, 0.0).astype(BF16)


def spreading(level):
    dims = (BLOCK, BLOCK >> level)
    return jnp.where((iota(dims, 0) >> level) == iota(dims, 1), 2.0**-level, 0.0).astype(BF16)


def halves(x):
    high = x.astype(BF16)
    return high, (x - high.astype(F32)).astype(BF16)


def at_block(b):
    return slice(b * BLOCK, (b + 1) * BLOCK)


def sibling(b):
    return (b >> 1) ^ 1


def rim_present(groups):
    group = lax.axis_index("seq") // GROUP
    return group > 0, group < groups - 1


def member():
    return lax.rem(lax.axis_index("seq"), GROUP)


def columns(index):
    return pl.ds(pl.multiple_of(index * HEAD_DIM, HEAD_DIM), HEAD_DIM)


def pack_kernel(q, k, v, out_grad, *refs):
    outs, (out_grad_out, sems) = refs[:GROUP], refs[GROUP:]
    me = member()
    copies = [pltpu.make_async_copy(out_grad, out_grad_out, sems.at[0])]
    for step in (3, 1, 2, 0):
        for part, source in enumerate((k, v, q)):
            piece = source.at[:, columns(me ^ step)]
            copies.append(pltpu.make_async_copy(piece, outs[step].at[part], sems.at[len(copies)]))
    for copy in copies:
        copy.start()
    for copy in copies:
        copy.wait()


def copy_kernel(x, out):
    out[...] = x[...]


def gather_kernel(nb, groups, far, *refs):
    chunks, (far_out, near, queries, level_1, *rims) = refs[:GROUP], refs[GROUP:]
    far_out[...] = far[...]
    me = member()
    for step, chunk in enumerate(chunks):
        near[me ^ step] = chunk[:2]
        queries[me ^ step] = chunk[2]
    pool = pooling()
    half = BLOCK // 2
    for part in range(2):
        for b in range(nb):
            level_1[part, b * half : (b + 1) * half] = dot(pool, near[b, part]).astype(BF16)
        for c in range(nb // 2):
            block = dot(pool, level_1[part, at_block(c)]).astype(BF16)
            rims[0][part, c * half : (c + 1) * half] = block
    if groups == 2:
        upper = lax.axis_index("seq") >= GROUP
        rims[0][2:] = jnp.where(upper, near[0], near[nb - 1])
    else:
        rims[1][...] = near[nb - 1]
        rims[2][...] = near[0]


def from_others(groups, refs):
    if groups == 2:
        return (refs[0].at[:2], refs[0].at[2:], refs[0].at[2:]), refs[1:]
    return refs[:3], refs[3:]


def near_sides(b, nb):
    return [side for side in range(3) if 0 <= b + side - 1 < nb]


def local_kernel(nb, near, queries, level_1, _, query, k_t, v_t, k1_t, v1_t, weights, stats):
    even_1, even_2 = averaging(1), averaging(2)
    for b in range(nb):
        query[0, b] = queries[b]
        once = dot(even_1, queries[b]).astype(BF16)
        query[1, b] = once
        query[2, b] = dot(even_2, once).astype(BF16)
        for part, transposed in enumerate((k_t, v_t)):
            transposed[:, at_block(b)] = near[b, part].T
    for c in range(nb // 2):
        for part, transposed in enumerate((k1_t, v1_t)):
            transposed[:, at_block(c)] = level_1[part, at_block(c)].T
    for b in range(nb):
        sides = near_sides(b, nb)
        scores = [dot_nt(near[b + side - 1, 0], query[0, b]) * (SCALE * LOG2E) for side in sides]
        coarse = dot_nt(level_1[0, at_block(sibling(b))], query[1, b]) * (SCALE * LOG2E)
        top = coarse.max(0, keepdims=True)
        for score in scores:
            top = jnp.maximum(top, score.max(0, keepdims=True))
        weight = 2.0 * jnp.exp2(coarse - top)
        weights[b, 3] = weight
        total = weight.sum(0, keepdims=True)
        for side, score in zip(sides, scores):
            weight = jnp.exp2(score - top)
            weights[b, side] = weight
            total = total + weight.sum(0, keepdims=True)
        stats[b, :1] = top
        stats[b, 1:2] = total


def rim_sides(b, nb):
    return [side for side in range(3) if not 0 <= b + side - 1 < nb]


def forward_kernel(nb, groups, *refs):
    (query, v_t, v1_t, weights, stats), refs = refs[:5], refs[5:]
    (top_2, rim_low, rim_high), refs = from_others(groups, refs)
    prob, *outs, attended = refs[GROUP:]
    present = rim_present(groups)
    v2_t = top_2[1].T
    for b in range(nb):
        sides = rim_sides(b, nb)
        scores = []
        for side in sides:
            score = dot_nt((rim_high if side else rim_low)[0], query[0, b]) * (SCALE * LOG2E)
            scores.append(jnp.where(present[side // 2], score, -jnp.inf))
        coarse = dot_nt(top_2[0], query[2, b]) * (SCALE * LOG2E)
        old = stats[b, :1]
        top = jnp.maximum(old, coarse.max(0, keepdims=True))
        for score in scores:
            top = jnp.maximum(top, score.max(0, keepdims=True))
        shrink = jnp.exp2(old - top)
        far = 4.0 * jnp.exp2(coarse - top)
        total = shrink * stats[b, 1:2] + far.sum(0, keepdims=True)
        fresh = []
        for score in scores:
            fresh.append(jnp.exp2(score - top))
            total = total + fresh[-1].sum(0, keepdims=True)
        inverse = 1.0 / total
        shrink = shrink * inverse
        prob[b, 4] = (far * inverse).astype(BF16)
        prob[b, 3] = (weights[b, 3] * shrink).astype(BF16)
        context = dot(v2_t, prob[b, 4]) + dot(v1_t[:, at_block(sibling(b))], prob[b, 3])
        for side in near_sides(b, nb):
            prob[b, side] = (weights[b, side] * shrink).astype(BF16)
            context = context + dot(v_t[:, at_block(b + side - 1)], prob[b, side])
        for side, weight in zip(sides, fresh):
            prob[b, side] = (weight * inverse).astype(BF16)
            context = context + dot((rim_high if side else rim_low)[1].T, prob[b, side])
        attended[b] = context.T.astype(BF16)
    me = member()
    for step, out in enumerate(outs):
        out[...] = attended[me ^ step]


def slope_kernel(nb, groups, *refs):
    (query, near, level_1, prob), refs = refs[:4], refs[4:]
    (top_2, rim_low, rim_high), refs = from_others(groups, refs)
    chunks, (grads, shift, *rim_outs, sums, rim_sums) = refs[:GROUP], refs[GROUP:]
    me = member()
    for step, chunk in enumerate(chunks):
        grads[me ^ step] = chunk[...]
    for b in range(nb):
        grad = grads[b]
        slopes = []
        for side in range(3):
            if side in near_sides(b, nb):
                value = near[b + side - 1, 1]
            else:
                value = (rim_high if side else rim_low)[1]
            slopes.append(dot_nt(value, grad))
        slopes.append(dot_nt(level_1[1, at_block(sibling(b))], grad))
        slopes.append(dot_nt(top_2[1], grad))
        delta = 0.0
        for part, slope in enumerate(slopes):
            delta = delta + (prob[b, part].astype(F32) * slope).sum(0, keepdims=True)
        for part, slope in enumerate(slopes):
            shift[b, part] = (prob[b, part].astype(F32) * (slope - delta)).astype(BF16)
        for side in rim_sides(b, nb):
            rim_sums[side // 2, 0] = SCALE * dot(shift[b, side], query[0, b])
            rim_sums[side // 2, 1] = dot(prob[b, side], grad)
        key, value = SCALE * dot(shift[b, 4], query[2, b]), dot(prob[b, 4], grad)
        if b:
            key, value = key + sums[0], value + sums[1]
        if b < nb - 1:
            sums[0], sums[1] = key, value
        else:
            rim_outs[0][0], rim_outs[0][1] = key.astype(BF16), value.astype(BF16)
    low, high = rim_sums[0], rim_sums[1]
    if groups == 2:
        upper = lax.axis_index("seq") >= GROUP
        rim_outs[0][2:] = jnp.where(upper, low, high).astype(BF16)
    else:
        rim_outs[1][...] = high.astype(BF16)
        rim_outs[2][...] = low.astype(BF16)


def backward_kernel(nb, groups, *refs):
    (query, k_t, k1_t, prob, shift, grads), refs = refs[:6], refs[6:]
    (top_2, rim_low, rim_high), refs = from_others(groups, refs)
    grad_q, grad_kv, sums_1 = refs
    k2_t = top_2[0].T
    even_1, even_2 = averaging(1), averaging(2)
    for b in range(nb):
        grad_t = 0.0
        for side in range(3):
            if side in near_sides(b, nb):
                key_t = k_t[:, at_block(b + side - 1)]
            else:
                key_t = (rim_high if side else rim_low)[0].T
            grad_t = grad_t + dot(key_t, shift[b, side])
        for spread, key_t, part in ((even_1, k1_t[:, at_block(sibling(b))], 3), (even_2, k2_t, 4)):
            high, low = halves(dot(key_t, shift[b, part]))
            grad_t = grad_t + (dot(high, spread) + dot(low, spread))
        grad_q[b] = (SCALE * grad_t).T.astype(BF16)
    for c in range(nb // 2):
        users = [b for b in range(nb) if sibling(b) == c]
        sums_1[0, at_block(c)] = SCALE * sum(dot(shift[b, 3], query[1, b]) for b in users)
        sums_1[1, at_block(c)] = sum(dot(prob[b, 3], grads[b]) for b in users)
    spread = spreading(1)
    half = BLOCK // 2
    for s in range(nb):
        users = [(s + 1 - side, side) for side in range(3) if 0 <= s + 1 - side < nb]
        key = SCALE * sum(dot(shift[b, side], query[0, b]) for b, side in users)
        value = sum(dot(prob[b, side], grads[b]) for b, side in users)
        for part, total in enumerate((key, value)):
            high, low = halves(sums_1[part, s * half : (s + 1) * half])
            grad_kv[part, s] = total + (dot(spread, high) + dot(spread, low))


def share_kernel(kept, got, _, across, here):
    across[...] = (kept[1].astype(F32) + got[1].astype(F32)).astype(BF16)
    here[...] = kept[0].astype(F32) + got[0].astype(F32)


def combine_kernel(nb, groups, grad_q, grad_kv, *refs):
    (got_top, got_low, got_high), (*outs, out) = from_others(groups, refs)
    present = rim_present(groups)
    spread = spreading(2)
    quarter = BLOCK // 4
    for b in range(nb):
        for part in range(2):
            total = grad_kv[part, b] + dot(spread, got_top[part, b * quarter : (b + 1) * quarter])
            if b == 0:
                total = total + jnp.where(present[0], got_low[part].astype(F32), 0.0)
            if b == nb - 1:
                total = total + jnp.where(present[1], got_high[part].astype(F32), 0.0)
            out[b, part] = total.astype(BF16)
    me = member()
    for step, chunk in enumerate(outs):
        chunk[:2] = out[me ^ step]
        chunk[2] = grad_q[me ^ step]


def unpack_kernel(*refs):
    here, across, *refs = refs
    chunks, (*outs, mixed) = refs[:GROUP], refs[GROUP:]
    mixed[...] = (here[...] + across[...].astype(F32)).astype(BF16)
    me = member()
    for step in range(GROUP):
        at = columns(me ^ step)
        for part, out in enumerate(outs):
            out[:, at] = chunks[step][part]


def share():
    return lax.axis_index("mp")


def grad_kernel(*refs):
    pieces, out_weight, outs, (whole, heads) = refs[:N_MP], refs[N_MP], refs[N_MP + 1 : -2], refs[-2:]
    me = member()
    for step, piece in enumerate(pieces):
        whole[span(share() ^ step, piece.shape[0]), :] = piece[...]
    heads[...] = dot_nt(whole[...], out_weight[...]).astype(BF16)
    for step, out in enumerate(outs):
        out[...] = heads[:, columns(me ^ step)]


def project_kernel(*refs):
    chunks, out_weight, (kept, sent, attended, whole) = refs[:GROUP], refs[GROUP], refs[-4:]
    me = member()
    for step, chunk in enumerate(chunks):
        attended[:, columns(me ^ step)] = chunk[...]
    whole[...] = dot(attended[...], out_weight[...]).astype(BF16)
    rows = kept.shape[1]
    for far in range(2):
        kept[far] = whole[span(share() ^ (2 * far), rows), :]
        sent[far] = whole[span(share() ^ (2 * far + 1), rows), :]


def swapped(x, axis, step):
    return lax.ppermute(x, axis, [(i, i ^ step) for i in range(lax.axis_size(axis))])


def exchanged(chunks):
    got = {step: swapped(chunks[step], "seq", step) for step in (3, 1, 2)}
    return [chunks[0]] + [got[step] for step in range(1, GROUP)]


def crossed(arrays):
    count = lax.axis_size("seq")
    across = swapped(arrays[0], "seq", GROUP)
    if len(arrays) == 1:
        return [across]
    up = [(i, i + GROUP) for i in range(count - GROUP)]
    down = [(j, i) for i, j in up]
    return [across, lax.ppermute(arrays[1], "seq", up), lax.ppermute(arrays[2], "seq", down)]


def per_device(queries, keys, values, out_weight, out_grad):
    rows, width = queries.shape
    assert width == GROUP * HEAD_DIM and rows == BLOCK and lax.axis_size("mp") == N_MP
    count = lax.axis_size("seq")
    assert count % (2 * GROUP) == 0
    groups = count // GROUP
    nb = GROUP
    tokens = nb * rows
    half, quarter = rows // 2, rows // 4
    model = out_weight.shape[1]
    block = shape(2, rows, HEAD_DIM)
    sent = [shape(4, rows, HEAD_DIM)] if groups == 2 else [block] * 3
    score_flops = 2 * tokens * 5 * BLOCK * HEAD_DIM
    weight_flops = 2 * rows * out_weight.size

    chunk = shape(rows, HEAD_DIM)
    triple = shape(3, rows, HEAD_DIM)
    *chunks, own_grad = call(
        pack_kernel,
        [triple] * GROUP + [shape(*out_grad.shape)],
        (queries, keys, values, out_grad),
        scratch=[pltpu.SemaphoreType.DMA((1 + 3 * GROUP,))],
        space=pltpu.HBM,
        limit=56,
    )
    far = swapped(own_grad, "mp", 2)
    chunks = exchanged(chunks)
    chunks[:1] = call(copy_kernel, [triple], chunks[:1])
    far, near, queries, level_1, *refs = call(
        functools.partial(gather_kernel, nb, groups),
        [
            shape(*out_grad.shape),
            shape(nb, 2, rows, HEAD_DIM),
            shape(nb, rows, HEAD_DIM),
            shape(2, tokens // 2, HEAD_DIM),
        ]
        + sent,
        (far, *chunks),
    )
    others = crossed(refs)
    grad_chunks = call(
        grad_kernel,
        [chunk] * GROUP,
        (own_grad, swapped(own_grad, "mp", 1), far, swapped(far, "mp", 1), out_weight),
        scratch=[pltpu.VMEM((rows, model), BF16), pltpu.VMEM((rows, width), BF16)],
        flops=weight_flops,
    )
    query, k_t, v_t, k1_t, v1_t, weights, stats = call(
        functools.partial(local_kernel, nb),
        [
            shape(3, nb, rows, HEAD_DIM),
            shape(HEAD_DIM, tokens),
            shape(HEAD_DIM, tokens),
            shape(HEAD_DIM, tokens // 2),
            shape(HEAD_DIM, tokens // 2),
            shape(nb, 4, BLOCK, BLOCK, dtype=F32),
            shape(nb, 8, BLOCK, dtype=F32),
        ],
        (near, queries, level_1, grad_chunks[0]),
        flops=score_flops,
    )
    grad_chunks = exchanged(grad_chunks)
    prob, *attended = call(
        functools.partial(forward_kernel, nb, groups),
        [shape(nb, 5, BLOCK, BLOCK)] + [chunk] * GROUP,
        (query, v_t, v1_t, weights, stats, *others, *grad_chunks),
        scratch=[pltpu.VMEM((nb, rows, HEAD_DIM), BF16)],
        flops=score_flops,
    )
    attended = exchanged(attended)
    grads, shift, *rim_grads = call(
        functools.partial(slope_kernel, nb, groups),
        [shape(nb, rows, HEAD_DIM), shape(nb, 5, BLOCK, BLOCK)] + sent,
        (query, near, level_1, prob, *others, *grad_chunks),
        scratch=[pltpu.VMEM((2, BLOCK, HEAD_DIM), F32), pltpu.VMEM((2, 2, BLOCK, HEAD_DIM), F32)],
        flops=score_flops,
    )
    other_grads = crossed(rim_grads)
    grad_q, grad_kv = call(
        functools.partial(backward_kernel, nb, groups),
        [shape(nb, rows, HEAD_DIM), shape(2, nb, rows, HEAD_DIM, dtype=F32)],
        (query, k_t, k1_t, prob, shift, grads, *others),
        scratch=[pltpu.VMEM((2, tokens // 2, HEAD_DIM), F32)],
        flops=1,
    )
    local = rows // N_MP
    shares = shape(2, local, model)
    kept, given = call(
        project_kernel,
        [shares] * 2,
        (*attended, out_weight, grads),
        scratch=[pltpu.VMEM((rows, width), BF16), pltpu.VMEM((rows, model), BF16)],
        flops=weight_flops,
    )
    chunks = call(
        functools.partial(combine_kernel, nb, groups),
        [triple] * GROUP,
        (grad_q, grad_kv, *other_grads),
        scratch=[pltpu.VMEM((nb, 2, rows, HEAD_DIM), BF16)],
        flops=20 * score_flops,
    )
    across, here = call(
        share_kernel,
        [shape(local, model), shape(local, model, dtype=F32)],
        (kept, swapped(given, "mp", 1), chunks[0]),
    )
    chunks = exchanged(chunks)
    across = swapped(across, "mp", 2)
    grad_k, grad_v, grad_q, mixed = call(
        unpack_kernel,
        [shape(rows, width)] * 3 + [shape(local, model)],
        (here, across, *chunks),
    )
    return mixed, grad_q, grad_k, grad_v


def solution(mesh):
    return jax.shard_map(
        per_device,
        mesh=mesh,
        in_specs=(
            P("seq", "mp"),
            P("seq", "mp"),
            P("seq", "mp"),
            P("mp", None),
            P(("seq", "mp"), None),
        ),
        out_specs=(P(("seq", "mp"), None), P("seq", "mp"), P("seq", "mp"), P("seq", "mp")),
        check_vma=False,
    )
```

```python
import functools

import jax
import jax.numpy as jnp
from jax import lax
from jax.experimental import pallas as pl
from jax.experimental.pallas import tpu as pltpu
from jax.sharding import PartitionSpec as P

HEAD_DIM = 128
BLOCK = 256
LEVELS = 2
GROUP = 4
N_MP = 4
SCALE = HEAD_DIM**-0.5
LOG2E = 1.4426950408889634
BF16 = jnp.bfloat16
F32 = jnp.float32


def dot(a, b):
    return lax.dot_general(a, b, (((1,), (0,)), ((), ())), preferred_element_type=F32)


def dot_nt(a, b):
    return lax.dot_general(a, b, (((1,), (1,)), ((), ())), preferred_element_type=F32)


def shape(*dims, dtype=BF16):
    return jax.ShapeDtypeStruct(dims, dtype)


def call(kernel, out_shape, args, scratch=(), flops=0, limit=32, space=pltpu.VMEM):
    whole = pl.BlockSpec(memory_space=space)
    moved = sum(x.size * x.dtype.itemsize for x in (*args, *out_shape))
    return pl.pallas_call(
        kernel,
        out_shape=out_shape,
        in_specs=[whole] * len(args),
        out_specs=[whole] * len(out_shape),
        scratch_shapes=scratch,
        compiler_params=pltpu.CompilerParams(vmem_limit_bytes=limit << 20),
        cost_estimate=pl.CostEstimate(flops=flops, bytes_accessed=moved if flops else 0, transcendentals=0),
    )(*args)


def columns(index):
    return pl.ds(pl.multiple_of(index * HEAD_DIM, HEAD_DIM), HEAD_DIM)


def span(index, size):
    return pl.ds(pl.multiple_of(index * size, size), size)


def iota(dims, axis):
    return lax.broadcasted_iota(jnp.int32, dims, axis)


def averaging(level):
    dims = (BLOCK, BLOCK)
    same = (iota(dims, 0) >> level) == (iota(dims, 1) >> level)
    return jnp.where(same, 2.0**-level, 0.0).astype(BF16)


def pooling():
    dims = (BLOCK // 2, BLOCK)
    return jnp.where(iota(dims, 0) == (iota(dims, 1) >> 1), 0.5, 0.0).astype(BF16)


def spreading(level):
    dims = (BLOCK, BLOCK >> level)
    return jnp.where((iota(dims, 0) >> level) == iota(dims, 1), 2.0**-level, 0.0).astype(BF16)


def halves(x):
    high = x.astype(BF16)
    return high, (x - high.astype(F32)).astype(BF16)


def at_block(b):
    return slice(b * BLOCK, (b + 1) * BLOCK)


def sibling(b):
    return (b >> 1) ^ 1


def rim_present(groups):
    group = lax.axis_index("seq") // GROUP
    return group > 0, group < groups - 1


def member():
    return lax.rem(lax.axis_index("seq"), GROUP)


def columns(index):
    return pl.ds(pl.multiple_of(index * HEAD_DIM, HEAD_DIM), HEAD_DIM)


def pack_kernel(q, k, v, out_grad, *refs):
    outs, (out_grad_out, sems) = refs[:GROUP], refs[GROUP:]
    me = member()
    copies = [pltpu.make_async_copy(out_grad, out_grad_out, sems.at[0])]
    for step in (3, 1, 2, 0):
        for part, source in enumerate((k, v, q)):
            piece = source.at[:, columns(me ^ step)]
            copies.append(pltpu.make_async_copy(piece, outs[step].at[part], sems.at[len(copies)]))
    for copy in copies:
        copy.start()
    for copy in copies:
        copy.wait()


def pool_kernel(k, v, out):
    pool = pooling()
    half = BLOCK // 2
    for part, source in enumerate((k, v)):
        once = dot(pool, source[...]).astype(BF16)
        twice = dot(pool[: half // 2, :half], once).astype(BF16)
        for head in range(GROUP):
            out[head, part] = twice[:, head * HEAD_DIM : (head + 1) * HEAD_DIM]


def copy_kernel(x, y, x_out, y_out):
    x_out[...] = x[...]
    y_out[...] = y[...]


def gather_kernel(nb, groups, far, _, *refs):
    chunks, (far_out, near, queries, level_1, *rims) = refs[:GROUP], refs[GROUP:]
    far_out[...] = far[...]
    me = member()
    for step, chunk in enumerate(chunks):
        near[me ^ step] = chunk[:2]
        queries[me ^ step] = chunk[2]
    pool = pooling()
    half = BLOCK // 2
    for part in range(2):
        for b in range(nb):
            level_1[part, b * half : (b + 1) * half] = dot(pool, near[b, part]).astype(BF16)
    if groups == 2:
        upper = lax.axis_index("seq") >= GROUP
        rims[0][...] = jnp.where(upper, near[0], near[nb - 1])
    else:
        rims[0][...] = near[nb - 1]
        rims[1][...] = near[0]


def from_beside(groups, refs):
    if groups == 2:
        return (refs[0], refs[0]), refs[1:]
    return refs[:2], refs[2:]


def from_others(groups, refs):
    if groups == 2:
        return (refs[0].at[:2], refs[0].at[2:], refs[0].at[2:]), refs[1:]
    return refs[:3], refs[3:]


def near_sides(b, nb):
    return [side for side in range(3) if 0 <= b + side - 1 < nb]


def local_kernel(nb, near, queries, level_1, _, query, k_t, v_t, k1_t, v1_t, weights, stats):
    even_1, even_2 = averaging(1), averaging(2)
    for b in range(nb):
        query[0, b] = queries[b]
        once = dot(even_1, queries[b]).astype(BF16)
        query[1, b] = once
        query[2, b] = dot(even_2, once).astype(BF16)
        for part, transposed in enumerate((k_t, v_t)):
            transposed[:, at_block(b)] = near[b, part].T
    for c in range(nb // 2):
        for part, transposed in enumerate((k1_t, v1_t)):
            transposed[:, at_block(c)] = level_1[part, at_block(c)].T
    for b in range(nb):
        sides = near_sides(b, nb)
        scores = [dot_nt(near[b + side - 1, 0], query[0, b]) * (SCALE * LOG2E) for side in sides]
        coarse = dot_nt(level_1[0, at_block(sibling(b))], query[1, b]) * (SCALE * LOG2E)
        top = coarse.max(0, keepdims=True)
        for score in scores:
            top = jnp.maximum(top, score.max(0, keepdims=True))
        weight = 2.0 * jnp.exp2(coarse - top)
        weights[b, 3] = weight
        total = weight.sum(0, keepdims=True)
        for side, score in zip(sides, scores):
            weight = jnp.exp2(score - top)
            weights[b, side] = weight
            total = total + weight.sum(0, keepdims=True)
        stats[b, :1] = top
        stats[b, 1:2] = total


def rim_sides(b, nb):
    return [side for side in range(3) if not 0 <= b + side - 1 < nb]


def forward_kernel(nb, groups, *refs):
    (query, v_t, v1_t, weights, stats), refs = refs[:5], refs[5:]
    (rim_low, rim_high), refs = from_beside(groups, refs)
    chunks, (prob, grads, top_2, *outs, attended) = refs[:GROUP], refs[GROUP:]
    present = rim_present(groups)
    me = member()
    quarter = BLOCK // 4
    for step, chunk in enumerate(chunks):
        grads[me ^ step] = chunk[:BLOCK]
        for part in range(2):
            level = chunk[BLOCK + part * quarter : BLOCK + (part + 1) * quarter]
            top_2[part, span(me ^ step, quarter), :] = level
    v2_t = top_2[1].T
    for b in range(nb):
        sides = rim_sides(b, nb)
        scores = []
        for side in sides:
            score = dot_nt((rim_high if side else rim_low)[0], query[0, b]) * (SCALE * LOG2E)
            scores.append(jnp.where(present[side // 2], score, -jnp.inf))
        coarse = dot_nt(top_2[0], query[2, b]) * (SCALE * LOG2E)
        old = stats[b, :1]
        top = jnp.maximum(old, coarse.max(0, keepdims=True))
        for score in scores:
            top = jnp.maximum(top, score.max(0, keepdims=True))
        shrink = jnp.exp2(old - top)
        far = 4.0 * jnp.exp2(coarse - top)
        total = shrink * stats[b, 1:2] + far.sum(0, keepdims=True)
        fresh = []
        for score in scores:
            fresh.append(jnp.exp2(score - top))
            total = total + fresh[-1].sum(0, keepdims=True)
        inverse = 1.0 / total
        shrink = shrink * inverse
        prob[b, 4] = (far * inverse).astype(BF16)
        prob[b, 3] = (weights[b, 3] * shrink).astype(BF16)
        context = dot(v2_t, prob[b, 4]) + dot(v1_t[:, at_block(sibling(b))], prob[b, 3])
        for side in near_sides(b, nb):
            prob[b, side] = (weights[b, side] * shrink).astype(BF16)
            context = context + dot(v_t[:, at_block(b + side - 1)], prob[b, side])
        for side, weight in zip(sides, fresh):
            prob[b, side] = (weight * inverse).astype(BF16)
            context = context + dot((rim_high if side else rim_low)[1].T, prob[b, side])
        attended[b] = context.T.astype(BF16)
    for step, out in enumerate(outs):
        out[...] = attended[me ^ step]


def slope_kernel(nb, groups, *refs):
    (query, near, level_1, prob, grads, top_2), refs = refs[:6], refs[6:]
    (rim_low, rim_high), (shift, *rim_outs, sums, rim_sums) = from_beside(groups, refs)
    for b in range(nb):
        grad = grads[b]
        slopes = []
        for side in range(3):
            if side in near_sides(b, nb):
                value = near[b + side - 1, 1]
            else:
                value = (rim_high if side else rim_low)[1]
            slopes.append(dot_nt(value, grad))
        slopes.append(dot_nt(level_1[1, at_block(sibling(b))], grad))
        slopes.append(dot_nt(top_2[1], grad))
        delta = 0.0
        for part, slope in enumerate(slopes):
            delta = delta + (prob[b, part].astype(F32) * slope).sum(0, keepdims=True)
        for part, slope in enumerate(slopes):
            shift[b, part] = (prob[b, part].astype(F32) * (slope - delta)).astype(BF16)
        for side in rim_sides(b, nb):
            rim_sums[side // 2, 0] = SCALE * dot(shift[b, side], query[0, b])
            rim_sums[side // 2, 1] = dot(prob[b, side], grad)
        key, value = SCALE * dot(shift[b, 4], query[2, b]), dot(prob[b, 4], grad)
        if b:
            key, value = key + sums[0], value + sums[1]
        if b < nb - 1:
            sums[0], sums[1] = key, value
        else:
            rim_outs[0][0], rim_outs[0][1] = key.astype(BF16), value.astype(BF16)
    low, high = rim_sums[0], rim_sums[1]
    if groups == 2:
        upper = lax.axis_index("seq") >= GROUP
        rim_outs[0][2:] = jnp.where(upper, low, high).astype(BF16)
    else:
        rim_outs[1][...] = high.astype(BF16)
        rim_outs[2][...] = low.astype(BF16)


def backward_kernel(nb, groups, *refs):
    (query, k_t, k1_t, prob, shift, grads, top_2), refs = refs[:7], refs[7:]
    (rim_low, rim_high), refs = from_beside(groups, refs)
    grad_q, grad_kv, sums_1 = refs
    k2_t = top_2[0].T
    even_1, even_2 = averaging(1), averaging(2)
    for b in range(nb):
        grad_t = 0.0
        for side in range(3):
            if side in near_sides(b, nb):
                key_t = k_t[:, at_block(b + side - 1)]
            else:
                key_t = (rim_high if side else rim_low)[0].T
            grad_t = grad_t + dot(key_t, shift[b, side])
        for spread, key_t, part in ((even_1, k1_t[:, at_block(sibling(b))], 3), (even_2, k2_t, 4)):
            high, low = halves(dot(key_t, shift[b, part]))
            grad_t = grad_t + (dot(high, spread) + dot(low, spread))
        grad_q[b] = (SCALE * grad_t).T.astype(BF16)
    for c in range(nb // 2):
        users = [b for b in range(nb) if sibling(b) == c]
        sums_1[0, at_block(c)] = SCALE * sum(dot(shift[b, 3], query[1, b]) for b in users)
        sums_1[1, at_block(c)] = sum(dot(prob[b, 3], grads[b]) for b in users)
    spread = spreading(1)
    half = BLOCK // 2
    for s in range(nb):
        users = [(s + 1 - side, side) for side in range(3) if 0 <= s + 1 - side < nb]
        key = SCALE * sum(dot(shift[b, side], query[0, b]) for b, side in users)
        value = sum(dot(prob[b, side], grads[b]) for b, side in users)
        for part, total in enumerate((key, value)):
            high, low = halves(sums_1[part, s * half : (s + 1) * half])
            grad_kv[part, s] = total + (dot(spread, high) + dot(spread, low))


def share_kernel(kept, got, _, across, here):
    across[...] = (kept[1].astype(F32) + got[1].astype(F32)).astype(BF16)
    here[...] = kept[0].astype(F32) + got[0].astype(F32)


def combine_kernel(nb, groups, grad_q, grad_kv, *refs):
    (got_top, got_low, got_high), (*outs, out) = from_others(groups, refs)
    present = rim_present(groups)
    spread = spreading(2)
    quarter = BLOCK // 4
    for b in range(nb):
        for part in range(2):
            total = grad_kv[part, b] + dot(spread, got_top[part, b * quarter : (b + 1) * quarter])
            if b == 0:
                total = total + jnp.where(present[0], got_low[part].astype(F32), 0.0)
            if b == nb - 1:
                total = total + jnp.where(present[1], got_high[part].astype(F32), 0.0)
            out[b, part] = total.astype(BF16)
    me = member()
    for step, chunk in enumerate(outs):
        chunk[:2] = out[me ^ step]
        chunk[2] = grad_q[me ^ step]


def unpack_kernel(*refs):
    here, across, *refs = refs
    chunks, (*outs, mixed) = refs[:GROUP], refs[GROUP:]
    mixed[...] = (here[...] + across[...].astype(F32)).astype(BF16)
    me = member()
    for step in range(GROUP):
        at = columns(me ^ step)
        for part, out in enumerate(outs):
            out[:, at] = chunks[step][part]


def share():
    return lax.axis_index("mp")


def grad_kernel(*refs):
    pieces, (out_weight, tops), refs = refs[:N_MP], refs[N_MP : N_MP + 2], refs[N_MP + 2 :]
    *outs, whole, heads = refs
    me = member()
    for step, piece in enumerate(pieces):
        whole[span(share() ^ step, piece.shape[0]), :] = piece[...]
    heads[...] = dot_nt(whole[...], out_weight[...]).astype(BF16)
    quarter = tops.shape[2]
    for step, out in enumerate(outs):
        out[:BLOCK] = heads[:, columns(me ^ step)]
        for part in range(2):
            out[BLOCK + part * quarter : BLOCK + (part + 1) * quarter] = tops[me ^ step, part]


def project_kernel(*refs):
    chunks, out_weight, (kept, sent, attended, whole) = refs[:GROUP], refs[GROUP], refs[-4:]
    me = member()
    for step, chunk in enumerate(chunks):
        attended[:, columns(me ^ step)] = chunk[...]
    whole[...] = dot(attended[...], out_weight[...]).astype(BF16)
    rows = kept.shape[1]
    for far in range(2):
        kept[far] = whole[span(share() ^ (2 * far), rows), :]
        sent[far] = whole[span(share() ^ (2 * far + 1), rows), :]


def swapped(x, axis, step):
    return lax.ppermute(x, axis, [(i, i ^ step) for i in range(lax.axis_size(axis))])


def exchanged(chunks):
    got = {step: swapped(chunks[step], "seq", step) for step in (3, 1, 2)}
    return [chunks[0]] + [got[step] for step in range(1, GROUP)]


def beside(arrays):
    count = lax.axis_size("seq")
    if len(arrays) == 1:
        return [swapped(arrays[0], "seq", GROUP)]
    up = [(i, i + GROUP) for i in range(count - GROUP)]
    down = [(j, i) for i, j in up]
    return [lax.ppermute(arrays[0], "seq", up), lax.ppermute(arrays[1], "seq", down)]


def crossed(arrays):
    count = lax.axis_size("seq")
    across = swapped(arrays[0], "seq", GROUP)
    if len(arrays) == 1:
        return [across]
    up = [(i, i + GROUP) for i in range(count - GROUP)]
    down = [(j, i) for i, j in up]
    return [across, lax.ppermute(arrays[1], "seq", up), lax.ppermute(arrays[2], "seq", down)]


def per_device(queries, keys, values, out_weight, out_grad):
    rows, width = queries.shape
    assert width == GROUP * HEAD_DIM and rows == BLOCK and lax.axis_size("mp") == N_MP
    count = lax.axis_size("seq")
    assert count % (2 * GROUP) == 0
    groups = count // GROUP
    nb = GROUP
    tokens = nb * rows
    half, quarter = rows // 2, rows // 4
    model = out_weight.shape[1]
    block = shape(2, rows, HEAD_DIM)
    sent = [shape(4, rows, HEAD_DIM)] if groups == 2 else [block] * 3
    rims = [block] * (1 if groups == 2 else 2)
    quarter = rows // 4
    in_order = shape(nb, rows, HEAD_DIM)
    score_flops = 2 * tokens * 5 * BLOCK * HEAD_DIM
    weight_flops = 2 * rows * out_weight.size

    chunk = shape(rows, HEAD_DIM)
    triple = shape(3, rows, HEAD_DIM)
    *chunks, own_grad = call(
        pack_kernel,
        [triple] * GROUP + [shape(*out_grad.shape)],
        (queries, keys, values, out_grad),
        scratch=[pltpu.SemaphoreType.DMA((1 + 3 * GROUP,))],
        space=pltpu.HBM,
        limit=56,
    )
    far = swapped(own_grad, "mp", 2)
    chunks = exchanged(chunks)
    (tops,) = call(pool_kernel, [shape(GROUP, 2, quarter, HEAD_DIM)], (keys, values))
    tops = swapped(tops, "seq", GROUP)
    chunks[0], own_grad = call(copy_kernel, [triple, shape(*out_grad.shape)], (chunks[0], own_grad))
    far, near, queries, level_1, *refs = call(
        functools.partial(gather_kernel, nb, groups),
        [
            shape(*out_grad.shape),
            shape(nb, 2, rows, HEAD_DIM),
            shape(nb, rows, HEAD_DIM),
            shape(2, tokens // 2, HEAD_DIM),
        ]
        + rims,
        (far, tops, *chunks),
    )
    rim_blocks = beside(refs)
    grad_chunks = call(
        grad_kernel,
        [shape(rows + 2 * quarter, HEAD_DIM)] * GROUP,
        (own_grad, swapped(own_grad, "mp", 1), far, swapped(far, "mp", 1), out_weight, tops),
        scratch=[pltpu.VMEM((rows, model), BF16), pltpu.VMEM((rows, width), BF16)],
        flops=weight_flops,
    )
    query, k_t, v_t, k1_t, v1_t, weights, stats = call(
        functools.partial(local_kernel, nb),
        [
            shape(3, nb, rows, HEAD_DIM),
            shape(HEAD_DIM, tokens),
            shape(HEAD_DIM, tokens),
            shape(HEAD_DIM, tokens // 2),
            shape(HEAD_DIM, tokens // 2),
            shape(nb, 4, BLOCK, BLOCK, dtype=F32),
            shape(nb, 8, BLOCK, dtype=F32),
        ],
        (near, queries, level_1, grad_chunks[0]),
        flops=score_flops,
    )
    grad_chunks = exchanged(grad_chunks)
    prob, grads, top_2, *attended = call(
        functools.partial(forward_kernel, nb, groups),
        [shape(nb, 5, BLOCK, BLOCK), in_order, block] + [chunk] * GROUP,
        (query, v_t, v1_t, weights, stats, *rim_blocks, *grad_chunks),
        scratch=[pltpu.VMEM((nb, rows, HEAD_DIM), BF16)],
        flops=score_flops,
    )
    attended = exchanged(attended)
    shift, *rim_grads = call(
        functools.partial(slope_kernel, nb, groups),
        [shape(nb, 5, BLOCK, BLOCK)] + sent,
        (query, near, level_1, prob, grads, top_2, *rim_blocks),
        scratch=[pltpu.VMEM((2, BLOCK, HEAD_DIM), F32), pltpu.VMEM((2, 2, BLOCK, HEAD_DIM), F32)],
        flops=score_flops,
    )
    other_grads = crossed(rim_grads)
    grad_q, grad_kv = call(
        functools.partial(backward_kernel, nb, groups),
        [in_order, shape(2, nb, rows, HEAD_DIM, dtype=F32)],
        (query, k_t, k1_t, prob, shift, grads, top_2, *rim_blocks),
        scratch=[pltpu.VMEM((2, tokens // 2, HEAD_DIM), F32)],
        flops=1,
    )
    local = rows // N_MP
    shares = shape(2, local, model)
    kept, given = call(
        project_kernel,
        [shares] * 2,
        (*attended, out_weight, shift),
        scratch=[pltpu.VMEM((rows, width), BF16), pltpu.VMEM((rows, model), BF16)],
        flops=weight_flops,
    )
    chunks = call(
        functools.partial(combine_kernel, nb, groups),
        [triple] * GROUP,
        (grad_q, grad_kv, *other_grads),
        scratch=[pltpu.VMEM((nb, 2, rows, HEAD_DIM), BF16)],
        flops=20 * score_flops,
    )
    across, here = call(
        share_kernel,
        [shape(local, model), shape(local, model, dtype=F32)],
        (kept, swapped(given, "mp", 1), chunks[0]),
    )
    chunks = exchanged(chunks)
    across = swapped(across, "mp", 2)
    grad_k, grad_v, grad_q, mixed = call(
        unpack_kernel,
        [shape(rows, width)] * 3 + [shape(local, model)],
        (here, across, *chunks),
    )
    return mixed, grad_q, grad_k, grad_v


def solution(mesh):
    return jax.shard_map(
        per_device,
        mesh=mesh,
        in_specs=(
            P("seq", "mp"),
            P("seq", "mp"),
            P("seq", "mp"),
            P("mp", None),
            P(("seq", "mp"), None),
        ),
        out_specs=(P(("seq", "mp"), None), P("seq", "mp"), P("seq", "mp"), P("seq", "mp")),
        check_vma=False,
    )
```

```python
import functools

import jax
import jax.numpy as jnp
from jax import lax
from jax.experimental import pallas as pl
from jax.experimental.pallas import tpu as pltpu
from jax.sharding import PartitionSpec as P

HEAD_DIM = 128
BLOCK = 256
LEVELS = 2
GROUP = 4
N_MP = 4
SCALE = HEAD_DIM**-0.5
LOG2E = 1.4426950408889634
BF16 = jnp.bfloat16
F32 = jnp.float32


def dot(a, b):
    return lax.dot_general(a, b, (((1,), (0,)), ((), ())), preferred_element_type=F32)


def dot_nt(a, b):
    return lax.dot_general(a, b, (((1,), (1,)), ((), ())), preferred_element_type=F32)


def shape(*dims, dtype=BF16):
    return jax.ShapeDtypeStruct(dims, dtype)


def call(kernel, out_shape, args, scratch=(), flops=0, limit=32, space=pltpu.VMEM):
    whole = pl.BlockSpec(memory_space=space)
    moved = sum(x.size * x.dtype.itemsize for x in (*args, *out_shape))
    return pl.pallas_call(
        kernel,
        out_shape=out_shape,
        in_specs=[whole] * len(args),
        out_specs=[whole] * len(out_shape),
        scratch_shapes=scratch,
        compiler_params=pltpu.CompilerParams(vmem_limit_bytes=limit << 20),
        cost_estimate=pl.CostEstimate(flops=flops, bytes_accessed=moved if flops else 0, transcendentals=0),
    )(*args)


def columns(index):
    return pl.ds(pl.multiple_of(index * HEAD_DIM, HEAD_DIM), HEAD_DIM)


def span(index, size):
    return pl.ds(pl.multiple_of(index * size, size), size)


def iota(dims, axis):
    return lax.broadcasted_iota(jnp.int32, dims, axis)


def averaging(level):
    dims = (BLOCK, BLOCK)
    same = (iota(dims, 0) >> level) == (iota(dims, 1) >> level)
    return jnp.where(same, 2.0**-level, 0.0).astype(BF16)


def pooling():
    dims = (BLOCK // 2, BLOCK)
    return jnp.where(iota(dims, 0) == (iota(dims, 1) >> 1), 0.5, 0.0).astype(BF16)


def spreading(level):
    dims = (BLOCK, BLOCK >> level)
    return jnp.where((iota(dims, 0) >> level) == iota(dims, 1), 2.0**-level, 0.0).astype(BF16)


def halves(x):
    high = x.astype(BF16)
    return high, (x - high.astype(F32)).astype(BF16)


def at_block(b):
    return slice(b * BLOCK, (b + 1) * BLOCK)


def sibling(b):
    return (b >> 1) ^ 1


def rim_present(groups):
    group = lax.axis_index("seq") // GROUP
    return group > 0, group < groups - 1


def member():
    return lax.rem(lax.axis_index("seq"), GROUP)


def columns(index):
    return pl.ds(pl.multiple_of(index * HEAD_DIM, HEAD_DIM), HEAD_DIM)


def pack_kernel(q, k, v, *refs):
    *outs, sems = refs
    me = member()
    copies = []
    for step in (3, 1, 2, 0):
        for part, source in enumerate((k, v, q)):
            piece = source.at[:, columns(me ^ step)]
            copies.append(pltpu.make_async_copy(piece, outs[step].at[part], sems.at[len(copies)]))
    for copy in copies:
        copy.start()
    for copy in copies:
        copy.wait()


def pool_kernel(k, v, out):
    pool = pooling()
    half = BLOCK // 2
    for part, source in enumerate((k, v)):
        once = dot(pool, source[...]).astype(BF16)
        twice = dot(pool[: half // 2, :half], once).astype(BF16)
        for head in range(GROUP):
            out[head, part] = twice[:, head * HEAD_DIM : (head + 1) * HEAD_DIM]


def copy_kernel(x, _, out):
    out[...] = x[...]


def gather_kernel(nb, groups, far, _, *refs):
    chunks, (far_out, near, queries, level_1, *rims) = refs[:GROUP], refs[GROUP:]
    far_out[...] = far[...]
    me = member()
    for step, chunk in enumerate(chunks):
        near[me ^ step] = chunk[:2]
        queries[me ^ step] = chunk[2]
    pool = pooling()
    half = BLOCK // 2
    for part in range(2):
        for b in range(nb):
            level_1[part, b * half : (b + 1) * half] = dot(pool, near[b, part]).astype(BF16)
    if groups == 2:
        upper = lax.axis_index("seq") >= GROUP
        rims[0][...] = jnp.where(upper, near[0], near[nb - 1])
    else:
        rims[0][...] = near[nb - 1]
        rims[1][...] = near[0]


def from_beside(groups, refs):
    if groups == 2:
        return (refs[0], refs[0]), refs[1:]
    return refs[:2], refs[2:]


def from_others(groups, refs):
    if groups == 2:
        return (refs[0].at[:2], refs[0].at[2:], refs[0].at[2:]), refs[1:]
    return refs[:3], refs[3:]


def near_sides(b, nb):
    return [side for side in range(3) if 0 <= b + side - 1 < nb]


def local_kernel(nb, near, queries, level_1, _, query, k_t, v_t, k1_t, v1_t, weights, stats):
    even_1, even_2 = averaging(1), averaging(2)
    for b in range(nb):
        query[0, b] = queries[b]
        once = dot(even_1, queries[b]).astype(BF16)
        query[1, b] = once
        query[2, b] = dot(even_2, once).astype(BF16)
        for part, transposed in enumerate((k_t, v_t)):
            transposed[:, at_block(b)] = near[b, part].T
    for c in range(nb // 2):
        for part, transposed in enumerate((k1_t, v1_t)):
            transposed[:, at_block(c)] = level_1[part, at_block(c)].T
    for b in range(nb):
        sides = near_sides(b, nb)
        scores = [dot_nt(near[b + side - 1, 0], query[0, b]) * (SCALE * LOG2E) for side in sides]
        coarse = dot_nt(level_1[0, at_block(sibling(b))], query[1, b]) * (SCALE * LOG2E)
        top = coarse.max(0, keepdims=True)
        for score in scores:
            top = jnp.maximum(top, score.max(0, keepdims=True))
        weight = 2.0 * jnp.exp2(coarse - top)
        weights[b, 3] = weight
        total = weight.sum(0, keepdims=True)
        for side, score in zip(sides, scores):
            weight = jnp.exp2(score - top)
            weights[b, side] = weight
            total = total + weight.sum(0, keepdims=True)
        stats[b, :1] = top
        stats[b, 1:2] = total


def rim_sides(b, nb):
    return [side for side in range(3) if not 0 <= b + side - 1 < nb]


def forward_kernel(nb, groups, *refs):
    (query, v_t, v1_t, weights, stats), refs = refs[:5], refs[5:]
    (rim_low, rim_high), refs = from_beside(groups, refs)
    chunks, (prob, grads, top_2, *outs, attended) = refs[:GROUP], refs[GROUP:]
    present = rim_present(groups)
    me = member()
    quarter = BLOCK // 4
    for step, chunk in enumerate(chunks):
        grads[me ^ step] = chunk[:BLOCK]
        for part in range(2):
            level = chunk[BLOCK + part * quarter : BLOCK + (part + 1) * quarter]
            top_2[part, span(me ^ step, quarter), :] = level
    v2_t = top_2[1].T
    for b in range(nb):
        sides = rim_sides(b, nb)
        scores = []
        for side in sides:
            score = dot_nt((rim_high if side else rim_low)[0], query[0, b]) * (SCALE * LOG2E)
            scores.append(jnp.where(present[side // 2], score, -jnp.inf))
        coarse = dot_nt(top_2[0], query[2, b]) * (SCALE * LOG2E)
        old = stats[b, :1]
        top = jnp.maximum(old, coarse.max(0, keepdims=True))
        for score in scores:
            top = jnp.maximum(top, score.max(0, keepdims=True))
        shrink = jnp.exp2(old - top)
        far = 4.0 * jnp.exp2(coarse - top)
        total = shrink * stats[b, 1:2] + far.sum(0, keepdims=True)
        fresh = []
        for score in scores:
            fresh.append(jnp.exp2(score - top))
            total = total + fresh[-1].sum(0, keepdims=True)
        inverse = 1.0 / total
        shrink = shrink * inverse
        prob[b, 4] = (far * inverse).astype(BF16)
        prob[b, 3] = (weights[b, 3] * shrink).astype(BF16)
        context = dot(v2_t, prob[b, 4]) + dot(v1_t[:, at_block(sibling(b))], prob[b, 3])
        for side in near_sides(b, nb):
            prob[b, side] = (weights[b, side] * shrink).astype(BF16)
            context = context + dot(v_t[:, at_block(b + side - 1)], prob[b, side])
        for side, weight in zip(sides, fresh):
            prob[b, side] = (weight * inverse).astype(BF16)
            context = context + dot((rim_high if side else rim_low)[1].T, prob[b, side])
        attended[b] = context.T.astype(BF16)
    for step, out in enumerate(outs):
        out[...] = attended[me ^ step]


def slope_kernel(nb, groups, *refs):
    (query, near, level_1, prob, grads, top_2), refs = refs[:6], refs[6:]
    (rim_low, rim_high), (shift, *rim_outs, sums, rim_sums) = from_beside(groups, refs)
    for b in range(nb):
        grad = grads[b]
        slopes = []
        for side in range(3):
            if side in near_sides(b, nb):
                value = near[b + side - 1, 1]
            else:
                value = (rim_high if side else rim_low)[1]
            slopes.append(dot_nt(value, grad))
        slopes.append(dot_nt(level_1[1, at_block(sibling(b))], grad))
        slopes.append(dot_nt(top_2[1], grad))
        delta = 0.0
        for part, slope in enumerate(slopes):
            delta = delta + (prob[b, part].astype(F32) * slope).sum(0, keepdims=True)
        for part, slope in enumerate(slopes):
            shift[b, part] = (prob[b, part].astype(F32) * (slope - delta)).astype(BF16)
        for side in rim_sides(b, nb):
            rim_sums[side // 2, 0] = SCALE * dot(shift[b, side], query[0, b])
            rim_sums[side // 2, 1] = dot(prob[b, side], grad)
        key, value = SCALE * dot(shift[b, 4], query[2, b]), dot(prob[b, 4], grad)
        if b:
            key, value = key + sums[0], value + sums[1]
        if b < nb - 1:
            sums[0], sums[1] = key, value
        else:
            rim_outs[0][0], rim_outs[0][1] = key.astype(BF16), value.astype(BF16)
    low, high = rim_sums[0], rim_sums[1]
    if groups == 2:
        upper = lax.axis_index("seq") >= GROUP
        rim_outs[0][2:] = jnp.where(upper, low, high).astype(BF16)
    else:
        rim_outs[1][...] = high.astype(BF16)
        rim_outs[2][...] = low.astype(BF16)


def backward_kernel(nb, groups, *refs):
    (query, k_t, k1_t, prob, shift, grads, top_2), refs = refs[:7], refs[7:]
    (rim_low, rim_high), refs = from_beside(groups, refs)
    grad_q, grad_kv, sums_1 = refs
    k2_t = top_2[0].T
    even_1, even_2 = averaging(1), averaging(2)
    for b in range(nb):
        grad_t = 0.0
        for side in range(3):
            if side in near_sides(b, nb):
                key_t = k_t[:, at_block(b + side - 1)]
            else:
                key_t = (rim_high if side else rim_low)[0].T
            grad_t = grad_t + dot(key_t, shift[b, side])
        for spread, key_t, part in ((even_1, k1_t[:, at_block(sibling(b))], 3), (even_2, k2_t, 4)):
            high, low = halves(dot(key_t, shift[b, part]))
            grad_t = grad_t + (dot(high, spread) + dot(low, spread))
        grad_q[b] = (SCALE * grad_t).T.astype(BF16)
    for c in range(nb // 2):
        users = [b for b in range(nb) if sibling(b) == c]
        sums_1[0, at_block(c)] = SCALE * sum(dot(shift[b, 3], query[1, b]) for b in users)
        sums_1[1, at_block(c)] = sum(dot(prob[b, 3], grads[b]) for b in users)
    spread = spreading(1)
    half = BLOCK // 2
    for s in range(nb):
        users = [(s + 1 - side, side) for side in range(3) if 0 <= s + 1 - side < nb]
        key = SCALE * sum(dot(shift[b, side], query[0, b]) for b, side in users)
        value = sum(dot(prob[b, side], grads[b]) for b, side in users)
        for part, total in enumerate((key, value)):
            high, low = halves(sums_1[part, s * half : (s + 1) * half])
            grad_kv[part, s] = total + (dot(spread, high) + dot(spread, low))


def share_kernel(kept, got, _, across, here):
    across[...] = (kept[1].astype(F32) + got[1].astype(F32)).astype(BF16)
    here[...] = kept[0].astype(F32) + got[0].astype(F32)


def combine_kernel(nb, groups, grad_q, grad_kv, *refs):
    (got_top, got_low, got_high), (*outs, out) = from_others(groups, refs)
    present = rim_present(groups)
    spread = spreading(2)
    quarter = BLOCK // 4
    for b in range(nb):
        for part in range(2):
            total = grad_kv[part, b] + dot(spread, got_top[part, b * quarter : (b + 1) * quarter])
            if b == 0:
                total = total + jnp.where(present[0], got_low[part].astype(F32), 0.0)
            if b == nb - 1:
                total = total + jnp.where(present[1], got_high[part].astype(F32), 0.0)
            out[b, part] = total.astype(BF16)
    me = member()
    for step, chunk in enumerate(outs):
        chunk[:2] = out[me ^ step]
        chunk[2] = grad_q[me ^ step]


def unpack_kernel(*refs):
    here, across, *refs = refs
    chunks, (*outs, mixed) = refs[:GROUP], refs[GROUP:]
    mixed[...] = (here[...] + across[...].astype(F32)).astype(BF16)
    me = member()
    for step in range(GROUP):
        at = columns(me ^ step)
        for part, out in enumerate(outs):
            out[:, at] = chunks[step][part]


def share():
    return lax.axis_index("mp")


def grad_kernel(*refs):
    pieces, (out_weight, tops), refs = refs[:N_MP], refs[N_MP : N_MP + 2], refs[N_MP + 2 :]
    *outs, whole, heads = refs
    me = member()
    for step, piece in enumerate(pieces):
        whole[span(share() ^ step, piece.shape[0]), :] = piece[...]
    heads[...] = dot_nt(whole[...], out_weight[...]).astype(BF16)
    quarter = tops.shape[2]
    for step, out in enumerate(outs):
        out[:BLOCK] = heads[:, columns(me ^ step)]
        for part in range(2):
            out[BLOCK + part * quarter : BLOCK + (part + 1) * quarter] = tops[me ^ step, part]


def project_kernel(*refs):
    chunks, out_weight, (kept, sent, attended, whole) = refs[:GROUP], refs[GROUP], refs[-4:]
    me = member()
    for step, chunk in enumerate(chunks):
        attended[:, columns(me ^ step)] = chunk[...]
    whole[...] = dot(attended[...], out_weight[...]).astype(BF16)
    rows = kept.shape[1]
    for far in range(2):
        kept[far] = whole[span(share() ^ (2 * far), rows), :]
        sent[far] = whole[span(share() ^ (2 * far + 1), rows), :]


def swapped(x, axis, step):
    return lax.ppermute(x, axis, [(i, i ^ step) for i in range(lax.axis_size(axis))])


def exchanged(chunks):
    got = {step: swapped(chunks[step], "seq", step) for step in (3, 1, 2)}
    return [chunks[0]] + [got[step] for step in range(1, GROUP)]


def beside(arrays):
    count = lax.axis_size("seq")
    if len(arrays) == 1:
        return [swapped(arrays[0], "seq", GROUP)]
    up = [(i, i + GROUP) for i in range(count - GROUP)]
    down = [(j, i) for i, j in up]
    return [lax.ppermute(arrays[0], "seq", up), lax.ppermute(arrays[1], "seq", down)]


def crossed(arrays):
    count = lax.axis_size("seq")
    across = swapped(arrays[0], "seq", GROUP)
    if len(arrays) == 1:
        return [across]
    up = [(i, i + GROUP) for i in range(count - GROUP)]
    down = [(j, i) for i, j in up]
    return [across, lax.ppermute(arrays[1], "seq", up), lax.ppermute(arrays[2], "seq", down)]


def per_device(queries, keys, values, out_weight, out_grad):
    rows, width = queries.shape
    assert width == GROUP * HEAD_DIM and rows == BLOCK and lax.axis_size("mp") == N_MP
    count = lax.axis_size("seq")
    assert count % (2 * GROUP) == 0
    groups = count // GROUP
    nb = GROUP
    tokens = nb * rows
    half, quarter = rows // 2, rows // 4
    model = out_weight.shape[1]
    block = shape(2, rows, HEAD_DIM)
    sent = [shape(4, rows, HEAD_DIM)] if groups == 2 else [block] * 3
    rims = [block] * (1 if groups == 2 else 2)
    quarter = rows // 4
    in_order = shape(nb, rows, HEAD_DIM)
    score_flops = 2 * tokens * 5 * BLOCK * HEAD_DIM
    weight_flops = 2 * rows * out_weight.size

    chunk = shape(rows, HEAD_DIM)
    triple = shape(3, rows, HEAD_DIM)
    chunks = call(
        pack_kernel,
        [triple] * GROUP,
        (queries, keys, values),
        scratch=[pltpu.SemaphoreType.DMA((3 * GROUP,))],
        space=pltpu.HBM,
        limit=53,
    )
    far = swapped(out_grad, "mp", 2)
    chunks = exchanged(chunks)
    (tops,) = call(pool_kernel, [shape(GROUP, 2, quarter, HEAD_DIM)], (keys, values))
    tops = swapped(tops, "seq", GROUP)
    (own_grad,) = call(copy_kernel, [shape(*out_grad.shape)], (out_grad, chunks[1]))
    far, near, queries, level_1, *refs = call(
        functools.partial(gather_kernel, nb, groups),
        [
            shape(*out_grad.shape),
            shape(nb, 2, rows, HEAD_DIM),
            shape(nb, rows, HEAD_DIM),
            shape(2, tokens // 2, HEAD_DIM),
        ]
        + rims,
        (far, tops, *chunks),
    )
    rim_blocks = beside(refs)
    grad_chunks = call(
        grad_kernel,
        [shape(rows + 2 * quarter, HEAD_DIM)] * GROUP,
        (own_grad, swapped(own_grad, "mp", 1), far, swapped(far, "mp", 1), out_weight, tops),
        scratch=[pltpu.VMEM((rows, model), BF16), pltpu.VMEM((rows, width), BF16)],
        flops=weight_flops,
    )
    query, k_t, v_t, k1_t, v1_t, weights, stats = call(
        functools.partial(local_kernel, nb),
        [
            shape(3, nb, rows, HEAD_DIM),
            shape(HEAD_DIM, tokens),
            shape(HEAD_DIM, tokens),
            shape(HEAD_DIM, tokens // 2),
            shape(HEAD_DIM, tokens // 2),
            shape(nb, 4, BLOCK, BLOCK, dtype=F32),
            shape(nb, 8, BLOCK, dtype=F32),
        ],
        (near, queries, level_1, grad_chunks[0]),
        flops=score_flops,
    )
    grad_chunks = exchanged(grad_chunks)
    prob, grads, top_2, *attended = call(
        functools.partial(forward_kernel, nb, groups),
        [shape(nb, 5, BLOCK, BLOCK), in_order, block] + [chunk] * GROUP,
        (query, v_t, v1_t, weights, stats, *rim_blocks, *grad_chunks),
        scratch=[pltpu.VMEM((nb, rows, HEAD_DIM), BF16)],
        flops=score_flops,
    )
    attended = exchanged(attended)
    shift, *rim_grads = call(
        functools.partial(slope_kernel, nb, groups),
        [shape(nb, 5, BLOCK, BLOCK)] + sent,
        (query, near, level_1, prob, grads, top_2, *rim_blocks),
        scratch=[pltpu.VMEM((2, BLOCK, HEAD_DIM), F32), pltpu.VMEM((2, 2, BLOCK, HEAD_DIM), F32)],
        flops=score_flops,
    )
    other_grads = crossed(rim_grads)
    grad_q, grad_kv = call(
        functools.partial(backward_kernel, nb, groups),
        [in_order, shape(2, nb, rows, HEAD_DIM, dtype=F32)],
        (query, k_t, k1_t, prob, shift, grads, top_2, *rim_blocks),
        scratch=[pltpu.VMEM((2, tokens // 2, HEAD_DIM), F32)],
        flops=1,
    )
    local = rows // N_MP
    shares = shape(2, local, model)
    kept, given = call(
        project_kernel,
        [shares] * 2,
        (*attended, out_weight, shift),
        scratch=[pltpu.VMEM((rows, width), BF16), pltpu.VMEM((rows, model), BF16)],
        flops=weight_flops,
    )
    chunks = call(
        functools.partial(combine_kernel, nb, groups),
        [triple] * GROUP,
        (grad_q, grad_kv, *other_grads),
        scratch=[pltpu.VMEM((nb, 2, rows, HEAD_DIM), BF16)],
        flops=20 * score_flops,
    )
    across, here = call(
        share_kernel,
        [shape(local, model), shape(local, model, dtype=F32)],
        (kept, swapped(given, "mp", 1), chunks[0]),
    )
    chunks = exchanged(chunks)
    across = swapped(across, "mp", 2)
    grad_k, grad_v, grad_q, mixed = call(
        unpack_kernel,
        [shape(rows, width)] * 3 + [shape(local, model)],
        (here, across, *chunks),
    )
    return mixed, grad_q, grad_k, grad_v


def solution(mesh):
    return jax.shard_map(
        per_device,
        mesh=mesh,
        in_specs=(
            P("seq", "mp"),
            P("seq", "mp"),
            P("seq", "mp"),
            P("mp", None),
            P(("seq", "mp"), None),
        ),
        out_specs=(P(("seq", "mp"), None), P("seq", "mp"), P("seq", "mp"), P("seq", "mp")),
        check_vma=False,
    )
```

```python
import functools

import jax
import jax.numpy as jnp
from jax import lax
from jax.experimental import pallas as pl
from jax.experimental.pallas import tpu as pltpu
from jax.sharding import PartitionSpec as P

HEAD_DIM = 128
BLOCK = 256
LEVELS = 2
GROUP = 4
N_MP = 4
SCALE = HEAD_DIM**-0.5
LOG2E = 1.4426950408889634
BF16 = jnp.bfloat16
F32 = jnp.float32


def dot(a, b):
    return lax.dot_general(a, b, (((1,), (0,)), ((), ())), preferred_element_type=F32)


def dot_nt(a, b):
    return lax.dot_general(a, b, (((1,), (1,)), ((), ())), preferred_element_type=F32)


def shape(*dims, dtype=BF16):
    return jax.ShapeDtypeStruct(dims, dtype)


def call(kernel, out_shape, args, scratch=(), flops=0, limit=32, space=pltpu.VMEM):
    whole = pl.BlockSpec(memory_space=space)
    moved = sum(x.size * x.dtype.itemsize for x in (*args, *out_shape))
    return pl.pallas_call(
        kernel,
        out_shape=out_shape,
        in_specs=[whole] * len(args),
        out_specs=[whole] * len(out_shape),
        scratch_shapes=scratch,
        compiler_params=pltpu.CompilerParams(vmem_limit_bytes=limit << 20),
        cost_estimate=pl.CostEstimate(flops=flops, bytes_accessed=moved if flops else 0, transcendentals=0),
    )(*args)


def columns(index):
    return pl.ds(pl.multiple_of(index * HEAD_DIM, HEAD_DIM), HEAD_DIM)


def span(index, size):
    return pl.ds(pl.multiple_of(index * size, size), size)


def iota(dims, axis):
    return lax.broadcasted_iota(jnp.int32, dims, axis)


def averaging(level):
    dims = (BLOCK, BLOCK)
    same = (iota(dims, 0) >> level) == (iota(dims, 1) >> level)
    return jnp.where(same, 2.0**-level, 0.0).astype(BF16)


def pooling():
    dims = (BLOCK // 2, BLOCK)
    return jnp.where(iota(dims, 0) == (iota(dims, 1) >> 1), 0.5, 0.0).astype(BF16)


def spreading(level):
    dims = (BLOCK, BLOCK >> level)
    return jnp.where((iota(dims, 0) >> level) == iota(dims, 1), 2.0**-level, 0.0).astype(BF16)


def halves(x):
    high = x.astype(BF16)
    return high, (x - high.astype(F32)).astype(BF16)


def at_block(b):
    return slice(b * BLOCK, (b + 1) * BLOCK)


def sibling(b):
    return (b >> 1) ^ 1


def rim_present(groups):
    group = lax.axis_index("seq") // GROUP
    return group > 0, group < groups - 1


def member():
    return lax.rem(lax.axis_index("seq"), GROUP)


def columns(index):
    return pl.ds(pl.multiple_of(index * HEAD_DIM, HEAD_DIM), HEAD_DIM)


def pack_kernel(q, k, v, *refs):
    *outs, sems = refs
    me = member()
    copies = []
    for step in (3, 1, 2, 0):
        for part, source in enumerate((k, v, q)):
            piece = source.at[:, columns(me ^ step)]
            copies.append(pltpu.make_async_copy(piece, outs[step].at[part], sems.at[len(copies)]))
    for copy in copies:
        copy.start()
    for copy in copies:
        copy.wait()


def pool_kernel(k, v, out):
    pool = pooling()
    half = BLOCK // 2
    for part, source in enumerate((k, v)):
        once = dot(pool, source[...]).astype(BF16)
        twice = dot(pool[: half // 2, :half], once).astype(BF16)
        for head in range(GROUP):
            out[head, part] = twice[:, head * HEAD_DIM : (head + 1) * HEAD_DIM]


def copy_kernel(x, _, out):
    out[...] = x[...]


def gather_kernel(nb, groups, far, _, *refs):
    chunks, (far_out, near, queries, level_1, *rims) = refs[:GROUP], refs[GROUP:]
    far_out[...] = far[...]
    me = member()
    for step, chunk in enumerate(chunks):
        near[me ^ step] = chunk[:2]
        queries[me ^ step] = chunk[2]
    pool = pooling()
    half = BLOCK // 2
    for part in range(2):
        for b in range(nb):
            level_1[part, b * half : (b + 1) * half] = dot(pool, near[b, part]).astype(BF16)
    if groups == 2:
        upper = lax.axis_index("seq") >= GROUP
        rims[0][...] = jnp.where(upper, near[0], near[nb - 1])
    else:
        rims[0][...] = near[nb - 1]
        rims[1][...] = near[0]


def from_beside(groups, refs):
    if groups == 2:
        return (refs[0], refs[0]), refs[1:]
    return refs[:2], refs[2:]


def from_others(groups, refs):
    if groups == 2:
        return (refs[0].at[:2], refs[0].at[2:], refs[0].at[2:]), refs[1:]
    return refs[:3], refs[3:]


def near_sides(b, nb):
    return [side for side in range(3) if 0 <= b + side - 1 < nb]


def local_kernel(nb, near, queries, level_1, _, query, k_t, v_t, k1_t, v1_t, weights, stats):
    even_1, even_2 = averaging(1), averaging(2)
    for b in range(nb):
        query[0, b] = queries[b]
        once = dot(even_1, queries[b]).astype(BF16)
        query[1, b] = once
        query[2, b] = dot(even_2, once).astype(BF16)
        for part, transposed in enumerate((k_t, v_t)):
            transposed[:, at_block(b)] = near[b, part].T
    for c in range(nb // 2):
        for part, transposed in enumerate((k1_t, v1_t)):
            transposed[:, at_block(c)] = level_1[part, at_block(c)].T
    for b in range(nb):
        sides = near_sides(b, nb)
        scores = [dot_nt(near[b + side - 1, 0], query[0, b]) * (SCALE * LOG2E) for side in sides]
        coarse = dot_nt(level_1[0, at_block(sibling(b))], query[1, b]) * (SCALE * LOG2E)
        top = coarse.max(0, keepdims=True)
        for score in scores:
            top = jnp.maximum(top, score.max(0, keepdims=True))
        weight = 2.0 * jnp.exp2(coarse - top)
        weights[b, 3] = weight
        total = weight.sum(0, keepdims=True)
        for side, score in zip(sides, scores):
            weight = jnp.exp2(score - top)
            weights[b, side] = weight
            total = total + weight.sum(0, keepdims=True)
        stats[b, :1] = top
        stats[b, 1:2] = total


def rim_sides(b, nb):
    return [side for side in range(3) if not 0 <= b + side - 1 < nb]


def forward_kernel(nb, groups, *refs):
    (query, v_t, v1_t, weights, stats), refs = refs[:5], refs[5:]
    (rim_low, rim_high), refs = from_beside(groups, refs)
    chunks, refs = refs[:GROUP], refs[GROUP:]
    (prob, grads, top_2, deltas, far_shift), refs = refs[:5], refs[5:]
    outs, (*rim_outs, attended, sums, rim_sums) = refs[:GROUP], refs[GROUP:]
    ones = jnp.ones((8, HEAD_DIM), BF16)
    present = rim_present(groups)
    me = member()
    quarter = BLOCK // 4
    for step, chunk in enumerate(chunks):
        grads[me ^ step] = chunk[:BLOCK]
        for part in range(2):
            level = chunk[BLOCK + part * quarter : BLOCK + (part + 1) * quarter]
            top_2[part, span(me ^ step, quarter), :] = level
    v2_t = top_2[1].T
    for b in range(nb):
        sides = rim_sides(b, nb)
        scores = []
        for side in sides:
            score = dot_nt((rim_high if side else rim_low)[0], query[0, b]) * (SCALE * LOG2E)
            scores.append(jnp.where(present[side // 2], score, -jnp.inf))
        coarse = dot_nt(top_2[0], query[2, b]) * (SCALE * LOG2E)
        old = stats[b, :1]
        top = jnp.maximum(old, coarse.max(0, keepdims=True))
        for score in scores:
            top = jnp.maximum(top, score.max(0, keepdims=True))
        shrink = jnp.exp2(old - top)
        far = 4.0 * jnp.exp2(coarse - top)
        total = shrink * stats[b, 1:2] + far.sum(0, keepdims=True)
        fresh = []
        for score in scores:
            fresh.append(jnp.exp2(score - top))
            total = total + fresh[-1].sum(0, keepdims=True)
        inverse = 1.0 / total
        shrink = shrink * inverse
        prob[b, 4] = (far * inverse).astype(BF16)
        prob[b, 3] = (weights[b, 3] * shrink).astype(BF16)
        context = dot(v2_t, prob[b, 4]) + dot(v1_t[:, at_block(sibling(b))], prob[b, 3])
        for side in near_sides(b, nb):
            prob[b, side] = (weights[b, side] * shrink).astype(BF16)
            context = context + dot(v_t[:, at_block(b + side - 1)], prob[b, side])
        for side, weight in zip(sides, fresh):
            prob[b, side] = (weight * inverse).astype(BF16)
            context = context + dot((rim_high if side else rim_low)[1].T, prob[b, side])
        context = context.T
        attended[b] = context.astype(BF16)
        high, low = halves(grads[b].astype(F32) * context)
        deltas[b] = dot_nt(ones, high) + dot_nt(ones, low)
    for step, out in enumerate(outs):
        out[...] = attended[me ^ step]
    for b in range(nb):
        grad, delta = grads[b], deltas[b, :1]
        shift = (prob[b, 4].astype(F32) * (dot_nt(top_2[1], grad) - delta)).astype(BF16)
        far_shift[b, 0] = shift
        key, value = SCALE * dot(shift, query[2, b]), dot(prob[b, 4], grad)
        sums[0], sums[1] = (key, value) if b == 0 else (key + sums[0], value + sums[1])
        for side in rim_sides(b, nb):
            slope = dot_nt((rim_high if side else rim_low)[1], grad)
            shift = (prob[b, side].astype(F32) * (slope - delta)).astype(BF16)
            far_shift[b, 1] = shift
            rim_sums[side // 2, 0] = SCALE * dot(shift, query[0, b])
            rim_sums[side // 2, 1] = dot(prob[b, side], grad)
    rim_outs[0][:2] = sums[...].astype(BF16)
    low, high = rim_sums[0], rim_sums[1]
    if groups == 2:
        upper = lax.axis_index("seq") >= GROUP
        rim_outs[0][2:] = jnp.where(upper, low, high).astype(BF16)
    else:
        rim_outs[1][...] = high.astype(BF16)
        rim_outs[2][...] = low.astype(BF16)


def backward_kernel(nb, groups, *refs):
    (query, near, level_1, k_t, k1_t, prob, grads, top_2, deltas, far_shift), refs = refs[:10], refs[10:]
    (rim_low, rim_high), refs = from_beside(groups, refs)
    grad_q, grad_kv, shift, sums_1 = refs
    k2_t = top_2[0].T
    even_1, even_2 = averaging(1), averaging(2)
    for b in range(nb):
        grad, delta = grads[b], deltas[b, :1]
        grad_t = 0.0
        for side in range(3):
            if side in near_sides(b, nb):
                slope = dot_nt(near[b + side - 1, 1], grad)
                part = (prob[b, side].astype(F32) * (slope - delta)).astype(BF16)
                shift[b, side] = part
                grad_t = grad_t + dot(k_t[:, at_block(b + side - 1)], part)
            else:
                grad_t = grad_t + dot((rim_high if side else rim_low)[0].T, far_shift[b, 1])
        slope = dot_nt(level_1[1, at_block(sibling(b))], grad)
        part = (prob[b, 3].astype(F32) * (slope - delta)).astype(BF16)
        shift[b, 3] = part
        coarse = ((even_1, k1_t[:, at_block(sibling(b))], part), (even_2, k2_t, far_shift[b, 0]))
        for spread, key_t, part in coarse:
            high, low = halves(dot(key_t, part))
            grad_t = grad_t + (dot(high, spread) + dot(low, spread))
        grad_q[b] = (SCALE * grad_t).T.astype(BF16)
    for c in range(nb // 2):
        users = [b for b in range(nb) if sibling(b) == c]
        sums_1[0, at_block(c)] = SCALE * sum(dot(shift[b, 3], query[1, b]) for b in users)
        sums_1[1, at_block(c)] = sum(dot(prob[b, 3], grads[b]) for b in users)
    spread = spreading(1)
    half = BLOCK // 2
    for s in range(nb):
        users = [(s + 1 - side, side) for side in range(3) if 0 <= s + 1 - side < nb]
        key = SCALE * sum(dot(shift[b, side], query[0, b]) for b, side in users)
        value = sum(dot(prob[b, side], grads[b]) for b, side in users)
        for part, total in enumerate((key, value)):
            high, low = halves(sums_1[part, s * half : (s + 1) * half])
            grad_kv[part, s] = total + (dot(spread, high) + dot(spread, low))


def share_kernel(kept, got, _, across, here):
    across[...] = (kept[1].astype(F32) + got[1].astype(F32)).astype(BF16)
    here[...] = kept[0].astype(F32) + got[0].astype(F32)


def combine_kernel(nb, groups, grad_q, grad_kv, *refs):
    (got_top, got_low, got_high), (*outs, out) = from_others(groups, refs)
    present = rim_present(groups)
    spread = spreading(2)
    quarter = BLOCK // 4
    for b in range(nb):
        for part in range(2):
            total = grad_kv[part, b] + dot(spread, got_top[part, b * quarter : (b + 1) * quarter])
            if b == 0:
                total = total + jnp.where(present[0], got_low[part].astype(F32), 0.0)
            if b == nb - 1:
                total = total + jnp.where(present[1], got_high[part].astype(F32), 0.0)
            out[b, part] = total.astype(BF16)
    me = member()
    for step, chunk in enumerate(outs):
        chunk[:2] = out[me ^ step]
        chunk[2] = grad_q[me ^ step]


def unpack_kernel(*refs):
    here, across, *refs = refs
    chunks, (*outs, mixed) = refs[:GROUP], refs[GROUP:]
    mixed[...] = (here[...] + across[...].astype(F32)).astype(BF16)
    me = member()
    for step in range(GROUP):
        at = columns(me ^ step)
        for part, out in enumerate(outs):
            out[:, at] = chunks[step][part]


def share():
    return lax.axis_index("mp")


def grad_kernel(*refs):
    pieces, (out_weight, tops), refs = refs[:N_MP], refs[N_MP : N_MP + 2], refs[N_MP + 2 :]
    *outs, whole, heads = refs
    me = member()
    for step, piece in enumerate(pieces):
        whole[span(share() ^ step, piece.shape[0]), :] = piece[...]
    heads[...] = dot_nt(whole[...], out_weight[...]).astype(BF16)
    quarter = tops.shape[2]
    for step, out in enumerate(outs):
        out[:BLOCK] = heads[:, columns(me ^ step)]
        for part in range(2):
            out[BLOCK + part * quarter : BLOCK + (part + 1) * quarter] = tops[me ^ step, part]


def project_kernel(*refs):
    chunks, out_weight, (kept, sent, attended, whole) = refs[:GROUP], refs[GROUP], refs[-4:]
    me = member()
    for step, chunk in enumerate(chunks):
        attended[:, columns(me ^ step)] = chunk[...]
    whole[...] = dot(attended[...], out_weight[...]).astype(BF16)
    rows = kept.shape[1]
    for far in range(2):
        kept[far] = whole[span(share() ^ (2 * far), rows), :]
        sent[far] = whole[span(share() ^ (2 * far + 1), rows), :]


def swapped(x, axis, step):
    return lax.ppermute(x, axis, [(i, i ^ step) for i in range(lax.axis_size(axis))])


def exchanged(chunks):
    got = {step: swapped(chunks[step], "seq", step) for step in (3, 1, 2)}
    return [chunks[0]] + [got[step] for step in range(1, GROUP)]


def beside(arrays):
    count = lax.axis_size("seq")
    if len(arrays) == 1:
        return [swapped(arrays[0], "seq", GROUP)]
    up = [(i, i + GROUP) for i in range(count - GROUP)]
    down = [(j, i) for i, j in up]
    return [lax.ppermute(arrays[0], "seq", up), lax.ppermute(arrays[1], "seq", down)]


def crossed(arrays):
    count = lax.axis_size("seq")
    across = swapped(arrays[0], "seq", GROUP)
    if len(arrays) == 1:
        return [across]
    up = [(i, i + GROUP) for i in range(count - GROUP)]
    down = [(j, i) for i, j in up]
    return [across, lax.ppermute(arrays[1], "seq", up), lax.ppermute(arrays[2], "seq", down)]


def per_device(queries, keys, values, out_weight, out_grad):
    rows, width = queries.shape
    assert width == GROUP * HEAD_DIM and rows == BLOCK and lax.axis_size("mp") == N_MP
    count = lax.axis_size("seq")
    assert count % (2 * GROUP) == 0
    groups = count // GROUP
    nb = GROUP
    tokens = nb * rows
    half, quarter = rows // 2, rows // 4
    model = out_weight.shape[1]
    block = shape(2, rows, HEAD_DIM)
    sent = [shape(4, rows, HEAD_DIM)] if groups == 2 else [block] * 3
    rims = [block] * (1 if groups == 2 else 2)
    quarter = rows // 4
    in_order = shape(nb, rows, HEAD_DIM)
    score_flops = 2 * tokens * 5 * BLOCK * HEAD_DIM
    weight_flops = 2 * rows * out_weight.size

    chunk = shape(rows, HEAD_DIM)
    triple = shape(3, rows, HEAD_DIM)
    chunks = call(
        pack_kernel,
        [triple] * GROUP,
        (queries, keys, values),
        scratch=[pltpu.SemaphoreType.DMA((3 * GROUP,))],
        space=pltpu.HBM,
        limit=53,
    )
    far = swapped(out_grad, "mp", 2)
    chunks = exchanged(chunks)
    (tops,) = call(pool_kernel, [shape(GROUP, 2, quarter, HEAD_DIM)], (keys, values))
    tops = swapped(tops, "seq", GROUP)
    (own_grad,) = call(copy_kernel, [shape(*out_grad.shape)], (out_grad, chunks[1]))
    far, near, queries, level_1, *refs = call(
        functools.partial(gather_kernel, nb, groups),
        [
            shape(*out_grad.shape),
            shape(nb, 2, rows, HEAD_DIM),
            shape(nb, rows, HEAD_DIM),
            shape(2, tokens // 2, HEAD_DIM),
        ]
        + rims,
        (far, tops, *chunks),
    )
    rim_blocks = beside(refs)
    grad_chunks = call(
        grad_kernel,
        [shape(rows + 2 * quarter, HEAD_DIM)] * GROUP,
        (own_grad, swapped(own_grad, "mp", 1), far, swapped(far, "mp", 1), out_weight, tops),
        scratch=[pltpu.VMEM((rows, model), BF16), pltpu.VMEM((rows, width), BF16)],
        flops=weight_flops,
    )
    query, k_t, v_t, k1_t, v1_t, weights, stats = call(
        functools.partial(local_kernel, nb),
        [
            shape(3, nb, rows, HEAD_DIM),
            shape(HEAD_DIM, tokens),
            shape(HEAD_DIM, tokens),
            shape(HEAD_DIM, tokens // 2),
            shape(HEAD_DIM, tokens // 2),
            shape(nb, 4, BLOCK, BLOCK, dtype=F32),
            shape(nb, 8, BLOCK, dtype=F32),
        ],
        (near, queries, level_1, grad_chunks[0]),
        flops=score_flops,
    )
    grad_chunks = exchanged(grad_chunks)
    stat = shape(nb, 8, BLOCK, dtype=F32)
    prob, grads, top_2, deltas, far_shift, *refs = call(
        functools.partial(forward_kernel, nb, groups),
        [shape(nb, 5, BLOCK, BLOCK), in_order, block, stat, shape(nb, 2, BLOCK, BLOCK)]
        + [chunk] * GROUP
        + sent,
        (query, v_t, v1_t, weights, stats, *rim_blocks, *grad_chunks),
        scratch=[
            pltpu.VMEM((nb, rows, HEAD_DIM), BF16),
            pltpu.VMEM((2, BLOCK, HEAD_DIM), F32),
            pltpu.VMEM((2, 2, BLOCK, HEAD_DIM), F32),
        ],
        flops=score_flops,
    )
    attended = exchanged(refs[:GROUP])
    rim_grads = refs[GROUP:]
    other_grads = crossed(rim_grads)
    grad_q, grad_kv = call(
        functools.partial(backward_kernel, nb, groups),
        [in_order, shape(2, nb, rows, HEAD_DIM, dtype=F32)],
        (query, near, level_1, k_t, k1_t, prob, grads, top_2, deltas, far_shift, *rim_blocks),
        scratch=[
            pltpu.VMEM((nb, 4, BLOCK, BLOCK), BF16),
            pltpu.VMEM((2, tokens // 2, HEAD_DIM), F32),
        ],
        flops=1,
    )
    local = rows // N_MP
    shares = shape(2, local, model)
    kept, given = call(
        project_kernel,
        [shares] * 2,
        (*attended, out_weight, grad_q),
        scratch=[pltpu.VMEM((rows, width), BF16), pltpu.VMEM((rows, model), BF16)],
        flops=weight_flops,
    )
    chunks = call(
        functools.partial(combine_kernel, nb, groups),
        [triple] * GROUP,
        (grad_q, grad_kv, *other_grads),
        scratch=[pltpu.VMEM((nb, 2, rows, HEAD_DIM), BF16)],
        flops=20 * score_flops,
    )
    across, here = call(
        share_kernel,
        [shape(local, model), shape(local, model, dtype=F32)],
        (kept, swapped(given, "mp", 1), chunks[0]),
    )
    chunks = exchanged(chunks)
    across = swapped(across, "mp", 2)
    grad_k, grad_v, grad_q, mixed = call(
        unpack_kernel,
        [shape(rows, width)] * 3 + [shape(local, model)],
        (here, across, *chunks),
    )
    return mixed, grad_q, grad_k, grad_v


def solution(mesh):
    return jax.shard_map(
        per_device,
        mesh=mesh,
        in_specs=(
            P("seq", "mp"),
            P("seq", "mp"),
            P("seq", "mp"),
            P("mp", None),
            P(("seq", "mp"), None),
        ),
        out_specs=(P(("seq", "mp"), None), P("seq", "mp"), P("seq", "mp"), P("seq", "mp")),
        check_vma=False,
    )
```

```python
import functools

import jax
import jax.numpy as jnp
from jax import lax
from jax.experimental import pallas as pl
from jax.experimental.pallas import tpu as pltpu
from jax.sharding import PartitionSpec as P

HEAD_DIM = 128
BLOCK = 256
LEVELS = 2
GROUP = 4
N_MP = 4
SCALE = HEAD_DIM**-0.5
LOG2E = 1.4426950408889634
BF16 = jnp.bfloat16
F32 = jnp.float32


def dot(a, b):
    return lax.dot_general(a, b, (((1,), (0,)), ((), ())), preferred_element_type=F32)


def dot_nt(a, b):
    return lax.dot_general(a, b, (((1,), (1,)), ((), ())), preferred_element_type=F32)


def shape(*dims, dtype=BF16):
    return jax.ShapeDtypeStruct(dims, dtype)


def call(kernel, out_shape, args, scratch=(), flops=0, limit=32, space=pltpu.VMEM):
    whole = pl.BlockSpec(memory_space=space)
    moved = sum(x.size * x.dtype.itemsize for x in (*args, *out_shape))
    return pl.pallas_call(
        kernel,
        out_shape=out_shape,
        in_specs=[whole] * len(args),
        out_specs=[whole] * len(out_shape),
        scratch_shapes=scratch,
        compiler_params=pltpu.CompilerParams(vmem_limit_bytes=limit << 20),
        cost_estimate=pl.CostEstimate(flops=flops, bytes_accessed=moved if flops else 0, transcendentals=0),
    )(*args)


def columns(index):
    return pl.ds(pl.multiple_of(index * HEAD_DIM, HEAD_DIM), HEAD_DIM)


def span(index, size):
    return pl.ds(pl.multiple_of(index * size, size), size)


def iota(dims, axis):
    return lax.broadcasted_iota(jnp.int32, dims, axis)


def averaging(level):
    dims = (BLOCK, BLOCK)
    same = (iota(dims, 0) >> level) == (iota(dims, 1) >> level)
    return jnp.where(same, 2.0**-level, 0.0).astype(BF16)


def pooling():
    dims = (BLOCK // 2, BLOCK)
    return jnp.where(iota(dims, 0) == (iota(dims, 1) >> 1), 0.5, 0.0).astype(BF16)


def spreading(level):
    dims = (BLOCK, BLOCK >> level)
    return jnp.where((iota(dims, 0) >> level) == iota(dims, 1), 2.0**-level, 0.0).astype(BF16)


def halves(x):
    high = x.astype(BF16)
    return high, (x - high.astype(F32)).astype(BF16)


def at_block(b):
    return slice(b * BLOCK, (b + 1) * BLOCK)


def sibling(b):
    return (b >> 1) ^ 1


def rim_present(groups):
    group = lax.axis_index("seq") // GROUP
    return group > 0, group < groups - 1


def member():
    return lax.rem(lax.axis_index("seq"), GROUP)


def columns(index):
    return pl.ds(pl.multiple_of(index * HEAD_DIM, HEAD_DIM), HEAD_DIM)


def pack_kernel(q, k, v, *refs):
    *outs, sems = refs
    me = member()
    copies = []
    for step in (3, 1, 2, 0):
        for part, source in enumerate((k, v, q)):
            piece = source.at[:, columns(me ^ step)]
            copies.append(pltpu.make_async_copy(piece, outs[step].at[part], sems.at[len(copies)]))
    for copy in copies:
        copy.start()
    for copy in copies:
        copy.wait()


def pool_kernel(k, v, out):
    pool = pooling()
    half = BLOCK // 2
    for part, source in enumerate((k, v)):
        once = dot(pool, source[...]).astype(BF16)
        twice = dot(pool[: half // 2, :half], once).astype(BF16)
        for head in range(GROUP):
            out[head, part] = twice[:, head * HEAD_DIM : (head + 1) * HEAD_DIM]


def copy_kernel(x, _, out):
    out[...] = x[...]


def gather_kernel(nb, groups, far, _, *refs):
    chunks, (far_out, near, queries, level_1, *rims) = refs[:GROUP], refs[GROUP:]
    far_out[...] = far[...]
    me = member()
    for step, chunk in enumerate(chunks):
        near[me ^ step] = chunk[:2]
        queries[me ^ step] = chunk[2]
    pool = pooling()
    half = BLOCK // 2
    for part in range(2):
        for b in range(nb):
            level_1[part, b * half : (b + 1) * half] = dot(pool, near[b, part]).astype(BF16)
    if groups == 2:
        upper = lax.axis_index("seq") >= GROUP
        rims[0][...] = jnp.where(upper, near[0], near[nb - 1])
    else:
        rims[0][...] = near[nb - 1]
        rims[1][...] = near[0]


def from_beside(groups, refs):
    if groups == 2:
        return (refs[0], refs[0]), refs[1:]
    return refs[:2], refs[2:]


def from_others(groups, refs):
    if groups == 2:
        return (refs[0].at[:2], refs[0].at[2:], refs[0].at[2:]), refs[1:]
    return refs[:3], refs[3:]


def near_sides(b, nb):
    return [side for side in range(3) if 0 <= b + side - 1 < nb]


def local_kernel(nb, near, queries, level_1, _, query, k_t, v_t, k1_t, v1_t, weights, stats):
    even_1, even_2 = averaging(1), averaging(2)
    for b in range(nb):
        query[0, b] = queries[b]
        once = dot(even_1, queries[b]).astype(BF16)
        query[1, b] = once
        query[2, b] = dot(even_2, once).astype(BF16)
        for part, transposed in enumerate((k_t, v_t)):
            transposed[:, at_block(b)] = near[b, part].T
    for c in range(nb // 2):
        for part, transposed in enumerate((k1_t, v1_t)):
            transposed[:, at_block(c)] = level_1[part, at_block(c)].T
    for b in range(nb):
        sides = near_sides(b, nb)
        scores = [dot_nt(near[b + side - 1, 0], query[0, b]) * (SCALE * LOG2E) for side in sides]
        coarse = dot_nt(level_1[0, at_block(sibling(b))], query[1, b]) * (SCALE * LOG2E)
        top = coarse.max(0, keepdims=True)
        for score in scores:
            top = jnp.maximum(top, score.max(0, keepdims=True))
        weight = 2.0 * jnp.exp2(coarse - top)
        weights[b, 3] = weight
        total = weight.sum(0, keepdims=True)
        for side, score in zip(sides, scores):
            weight = jnp.exp2(score - top)
            weights[b, side] = weight
            total = total + weight.sum(0, keepdims=True)
        stats[:1, at_block(b)] = top
        stats[1:2, at_block(b)] = total


def rims_of(nb, groups, low, high):
    group = lax.axis_index("seq") // GROUP
    if groups == 2:
        return [(jnp.where(group > 0, 0, nb - 1), low, None)]
    return [(0, low, group > 0), (nb - 1, high, group < groups - 1)]


def forward_kernel(nb, groups, *refs):
    (query, v_t, v1_t, weights, stats), refs = refs[:5], refs[5:]
    (rim_low, rim_high), refs = from_beside(groups, refs)
    chunks, refs = refs[:GROUP], refs[GROUP:]
    (prob, grads, top_2, deltas, far_shift, rim_shift), refs = refs[:6], refs[6:]
    outs, (*rim_outs, attended, far_prob, rim_prob, row, context_t) = refs[:GROUP], refs[GROUP:]
    rims = rims_of(nb, groups, rim_low, rim_high)
    me = member()
    quarter = BLOCK // 4
    tokens = nb * BLOCK
    for step, chunk in enumerate(chunks):
        grads[me ^ step] = chunk[:BLOCK]
        for part in range(2):
            level = chunk[BLOCK + part * quarter : BLOCK + (part + 1) * quarter]
            top_2[part, span(me ^ step, quarter), :] = level
    coarse_query = query[2].reshape(tokens, HEAD_DIM)
    coarse = dot_nt(top_2[0], coarse_query) * (SCALE * LOG2E)
    row[:1] = jnp.maximum(stats[:1], coarse.max(0, keepdims=True))
    scores = []
    for b, block, present in rims:
        score = dot_nt(block[0], query[0, b]) * (SCALE * LOG2E)
        if present is not None:
            score = jnp.where(present, score, -jnp.inf)
        at = span(b, BLOCK)
        row[:1, at] = jnp.maximum(row[:1, at], score.max(0, keepdims=True))
        scores.append(score)
    top = row[:1]
    shrink = jnp.exp2(stats[:1] - top)
    far = 4.0 * jnp.exp2(coarse - top)
    row[1:2] = shrink * stats[1:2] + far.sum(0, keepdims=True)
    fresh = []
    for (b, _, _), score in zip(rims, scores):
        at = span(b, BLOCK)
        fresh.append(jnp.exp2(score - row[:1, at]))
        row[1:2, at] += fresh[-1].sum(0, keepdims=True)
    inverse = 1.0 / row[1:2]
    row[2:3] = inverse
    row[3:4] = shrink * inverse
    far_prob[...] = (far * inverse).astype(BF16)
    context_t[...] = dot(top_2[1].T, far_prob[...])
    for i, (b, block, _) in enumerate(rims):
        at = span(b, BLOCK)
        rim_prob[i] = (fresh[i] * row[2:3, at]).astype(BF16)
        context_t[:, at] += dot(block[1].T, rim_prob[i])
    for b in range(nb):
        shrink = row[3:4, at_block(b)]
        prob[b, 3] = (weights[b, 3] * shrink).astype(BF16)
        context = context_t[:, at_block(b)] + dot(v1_t[:, at_block(sibling(b))], prob[b, 3])
        for side in near_sides(b, nb):
            prob[b, side] = (weights[b, side] * shrink).astype(BF16)
            context = context + dot(v_t[:, at_block(b + side - 1)], prob[b, side])
        attended[b] = context.T.astype(BF16)
        deltas[:1, at_block(b)] = (grads[b].T.astype(F32) * context).sum(0, keepdims=True)
    grad = grads[...].reshape(tokens, HEAD_DIM)
    slope = dot_nt(top_2[1], grad)
    far_shift[...] = (far_prob[...].astype(F32) * (slope - deltas[:1])).astype(BF16)
    rim_outs[0][0] = (SCALE * dot(far_shift[...], coarse_query)).astype(BF16)
    rim_outs[0][1] = dot(far_prob[...], grad).astype(BF16)
    pairs = []
    for i, (b, block, _) in enumerate(rims):
        slope = dot_nt(block[1], grads[b])
        rim_shift[i] = (rim_prob[i].astype(F32) * (slope - deltas[:1, span(b, BLOCK)])).astype(BF16)
        pairs.append((SCALE * dot(rim_shift[i], query[0, b]), dot(rim_prob[i], grads[b])))
    for part in range(2):
        if groups == 2:
            rim_outs[0][2 + part] = pairs[0][part].astype(BF16)
        else:
            rim_outs[1][part] = pairs[1][part].astype(BF16)
            rim_outs[2][part] = pairs[0][part].astype(BF16)
    for step, out in enumerate(outs):
        out[...] = attended[me ^ step]


def backward_kernel(nb, groups, *refs):
    (query, near, level_1, k_t, k1_t, prob, grads, top_2, deltas, far_shift, rim_shift), refs = refs[:11], refs[11:]
    (rim_low, rim_high), refs = from_beside(groups, refs)
    grad_q, grad_kv, shift, sums_1, query_t = refs
    even_1, even_2 = averaging(1), averaging(2)
    coarse = dot(top_2[0].T, far_shift[...])
    for b in range(nb):
        high, low = halves(coarse[:, at_block(b)])
        query_t[:, at_block(b)] = dot(high, even_2) + dot(low, even_2)
    for i, (b, block, _) in enumerate(rims_of(nb, groups, rim_low, rim_high)):
        query_t[:, span(b, BLOCK)] += dot(block[0].T, rim_shift[i])
    for b in range(nb):
        grad, delta = grads[b], deltas[:1, at_block(b)]
        grad_t = query_t[:, at_block(b)]
        for side in near_sides(b, nb):
            slope = dot_nt(near[b + side - 1, 1], grad)
            part = (prob[b, side].astype(F32) * (slope - delta)).astype(BF16)
            shift[b, side] = part
            grad_t = grad_t + dot(k_t[:, at_block(b + side - 1)], part)
        slope = dot_nt(level_1[1, at_block(sibling(b))], grad)
        part = (prob[b, 3].astype(F32) * (slope - delta)).astype(BF16)
        shift[b, 3] = part
        high, low = halves(dot(k1_t[:, at_block(sibling(b))], part))
        grad_t = grad_t + (dot(high, even_1) + dot(low, even_1))
        grad_q[b] = (SCALE * grad_t).T.astype(BF16)
    for c in range(nb // 2):
        users = [b for b in range(nb) if sibling(b) == c]
        sums_1[0, at_block(c)] = SCALE * sum(dot(shift[b, 3], query[1, b]) for b in users)
        sums_1[1, at_block(c)] = sum(dot(prob[b, 3], grads[b]) for b in users)
    spread = spreading(1)
    half = BLOCK // 2
    for s in range(nb):
        users = [(s + 1 - side, side) for side in range(3) if 0 <= s + 1 - side < nb]
        key = SCALE * sum(dot(shift[b, side], query[0, b]) for b, side in users)
        value = sum(dot(prob[b, side], grads[b]) for b, side in users)
        for part, total in enumerate((key, value)):
            high, low = halves(sums_1[part, s * half : (s + 1) * half])
            grad_kv[part, s] = total + (dot(spread, high) + dot(spread, low))


def share_kernel(kept, got, _, across, here):
    across[...] = (kept[1].astype(F32) + got[1].astype(F32)).astype(BF16)
    here[...] = kept[0].astype(F32) + got[0].astype(F32)


def combine_kernel(nb, groups, grad_q, grad_kv, *refs):
    (got_top, got_low, got_high), (*outs, out) = from_others(groups, refs)
    present = rim_present(groups)
    spread = spreading(2)
    quarter = BLOCK // 4
    for b in range(nb):
        for part in range(2):
            total = grad_kv[part, b] + dot(spread, got_top[part, b * quarter : (b + 1) * quarter])
            if b == 0:
                total = total + jnp.where(present[0], got_low[part].astype(F32), 0.0)
            if b == nb - 1:
                total = total + jnp.where(present[1], got_high[part].astype(F32), 0.0)
            out[b, part] = total.astype(BF16)
    me = member()
    for step, chunk in enumerate(outs):
        chunk[:2] = out[me ^ step]
        chunk[2] = grad_q[me ^ step]


def unpack_kernel(*refs):
    here, across, *refs = refs
    chunks, (*outs, mixed) = refs[:GROUP], refs[GROUP:]
    mixed[...] = (here[...] + across[...].astype(F32)).astype(BF16)
    me = member()
    for step in range(GROUP):
        at = columns(me ^ step)
        for part, out in enumerate(outs):
            out[:, at] = chunks[step][part]


def share():
    return lax.axis_index("mp")


def grad_kernel(*refs):
    pieces, (out_weight, tops), refs = refs[:N_MP], refs[N_MP : N_MP + 2], refs[N_MP + 2 :]
    *outs, whole, heads = refs
    me = member()
    for step, piece in enumerate(pieces):
        whole[span(share() ^ step, piece.shape[0]), :] = piece[...]
    heads[...] = dot_nt(whole[...], out_weight[...]).astype(BF16)
    quarter = tops.shape[2]
    for step, out in enumerate(outs):
        out[:BLOCK] = heads[:, columns(me ^ step)]
        for part in range(2):
            out[BLOCK + part * quarter : BLOCK + (part + 1) * quarter] = tops[me ^ step, part]


def project_kernel(*refs):
    chunks, out_weight, (kept, sent, attended, whole) = refs[:GROUP], refs[GROUP], refs[-4:]
    me = member()
    for step, chunk in enumerate(chunks):
        attended[:, columns(me ^ step)] = chunk[...]
    whole[...] = dot(attended[...], out_weight[...]).astype(BF16)
    rows = kept.shape[1]
    for far in range(2):
        kept[far] = whole[span(share() ^ (2 * far), rows), :]
        sent[far] = whole[span(share() ^ (2 * far + 1), rows), :]


def swapped(x, axis, step):
    return lax.ppermute(x, axis, [(i, i ^ step) for i in range(lax.axis_size(axis))])


def exchanged(chunks):
    got = {step: swapped(chunks[step], "seq", step) for step in (3, 1, 2)}
    return [chunks[0]] + [got[step] for step in range(1, GROUP)]


def beside(arrays):
    count = lax.axis_size("seq")
    if len(arrays) == 1:
        return [swapped(arrays[0], "seq", GROUP)]
    up = [(i, i + GROUP) for i in range(count - GROUP)]
    down = [(j, i) for i, j in up]
    return [lax.ppermute(arrays[0], "seq", up), lax.ppermute(arrays[1], "seq", down)]


def crossed(arrays):
    count = lax.axis_size("seq")
    across = swapped(arrays[0], "seq", GROUP)
    if len(arrays) == 1:
        return [across]
    up = [(i, i + GROUP) for i in range(count - GROUP)]
    down = [(j, i) for i, j in up]
    return [across, lax.ppermute(arrays[1], "seq", up), lax.ppermute(arrays[2], "seq", down)]


def per_device(queries, keys, values, out_weight, out_grad):
    rows, width = queries.shape
    assert width == GROUP * HEAD_DIM and rows == BLOCK and lax.axis_size("mp") == N_MP
    count = lax.axis_size("seq")
    assert count % (2 * GROUP) == 0
    groups = count // GROUP
    nb = GROUP
    tokens = nb * rows
    half, quarter = rows // 2, rows // 4
    model = out_weight.shape[1]
    block = shape(2, rows, HEAD_DIM)
    sent = [shape(4, rows, HEAD_DIM)] if groups == 2 else [block] * 3
    rims = [block] * (1 if groups == 2 else 2)
    quarter = rows // 4
    in_order = shape(nb, rows, HEAD_DIM)
    score_flops = 2 * tokens * 5 * BLOCK * HEAD_DIM
    weight_flops = 2 * rows * out_weight.size

    chunk = shape(rows, HEAD_DIM)
    triple = shape(3, rows, HEAD_DIM)
    chunks = call(
        pack_kernel,
        [triple] * GROUP,
        (queries, keys, values),
        scratch=[pltpu.SemaphoreType.DMA((3 * GROUP,))],
        space=pltpu.HBM,
        limit=53,
    )
    far = swapped(out_grad, "mp", 2)
    chunks = exchanged(chunks)
    (tops,) = call(pool_kernel, [shape(GROUP, 2, quarter, HEAD_DIM)], (keys, values))
    tops = swapped(tops, "seq", GROUP)
    (own_grad,) = call(copy_kernel, [shape(*out_grad.shape)], (out_grad, chunks[1]))
    far, near, queries, level_1, *refs = call(
        functools.partial(gather_kernel, nb, groups),
        [
            shape(*out_grad.shape),
            shape(nb, 2, rows, HEAD_DIM),
            shape(nb, rows, HEAD_DIM),
            shape(2, tokens // 2, HEAD_DIM),
        ]
        + rims,
        (far, tops, *chunks),
    )
    rim_blocks = beside(refs)
    grad_chunks = call(
        grad_kernel,
        [shape(rows + 2 * quarter, HEAD_DIM)] * GROUP,
        (own_grad, swapped(own_grad, "mp", 1), far, swapped(far, "mp", 1), out_weight, tops),
        scratch=[pltpu.VMEM((rows, model), BF16), pltpu.VMEM((rows, width), BF16)],
        flops=weight_flops,
    )
    query, k_t, v_t, k1_t, v1_t, weights, stats = call(
        functools.partial(local_kernel, nb),
        [
            shape(3, nb, rows, HEAD_DIM),
            shape(HEAD_DIM, tokens),
            shape(HEAD_DIM, tokens),
            shape(HEAD_DIM, tokens // 2),
            shape(HEAD_DIM, tokens // 2),
            shape(nb, 4, BLOCK, BLOCK, dtype=F32),
            shape(8, tokens, dtype=F32),
        ],
        (near, queries, level_1, grad_chunks[0]),
        flops=score_flops,
    )
    grad_chunks = exchanged(grad_chunks)
    rim_square = shape(len(rims), BLOCK, BLOCK)
    prob, grads, top_2, deltas, far_shift, rim_shift, *refs = call(
        functools.partial(forward_kernel, nb, groups),
        [
            shape(nb, 4, BLOCK, BLOCK),
            in_order,
            block,
            shape(8, tokens, dtype=F32),
            shape(BLOCK, tokens),
            rim_square,
        ]
        + [chunk] * GROUP
        + sent,
        (query, v_t, v1_t, weights, stats, *rim_blocks, *grad_chunks),
        scratch=[
            pltpu.VMEM((nb, rows, HEAD_DIM), BF16),
            pltpu.VMEM((BLOCK, tokens), BF16),
            pltpu.VMEM(rim_square.shape, BF16),
            pltpu.VMEM((8, tokens), F32),
            pltpu.VMEM((HEAD_DIM, tokens), F32),
        ],
        flops=score_flops,
    )
    attended = exchanged(refs[:GROUP])
    rim_grads = refs[GROUP:]
    other_grads = crossed(rim_grads)
    grad_q, grad_kv = call(
        functools.partial(backward_kernel, nb, groups),
        [in_order, shape(2, nb, rows, HEAD_DIM, dtype=F32)],
        (query, near, level_1, k_t, k1_t, prob, grads, top_2, deltas, far_shift, rim_shift, *rim_blocks),
        scratch=[
            pltpu.VMEM((nb, 4, BLOCK, BLOCK), BF16),
            pltpu.VMEM((2, tokens // 2, HEAD_DIM), F32),
            pltpu.VMEM((HEAD_DIM, tokens), F32),
        ],
        flops=1,
    )
    local = rows // N_MP
    shares = shape(2, local, model)
    kept, given = call(
        project_kernel,
        [shares] * 2,
        (*attended, out_weight, grad_q),
        scratch=[pltpu.VMEM((rows, width), BF16), pltpu.VMEM((rows, model), BF16)],
        flops=weight_flops,
    )
    chunks = call(
        functools.partial(combine_kernel, nb, groups),
        [triple] * GROUP,
        (grad_q, grad_kv, *other_grads),
        scratch=[pltpu.VMEM((nb, 2, rows, HEAD_DIM), BF16)],
        flops=20 * score_flops,
    )
    across, here = call(
        share_kernel,
        [shape(local, model), shape(local, model, dtype=F32)],
        (kept, swapped(given, "mp", 1), chunks[0]),
    )
    chunks = exchanged(chunks)
    across = swapped(across, "mp", 2)
    grad_k, grad_v, grad_q, mixed = call(
        unpack_kernel,
        [shape(rows, width)] * 3 + [shape(local, model)],
        (here, across, *chunks),
    )
    return mixed, grad_q, grad_k, grad_v


def solution(mesh):
    return jax.shard_map(
        per_device,
        mesh=mesh,
        in_specs=(
            P("seq", "mp"),
            P("seq", "mp"),
            P("seq", "mp"),
            P("mp", None),
            P(("seq", "mp"), None),
        ),
        out_specs=(P(("seq", "mp"), None), P("seq", "mp"), P("seq", "mp"), P("seq", "mp")),
        check_vma=False,
    )
```

```python
import functools

import jax
import jax.numpy as jnp
from jax import lax
from jax.experimental import pallas as pl
from jax.experimental.pallas import tpu as pltpu
from jax.sharding import PartitionSpec as P

HEAD_DIM = 128
BLOCK = 256
LEVELS = 2
GROUP = 4
STEPS = (0, 3, 2, 1)
N_MP = 4
SCALE = HEAD_DIM**-0.5
LOG2E = 1.4426950408889634
BF16 = jnp.bfloat16
F32 = jnp.float32


def dot(a, b):
    return lax.dot_general(a, b, (((1,), (0,)), ((), ())), preferred_element_type=F32)


def dot_nt(a, b):
    return lax.dot_general(a, b, (((1,), (1,)), ((), ())), preferred_element_type=F32)


def shape(*dims, dtype=BF16):
    return jax.ShapeDtypeStruct(dims, dtype)


def call(kernel, out_shape, args, scratch=(), flops=0, limit=32, space=pltpu.VMEM):
    whole = pl.BlockSpec(memory_space=space)
    moved = sum(x.size * x.dtype.itemsize for x in (*args, *out_shape))
    return pl.pallas_call(
        kernel,
        out_shape=out_shape,
        in_specs=[whole] * len(args),
        out_specs=[whole] * len(out_shape),
        scratch_shapes=scratch,
        compiler_params=pltpu.CompilerParams(vmem_limit_bytes=limit << 20),
        cost_estimate=pl.CostEstimate(flops=flops, bytes_accessed=moved if flops else 0, transcendentals=0),
    )(*args)


def columns(index):
    return pl.ds(pl.multiple_of(index * HEAD_DIM, HEAD_DIM), HEAD_DIM)


def span(index, size):
    return pl.ds(pl.multiple_of(index * size, size), size)


def iota(dims, axis):
    return lax.broadcasted_iota(jnp.int32, dims, axis)


def averaging(level):
    dims = (BLOCK, BLOCK)
    same = (iota(dims, 0) >> level) == (iota(dims, 1) >> level)
    return jnp.where(same, 2.0**-level, 0.0).astype(BF16)


def pooling():
    dims = (BLOCK // 2, BLOCK)
    return jnp.where(iota(dims, 0) == (iota(dims, 1) >> 1), 0.5, 0.0).astype(BF16)


def spreading(level):
    dims = (BLOCK, BLOCK >> level)
    return jnp.where((iota(dims, 0) >> level) == iota(dims, 1), 2.0**-level, 0.0).astype(BF16)


def halves(x):
    high = x.astype(BF16)
    return high, (x - high.astype(F32)).astype(BF16)


def at_block(b):
    return slice(b * BLOCK, (b + 1) * BLOCK)


def sibling(b):
    return (b >> 1) ^ 1


def rim_present(groups):
    group = lax.axis_index("seq") // GROUP
    return group > 0, group < groups - 1


def member():
    return lax.rem(lax.axis_index("seq"), GROUP)


def columns(index):
    return pl.ds(pl.multiple_of(index * HEAD_DIM, HEAD_DIM), HEAD_DIM)


def pack_kernel(q, k, v, *refs):
    *outs, sems = refs
    me = member()
    copies = []
    for step, out in zip(STEPS, outs):
        for part, source in enumerate((k, v, q)):
            piece = source.at[:, columns(me ^ step)]
            copies.append(pltpu.make_async_copy(piece, out.at[part], sems.at[len(copies)]))
    for copy in copies:
        copy.start()
    for copy in copies:
        copy.wait()


def pool_kernel(k, v, out):
    pool = pooling()
    half = BLOCK // 2
    for part, source in enumerate((k, v)):
        once = dot(pool, source[...]).astype(BF16)
        twice = dot(pool[: half // 2, :half], once).astype(BF16)
        for head in range(GROUP):
            out[head, part] = twice[:, head * HEAD_DIM : (head + 1) * HEAD_DIM]


def copy_kernel(x, _, out):
    out[...] = x[...]


def gather_kernel(nb, groups, far, _, *refs):
    chunks, (far_out, near, queries, level_1, *rims) = refs[:GROUP], refs[GROUP:]
    far_out[...] = far[...]
    me = member()
    for step, chunk in zip(STEPS, chunks):
        near[me ^ step] = chunk[:2]
        queries[me ^ step] = chunk[2]
    pool = pooling()
    half = BLOCK // 2
    for part in range(2):
        for b in range(nb):
            level_1[part, b * half : (b + 1) * half] = dot(pool, near[b, part]).astype(BF16)
    if groups == 2:
        upper = lax.axis_index("seq") >= GROUP
        rims[0][...] = jnp.where(upper, near[0], near[nb - 1])
    else:
        rims[0][...] = near[nb - 1]
        rims[1][...] = near[0]


def from_beside(groups, refs):
    if groups == 2:
        return (refs[0], refs[0]), refs[1:]
    return refs[:2], refs[2:]


def from_others(groups, refs):
    if groups == 2:
        return (refs[0].at[:2], refs[0].at[2:], refs[0].at[2:]), refs[1:]
    return refs[:3], refs[3:]


def near_sides(b, nb):
    return [side for side in range(3) if 0 <= b + side - 1 < nb]


def local_kernel(nb, near, queries, level_1, _, query, k_t, v_t, k1_t, v1_t, weights, stats):
    even_1, even_2 = averaging(1), averaging(2)
    for b in range(nb):
        query[0, b] = queries[b]
        once = dot(even_1, queries[b]).astype(BF16)
        query[1, b] = once
        query[2, b] = dot(even_2, once).astype(BF16)
        for part, transposed in enumerate((k_t, v_t)):
            transposed[:, at_block(b)] = near[b, part].T
    for c in range(nb // 2):
        for part, transposed in enumerate((k1_t, v1_t)):
            transposed[:, at_block(c)] = level_1[part, at_block(c)].T
    for b in range(nb):
        sides = near_sides(b, nb)
        scores = [dot_nt(near[b + side - 1, 0], query[0, b]) * (SCALE * LOG2E) for side in sides]
        coarse = dot_nt(level_1[0, at_block(sibling(b))], query[1, b]) * (SCALE * LOG2E)
        top = coarse.max(0, keepdims=True)
        for score in scores:
            top = jnp.maximum(top, score.max(0, keepdims=True))
        weight = 2.0 * jnp.exp2(coarse - top)
        weights[b, 3] = weight
        total = weight.sum(0, keepdims=True)
        for side, score in zip(sides, scores):
            weight = jnp.exp2(score - top)
            weights[b, side] = weight
            total = total + weight.sum(0, keepdims=True)
        stats[:1, at_block(b)] = top
        stats[1:2, at_block(b)] = total


def rims_of(nb, groups, low, high):
    group = lax.axis_index("seq") // GROUP
    if groups == 2:
        return [(jnp.where(group > 0, 0, nb - 1), low, None)]
    return [(0, low, group > 0), (nb - 1, high, group < groups - 1)]


def forward_kernel(nb, groups, *refs):
    (query, v_t, v1_t, weights, stats), refs = refs[:5], refs[5:]
    (rim_low, rim_high), refs = from_beside(groups, refs)
    chunks, refs = refs[:GROUP], refs[GROUP:]
    (prob, grads, top_2, deltas, far_shift, rim_shift), refs = refs[:6], refs[6:]
    outs, (*rim_outs, attended, far_prob, rim_prob, row, context_t) = refs[:GROUP], refs[GROUP:]
    rims = rims_of(nb, groups, rim_low, rim_high)
    me = member()
    quarter = BLOCK // 4
    tokens = nb * BLOCK
    for step, chunk in zip(STEPS, chunks):
        grads[me ^ step] = chunk[:BLOCK]
        for part in range(2):
            level = chunk[BLOCK + part * quarter : BLOCK + (part + 1) * quarter]
            top_2[part, span(me ^ step, quarter), :] = level
    coarse_query = query[2].reshape(tokens, HEAD_DIM)
    coarse = dot_nt(top_2[0], coarse_query) * (SCALE * LOG2E)
    row[:1] = jnp.maximum(stats[:1], coarse.max(0, keepdims=True))
    scores = []
    for b, block, present in rims:
        score = dot_nt(block[0], query[0, b]) * (SCALE * LOG2E)
        if present is not None:
            score = jnp.where(present, score, -jnp.inf)
        at = span(b, BLOCK)
        row[:1, at] = jnp.maximum(row[:1, at], score.max(0, keepdims=True))
        scores.append(score)
    top = row[:1]
    shrink = jnp.exp2(stats[:1] - top)
    far = 4.0 * jnp.exp2(coarse - top)
    row[1:2] = shrink * stats[1:2] + far.sum(0, keepdims=True)
    fresh = []
    for (b, _, _), score in zip(rims, scores):
        at = span(b, BLOCK)
        fresh.append(jnp.exp2(score - row[:1, at]))
        row[1:2, at] += fresh[-1].sum(0, keepdims=True)
    inverse = 1.0 / row[1:2]
    row[2:3] = inverse
    row[3:4] = shrink * inverse
    far_prob[...] = (far * inverse).astype(BF16)
    context_t[...] = dot(top_2[1].T, far_prob[...])
    for i, (b, block, _) in enumerate(rims):
        at = span(b, BLOCK)
        rim_prob[i] = (fresh[i] * row[2:3, at]).astype(BF16)
        context_t[:, at] += dot(block[1].T, rim_prob[i])
    for b in range(nb):
        shrink = row[3:4, at_block(b)]
        prob[b, 3] = (weights[b, 3] * shrink).astype(BF16)
        context = context_t[:, at_block(b)] + dot(v1_t[:, at_block(sibling(b))], prob[b, 3])
        for side in near_sides(b, nb):
            prob[b, side] = (weights[b, side] * shrink).astype(BF16)
            context = context + dot(v_t[:, at_block(b + side - 1)], prob[b, side])
        attended[b] = context.T.astype(BF16)
        deltas[:1, at_block(b)] = (grads[b].T.astype(F32) * context).sum(0, keepdims=True)
    grad = grads[...].reshape(tokens, HEAD_DIM)
    slope = dot_nt(top_2[1], grad)
    far_shift[...] = (far_prob[...].astype(F32) * (slope - deltas[:1])).astype(BF16)
    rim_outs[0][0] = (SCALE * dot(far_shift[...], coarse_query)).astype(BF16)
    rim_outs[0][1] = dot(far_prob[...], grad).astype(BF16)
    pairs = []
    for i, (b, block, _) in enumerate(rims):
        slope = dot_nt(block[1], grads[b])
        rim_shift[i] = (rim_prob[i].astype(F32) * (slope - deltas[:1, span(b, BLOCK)])).astype(BF16)
        pairs.append((SCALE * dot(rim_shift[i], query[0, b]), dot(rim_prob[i], grads[b])))
    for part in range(2):
        if groups == 2:
            rim_outs[0][2 + part] = pairs[0][part].astype(BF16)
        else:
            rim_outs[1][part] = pairs[1][part].astype(BF16)
            rim_outs[2][part] = pairs[0][part].astype(BF16)
    for step, out in zip(STEPS, outs):
        out[...] = attended[me ^ step]


def backward_kernel(nb, groups, *refs):
    (query, near, level_1, k_t, k1_t, prob, grads, top_2, deltas, far_shift, rim_shift), refs = refs[:11], refs[11:]
    (rim_low, rim_high), refs = from_beside(groups, refs)
    grad_q, grad_kv, shift, sums_1, query_t = refs
    even_1, even_2 = averaging(1), averaging(2)
    coarse = dot(top_2[0].T, far_shift[...])
    for b in range(nb):
        high, low = halves(coarse[:, at_block(b)])
        query_t[:, at_block(b)] = dot(high, even_2) + dot(low, even_2)
    for i, (b, block, _) in enumerate(rims_of(nb, groups, rim_low, rim_high)):
        query_t[:, span(b, BLOCK)] += dot(block[0].T, rim_shift[i])
    for b in range(nb):
        grad, delta = grads[b], deltas[:1, at_block(b)]
        grad_t = query_t[:, at_block(b)]
        for side in near_sides(b, nb):
            slope = dot_nt(near[b + side - 1, 1], grad)
            part = (prob[b, side].astype(F32) * (slope - delta)).astype(BF16)
            shift[b, side] = part
            grad_t = grad_t + dot(k_t[:, at_block(b + side - 1)], part)
        slope = dot_nt(level_1[1, at_block(sibling(b))], grad)
        part = (prob[b, 3].astype(F32) * (slope - delta)).astype(BF16)
        shift[b, 3] = part
        high, low = halves(dot(k1_t[:, at_block(sibling(b))], part))
        grad_t = grad_t + (dot(high, even_1) + dot(low, even_1))
        grad_q[b] = (SCALE * grad_t).T.astype(BF16)
    for c in range(nb // 2):
        users = [b for b in range(nb) if sibling(b) == c]
        sums_1[0, at_block(c)] = SCALE * sum(dot(shift[b, 3], query[1, b]) for b in users)
        sums_1[1, at_block(c)] = sum(dot(prob[b, 3], grads[b]) for b in users)
    spread = spreading(1)
    half = BLOCK // 2
    for s in range(nb):
        users = [(s + 1 - side, side) for side in range(3) if 0 <= s + 1 - side < nb]
        key = SCALE * sum(dot(shift[b, side], query[0, b]) for b, side in users)
        value = sum(dot(prob[b, side], grads[b]) for b, side in users)
        for part, total in enumerate((key, value)):
            high, low = halves(sums_1[part, s * half : (s + 1) * half])
            grad_kv[part, s] = total + (dot(spread, high) + dot(spread, low))


def share_kernel(kept, *refs):
    *got, across, here = refs
    half = across.shape[0] // 2
    for i, piece in enumerate(got):
        far, at = i // 2, pl.ds(i % 2 * half, half)
        total = kept[far, at, :].astype(F32) + piece[...].astype(F32)
        if far:
            across[at, :] = total.astype(BF16)
        else:
            here[at, :] = total


def combine_kernel(nb, groups, grad_q, grad_kv, _, *refs):
    (got_top, got_low, got_high), (*outs, out) = from_others(groups, refs)
    present = rim_present(groups)
    spread = spreading(2)
    quarter = BLOCK // 4
    for b in range(nb):
        for part in range(2):
            total = grad_kv[part, b] + dot(spread, got_top[part, b * quarter : (b + 1) * quarter])
            if b == 0:
                total = total + jnp.where(present[0], got_low[part].astype(F32), 0.0)
            if b == nb - 1:
                total = total + jnp.where(present[1], got_high[part].astype(F32), 0.0)
            out[b, part] = total.astype(BF16)
    me = member()
    for step, chunk in zip(STEPS, outs):
        chunk[:2] = out[me ^ step]
        chunk[2] = grad_q[me ^ step]


def unpack_kernel(*refs):
    here, across, *refs = refs
    chunks, (*outs, mixed) = refs[:GROUP], refs[GROUP:]
    mixed[...] = (here[...] + across[...].astype(F32)).astype(BF16)
    me = member()
    for step, chunk in zip(STEPS, chunks):
        at = columns(me ^ step)
        for part, out in enumerate(outs):
            out[:, at] = chunk[part]


def share():
    return lax.axis_index("mp")


def grad_kernel(*refs):
    pieces, (out_weight, tops), refs = refs[:N_MP], refs[N_MP : N_MP + 2], refs[N_MP + 2 :]
    *outs, whole, heads = refs
    me = member()
    for step, piece in enumerate(pieces):
        whole[span(share() ^ step, piece.shape[0]), :] = piece[...]
    heads[...] = dot_nt(whole[...], out_weight[...]).astype(BF16)
    quarter = tops.shape[2]
    for step, out in zip(STEPS, outs):
        out[:BLOCK] = heads[:, columns(me ^ step)]
        for part in range(2):
            out[BLOCK + part * quarter : BLOCK + (part + 1) * quarter] = tops[me ^ step, part]


def project_kernel(*refs):
    chunks, out_weight, (kept, *sent, attended, whole) = refs[:GROUP], refs[GROUP], refs[GROUP + 2 :]
    me = member()
    for step, chunk in zip(STEPS, chunks):
        attended[:, columns(me ^ step)] = chunk[...]
    whole[...] = dot(attended[...], out_weight[...]).astype(BF16)
    rows = kept.shape[1]
    for far in range(2):
        kept[far] = whole[span(share() ^ (2 * far), rows), :]
        for part in range(2):
            half = rows // 2
            at = 2 * (share() ^ (2 * far + 1)) + part
            sent[2 * far + part][...] = whole[span(at, half), :]


def swapped(x, axis, step):
    return lax.ppermute(x, axis, [(i, i ^ step) for i in range(lax.axis_size(axis))])


def exchanged(chunks):
    return [chunks[0]] + [swapped(chunk, "seq", step) for step, chunk in zip(STEPS[1:], chunks[1:])]


def beside(arrays):
    count = lax.axis_size("seq")
    if len(arrays) == 1:
        return [swapped(arrays[0], "seq", GROUP)]
    up = [(i, i + GROUP) for i in range(count - GROUP)]
    down = [(j, i) for i, j in up]
    return [lax.ppermute(arrays[0], "seq", up), lax.ppermute(arrays[1], "seq", down)]


def crossed(arrays):
    count = lax.axis_size("seq")
    across = swapped(arrays[0], "seq", GROUP)
    if len(arrays) == 1:
        return [across]
    up = [(i, i + GROUP) for i in range(count - GROUP)]
    down = [(j, i) for i, j in up]
    return [across, lax.ppermute(arrays[1], "seq", up), lax.ppermute(arrays[2], "seq", down)]


def per_device(queries, keys, values, out_weight, out_grad):
    rows, width = queries.shape
    assert width == GROUP * HEAD_DIM and rows == BLOCK and lax.axis_size("mp") == N_MP
    count = lax.axis_size("seq")
    assert count % (2 * GROUP) == 0
    groups = count // GROUP
    nb = GROUP
    tokens = nb * rows
    half, quarter = rows // 2, rows // 4
    model = out_weight.shape[1]
    block = shape(2, rows, HEAD_DIM)
    sent = [shape(4, rows, HEAD_DIM)] if groups == 2 else [block] * 3
    rims = [block] * (1 if groups == 2 else 2)
    quarter = rows // 4
    in_order = shape(nb, rows, HEAD_DIM)
    score_flops = 2 * tokens * 5 * BLOCK * HEAD_DIM
    weight_flops = 2 * rows * out_weight.size

    chunk = shape(rows, HEAD_DIM)
    triple = shape(3, rows, HEAD_DIM)
    chunks = call(
        pack_kernel,
        [triple] * GROUP,
        (queries, keys, values),
        scratch=[pltpu.SemaphoreType.DMA((3 * GROUP,))],
        space=pltpu.HBM,
        limit=53,
    )
    far = swapped(out_grad, "mp", 2)
    chunks = exchanged(chunks)
    (tops,) = call(pool_kernel, [shape(GROUP, 2, quarter, HEAD_DIM)], (keys, values))
    tops = swapped(tops, "seq", GROUP)
    (own_grad,) = call(copy_kernel, [shape(*out_grad.shape)], (out_grad, chunks[1]))
    far, near, queries, level_1, *refs = call(
        functools.partial(gather_kernel, nb, groups),
        [
            shape(*out_grad.shape),
            shape(nb, 2, rows, HEAD_DIM),
            shape(nb, rows, HEAD_DIM),
            shape(2, tokens // 2, HEAD_DIM),
        ]
        + rims,
        (far, tops, *chunks),
    )
    rim_blocks = beside(refs)
    grad_chunks = call(
        grad_kernel,
        [shape(rows + 2 * quarter, HEAD_DIM)] * GROUP,
        (own_grad, swapped(own_grad, "mp", 1), far, swapped(far, "mp", 1), out_weight, tops),
        scratch=[pltpu.VMEM((rows, model), BF16), pltpu.VMEM((rows, width), BF16)],
        flops=weight_flops,
    )
    query, k_t, v_t, k1_t, v1_t, weights, stats = call(
        functools.partial(local_kernel, nb),
        [
            shape(3, nb, rows, HEAD_DIM),
            shape(HEAD_DIM, tokens),
            shape(HEAD_DIM, tokens),
            shape(HEAD_DIM, tokens // 2),
            shape(HEAD_DIM, tokens // 2),
            shape(nb, 4, BLOCK, BLOCK, dtype=F32),
            shape(8, tokens, dtype=F32),
        ],
        (near, queries, level_1, grad_chunks[0]),
        flops=score_flops,
    )
    grad_chunks = exchanged(grad_chunks)
    rim_square = shape(len(rims), BLOCK, BLOCK)
    prob, grads, top_2, deltas, far_shift, rim_shift, *refs = call(
        functools.partial(forward_kernel, nb, groups),
        [
            shape(nb, 4, BLOCK, BLOCK),
            in_order,
            block,
            shape(8, tokens, dtype=F32),
            shape(BLOCK, tokens),
            rim_square,
        ]
        + [chunk] * GROUP
        + sent,
        (query, v_t, v1_t, weights, stats, *rim_blocks, *grad_chunks),
        scratch=[
            pltpu.VMEM((nb, rows, HEAD_DIM), BF16),
            pltpu.VMEM((BLOCK, tokens), BF16),
            pltpu.VMEM(rim_square.shape, BF16),
            pltpu.VMEM((8, tokens), F32),
            pltpu.VMEM((HEAD_DIM, tokens), F32),
        ],
        flops=score_flops,
    )
    attended = exchanged(refs[:GROUP])
    rim_grads = refs[GROUP:]
    other_grads = crossed(rim_grads)
    grad_q, grad_kv = call(
        functools.partial(backward_kernel, nb, groups),
        [in_order, shape(2, nb, rows, HEAD_DIM, dtype=F32)],
        (query, near, level_1, k_t, k1_t, prob, grads, top_2, deltas, far_shift, rim_shift, *rim_blocks),
        scratch=[
            pltpu.VMEM((nb, 4, BLOCK, BLOCK), BF16),
            pltpu.VMEM((2, tokens // 2, HEAD_DIM), F32),
            pltpu.VMEM((HEAD_DIM, tokens), F32),
        ],
        flops=1,
    )
    local = rows // N_MP
    kept, *given = call(
        project_kernel,
        [shape(2, local, model)] + [shape(local // 2, model)] * 4,
        (*attended, out_weight, grad_q),
        scratch=[pltpu.VMEM((rows, width), BF16), pltpu.VMEM((rows, model), BF16)],
        flops=weight_flops,
    )
    across, here = call(
        share_kernel,
        [shape(local, model), shape(local, model, dtype=F32)],
        (kept, *(swapped(piece, "mp", 1) for piece in given)),
    )
    chunks = call(
        functools.partial(combine_kernel, nb, groups),
        [triple] * GROUP,
        (grad_q, grad_kv, across, *other_grads),
        scratch=[pltpu.VMEM((nb, 2, rows, HEAD_DIM), BF16)],
        flops=20 * score_flops,
    )
    chunks = exchanged(chunks)
    across = swapped(across, "mp", 2)
    grad_k, grad_v, grad_q, mixed = call(
        unpack_kernel,
        [shape(rows, width)] * 3 + [shape(local, model)],
        (here, across, *chunks),
    )
    return mixed, grad_q, grad_k, grad_v


def solution(mesh):
    return jax.shard_map(
        per_device,
        mesh=mesh,
        in_specs=(
            P("seq", "mp"),
            P("seq", "mp"),
            P("seq", "mp"),
            P("mp", None),
            P(("seq", "mp"), None),
        ),
        out_specs=(P(("seq", "mp"), None), P("seq", "mp"), P("seq", "mp"), P("seq", "mp")),
        check_vma=False,
    )
```

```python
import functools

import jax
import jax.numpy as jnp
from jax import lax
from jax.experimental import pallas as pl
from jax.experimental.pallas import tpu as pltpu
from jax.sharding import PartitionSpec as P

HEAD_DIM = 128
BLOCK = 256
LEVELS = 2
GROUP = 4
STEPS = (0, 3, 2, 1)
N_MP = 4
SCALE = HEAD_DIM**-0.5
LOG2E = 1.4426950408889634
BF16 = jnp.bfloat16
F32 = jnp.float32


def dot(a, b):
    return lax.dot_general(a, b, (((1,), (0,)), ((), ())), preferred_element_type=F32)


def dot_nt(a, b):
    return lax.dot_general(a, b, (((1,), (1,)), ((), ())), preferred_element_type=F32)


def shape(*dims, dtype=BF16):
    return jax.ShapeDtypeStruct(dims, dtype)


def call(kernel, out_shape, args, scratch=(), flops=0, limit=32, copied=0):
    whole = pl.BlockSpec(memory_space=pltpu.VMEM)
    kept = pl.BlockSpec(memory_space=pltpu.HBM)
    moved = sum(x.size * x.dtype.itemsize for x in (*args, *out_shape))
    return pl.pallas_call(
        kernel,
        out_shape=out_shape,
        in_specs=[kept if copied else whole] * len(args),
        out_specs=[kept] * copied + [whole] * (len(out_shape) - copied),
        scratch_shapes=scratch,
        compiler_params=pltpu.CompilerParams(vmem_limit_bytes=limit << 20),
        cost_estimate=pl.CostEstimate(flops=flops, bytes_accessed=moved if flops else 0, transcendentals=0),
    )(*args)


def columns(index):
    return pl.ds(pl.multiple_of(index * HEAD_DIM, HEAD_DIM), HEAD_DIM)


def span(index, size):
    return pl.ds(pl.multiple_of(index * size, size), size)


def iota(dims, axis):
    return lax.broadcasted_iota(jnp.int32, dims, axis)


def averaging(level):
    dims = (BLOCK, BLOCK)
    same = (iota(dims, 0) >> level) == (iota(dims, 1) >> level)
    return jnp.where(same, 2.0**-level, 0.0).astype(BF16)


def pooling():
    dims = (BLOCK // 2, BLOCK)
    return jnp.where(iota(dims, 0) == (iota(dims, 1) >> 1), 0.5, 0.0).astype(BF16)


def spreading(level):
    dims = (BLOCK, BLOCK >> level)
    return jnp.where((iota(dims, 0) >> level) == iota(dims, 1), 2.0**-level, 0.0).astype(BF16)


def halves(x):
    high = x.astype(BF16)
    return high, (x - high.astype(F32)).astype(BF16)


def at_block(b):
    return slice(b * BLOCK, (b + 1) * BLOCK)


def sibling(b):
    return (b >> 1) ^ 1


def rim_present(groups):
    group = lax.axis_index("seq") // GROUP
    return group > 0, group < groups - 1


def member():
    return lax.rem(lax.axis_index("seq"), GROUP)


def columns(index):
    return pl.ds(pl.multiple_of(index * HEAD_DIM, HEAD_DIM), HEAD_DIM)


def pack_kernel(q, k, v, *refs):
    *outs, tops, held, sems = refs
    me = member()
    copies = [pltpu.make_async_copy(x, held.at[i], sems.at[i]) for i, x in enumerate((k, v))]
    for step, out in zip(STEPS, outs):
        for part, source in enumerate((k, v, q)):
            piece = source.at[:, columns(me ^ step)]
            copies.append(pltpu.make_async_copy(piece, out.at[part], sems.at[len(copies)]))
    for copy in copies:
        copy.start()
    pool = pooling()
    half = BLOCK // 2
    for part in range(2):
        copies[part].wait()
        once = dot(pool, held[part]).astype(BF16)
        twice = dot(pool[: half // 2, :half], once).astype(BF16)
        for head in range(GROUP):
            tops[head, part] = twice[:, head * HEAD_DIM : (head + 1) * HEAD_DIM]
    for copy in copies[2:]:
        copy.wait()


def copy_kernel(x, y, _, x_out, y_out):
    x_out[...] = x[...]
    y_out[...] = y[...]


def gather_kernel(nb, groups, *refs):
    chunks, (near, queries, level_1, *rims) = refs[:GROUP], refs[GROUP:]
    me = member()
    for step, chunk in zip(STEPS, chunks):
        near[me ^ step] = chunk[:2]
        queries[me ^ step] = chunk[2]
    pool = pooling()
    half = BLOCK // 2
    for part in range(2):
        for b in range(nb):
            level_1[part, b * half : (b + 1) * half] = dot(pool, near[b, part]).astype(BF16)
    if groups == 2:
        upper = lax.axis_index("seq") >= GROUP
        rims[0][...] = jnp.where(upper, near[0], near[nb - 1])
    else:
        rims[0][...] = near[nb - 1]
        rims[1][...] = near[0]


def from_beside(groups, refs):
    if groups == 2:
        return (refs[0], refs[0]), refs[1:]
    return refs[:2], refs[2:]


def from_others(groups, refs):
    if groups == 2:
        return (refs[0].at[:2], refs[0].at[2:], refs[0].at[2:]), refs[1:]
    return refs[:3], refs[3:]


def near_sides(b, nb):
    return [side for side in range(3) if 0 <= b + side - 1 < nb]


def local_kernel(nb, near, queries, level_1, _, query, k_t, v_t, k1_t, v1_t, weights, stats):
    even_1, even_2 = averaging(1), averaging(2)
    for b in range(nb):
        query[0, b] = queries[b]
        once = dot(even_1, queries[b]).astype(BF16)
        query[1, b] = once
        query[2, b] = dot(even_2, once).astype(BF16)
        for part, transposed in enumerate((k_t, v_t)):
            transposed[:, at_block(b)] = near[b, part].T
    for c in range(nb // 2):
        for part, transposed in enumerate((k1_t, v1_t)):
            transposed[:, at_block(c)] = level_1[part, at_block(c)].T
    for b in range(nb):
        sides = near_sides(b, nb)
        scores = [dot_nt(near[b + side - 1, 0], query[0, b]) * (SCALE * LOG2E) for side in sides]
        coarse = dot_nt(level_1[0, at_block(sibling(b))], query[1, b]) * (SCALE * LOG2E)
        top = coarse.max(0, keepdims=True)
        for score in scores:
            top = jnp.maximum(top, score.max(0, keepdims=True))
        weight = 2.0 * jnp.exp2(coarse - top)
        weights[b, 3] = weight
        total = weight.sum(0, keepdims=True)
        for side, score in zip(sides, scores):
            weight = jnp.exp2(score - top)
            weights[b, side] = weight
            total = total + weight.sum(0, keepdims=True)
        stats[:1, at_block(b)] = top
        stats[1:2, at_block(b)] = total


def rims_of(nb, groups, low, high):
    group = lax.axis_index("seq") // GROUP
    if groups == 2:
        return [(jnp.where(group > 0, 0, nb - 1), low, None)]
    return [(0, low, group > 0), (nb - 1, high, group < groups - 1)]


def forward_kernel(nb, groups, *refs):
    (query, v_t, v1_t, weights, stats), refs = refs[:5], refs[5:]
    (rim_low, rim_high), refs = from_beside(groups, refs)
    chunks, refs = refs[:GROUP], refs[GROUP:]
    (prob, grads, top_2, deltas, far_shift, rim_shift), refs = refs[:6], refs[6:]
    outs, (*rim_outs, attended, far_prob, rim_prob, row, context_t) = refs[:GROUP], refs[GROUP:]
    rims = rims_of(nb, groups, rim_low, rim_high)
    me = member()
    quarter = BLOCK // 4
    tokens = nb * BLOCK
    for step, chunk in zip(STEPS, chunks):
        grads[me ^ step] = chunk[:BLOCK]
        for part in range(2):
            level = chunk[BLOCK + part * quarter : BLOCK + (part + 1) * quarter]
            top_2[part, span(me ^ step, quarter), :] = level
    coarse_query = query[2].reshape(tokens, HEAD_DIM)
    coarse = dot_nt(top_2[0], coarse_query) * (SCALE * LOG2E)
    row[:1] = jnp.maximum(stats[:1], coarse.max(0, keepdims=True))
    scores = []
    for b, block, present in rims:
        score = dot_nt(block[0], query[0, b]) * (SCALE * LOG2E)
        if present is not None:
            score = jnp.where(present, score, -jnp.inf)
        at = span(b, BLOCK)
        row[:1, at] = jnp.maximum(row[:1, at], score.max(0, keepdims=True))
        scores.append(score)
    top = row[:1]
    shrink = jnp.exp2(stats[:1] - top)
    far = 4.0 * jnp.exp2(coarse - top)
    row[1:2] = shrink * stats[1:2] + far.sum(0, keepdims=True)
    fresh = []
    for (b, _, _), score in zip(rims, scores):
        at = span(b, BLOCK)
        fresh.append(jnp.exp2(score - row[:1, at]))
        row[1:2, at] += fresh[-1].sum(0, keepdims=True)
    inverse = 1.0 / row[1:2]
    row[2:3] = inverse
    row[3:4] = shrink * inverse
    far_prob[...] = (far * inverse).astype(BF16)
    context_t[...] = dot(top_2[1].T, far_prob[...])
    for i, (b, block, _) in enumerate(rims):
        at = span(b, BLOCK)
        rim_prob[i] = (fresh[i] * row[2:3, at]).astype(BF16)
        context_t[:, at] += dot(block[1].T, rim_prob[i])
    for b in range(nb):
        shrink = row[3:4, at_block(b)]
        prob[b, 3] = (weights[b, 3] * shrink).astype(BF16)
        context = context_t[:, at_block(b)] + dot(v1_t[:, at_block(sibling(b))], prob[b, 3])
        for side in near_sides(b, nb):
            prob[b, side] = (weights[b, side] * shrink).astype(BF16)
            context = context + dot(v_t[:, at_block(b + side - 1)], prob[b, side])
        attended[b] = context.T.astype(BF16)
        deltas[:1, at_block(b)] = (grads[b].T.astype(F32) * context).sum(0, keepdims=True)
    grad = grads[...].reshape(tokens, HEAD_DIM)
    slope = dot_nt(top_2[1], grad)
    far_shift[...] = (far_prob[...].astype(F32) * (slope - deltas[:1])).astype(BF16)
    rim_outs[0][0] = (SCALE * dot(far_shift[...], coarse_query)).astype(BF16)
    rim_outs[0][1] = dot(far_prob[...], grad).astype(BF16)
    pairs = []
    for i, (b, block, _) in enumerate(rims):
        slope = dot_nt(block[1], grads[b])
        rim_shift[i] = (rim_prob[i].astype(F32) * (slope - deltas[:1, span(b, BLOCK)])).astype(BF16)
        pairs.append((SCALE * dot(rim_shift[i], query[0, b]), dot(rim_prob[i], grads[b])))
    for part in range(2):
        if groups == 2:
            rim_outs[0][2 + part] = pairs[0][part].astype(BF16)
        else:
            rim_outs[1][part] = pairs[1][part].astype(BF16)
            rim_outs[2][part] = pairs[0][part].astype(BF16)
    for step, out in zip(STEPS, outs):
        out[...] = attended[me ^ step]


def backward_kernel(nb, groups, *refs):
    (query, near, level_1, k_t, k1_t, prob, grads, top_2, deltas, far_shift, rim_shift), refs = refs[:11], refs[11:]
    (rim_low, rim_high), refs = from_beside(groups, refs)
    grad_q, grad_kv, shift, sums_1, query_t = refs
    even_1, even_2 = averaging(1), averaging(2)
    coarse = dot(top_2[0].T, far_shift[...])
    for b in range(nb):
        high, low = halves(coarse[:, at_block(b)])
        query_t[:, at_block(b)] = dot(high, even_2) + dot(low, even_2)
    for i, (b, block, _) in enumerate(rims_of(nb, groups, rim_low, rim_high)):
        query_t[:, span(b, BLOCK)] += dot(block[0].T, rim_shift[i])
    for b in range(nb):
        grad, delta = grads[b], deltas[:1, at_block(b)]
        grad_t = query_t[:, at_block(b)]
        for side in near_sides(b, nb):
            slope = dot_nt(near[b + side - 1, 1], grad)
            part = (prob[b, side].astype(F32) * (slope - delta)).astype(BF16)
            shift[b, side] = part
            grad_t = grad_t + dot(k_t[:, at_block(b + side - 1)], part)
        slope = dot_nt(level_1[1, at_block(sibling(b))], grad)
        part = (prob[b, 3].astype(F32) * (slope - delta)).astype(BF16)
        shift[b, 3] = part
        high, low = halves(dot(k1_t[:, at_block(sibling(b))], part))
        grad_t = grad_t + (dot(high, even_1) + dot(low, even_1))
        grad_q[b] = (SCALE * grad_t).T.astype(BF16)
    for c in range(nb // 2):
        users = [b for b in range(nb) if sibling(b) == c]
        sums_1[0, at_block(c)] = SCALE * sum(dot(shift[b, 3], query[1, b]) for b in users)
        sums_1[1, at_block(c)] = sum(dot(prob[b, 3], grads[b]) for b in users)
    spread = spreading(1)
    half = BLOCK // 2
    for s in range(nb):
        users = [(s + 1 - side, side) for side in range(3) if 0 <= s + 1 - side < nb]
        key = SCALE * sum(dot(shift[b, side], query[0, b]) for b, side in users)
        value = sum(dot(prob[b, side], grads[b]) for b, side in users)
        for part, total in enumerate((key, value)):
            high, low = halves(sums_1[part, s * half : (s + 1) * half])
            grad_kv[part, s] = total + (dot(spread, high) + dot(spread, low))


def share_kernel(kept, *refs):
    *got, across, here = refs
    half = across.shape[0] // 2
    for i, piece in enumerate(got):
        far, at = i // 2, pl.ds(i % 2 * half, half)
        total = kept[far, at, :].astype(F32) + piece[...].astype(F32)
        if far:
            across[at, :] = total.astype(BF16)
        else:
            here[at, :] = total


def combine_kernel(nb, groups, grad_q, grad_kv, _, *refs):
    (got_top, got_low, got_high), (*outs, out) = from_others(groups, refs)
    present = rim_present(groups)
    spread = spreading(2)
    quarter = BLOCK // 4
    for b in range(nb):
        for part in range(2):
            total = grad_kv[part, b] + dot(spread, got_top[part, b * quarter : (b + 1) * quarter])
            if b == 0:
                total = total + jnp.where(present[0], got_low[part].astype(F32), 0.0)
            if b == nb - 1:
                total = total + jnp.where(present[1], got_high[part].astype(F32), 0.0)
            out[b, part] = total.astype(BF16)
    me = member()
    for step, chunk in zip(STEPS, outs):
        chunk[:2] = out[me ^ step]
        chunk[2] = grad_q[me ^ step]


def unpack_kernel(*refs):
    here, across, *refs = refs
    chunks, (*outs, mixed) = refs[:GROUP], refs[GROUP:]
    mixed[...] = (here[...] + across[...].astype(F32)).astype(BF16)
    me = member()
    for step, chunk in zip(STEPS, chunks):
        at = columns(me ^ step)
        for part, out in enumerate(outs):
            out[:, at] = chunk[part]


def share():
    return lax.axis_index("mp")


def grad_kernel(*refs):
    pieces, (out_weight, tops), refs = refs[:N_MP], refs[N_MP : N_MP + 2], refs[N_MP + 2 :]
    *outs, whole, heads = refs
    me = member()
    for step, piece in enumerate(pieces):
        whole[span(share() ^ step, piece.shape[0]), :] = piece[...]
    heads[...] = dot_nt(whole[...], out_weight[...]).astype(BF16)
    quarter = tops.shape[2]
    for step, out in zip(STEPS, outs):
        out[:BLOCK] = heads[:, columns(me ^ step)]
        for part in range(2):
            out[BLOCK + part * quarter : BLOCK + (part + 1) * quarter] = tops[me ^ step, part]


def project_kernel(*refs):
    chunks, out_weight, (kept, *sent, attended, whole) = refs[:GROUP], refs[GROUP], refs[GROUP + 2 :]
    me = member()
    for step, chunk in zip(STEPS, chunks):
        attended[:, columns(me ^ step)] = chunk[...]
    whole[...] = dot(attended[...], out_weight[...]).astype(BF16)
    rows = kept.shape[1]
    for far in range(2):
        kept[far] = whole[span(share() ^ (2 * far), rows), :]
        for part in range(2):
            half = rows // 2
            at = 2 * (share() ^ (2 * far + 1)) + part
            sent[2 * far + part][...] = whole[span(at, half), :]


def swapped(x, axis, step):
    return lax.ppermute(x, axis, [(i, i ^ step) for i in range(lax.axis_size(axis))])


def exchanged(chunks):
    return [chunks[0]] + [swapped(chunk, "seq", step) for step, chunk in zip(STEPS[1:], chunks[1:])]


def beside(arrays):
    count = lax.axis_size("seq")
    if len(arrays) == 1:
        return [swapped(arrays[0], "seq", GROUP)]
    up = [(i, i + GROUP) for i in range(count - GROUP)]
    down = [(j, i) for i, j in up]
    return [lax.ppermute(arrays[0], "seq", up), lax.ppermute(arrays[1], "seq", down)]


def crossed(arrays):
    count = lax.axis_size("seq")
    across = swapped(arrays[0], "seq", GROUP)
    if len(arrays) == 1:
        return [across]
    up = [(i, i + GROUP) for i in range(count - GROUP)]
    down = [(j, i) for i, j in up]
    return [across, lax.ppermute(arrays[1], "seq", up), lax.ppermute(arrays[2], "seq", down)]


def per_device(queries, keys, values, out_weight, out_grad):
    rows, width = queries.shape
    assert width == GROUP * HEAD_DIM and rows == BLOCK and lax.axis_size("mp") == N_MP
    count = lax.axis_size("seq")
    assert count % (2 * GROUP) == 0
    groups = count // GROUP
    nb = GROUP
    tokens = nb * rows
    half, quarter = rows // 2, rows // 4
    model = out_weight.shape[1]
    block = shape(2, rows, HEAD_DIM)
    sent = [shape(4, rows, HEAD_DIM)] if groups == 2 else [block] * 3
    rims = [block] * (1 if groups == 2 else 2)
    quarter = rows // 4
    in_order = shape(nb, rows, HEAD_DIM)
    score_flops = 2 * tokens * 5 * BLOCK * HEAD_DIM
    weight_flops = 2 * rows * out_weight.size

    chunk = shape(rows, HEAD_DIM)
    triple = shape(3, rows, HEAD_DIM)
    *chunks, tops = call(
        pack_kernel,
        [triple] * GROUP + [shape(GROUP, 2, quarter, HEAD_DIM)],
        (queries, keys, values),
        scratch=[pltpu.VMEM((2, rows, width), BF16), pltpu.SemaphoreType.DMA((2 + 3 * GROUP,))],
        copied=GROUP,
        limit=53,
    )
    far = swapped(out_grad, "mp", 2)
    chunks = exchanged(chunks)
    tops = swapped(tops, "seq", GROUP)
    own_grad, far = call(copy_kernel, [shape(*out_grad.shape)] * 2, (out_grad, far, chunks[1]))
    near, queries, level_1, *refs = call(
        functools.partial(gather_kernel, nb, groups),
        [
            shape(nb, 2, rows, HEAD_DIM),
            shape(nb, rows, HEAD_DIM),
            shape(2, tokens // 2, HEAD_DIM),
        ]
        + rims,
        chunks,
        flops=20 * score_flops,
    )
    rim_blocks = beside(refs)
    grad_chunks = call(
        grad_kernel,
        [shape(rows + 2 * quarter, HEAD_DIM)] * GROUP,
        (own_grad, swapped(own_grad, "mp", 1), far, swapped(far, "mp", 1), out_weight, tops),
        scratch=[pltpu.VMEM((rows, model), BF16), pltpu.VMEM((rows, width), BF16)],
        flops=weight_flops,
    )
    query, k_t, v_t, k1_t, v1_t, weights, stats = call(
        functools.partial(local_kernel, nb),
        [
            shape(3, nb, rows, HEAD_DIM),
            shape(HEAD_DIM, tokens),
            shape(HEAD_DIM, tokens),
            shape(HEAD_DIM, tokens // 2),
            shape(HEAD_DIM, tokens // 2),
            shape(nb, 4, BLOCK, BLOCK, dtype=F32),
            shape(8, tokens, dtype=F32),
        ],
        (near, queries, level_1, grad_chunks[0]),
        flops=score_flops,
    )
    grad_chunks = exchanged(grad_chunks)
    rim_square = shape(len(rims), BLOCK, BLOCK)
    prob, grads, top_2, deltas, far_shift, rim_shift, *refs = call(
        functools.partial(forward_kernel, nb, groups),
        [
            shape(nb, 4, BLOCK, BLOCK),
            in_order,
            block,
            shape(8, tokens, dtype=F32),
            shape(BLOCK, tokens),
            rim_square,
        ]
        + [chunk] * GROUP
        + sent,
        (query, v_t, v1_t, weights, stats, *rim_blocks, *grad_chunks),
        scratch=[
            pltpu.VMEM((nb, rows, HEAD_DIM), BF16),
            pltpu.VMEM((BLOCK, tokens), BF16),
            pltpu.VMEM(rim_square.shape, BF16),
            pltpu.VMEM((8, tokens), F32),
            pltpu.VMEM((HEAD_DIM, tokens), F32),
        ],
        flops=score_flops,
    )
    attended = exchanged(refs[:GROUP])
    rim_grads = refs[GROUP:]
    other_grads = crossed(rim_grads)
    grad_q, grad_kv = call(
        functools.partial(backward_kernel, nb, groups),
        [in_order, shape(2, nb, rows, HEAD_DIM, dtype=F32)],
        (query, near, level_1, k_t, k1_t, prob, grads, top_2, deltas, far_shift, rim_shift, *rim_blocks),
        scratch=[
            pltpu.VMEM((nb, 4, BLOCK, BLOCK), BF16),
            pltpu.VMEM((2, tokens // 2, HEAD_DIM), F32),
            pltpu.VMEM((HEAD_DIM, tokens), F32),
        ],
        flops=1,
    )
    local = rows // N_MP
    kept, *given = call(
        project_kernel,
        [shape(2, local, model)] + [shape(local // 2, model)] * 4,
        (*attended, out_weight, grad_q),
        scratch=[pltpu.VMEM((rows, width), BF16), pltpu.VMEM((rows, model), BF16)],
        flops=weight_flops,
    )
    across, here = call(
        share_kernel,
        [shape(local, model), shape(local, model, dtype=F32)],
        (kept, *(swapped(piece, "mp", 1) for piece in given)),
    )
    chunks = call(
        functools.partial(combine_kernel, nb, groups),
        [triple] * GROUP,
        (grad_q, grad_kv, across, *other_grads),
        scratch=[pltpu.VMEM((nb, 2, rows, HEAD_DIM), BF16)],
        flops=20 * score_flops,
    )
    chunks = exchanged(chunks)
    across = swapped(across, "mp", 2)
    grad_k, grad_v, grad_q, mixed = call(
        unpack_kernel,
        [shape(rows, width)] * 3 + [shape(local, model)],
        (here, across, *chunks),
    )
    return mixed, grad_q, grad_k, grad_v


def solution(mesh):
    return jax.shard_map(
        per_device,
        mesh=mesh,
        in_specs=(
            P("seq", "mp"),
            P("seq", "mp"),
            P("seq", "mp"),
            P("mp", None),
            P(("seq", "mp"), None),
        ),
        out_specs=(P(("seq", "mp"), None), P("seq", "mp"), P("seq", "mp"), P("seq", "mp")),
        check_vma=False,
    )
```

```python
import functools

import jax
import jax.numpy as jnp
from jax import lax
from jax.experimental import pallas as pl
from jax.experimental.pallas import tpu as pltpu
from jax.sharding import PartitionSpec as P

HEAD_DIM = 128
BLOCK = 256
LEVELS = 2
GROUP = 4
STEPS = (0, 3, 2, 1)
N_MP = 4
SCALE = HEAD_DIM**-0.5
LOG2E = 1.4426950408889634
BF16 = jnp.bfloat16
F32 = jnp.float32


def dot(a, b):
    return lax.dot_general(a, b, (((1,), (0,)), ((), ())), preferred_element_type=F32)


def dot_nt(a, b):
    return lax.dot_general(a, b, (((1,), (1,)), ((), ())), preferred_element_type=F32)


def shape(*dims, dtype=BF16):
    return jax.ShapeDtypeStruct(dims, dtype)


def call(kernel, out_shape, args, scratch=(), flops=0, limit=32, copied=0):
    whole = pl.BlockSpec(memory_space=pltpu.VMEM)
    kept = pl.BlockSpec(memory_space=pltpu.HBM)
    moved = sum(x.size * x.dtype.itemsize for x in (*args, *out_shape))
    return pl.pallas_call(
        kernel,
        out_shape=out_shape,
        in_specs=[kept if copied else whole] * len(args),
        out_specs=[kept] * copied + [whole] * (len(out_shape) - copied),
        scratch_shapes=scratch,
        compiler_params=pltpu.CompilerParams(vmem_limit_bytes=limit << 20),
        cost_estimate=pl.CostEstimate(flops=flops, bytes_accessed=moved if flops else 0, transcendentals=0),
    )(*args)


def columns(index):
    return pl.ds(pl.multiple_of(index * HEAD_DIM, HEAD_DIM), HEAD_DIM)


def span(index, size):
    return pl.ds(pl.multiple_of(index * size, size), size)


def iota(dims, axis):
    return lax.broadcasted_iota(jnp.int32, dims, axis)


def averaging(level):
    dims = (BLOCK, BLOCK)
    same = (iota(dims, 0) >> level) == (iota(dims, 1) >> level)
    return jnp.where(same, 2.0**-level, 0.0).astype(BF16)


def pooling():
    dims = (BLOCK // 2, BLOCK)
    return jnp.where(iota(dims, 0) == (iota(dims, 1) >> 1), 0.5, 0.0).astype(BF16)


def spreading(level):
    dims = (BLOCK, BLOCK >> level)
    return jnp.where((iota(dims, 0) >> level) == iota(dims, 1), 2.0**-level, 0.0).astype(BF16)


def halves(x):
    high = x.astype(BF16)
    return high, (x - high.astype(F32)).astype(BF16)


def at_block(b):
    return slice(b * BLOCK, (b + 1) * BLOCK)


def sibling(b):
    return (b >> 1) ^ 1


def rim_present(groups):
    group = lax.axis_index("seq") // GROUP
    return group > 0, group < groups - 1


def member():
    return lax.rem(lax.axis_index("seq"), GROUP)


def columns(index):
    return pl.ds(pl.multiple_of(index * HEAD_DIM, HEAD_DIM), HEAD_DIM)


def pack_kernel(q, k, v, *refs):
    *outs, tops, held, sems = refs
    me = member()
    copies = [pltpu.make_async_copy(x, held.at[i], sems.at[i]) for i, x in enumerate((k, v))]
    for step, out in zip(STEPS, outs):
        for part, source in enumerate((k, v, q)):
            piece = source.at[:, columns(me ^ step)]
            copies.append(pltpu.make_async_copy(piece, out.at[part], sems.at[len(copies)]))
    for copy in copies:
        copy.start()
    pool = pooling()
    half = BLOCK // 2
    for part in range(2):
        copies[part].wait()
        once = dot(pool, held[part]).astype(BF16)
        twice = dot(pool[: half // 2, :half], once).astype(BF16)
        for head in range(GROUP):
            tops[head, part] = twice[:, head * HEAD_DIM : (head + 1) * HEAD_DIM]
    for copy in copies[2:]:
        copy.wait()


def copy_kernel(x, y, x_out, y_out):
    x_out[...] = x[...]
    y_out[...] = y[...]


def gather_kernel(nb, groups, *refs):
    chunks, (near, queries, level_1, *rims) = refs[:GROUP], refs[GROUP:]
    me = member()
    for step, chunk in zip(STEPS, chunks):
        near[me ^ step] = chunk[:2]
        queries[me ^ step] = chunk[2]
    pool = pooling()
    half = BLOCK // 2
    for part in range(2):
        for b in range(nb):
            level_1[part, b * half : (b + 1) * half] = dot(pool, near[b, part]).astype(BF16)
    if groups == 2:
        upper = lax.axis_index("seq") >= GROUP
        rims[0][...] = jnp.where(upper, near[0], near[nb - 1])
    else:
        rims[0][...] = near[nb - 1]
        rims[1][...] = near[0]


def from_beside(groups, refs):
    if groups == 2:
        return (refs[0], refs[0]), refs[1:]
    return refs[:2], refs[2:]


def from_others(groups, refs):
    if groups == 2:
        return (refs[0].at[:2], refs[0].at[2:], refs[0].at[2:]), refs[1:]
    return refs[:3], refs[3:]


def near_sides(b, nb):
    return [side for side in range(3) if 0 <= b + side - 1 < nb]


def local_kernel(nb, near, queries, level_1, _, query, k_t, v_t, k1_t, v1_t, weights, stats):
    even_1, even_2 = averaging(1), averaging(2)
    for b in range(nb):
        query[0, b] = queries[b]
        once = dot(even_1, queries[b]).astype(BF16)
        query[1, b] = once
        query[2, b] = dot(even_2, once).astype(BF16)
        for part, transposed in enumerate((k_t, v_t)):
            transposed[:, at_block(b)] = near[b, part].T
    for c in range(nb // 2):
        for part, transposed in enumerate((k1_t, v1_t)):
            transposed[:, at_block(c)] = level_1[part, at_block(c)].T
    for b in range(nb):
        sides = near_sides(b, nb)
        scores = [dot_nt(near[b + side - 1, 0], query[0, b]) * (SCALE * LOG2E) for side in sides]
        coarse = dot_nt(level_1[0, at_block(sibling(b))], query[1, b]) * (SCALE * LOG2E)
        top = coarse.max(0, keepdims=True)
        for score in scores:
            top = jnp.maximum(top, score.max(0, keepdims=True))
        weight = 2.0 * jnp.exp2(coarse - top)
        weights[b, 3] = weight
        total = weight.sum(0, keepdims=True)
        for side, score in zip(sides, scores):
            weight = jnp.exp2(score - top)
            weights[b, side] = weight
            total = total + weight.sum(0, keepdims=True)
        stats[:1, at_block(b)] = top
        stats[1:2, at_block(b)] = total


def rims_of(nb, groups, low, high):
    group = lax.axis_index("seq") // GROUP
    if groups == 2:
        return [(jnp.where(group > 0, 0, nb - 1), low, None)]
    return [(0, low, group > 0), (nb - 1, high, group < groups - 1)]


def forward_kernel(nb, groups, *refs):
    (query, v_t, v1_t, weights, stats), refs = refs[:5], refs[5:]
    (rim_low, rim_high), refs = from_beside(groups, refs)
    chunks, refs = refs[:GROUP], refs[GROUP:]
    (prob, grads, top_2, deltas, far_shift, rim_shift), refs = refs[:6], refs[6:]
    outs, (*rim_outs, attended, far_prob, rim_prob, row, context_t) = refs[:GROUP], refs[GROUP:]
    rims = rims_of(nb, groups, rim_low, rim_high)
    me = member()
    quarter = BLOCK // 4
    tokens = nb * BLOCK
    for step, chunk in zip(STEPS, chunks):
        grads[me ^ step] = chunk[:BLOCK]
        for part in range(2):
            level = chunk[BLOCK + part * quarter : BLOCK + (part + 1) * quarter]
            top_2[part, span(me ^ step, quarter), :] = level
    coarse_query = query[2].reshape(tokens, HEAD_DIM)
    coarse = dot_nt(top_2[0], coarse_query) * (SCALE * LOG2E)
    row[:1] = jnp.maximum(stats[:1], coarse.max(0, keepdims=True))
    scores = []
    for b, block, present in rims:
        score = dot_nt(block[0], query[0, b]) * (SCALE * LOG2E)
        if present is not None:
            score = jnp.where(present, score, -jnp.inf)
        at = span(b, BLOCK)
        row[:1, at] = jnp.maximum(row[:1, at], score.max(0, keepdims=True))
        scores.append(score)
    top = row[:1]
    shrink = jnp.exp2(stats[:1] - top)
    far = 4.0 * jnp.exp2(coarse - top)
    row[1:2] = shrink * stats[1:2] + far.sum(0, keepdims=True)
    fresh = []
    for (b, _, _), score in zip(rims, scores):
        at = span(b, BLOCK)
        fresh.append(jnp.exp2(score - row[:1, at]))
        row[1:2, at] += fresh[-1].sum(0, keepdims=True)
    inverse = 1.0 / row[1:2]
    row[2:3] = inverse
    row[3:4] = shrink * inverse
    far_prob[...] = (far * inverse).astype(BF16)
    context_t[...] = dot(top_2[1].T, far_prob[...])
    for i, (b, block, _) in enumerate(rims):
        at = span(b, BLOCK)
        rim_prob[i] = (fresh[i] * row[2:3, at]).astype(BF16)
        context_t[:, at] += dot(block[1].T, rim_prob[i])
    for b in range(nb):
        shrink = row[3:4, at_block(b)]
        prob[b, 3] = (weights[b, 3] * shrink).astype(BF16)
        context = context_t[:, at_block(b)] + dot(v1_t[:, at_block(sibling(b))], prob[b, 3])
        for side in near_sides(b, nb):
            prob[b, side] = (weights[b, side] * shrink).astype(BF16)
            context = context + dot(v_t[:, at_block(b + side - 1)], prob[b, side])
        attended[b] = context.T.astype(BF16)
        deltas[:1, at_block(b)] = (grads[b].T.astype(F32) * context).sum(0, keepdims=True)
    grad = grads[...].reshape(tokens, HEAD_DIM)
    slope = dot_nt(top_2[1], grad)
    far_shift[...] = (far_prob[...].astype(F32) * (slope - deltas[:1])).astype(BF16)
    rim_outs[0][0] = (SCALE * dot(far_shift[...], coarse_query)).astype(BF16)
    rim_outs[0][1] = dot(far_prob[...], grad).astype(BF16)
    pairs = []
    for i, (b, block, _) in enumerate(rims):
        slope = dot_nt(block[1], grads[b])
        rim_shift[i] = (rim_prob[i].astype(F32) * (slope - deltas[:1, span(b, BLOCK)])).astype(BF16)
        pairs.append((SCALE * dot(rim_shift[i], query[0, b]), dot(rim_prob[i], grads[b])))
    for part in range(2):
        if groups == 2:
            rim_outs[0][2 + part] = pairs[0][part].astype(BF16)
        else:
            rim_outs[1][part] = pairs[1][part].astype(BF16)
            rim_outs[2][part] = pairs[0][part].astype(BF16)
    for step, out in zip(STEPS, outs):
        out[...] = attended[me ^ step]


def backward_kernel(nb, groups, *refs):
    (query, near, level_1, k_t, k1_t, prob, grads, top_2, deltas, far_shift, rim_shift), refs = refs[:11], refs[11:]
    (rim_low, rim_high), refs = from_beside(groups, refs)
    grad_q, grad_kv, shift, sums_1, query_t = refs
    even_1, even_2 = averaging(1), averaging(2)
    coarse = dot(top_2[0].T, far_shift[...])
    for b in range(nb):
        high, low = halves(coarse[:, at_block(b)])
        query_t[:, at_block(b)] = dot(high, even_2) + dot(low, even_2)
    for i, (b, block, _) in enumerate(rims_of(nb, groups, rim_low, rim_high)):
        query_t[:, span(b, BLOCK)] += dot(block[0].T, rim_shift[i])
    for b in range(nb):
        grad, delta = grads[b], deltas[:1, at_block(b)]
        grad_t = query_t[:, at_block(b)]
        for side in near_sides(b, nb):
            slope = dot_nt(near[b + side - 1, 1], grad)
            part = (prob[b, side].astype(F32) * (slope - delta)).astype(BF16)
            shift[b, side] = part
            grad_t = grad_t + dot(k_t[:, at_block(b + side - 1)], part)
        slope = dot_nt(level_1[1, at_block(sibling(b))], grad)
        part = (prob[b, 3].astype(F32) * (slope - delta)).astype(BF16)
        shift[b, 3] = part
        high, low = halves(dot(k1_t[:, at_block(sibling(b))], part))
        grad_t = grad_t + (dot(high, even_1) + dot(low, even_1))
        grad_q[b] = (SCALE * grad_t).T.astype(BF16)
    for c in range(nb // 2):
        users = [b for b in range(nb) if sibling(b) == c]
        sums_1[0, at_block(c)] = SCALE * sum(dot(shift[b, 3], query[1, b]) for b in users)
        sums_1[1, at_block(c)] = sum(dot(prob[b, 3], grads[b]) for b in users)
    spread = spreading(1)
    half = BLOCK // 2
    for s in range(nb):
        users = [(s + 1 - side, side) for side in range(3) if 0 <= s + 1 - side < nb]
        key = SCALE * sum(dot(shift[b, side], query[0, b]) for b, side in users)
        value = sum(dot(prob[b, side], grads[b]) for b, side in users)
        for part, total in enumerate((key, value)):
            high, low = halves(sums_1[part, s * half : (s + 1) * half])
            grad_kv[part, s] = total + (dot(spread, high) + dot(spread, low))


def share_kernel(kept, *refs):
    *got, across, here = refs
    half = across.shape[0] // 2
    for i, piece in enumerate(got):
        far, at = i // 2, pl.ds(i % 2 * half, half)
        total = kept[far, at, :].astype(F32) + piece[...].astype(F32)
        if far:
            across[at, :] = total.astype(BF16)
        else:
            here[at, :] = total


def combine_kernel(nb, groups, grad_q, grad_kv, _, *refs):
    (got_top, got_low, got_high), (*outs, out) = from_others(groups, refs)
    present = rim_present(groups)
    spread = spreading(2)
    quarter = BLOCK // 4
    for b in range(nb):
        for part in range(2):
            total = grad_kv[part, b] + dot(spread, got_top[part, b * quarter : (b + 1) * quarter])
            if b == 0:
                total = total + jnp.where(present[0], got_low[part].astype(F32), 0.0)
            if b == nb - 1:
                total = total + jnp.where(present[1], got_high[part].astype(F32), 0.0)
            out[b, part] = total.astype(BF16)
    me = member()
    for step, chunk in zip(STEPS, outs):
        chunk[:2] = out[me ^ step]
        chunk[2] = grad_q[me ^ step]


def unpack_kernel(*refs):
    here, across, *refs = refs
    chunks, (*outs, mixed) = refs[:GROUP], refs[GROUP:]
    mixed[...] = (here[...] + across[...].astype(F32)).astype(BF16)
    me = member()
    for step, chunk in zip(STEPS, chunks):
        at = columns(me ^ step)
        for part, out in enumerate(outs):
            out[:, at] = chunk[part]


def share():
    return lax.axis_index("mp")


def grad_kernel(*refs):
    pieces, (out_weight, tops), refs = refs[:N_MP], refs[N_MP : N_MP + 2], refs[N_MP + 2 :]
    *outs, whole, heads = refs
    me = member()
    for step, piece in enumerate(pieces):
        whole[span(share() ^ step, piece.shape[0]), :] = piece[...]
    heads[...] = dot_nt(whole[...], out_weight[...]).astype(BF16)
    quarter = tops.shape[2]
    for step, out in zip(STEPS, outs):
        out[:BLOCK] = heads[:, columns(me ^ step)]
        for part in range(2):
            out[BLOCK + part * quarter : BLOCK + (part + 1) * quarter] = tops[me ^ step, part]


def project_kernel(*refs):
    chunks, out_weight, (kept, *sent, attended, whole) = refs[:GROUP], refs[GROUP], refs[GROUP + 2 :]
    me = member()
    for step, chunk in zip(STEPS, chunks):
        attended[:, columns(me ^ step)] = chunk[...]
    whole[...] = dot(attended[...], out_weight[...]).astype(BF16)
    rows = kept.shape[1]
    for far in range(2):
        kept[far] = whole[span(share() ^ (2 * far), rows), :]
        for part in range(2):
            half = rows // 2
            at = 2 * (share() ^ (2 * far + 1)) + part
            sent[2 * far + part][...] = whole[span(at, half), :]


def swapped(x, axis, step):
    return lax.ppermute(x, axis, [(i, i ^ step) for i in range(lax.axis_size(axis))])


def exchanged(chunks):
    return [chunks[0]] + [swapped(chunk, "seq", step) for step, chunk in zip(STEPS[1:], chunks[1:])]


def beside(arrays):
    count = lax.axis_size("seq")
    if len(arrays) == 1:
        return [swapped(arrays[0], "seq", GROUP)]
    up = [(i, i + GROUP) for i in range(count - GROUP)]
    down = [(j, i) for i, j in up]
    return [lax.ppermute(arrays[0], "seq", up), lax.ppermute(arrays[1], "seq", down)]


def crossed(arrays):
    count = lax.axis_size("seq")
    across = swapped(arrays[0], "seq", GROUP)
    if len(arrays) == 1:
        return [across]
    up = [(i, i + GROUP) for i in range(count - GROUP)]
    down = [(j, i) for i, j in up]
    return [across, lax.ppermute(arrays[1], "seq", up), lax.ppermute(arrays[2], "seq", down)]


def per_device(queries, keys, values, out_weight, out_grad):
    rows, width = queries.shape
    assert width == GROUP * HEAD_DIM and rows == BLOCK and lax.axis_size("mp") == N_MP
    count = lax.axis_size("seq")
    assert count % (2 * GROUP) == 0
    groups = count // GROUP
    nb = GROUP
    tokens = nb * rows
    half, quarter = rows // 2, rows // 4
    model = out_weight.shape[1]
    block = shape(2, rows, HEAD_DIM)
    sent = [shape(4, rows, HEAD_DIM)] if groups == 2 else [block] * 3
    rims = [block] * (1 if groups == 2 else 2)
    quarter = rows // 4
    in_order = shape(nb, rows, HEAD_DIM)
    score_flops = 2 * tokens * 5 * BLOCK * HEAD_DIM
    weight_flops = 2 * rows * out_weight.size

    chunk = shape(rows, HEAD_DIM)
    triple = shape(3, rows, HEAD_DIM)
    *chunks, tops = call(
        pack_kernel,
        [triple] * GROUP + [shape(GROUP, 2, quarter, HEAD_DIM)],
        (queries, keys, values),
        scratch=[pltpu.VMEM((2, rows, width), BF16), pltpu.SemaphoreType.DMA((2 + 3 * GROUP,))],
        copied=GROUP,
        limit=53,
    )
    far = swapped(out_grad, "mp", 2)
    chunks = exchanged(chunks)
    tops = swapped(tops, "seq", GROUP)
    own_grad, far = call(copy_kernel, [shape(*out_grad.shape)] * 2, (out_grad, far))
    near, queries, level_1, *refs = call(
        functools.partial(gather_kernel, nb, groups),
        [
            shape(nb, 2, rows, HEAD_DIM),
            shape(nb, rows, HEAD_DIM),
            shape(2, tokens // 2, HEAD_DIM),
        ]
        + rims,
        chunks,
        flops=20 * score_flops,
    )
    rim_blocks = beside(refs)
    grad_chunks = call(
        grad_kernel,
        [shape(rows + 2 * quarter, HEAD_DIM)] * GROUP,
        (own_grad, swapped(own_grad, "mp", 1), far, swapped(far, "mp", 1), out_weight, tops),
        scratch=[pltpu.VMEM((rows, model), BF16), pltpu.VMEM((rows, width), BF16)],
        flops=weight_flops,
    )
    query, k_t, v_t, k1_t, v1_t, weights, stats = call(
        functools.partial(local_kernel, nb),
        [
            shape(3, nb, rows, HEAD_DIM),
            shape(HEAD_DIM, tokens),
            shape(HEAD_DIM, tokens),
            shape(HEAD_DIM, tokens // 2),
            shape(HEAD_DIM, tokens // 2),
            shape(nb, 4, BLOCK, BLOCK, dtype=F32),
            shape(8, tokens, dtype=F32),
        ],
        (near, queries, level_1, grad_chunks[0]),
        flops=score_flops,
    )
    grad_chunks = exchanged(grad_chunks)
    rim_square = shape(len(rims), BLOCK, BLOCK)
    prob, grads, top_2, deltas, far_shift, rim_shift, *refs = call(
        functools.partial(forward_kernel, nb, groups),
        [
            shape(nb, 4, BLOCK, BLOCK),
            in_order,
            block,
            shape(8, tokens, dtype=F32),
            shape(BLOCK, tokens),
            rim_square,
        ]
        + [chunk] * GROUP
        + sent,
        (query, v_t, v1_t, weights, stats, *rim_blocks, *grad_chunks),
        scratch=[
            pltpu.VMEM((nb, rows, HEAD_DIM), BF16),
            pltpu.VMEM((BLOCK, tokens), BF16),
            pltpu.VMEM(rim_square.shape, BF16),
            pltpu.VMEM((8, tokens), F32),
            pltpu.VMEM((HEAD_DIM, tokens), F32),
        ],
        flops=score_flops,
    )
    attended = exchanged(refs[:GROUP])
    rim_grads = refs[GROUP:]
    other_grads = crossed(rim_grads)
    grad_q, grad_kv = call(
        functools.partial(backward_kernel, nb, groups),
        [in_order, shape(2, nb, rows, HEAD_DIM, dtype=F32)],
        (query, near, level_1, k_t, k1_t, prob, grads, top_2, deltas, far_shift, rim_shift, *rim_blocks),
        scratch=[
            pltpu.VMEM((nb, 4, BLOCK, BLOCK), BF16),
            pltpu.VMEM((2, tokens // 2, HEAD_DIM), F32),
            pltpu.VMEM((HEAD_DIM, tokens), F32),
        ],
        flops=1,
    )
    local = rows // N_MP
    kept, *given = call(
        project_kernel,
        [shape(2, local, model)] + [shape(local // 2, model)] * 4,
        (*attended, out_weight, grad_q),
        scratch=[pltpu.VMEM((rows, width), BF16), pltpu.VMEM((rows, model), BF16)],
        flops=weight_flops,
    )
    across, here = call(
        share_kernel,
        [shape(local, model), shape(local, model, dtype=F32)],
        (kept, *(swapped(piece, "mp", 1) for piece in given)),
    )
    chunks = call(
        functools.partial(combine_kernel, nb, groups),
        [triple] * GROUP,
        (grad_q, grad_kv, across, *other_grads),
        scratch=[pltpu.VMEM((nb, 2, rows, HEAD_DIM), BF16)],
        flops=20 * score_flops,
    )
    chunks = exchanged(chunks)
    across = swapped(across, "mp", 2)
    grad_k, grad_v, grad_q, mixed = call(
        unpack_kernel,
        [shape(rows, width)] * 3 + [shape(local, model)],
        (here, across, *chunks),
    )
    return mixed, grad_q, grad_k, grad_v


def solution(mesh):
    return jax.shard_map(
        per_device,
        mesh=mesh,
        in_specs=(
            P("seq", "mp"),
            P("seq", "mp"),
            P("seq", "mp"),
            P("mp", None),
            P(("seq", "mp"), None),
        ),
        out_specs=(P(("seq", "mp"), None), P("seq", "mp"), P("seq", "mp"), P("seq", "mp")),
        check_vma=False,
    )
```

```python
import functools

import jax
import jax.numpy as jnp
from jax import lax
from jax.experimental import pallas as pl
from jax.experimental.pallas import tpu as pltpu
from jax.sharding import PartitionSpec as P

HEAD_DIM = 128
BLOCK = 256
LEVELS = 2
GROUP = 4
STEPS = (0, 3, 2, 1)
N_MP = 4
SCALE = HEAD_DIM**-0.5
LOG2E = 1.4426950408889634
BF16 = jnp.bfloat16
F32 = jnp.float32


def dot(a, b):
    return lax.dot_general(a, b, (((1,), (0,)), ((), ())), preferred_element_type=F32)


def dot_nt(a, b):
    return lax.dot_general(a, b, (((1,), (1,)), ((), ())), preferred_element_type=F32)


def shape(*dims, dtype=BF16):
    return jax.ShapeDtypeStruct(dims, dtype)


def call(kernel, out_shape, args, scratch=(), flops=0, limit=32, copied=0):
    whole = pl.BlockSpec(memory_space=pltpu.VMEM)
    kept = pl.BlockSpec(memory_space=pltpu.HBM)
    moved = sum(x.size * x.dtype.itemsize for x in (*args, *out_shape))
    return pl.pallas_call(
        kernel,
        out_shape=out_shape,
        in_specs=[kept if copied else whole] * len(args),
        out_specs=[kept] * copied + [whole] * (len(out_shape) - copied),
        scratch_shapes=scratch,
        compiler_params=pltpu.CompilerParams(vmem_limit_bytes=limit << 20),
        cost_estimate=pl.CostEstimate(flops=flops, bytes_accessed=moved if flops else 0, transcendentals=0),
    )(*args)


def columns(index):
    return pl.ds(pl.multiple_of(index * HEAD_DIM, HEAD_DIM), HEAD_DIM)


def span(index, size):
    return pl.ds(pl.multiple_of(index * size, size), size)


def iota(dims, axis):
    return lax.broadcasted_iota(jnp.int32, dims, axis)


def averaging(level):
    dims = (BLOCK, BLOCK)
    same = (iota(dims, 0) >> level) == (iota(dims, 1) >> level)
    return jnp.where(same, 2.0**-level, 0.0).astype(BF16)


def pooling():
    dims = (BLOCK // 2, BLOCK)
    return jnp.where(iota(dims, 0) == (iota(dims, 1) >> 1), 0.5, 0.0).astype(BF16)


def spreading(level):
    dims = (BLOCK, BLOCK >> level)
    return jnp.where((iota(dims, 0) >> level) == iota(dims, 1), 2.0**-level, 0.0).astype(BF16)


def halves(x):
    high = x.astype(BF16)
    return high, (x - high.astype(F32)).astype(BF16)


def at_block(b):
    return slice(b * BLOCK, (b + 1) * BLOCK)


def sibling(b):
    return (b >> 1) ^ 1


def rim_present(groups):
    group = lax.axis_index("seq") // GROUP
    return group > 0, group < groups - 1


def member():
    return lax.rem(lax.axis_index("seq"), GROUP)


def columns(index):
    return pl.ds(pl.multiple_of(index * HEAD_DIM, HEAD_DIM), HEAD_DIM)


def pack_kernel(q, k, v, *refs):
    *outs, sems = refs
    me = member()
    copies = []
    for step, out in zip(STEPS, outs):
        for part, source in enumerate((k, v, q)):
            piece = source.at[:, columns(me ^ step)]
            copies.append(pltpu.make_async_copy(piece, out.at[part], sems.at[len(copies)]))
    for copy in copies:
        copy.start()
    for copy in copies:
        copy.wait()


def pool_kernel(*refs):
    *chunks, out = refs
    me = member()
    pool = pooling()
    half = BLOCK // 2
    for step, chunk in zip(STEPS, chunks):
        for part in range(2):
            once = dot(pool, chunk[part]).astype(BF16)
            out[me ^ step, part] = dot(pool[: half // 2, :half], once).astype(BF16)


def copy_kernel(*refs):
    count = len(refs) // 2
    for x, out in zip(refs[:count], refs[count:]):
        out[...] = x[...]


def gather_kernel(nb, groups, *refs):
    chunks, (near, queries, level_1, *rims) = refs[:GROUP], refs[GROUP:]
    me = member()
    for step, chunk in zip(STEPS, chunks):
        near[me ^ step] = chunk[:2]
        queries[me ^ step] = chunk[2]
    pool = pooling()
    half = BLOCK // 2
    for part in range(2):
        for b in range(nb):
            level_1[part, b * half : (b + 1) * half] = dot(pool, near[b, part]).astype(BF16)
    if groups == 2:
        upper = lax.axis_index("seq") >= GROUP
        rims[0][...] = jnp.where(upper, near[0], near[nb - 1])
    else:
        rims[0][...] = near[nb - 1]
        rims[1][...] = near[0]


def from_beside(groups, refs):
    if groups == 2:
        return (refs[0], refs[0]), refs[1:]
    return refs[:2], refs[2:]


def from_others(groups, refs):
    if groups == 2:
        return (refs[0].at[:2], refs[0].at[2:], refs[0].at[2:]), refs[1:]
    return refs[:3], refs[3:]


def near_sides(b, nb):
    return [side for side in range(3) if 0 <= b + side - 1 < nb]


def local_kernel(nb, near, queries, level_1, _, query, k_t, v_t, k1_t, v1_t, weights, stats):
    even_1, even_2 = averaging(1), averaging(2)
    for b in range(nb):
        query[0, b] = queries[b]
        once = dot(even_1, queries[b]).astype(BF16)
        query[1, b] = once
        query[2, b] = dot(even_2, once).astype(BF16)
        for part, transposed in enumerate((k_t, v_t)):
            transposed[:, at_block(b)] = near[b, part].T
    for c in range(nb // 2):
        for part, transposed in enumerate((k1_t, v1_t)):
            transposed[:, at_block(c)] = level_1[part, at_block(c)].T
    for b in range(nb):
        sides = near_sides(b, nb)
        scores = [dot_nt(near[b + side - 1, 0], query[0, b]) * (SCALE * LOG2E) for side in sides]
        coarse = dot_nt(level_1[0, at_block(sibling(b))], query[1, b]) * (SCALE * LOG2E)
        top = coarse.max(0, keepdims=True)
        for score in scores:
            top = jnp.maximum(top, score.max(0, keepdims=True))
        weight = 2.0 * jnp.exp2(coarse - top)
        weights[b, 3] = weight
        total = weight.sum(0, keepdims=True)
        for side, score in zip(sides, scores):
            weight = jnp.exp2(score - top)
            weights[b, side] = weight
            total = total + weight.sum(0, keepdims=True)
        stats[:1, at_block(b)] = top
        stats[1:2, at_block(b)] = total


def rims_of(nb, groups, low, high):
    group = lax.axis_index("seq") // GROUP
    if groups == 2:
        return [(jnp.where(group > 0, 0, nb - 1), low, None)]
    return [(0, low, group > 0), (nb - 1, high, group < groups - 1)]


def forward_kernel(nb, groups, *refs):
    (query, v_t, v1_t, weights, stats), refs = refs[:5], refs[5:]
    (rim_low, rim_high), refs = from_beside(groups, refs)
    chunks, refs = refs[:GROUP], refs[GROUP:]
    (prob, grads, top_2, deltas, far_shift, rim_shift), refs = refs[:6], refs[6:]
    outs, (*rim_outs, attended, far_prob, rim_prob, row, context_t) = refs[:GROUP], refs[GROUP:]
    rims = rims_of(nb, groups, rim_low, rim_high)
    me = member()
    quarter = BLOCK // 4
    tokens = nb * BLOCK
    for step, chunk in zip(STEPS, chunks):
        grads[me ^ step] = chunk[:BLOCK]
        for part in range(2):
            level = chunk[BLOCK + part * quarter : BLOCK + (part + 1) * quarter]
            top_2[part, span(me ^ step, quarter), :] = level
    coarse_query = query[2].reshape(tokens, HEAD_DIM)
    coarse = dot_nt(top_2[0], coarse_query) * (SCALE * LOG2E)
    row[:1] = jnp.maximum(stats[:1], coarse.max(0, keepdims=True))
    scores = []
    for b, block, present in rims:
        score = dot_nt(block[0], query[0, b]) * (SCALE * LOG2E)
        if present is not None:
            score = jnp.where(present, score, -jnp.inf)
        at = span(b, BLOCK)
        row[:1, at] = jnp.maximum(row[:1, at], score.max(0, keepdims=True))
        scores.append(score)
    top = row[:1]
    shrink = jnp.exp2(stats[:1] - top)
    far = 4.0 * jnp.exp2(coarse - top)
    row[1:2] = shrink * stats[1:2] + far.sum(0, keepdims=True)
    fresh = []
    for (b, _, _), score in zip(rims, scores):
        at = span(b, BLOCK)
        fresh.append(jnp.exp2(score - row[:1, at]))
        row[1:2, at] += fresh[-1].sum(0, keepdims=True)
    inverse = 1.0 / row[1:2]
    row[2:3] = inverse
    row[3:4] = shrink * inverse
    far_prob[...] = (far * inverse).astype(BF16)
    context_t[...] = dot(top_2[1].T, far_prob[...])
    for i, (b, block, _) in enumerate(rims):
        at = span(b, BLOCK)
        rim_prob[i] = (fresh[i] * row[2:3, at]).astype(BF16)
        context_t[:, at] += dot(block[1].T, rim_prob[i])
    for b in range(nb):
        shrink = row[3:4, at_block(b)]
        prob[b, 3] = (weights[b, 3] * shrink).astype(BF16)
        context = context_t[:, at_block(b)] + dot(v1_t[:, at_block(sibling(b))], prob[b, 3])
        for side in near_sides(b, nb):
            prob[b, side] = (weights[b, side] * shrink).astype(BF16)
            context = context + dot(v_t[:, at_block(b + side - 1)], prob[b, side])
        attended[b] = context.T.astype(BF16)
        deltas[:1, at_block(b)] = (grads[b].T.astype(F32) * context).sum(0, keepdims=True)
    grad = grads[...].reshape(tokens, HEAD_DIM)
    slope = dot_nt(top_2[1], grad)
    far_shift[...] = (far_prob[...].astype(F32) * (slope - deltas[:1])).astype(BF16)
    rim_outs[0][0] = (SCALE * dot(far_shift[...], coarse_query)).astype(BF16)
    rim_outs[0][1] = dot(far_prob[...], grad).astype(BF16)
    pairs = []
    for i, (b, block, _) in enumerate(rims):
        slope = dot_nt(block[1], grads[b])
        rim_shift[i] = (rim_prob[i].astype(F32) * (slope - deltas[:1, span(b, BLOCK)])).astype(BF16)
        pairs.append((SCALE * dot(rim_shift[i], query[0, b]), dot(rim_prob[i], grads[b])))
    for part in range(2):
        if groups == 2:
            rim_outs[0][2 + part] = pairs[0][part].astype(BF16)
        else:
            rim_outs[1][part] = pairs[1][part].astype(BF16)
            rim_outs[2][part] = pairs[0][part].astype(BF16)
    for step, out in zip(STEPS, outs):
        out[...] = attended[me ^ step]


def backward_kernel(nb, groups, *refs):
    (query, near, level_1, k_t, k1_t, prob, grads, top_2, deltas, far_shift, rim_shift), refs = refs[:11], refs[11:]
    (rim_low, rim_high), refs = from_beside(groups, refs)
    grad_q, grad_kv, shift, sums_1, query_t = refs
    even_1, even_2 = averaging(1), averaging(2)
    coarse = dot(top_2[0].T, far_shift[...])
    for b in range(nb):
        high, low = halves(coarse[:, at_block(b)])
        query_t[:, at_block(b)] = dot(high, even_2) + dot(low, even_2)
    for i, (b, block, _) in enumerate(rims_of(nb, groups, rim_low, rim_high)):
        query_t[:, span(b, BLOCK)] += dot(block[0].T, rim_shift[i])
    for b in range(nb):
        grad, delta = grads[b], deltas[:1, at_block(b)]
        grad_t = query_t[:, at_block(b)]
        for side in near_sides(b, nb):
            slope = dot_nt(near[b + side - 1, 1], grad)
            part = (prob[b, side].astype(F32) * (slope - delta)).astype(BF16)
            shift[b, side] = part
            grad_t = grad_t + dot(k_t[:, at_block(b + side - 1)], part)
        slope = dot_nt(level_1[1, at_block(sibling(b))], grad)
        part = (prob[b, 3].astype(F32) * (slope - delta)).astype(BF16)
        shift[b, 3] = part
        high, low = halves(dot(k1_t[:, at_block(sibling(b))], part))
        grad_t = grad_t + (dot(high, even_1) + dot(low, even_1))
        grad_q[b] = (SCALE * grad_t).T.astype(BF16)
    for c in range(nb // 2):
        users = [b for b in range(nb) if sibling(b) == c]
        sums_1[0, at_block(c)] = SCALE * sum(dot(shift[b, 3], query[1, b]) for b in users)
        sums_1[1, at_block(c)] = sum(dot(prob[b, 3], grads[b]) for b in users)
    spread = spreading(1)
    half = BLOCK // 2
    for s in range(nb):
        users = [(s + 1 - side, side) for side in range(3) if 0 <= s + 1 - side < nb]
        key = SCALE * sum(dot(shift[b, side], query[0, b]) for b, side in users)
        value = sum(dot(prob[b, side], grads[b]) for b, side in users)
        for part, total in enumerate((key, value)):
            high, low = halves(sums_1[part, s * half : (s + 1) * half])
            grad_kv[part, s] = total + (dot(spread, high) + dot(spread, low))


def share_kernel(kept, *refs):
    *got, across, here = refs
    half = across.shape[0] // 2
    for i, piece in enumerate(got):
        far, at = i // 2, pl.ds(i % 2 * half, half)
        total = kept[far, at, :].astype(F32) + piece[...].astype(F32)
        if far:
            across[at, :] = total.astype(BF16)
        else:
            here[at, :] = total


def combine_kernel(nb, groups, grad_q, grad_kv, _, *refs):
    (got_top, got_low, got_high), (*outs, out) = from_others(groups, refs)
    present = rim_present(groups)
    spread = spreading(2)
    quarter = BLOCK // 4
    for b in range(nb):
        for part in range(2):
            total = grad_kv[part, b] + dot(spread, got_top[part, b * quarter : (b + 1) * quarter])
            if b == 0:
                total = total + jnp.where(present[0], got_low[part].astype(F32), 0.0)
            if b == nb - 1:
                total = total + jnp.where(present[1], got_high[part].astype(F32), 0.0)
            out[b, part] = total.astype(BF16)
    me = member()
    for step, chunk in zip(STEPS, outs):
        chunk[:2] = out[me ^ step]
        chunk[2] = grad_q[me ^ step]


def unpack_kernel(*refs):
    here, across, *refs = refs
    chunks, (*outs, mixed) = refs[:GROUP], refs[GROUP:]
    mixed[...] = (here[...] + across[...].astype(F32)).astype(BF16)
    me = member()
    for step, chunk in zip(STEPS, chunks):
        at = columns(me ^ step)
        for part, out in enumerate(outs):
            out[:, at] = chunk[part]


def share():
    return lax.axis_index("mp")


def grad_kernel(*refs):
    pieces, (out_weight, tops), refs = refs[:N_MP], refs[N_MP : N_MP + 2], refs[N_MP + 2 :]
    *outs, whole, heads = refs
    me = member()
    for step, piece in enumerate(pieces):
        whole[span(share() ^ step, piece.shape[0]), :] = piece[...]
    heads[...] = dot_nt(whole[...], out_weight[...]).astype(BF16)
    quarter = tops.shape[2]
    for step, out in zip(STEPS, outs):
        out[:BLOCK] = heads[:, columns(me ^ step)]
        for part in range(2):
            out[BLOCK + part * quarter : BLOCK + (part + 1) * quarter] = tops[me ^ step, part]


def project_kernel(*refs):
    chunks, out_weight, (kept, *sent, attended, whole) = refs[:GROUP], refs[GROUP], refs[GROUP + 2 :]
    me = member()
    for step, chunk in zip(STEPS, chunks):
        attended[:, columns(me ^ step)] = chunk[...]
    whole[...] = dot(attended[...], out_weight[...]).astype(BF16)
    rows = kept.shape[1]
    for far in range(2):
        kept[far] = whole[span(share() ^ (2 * far), rows), :]
        for part in range(2):
            half = rows // 2
            at = 2 * (share() ^ (2 * far + 1)) + part
            sent[2 * far + part][...] = whole[span(at, half), :]


def swapped(x, axis, step):
    return lax.ppermute(x, axis, [(i, i ^ step) for i in range(lax.axis_size(axis))])


def exchanged(chunks):
    return [chunks[0]] + [swapped(chunk, "seq", step) for step, chunk in zip(STEPS[1:], chunks[1:])]


def beside(arrays):
    count = lax.axis_size("seq")
    if len(arrays) == 1:
        return [swapped(arrays[0], "seq", GROUP)]
    up = [(i, i + GROUP) for i in range(count - GROUP)]
    down = [(j, i) for i, j in up]
    return [lax.ppermute(arrays[0], "seq", up), lax.ppermute(arrays[1], "seq", down)]


def crossed(arrays):
    count = lax.axis_size("seq")
    across = swapped(arrays[0], "seq", GROUP)
    if len(arrays) == 1:
        return [across]
    up = [(i, i + GROUP) for i in range(count - GROUP)]
    down = [(j, i) for i, j in up]
    return [across, lax.ppermute(arrays[1], "seq", up), lax.ppermute(arrays[2], "seq", down)]


def per_device(queries, keys, values, out_weight, out_grad):
    rows, width = queries.shape
    assert width == GROUP * HEAD_DIM and rows == BLOCK and lax.axis_size("mp") == N_MP
    count = lax.axis_size("seq")
    assert count % (2 * GROUP) == 0
    groups = count // GROUP
    nb = GROUP
    tokens = nb * rows
    half, quarter = rows // 2, rows // 4
    model = out_weight.shape[1]
    block = shape(2, rows, HEAD_DIM)
    sent = [shape(4, rows, HEAD_DIM)] if groups == 2 else [block] * 3
    rims = [block] * (1 if groups == 2 else 2)
    quarter = rows // 4
    in_order = shape(nb, rows, HEAD_DIM)
    score_flops = 2 * tokens * 5 * BLOCK * HEAD_DIM
    weight_flops = 2 * rows * out_weight.size

    chunk = shape(rows, HEAD_DIM)
    triple = shape(3, rows, HEAD_DIM)
    chunks = call(
        pack_kernel,
        [triple] * GROUP,
        (queries, keys, values),
        scratch=[pltpu.SemaphoreType.DMA((3 * GROUP,))],
        copied=GROUP,
        limit=53,
    )
    far = swapped(out_grad, "mp", 2)
    (tops,) = call(pool_kernel, [shape(GROUP, 2, quarter, HEAD_DIM)], chunks)
    chunks = exchanged(chunks)
    tops = swapped(tops, "seq", GROUP)
    arrays = (out_grad, far, out_weight)
    own_grad, far, out_weight = call(copy_kernel, [shape(*x.shape) for x in arrays], arrays)
    near, queries, level_1, *refs = call(
        functools.partial(gather_kernel, nb, groups),
        [
            shape(nb, 2, rows, HEAD_DIM),
            shape(nb, rows, HEAD_DIM),
            shape(2, tokens // 2, HEAD_DIM),
        ]
        + rims,
        chunks,
        flops=20 * score_flops,
    )
    rim_blocks = beside(refs)
    grad_chunks = call(
        grad_kernel,
        [shape(rows + 2 * quarter, HEAD_DIM)] * GROUP,
        (own_grad, swapped(own_grad, "mp", 1), far, swapped(far, "mp", 1), out_weight, tops),
        scratch=[pltpu.VMEM((rows, model), BF16), pltpu.VMEM((rows, width), BF16)],
        flops=weight_flops,
    )
    query, k_t, v_t, k1_t, v1_t, weights, stats = call(
        functools.partial(local_kernel, nb),
        [
            shape(3, nb, rows, HEAD_DIM),
            shape(HEAD_DIM, tokens),
            shape(HEAD_DIM, tokens),
            shape(HEAD_DIM, tokens // 2),
            shape(HEAD_DIM, tokens // 2),
            shape(nb, 4, BLOCK, BLOCK, dtype=F32),
            shape(8, tokens, dtype=F32),
        ],
        (near, queries, level_1, grad_chunks[0]),
        flops=score_flops,
    )
    grad_chunks = exchanged(grad_chunks)
    rim_square = shape(len(rims), BLOCK, BLOCK)
    prob, grads, top_2, deltas, far_shift, rim_shift, *refs = call(
        functools.partial(forward_kernel, nb, groups),
        [
            shape(nb, 4, BLOCK, BLOCK),
            in_order,
            block,
            shape(8, tokens, dtype=F32),
            shape(BLOCK, tokens),
            rim_square,
        ]
        + [chunk] * GROUP
        + sent,
        (query, v_t, v1_t, weights, stats, *rim_blocks, *grad_chunks),
        scratch=[
            pltpu.VMEM((nb, rows, HEAD_DIM), BF16),
            pltpu.VMEM((BLOCK, tokens), BF16),
            pltpu.VMEM(rim_square.shape, BF16),
            pltpu.VMEM((8, tokens), F32),
            pltpu.VMEM((HEAD_DIM, tokens), F32),
        ],
        flops=score_flops,
    )
    attended = exchanged(refs[:GROUP])
    rim_grads = refs[GROUP:]
    other_grads = crossed(rim_grads)
    grad_q, grad_kv = call(
        functools.partial(backward_kernel, nb, groups),
        [in_order, shape(2, nb, rows, HEAD_DIM, dtype=F32)],
        (query, near, level_1, k_t, k1_t, prob, grads, top_2, deltas, far_shift, rim_shift, *rim_blocks),
        scratch=[
            pltpu.VMEM((nb, 4, BLOCK, BLOCK), BF16),
            pltpu.VMEM((2, tokens // 2, HEAD_DIM), F32),
            pltpu.VMEM((HEAD_DIM, tokens), F32),
        ],
        flops=1,
    )
    local = rows // N_MP
    kept, *given = call(
        project_kernel,
        [shape(2, local, model)] + [shape(local // 2, model)] * 4,
        (*attended, out_weight, grad_q),
        scratch=[pltpu.VMEM((rows, width), BF16), pltpu.VMEM((rows, model), BF16)],
        flops=weight_flops,
    )
    across, here = call(
        share_kernel,
        [shape(local, model), shape(local, model, dtype=F32)],
        (kept, *(swapped(piece, "mp", 1) for piece in given)),
    )
    chunks = call(
        functools.partial(combine_kernel, nb, groups),
        [triple] * GROUP,
        (grad_q, grad_kv, across, *other_grads),
        scratch=[pltpu.VMEM((nb, 2, rows, HEAD_DIM), BF16)],
        flops=20 * score_flops,
    )
    chunks = exchanged(chunks)
    across = swapped(across, "mp", 2)
    grad_k, grad_v, grad_q, mixed = call(
        unpack_kernel,
        [shape(rows, width)] * 3 + [shape(local, model)],
        (here, across, *chunks),
    )
    return mixed, grad_q, grad_k, grad_v


def solution(mesh):
    return jax.shard_map(
        per_device,
        mesh=mesh,
        in_specs=(
            P("seq", "mp"),
            P("seq", "mp"),
            P("seq", "mp"),
            P("mp", None),
            P(("seq", "mp"), None),
        ),
        out_specs=(P(("seq", "mp"), None), P("seq", "mp"), P("seq", "mp"), P("seq", "mp")),
        check_vma=False,
    )
```

```python
import functools

import jax
import jax.numpy as jnp
from jax import lax
from jax.experimental import pallas as pl
from jax.experimental.pallas import tpu as pltpu
from jax.sharding import PartitionSpec as P

HEAD_DIM = 128
BLOCK = 256
LEVELS = 2
GROUP = 4
STEPS = (0, 3, 2, 1)
N_MP = 4
SCALE = HEAD_DIM**-0.5
LOG2E = 1.4426950408889634
BF16 = jnp.bfloat16
F32 = jnp.float32


def dot(a, b):
    return lax.dot_general(a, b, (((1,), (0,)), ((), ())), preferred_element_type=F32)


def dot_nt(a, b):
    return lax.dot_general(a, b, (((1,), (1,)), ((), ())), preferred_element_type=F32)


def shape(*dims, dtype=BF16):
    return jax.ShapeDtypeStruct(dims, dtype)


def call(kernel, out_shape, args, scratch=(), flops=0, limit=32, copied=0):
    whole = pl.BlockSpec(memory_space=pltpu.VMEM)
    kept = pl.BlockSpec(memory_space=pltpu.HBM)
    moved = sum(x.size * x.dtype.itemsize for x in (*args, *out_shape))
    return pl.pallas_call(
        kernel,
        out_shape=out_shape,
        in_specs=[kept if copied else whole] * len(args),
        out_specs=[kept] * copied + [whole] * (len(out_shape) - copied),
        scratch_shapes=scratch,
        compiler_params=pltpu.CompilerParams(vmem_limit_bytes=limit << 20),
        cost_estimate=pl.CostEstimate(flops=flops, bytes_accessed=moved if flops else 0, transcendentals=0),
    )(*args)


def columns(index):
    return pl.ds(pl.multiple_of(index * HEAD_DIM, HEAD_DIM), HEAD_DIM)


def span(index, size):
    return pl.ds(pl.multiple_of(index * size, size), size)


def iota(dims, axis):
    return lax.broadcasted_iota(jnp.int32, dims, axis)


def averaging(level):
    dims = (BLOCK, BLOCK)
    same = (iota(dims, 0) >> level) == (iota(dims, 1) >> level)
    return jnp.where(same, 2.0**-level, 0.0).astype(BF16)


def pooling():
    dims = (BLOCK // 2, BLOCK)
    return jnp.where(iota(dims, 0) == (iota(dims, 1) >> 1), 0.5, 0.0).astype(BF16)


def spreading(level):
    dims = (BLOCK, BLOCK >> level)
    return jnp.where((iota(dims, 0) >> level) == iota(dims, 1), 2.0**-level, 0.0).astype(BF16)


def halves(x):
    high = x.astype(BF16)
    return high, (x - high.astype(F32)).astype(BF16)


def at_block(b):
    return slice(b * BLOCK, (b + 1) * BLOCK)


def sibling(b):
    return (b >> 1) ^ 1


def rim_present(groups):
    group = lax.axis_index("seq") // GROUP
    return group > 0, group < groups - 1


def member():
    return lax.rem(lax.axis_index("seq"), GROUP)


def columns(index):
    return pl.ds(pl.multiple_of(index * HEAD_DIM, HEAD_DIM), HEAD_DIM)


def pack_kernel(q, k, v, *refs):
    *outs, sems = refs
    me = member()
    copies = []
    for step, out in zip(STEPS, outs):
        for part, source in enumerate((k, v, q)):
            piece = source.at[:, columns(me ^ step)]
            copies.append(pltpu.make_async_copy(piece, out.at[part], sems.at[len(copies)]))
    for copy in copies:
        copy.start()
    for copy in copies:
        copy.wait()


def pool_kernel(*refs):
    *chunks, out = refs
    me = member()
    pool = pooling()
    half = BLOCK // 2
    for step, chunk in zip(STEPS, chunks):
        for part in range(2):
            once = dot(pool, chunk[part]).astype(BF16)
            out[me ^ step, part] = dot(pool[: half // 2, :half], once).astype(BF16)


def copy_kernel(*refs):
    count = len(refs) // 2
    for x, out in zip(refs[:count], refs[count:]):
        out[...] = x[...]


def gather_kernel(nb, groups, *refs):
    chunks, (near, queries, level_1, *rims) = refs[:GROUP], refs[GROUP:]
    me = member()
    for step, chunk in zip(STEPS, chunks):
        near[me ^ step] = chunk[:2]
        queries[me ^ step] = chunk[2]
    pool = pooling()
    half = BLOCK // 2
    for part in range(2):
        for b in range(nb):
            level_1[part, b * half : (b + 1) * half] = dot(pool, near[b, part]).astype(BF16)
    if groups == 2:
        upper = lax.axis_index("seq") >= GROUP
        rims[0][...] = jnp.where(upper, near[0], near[nb - 1])
    else:
        rims[0][...] = near[nb - 1]
        rims[1][...] = near[0]


def from_beside(groups, refs):
    if groups == 2:
        return (refs[0], refs[0]), refs[1:]
    return refs[:2], refs[2:]


def from_others(groups, refs):
    if groups == 2:
        return (refs[0].at[:2], refs[0].at[2:], refs[0].at[2:]), refs[1:]
    return refs[:3], refs[3:]


def near_sides(b, nb):
    return [side for side in range(3) if 0 <= b + side - 1 < nb]


def local_kernel(nb, near, queries, level_1, _, query, k_t, v_t, k1_t, v1_t, weights, stats):
    even_1, even_2 = averaging(1), averaging(2)
    for b in range(nb):
        query[0, b] = queries[b]
        once = dot(even_1, queries[b]).astype(BF16)
        query[1, b] = once
        query[2, b] = dot(even_2, once).astype(BF16)
        for part, transposed in enumerate((k_t, v_t)):
            transposed[:, at_block(b)] = near[b, part].T
    for c in range(nb // 2):
        for part, transposed in enumerate((k1_t, v1_t)):
            transposed[:, at_block(c)] = level_1[part, at_block(c)].T
    for b in range(nb):
        sides = near_sides(b, nb)
        scores = [dot_nt(near[b + side - 1, 0], query[0, b]) * (SCALE * LOG2E) for side in sides]
        coarse = dot_nt(level_1[0, at_block(sibling(b))], query[1, b]) * (SCALE * LOG2E)
        top = coarse.max(0, keepdims=True)
        for score in scores:
            top = jnp.maximum(top, score.max(0, keepdims=True))
        weight = 2.0 * jnp.exp2(coarse - top)
        weights[b, 3] = weight
        total = weight.sum(0, keepdims=True)
        for side, score in zip(sides, scores):
            weight = jnp.exp2(score - top)
            weights[b, side] = weight
            total = total + weight.sum(0, keepdims=True)
        stats[:1, at_block(b)] = top
        stats[1:2, at_block(b)] = total


def rims_of(nb, groups, low, high):
    group = lax.axis_index("seq") // GROUP
    if groups == 2:
        return [(jnp.where(group > 0, 0, nb - 1), low, None)]
    return [(0, low, group > 0), (nb - 1, high, group < groups - 1)]


def forward_kernel(nb, groups, *refs):
    (query, v_t, v1_t, weights, stats), refs = refs[:5], refs[5:]
    (rim_low, rim_high), refs = from_beside(groups, refs)
    chunks, refs = refs[:GROUP], refs[GROUP:]
    (prob, grads, top_2, deltas, far_shift, rim_shift), refs = refs[:6], refs[6:]
    outs, (*rim_outs, attended, far_prob, rim_prob, row, context_t) = refs[:GROUP], refs[GROUP:]
    rims = rims_of(nb, groups, rim_low, rim_high)
    me = member()
    quarter = BLOCK // 4
    tokens = nb * BLOCK
    for step, chunk in zip(STEPS, chunks):
        grads[me ^ step] = chunk[:BLOCK]
        for part in range(2):
            level = chunk[BLOCK + part * quarter : BLOCK + (part + 1) * quarter]
            top_2[part, span(me ^ step, quarter), :] = level
    coarse_query = query[2].reshape(tokens, HEAD_DIM)
    coarse = dot_nt(top_2[0], coarse_query) * (SCALE * LOG2E)
    row[:1] = jnp.maximum(stats[:1], coarse.max(0, keepdims=True))
    scores = []
    for b, block, present in rims:
        score = dot_nt(block[0], query[0, b]) * (SCALE * LOG2E)
        if present is not None:
            score = jnp.where(present, score, -jnp.inf)
        at = span(b, BLOCK)
        row[:1, at] = jnp.maximum(row[:1, at], score.max(0, keepdims=True))
        scores.append(score)
    top = row[:1]
    shrink = jnp.exp2(stats[:1] - top)
    far = 4.0 * jnp.exp2(coarse - top)
    row[1:2] = shrink * stats[1:2] + far.sum(0, keepdims=True)
    fresh = []
    for (b, _, _), score in zip(rims, scores):
        at = span(b, BLOCK)
        fresh.append(jnp.exp2(score - row[:1, at]))
        row[1:2, at] += fresh[-1].sum(0, keepdims=True)
    inverse = 1.0 / row[1:2]
    row[2:3] = inverse
    row[3:4] = shrink * inverse
    far_prob[...] = (far * inverse).astype(BF16)
    context_t[...] = dot(top_2[1].T, far_prob[...])
    for i, (b, block, _) in enumerate(rims):
        at = span(b, BLOCK)
        rim_prob[i] = (fresh[i] * row[2:3, at]).astype(BF16)
        context_t[:, at] += dot(block[1].T, rim_prob[i])
    for b in range(nb):
        shrink = row[3:4, at_block(b)]
        prob[b, 3] = (weights[b, 3] * shrink).astype(BF16)
        context = context_t[:, at_block(b)] + dot(v1_t[:, at_block(sibling(b))], prob[b, 3])
        for side in near_sides(b, nb):
            prob[b, side] = (weights[b, side] * shrink).astype(BF16)
            context = context + dot(v_t[:, at_block(b + side - 1)], prob[b, side])
        attended[b] = context.T.astype(BF16)
        deltas[:1, at_block(b)] = (grads[b].T.astype(F32) * context).sum(0, keepdims=True)
    grad = grads[...].reshape(tokens, HEAD_DIM)
    slope = dot_nt(top_2[1], grad)
    far_shift[...] = (far_prob[...].astype(F32) * (slope - deltas[:1])).astype(BF16)
    rim_outs[0][0] = (SCALE * dot(far_shift[...], coarse_query)).astype(BF16)
    rim_outs[0][1] = dot(far_prob[...], grad).astype(BF16)
    pairs = []
    for i, (b, block, _) in enumerate(rims):
        slope = dot_nt(block[1], grads[b])
        rim_shift[i] = (rim_prob[i].astype(F32) * (slope - deltas[:1, span(b, BLOCK)])).astype(BF16)
        pairs.append((SCALE * dot(rim_shift[i], query[0, b]), dot(rim_prob[i], grads[b])))
    for part in range(2):
        if groups == 2:
            rim_outs[0][2 + part] = pairs[0][part].astype(BF16)
        else:
            rim_outs[1][part] = pairs[1][part].astype(BF16)
            rim_outs[2][part] = pairs[0][part].astype(BF16)
    for step, out in zip(STEPS, outs):
        out[...] = attended[me ^ step]


def backward_kernel(nb, groups, *refs):
    (query, near, level_1, k_t, k1_t, prob, grads, top_2, deltas, far_shift, rim_shift), refs = refs[:11], refs[11:]
    (rim_low, rim_high), refs = from_beside(groups, refs)
    grad_q, grad_kv, shift, sums_1, query_t = refs
    even_1, even_2 = averaging(1), averaging(2)
    coarse = dot(top_2[0].T, far_shift[...])
    for b in range(nb):
        high, low = halves(coarse[:, at_block(b)])
        query_t[:, at_block(b)] = dot(high, even_2) + dot(low, even_2)
    for i, (b, block, _) in enumerate(rims_of(nb, groups, rim_low, rim_high)):
        query_t[:, span(b, BLOCK)] += dot(block[0].T, rim_shift[i])
    for b in range(nb):
        grad, delta = grads[b], deltas[:1, at_block(b)]
        grad_t = query_t[:, at_block(b)]
        for side in near_sides(b, nb):
            slope = dot_nt(near[b + side - 1, 1], grad)
            part = (prob[b, side].astype(F32) * (slope - delta)).astype(BF16)
            shift[b, side] = part
            grad_t = grad_t + dot(k_t[:, at_block(b + side - 1)], part)
        slope = dot_nt(level_1[1, at_block(sibling(b))], grad)
        part = (prob[b, 3].astype(F32) * (slope - delta)).astype(BF16)
        shift[b, 3] = part
        high, low = halves(dot(k1_t[:, at_block(sibling(b))], part))
        grad_t = grad_t + (dot(high, even_1) + dot(low, even_1))
        grad_q[b] = (SCALE * grad_t).T.astype(BF16)
    for c in range(nb // 2):
        users = [b for b in range(nb) if sibling(b) == c]
        sums_1[0, at_block(c)] = SCALE * sum(dot(shift[b, 3], query[1, b]) for b in users)
        sums_1[1, at_block(c)] = sum(dot(prob[b, 3], grads[b]) for b in users)
    spread = spreading(1)
    half = BLOCK // 2
    for s in range(nb):
        users = [(s + 1 - side, side) for side in range(3) if 0 <= s + 1 - side < nb]
        key = SCALE * sum(dot(shift[b, side], query[0, b]) for b, side in users)
        value = sum(dot(prob[b, side], grads[b]) for b, side in users)
        for part, total in enumerate((key, value)):
            high, low = halves(sums_1[part, s * half : (s + 1) * half])
            grad_kv[part, s] = total + (dot(spread, high) + dot(spread, low))


def share_kernel(kept, *refs):
    *got, across_0, across_1, here = refs
    half = across_0.shape[0]
    for i, piece in enumerate(got):
        far, at = i // 2, pl.ds(i % 2 * half, half)
        total = kept[far, at, :].astype(F32) + piece[...].astype(F32)
        if far:
            (across_0, across_1)[i % 2][...] = total.astype(BF16)
        else:
            here[at, :] = total


def combine_kernel(nb, groups, grad_q, grad_kv, _, *refs):
    (got_top, got_low, got_high), (*outs, out) = from_others(groups, refs)
    present = rim_present(groups)
    spread = spreading(2)
    quarter = BLOCK // 4
    for b in range(nb):
        for part in range(2):
            total = grad_kv[part, b] + dot(spread, got_top[part, b * quarter : (b + 1) * quarter])
            if b == 0:
                total = total + jnp.where(present[0], got_low[part].astype(F32), 0.0)
            if b == nb - 1:
                total = total + jnp.where(present[1], got_high[part].astype(F32), 0.0)
            out[b, part] = total.astype(BF16)
    me = member()
    for step, chunk in zip(STEPS, outs):
        chunk[:2] = out[me ^ step]
        chunk[2] = grad_q[me ^ step]


def unpack_kernel(*refs):
    here, across_0, across_1, *refs = refs
    chunks, (*outs, mixed) = refs[:GROUP], refs[GROUP:]
    half = across_0.shape[0]
    for part, across in enumerate((across_0, across_1)):
        at = pl.ds(part * half, half)
        mixed[at, :] = (here[at, :] + across[...].astype(F32)).astype(BF16)
    me = member()
    for step, chunk in zip(STEPS, chunks):
        at = columns(me ^ step)
        for part, out in enumerate(outs):
            out[:, at] = chunk[part]


def share():
    return lax.axis_index("mp")


def grad_kernel(*refs):
    pieces, (out_weight, tops), refs = refs[:N_MP], refs[N_MP : N_MP + 2], refs[N_MP + 2 :]
    *outs, whole, heads = refs
    me = member()
    for step, piece in enumerate(pieces):
        whole[span(share() ^ step, piece.shape[0]), :] = piece[...]
    heads[...] = dot_nt(whole[...], out_weight[...]).astype(BF16)
    quarter = tops.shape[2]
    for step, out in zip(STEPS, outs):
        out[:BLOCK] = heads[:, columns(me ^ step)]
        for part in range(2):
            out[BLOCK + part * quarter : BLOCK + (part + 1) * quarter] = tops[me ^ step, part]


def project_kernel(*refs):
    chunks, out_weight, (kept, *sent, attended, whole) = refs[:GROUP], refs[GROUP], refs[GROUP + 2 :]
    me = member()
    for step, chunk in zip(STEPS, chunks):
        attended[:, columns(me ^ step)] = chunk[...]
    whole[...] = dot(attended[...], out_weight[...]).astype(BF16)
    rows = kept.shape[1]
    for far in range(2):
        kept[far] = whole[span(share() ^ (2 * far), rows), :]
        for part in range(2):
            half = rows // 2
            at = 2 * (share() ^ (2 * far + 1)) + part
            sent[2 * far + part][...] = whole[span(at, half), :]


def swapped(x, axis, step):
    return lax.ppermute(x, axis, [(i, i ^ step) for i in range(lax.axis_size(axis))])


def exchanged(chunks):
    return [chunks[0]] + [swapped(chunk, "seq", step) for step, chunk in zip(STEPS[1:], chunks[1:])]


def beside(arrays):
    count = lax.axis_size("seq")
    if len(arrays) == 1:
        return [swapped(arrays[0], "seq", GROUP)]
    up = [(i, i + GROUP) for i in range(count - GROUP)]
    down = [(j, i) for i, j in up]
    return [lax.ppermute(arrays[0], "seq", up), lax.ppermute(arrays[1], "seq", down)]


def crossed(arrays):
    count = lax.axis_size("seq")
    across = swapped(arrays[0], "seq", GROUP)
    if len(arrays) == 1:
        return [across]
    up = [(i, i + GROUP) for i in range(count - GROUP)]
    down = [(j, i) for i, j in up]
    return [across, lax.ppermute(arrays[1], "seq", up), lax.ppermute(arrays[2], "seq", down)]


def per_device(queries, keys, values, out_weight, out_grad):
    rows, width = queries.shape
    assert width == GROUP * HEAD_DIM and rows == BLOCK and lax.axis_size("mp") == N_MP
    count = lax.axis_size("seq")
    assert count % (2 * GROUP) == 0
    groups = count // GROUP
    nb = GROUP
    tokens = nb * rows
    half, quarter = rows // 2, rows // 4
    model = out_weight.shape[1]
    block = shape(2, rows, HEAD_DIM)
    sent = [shape(4, rows, HEAD_DIM)] if groups == 2 else [block] * 3
    rims = [block] * (1 if groups == 2 else 2)
    quarter = rows // 4
    in_order = shape(nb, rows, HEAD_DIM)
    score_flops = 2 * tokens * 5 * BLOCK * HEAD_DIM
    weight_flops = 2 * rows * out_weight.size

    chunk = shape(rows, HEAD_DIM)
    triple = shape(3, rows, HEAD_DIM)
    chunks = call(
        pack_kernel,
        [triple] * GROUP,
        (queries, keys, values),
        scratch=[pltpu.SemaphoreType.DMA((3 * GROUP,))],
        copied=GROUP,
        limit=53,
    )
    far = swapped(out_grad, "mp", 2)
    (tops,) = call(pool_kernel, [shape(GROUP, 2, quarter, HEAD_DIM)], chunks)
    chunks = exchanged(chunks)
    tops = swapped(tops, "seq", GROUP)
    arrays = (out_grad, far, out_weight)
    own_grad, far, out_weight = call(copy_kernel, [shape(*x.shape) for x in arrays], arrays)
    near, queries, level_1, *refs = call(
        functools.partial(gather_kernel, nb, groups),
        [
            shape(nb, 2, rows, HEAD_DIM),
            shape(nb, rows, HEAD_DIM),
            shape(2, tokens // 2, HEAD_DIM),
        ]
        + rims,
        chunks,
        flops=20 * score_flops,
    )
    rim_blocks = beside(refs)
    grad_chunks = call(
        grad_kernel,
        [shape(rows + 2 * quarter, HEAD_DIM)] * GROUP,
        (own_grad, swapped(own_grad, "mp", 1), far, swapped(far, "mp", 1), out_weight, tops),
        scratch=[pltpu.VMEM((rows, model), BF16), pltpu.VMEM((rows, width), BF16)],
        flops=weight_flops,
    )
    query, k_t, v_t, k1_t, v1_t, weights, stats = call(
        functools.partial(local_kernel, nb),
        [
            shape(3, nb, rows, HEAD_DIM),
            shape(HEAD_DIM, tokens),
            shape(HEAD_DIM, tokens),
            shape(HEAD_DIM, tokens // 2),
            shape(HEAD_DIM, tokens // 2),
            shape(nb, 4, BLOCK, BLOCK, dtype=F32),
            shape(8, tokens, dtype=F32),
        ],
        (near, queries, level_1, grad_chunks[0]),
        flops=score_flops,
    )
    grad_chunks = exchanged(grad_chunks)
    rim_square = shape(len(rims), BLOCK, BLOCK)
    prob, grads, top_2, deltas, far_shift, rim_shift, *refs = call(
        functools.partial(forward_kernel, nb, groups),
        [
            shape(nb, 4, BLOCK, BLOCK),
            in_order,
            block,
            shape(8, tokens, dtype=F32),
            shape(BLOCK, tokens),
            rim_square,
        ]
        + [chunk] * GROUP
        + sent,
        (query, v_t, v1_t, weights, stats, *rim_blocks, *grad_chunks),
        scratch=[
            pltpu.VMEM((nb, rows, HEAD_DIM), BF16),
            pltpu.VMEM((BLOCK, tokens), BF16),
            pltpu.VMEM(rim_square.shape, BF16),
            pltpu.VMEM((8, tokens), F32),
            pltpu.VMEM((HEAD_DIM, tokens), F32),
        ],
        flops=score_flops,
    )
    attended = exchanged(refs[:GROUP])
    rim_grads = refs[GROUP:]
    other_grads = crossed(rim_grads)
    grad_q, grad_kv = call(
        functools.partial(backward_kernel, nb, groups),
        [in_order, shape(2, nb, rows, HEAD_DIM, dtype=F32)],
        (query, near, level_1, k_t, k1_t, prob, grads, top_2, deltas, far_shift, rim_shift, *rim_blocks),
        scratch=[
            pltpu.VMEM((nb, 4, BLOCK, BLOCK), BF16),
            pltpu.VMEM((2, tokens // 2, HEAD_DIM), F32),
            pltpu.VMEM((HEAD_DIM, tokens), F32),
        ],
        flops=1,
    )
    local = rows // N_MP
    kept, *given = call(
        project_kernel,
        [shape(2, local, model)] + [shape(local // 2, model)] * 4,
        (*attended, out_weight, grad_q),
        scratch=[pltpu.VMEM((rows, width), BF16), pltpu.VMEM((rows, model), BF16)],
        flops=weight_flops,
    )
    *across, here = call(
        share_kernel,
        [shape(local // 2, model)] * 2 + [shape(local, model, dtype=F32)],
        (kept, *(swapped(piece, "mp", 1) for piece in given)),
    )
    chunks = call(
        functools.partial(combine_kernel, nb, groups),
        [triple] * GROUP,
        (grad_q, grad_kv, here, *other_grads),
        scratch=[pltpu.VMEM((nb, 2, rows, HEAD_DIM), BF16)],
        flops=20 * score_flops,
    )
    chunks = exchanged(chunks)
    across = [swapped(piece, "mp", 2) for piece in across]
    grad_k, grad_v, grad_q, mixed = call(
        unpack_kernel,
        [shape(rows, width)] * 3 + [shape(local, model)],
        (here, *across, *chunks),
    )
    return mixed, grad_q, grad_k, grad_v


def solution(mesh):
    return jax.shard_map(
        per_device,
        mesh=mesh,
        in_specs=(
            P("seq", "mp"),
            P("seq", "mp"),
            P("seq", "mp"),
            P("mp", None),
            P(("seq", "mp"), None),
        ),
        out_specs=(P(("seq", "mp"), None), P("seq", "mp"), P("seq", "mp"), P("seq", "mp")),
        check_vma=False,
    )
```

```python
import functools

import jax
import jax.numpy as jnp
from jax import lax
from jax.experimental import pallas as pl
from jax.experimental.pallas import tpu as pltpu
from jax.sharding import PartitionSpec as P

HEAD_DIM = 128
BLOCK = 256
REST = 3 * BLOCK // 4
LEVELS = 2
GROUP = 4
STEPS = (0, 3, 2, 1)
N_MP = 4
SCALE = HEAD_DIM**-0.5
LOG2E = 1.4426950408889634
BF16 = jnp.bfloat16
F32 = jnp.float32


def dot(a, b):
    return lax.dot_general(a, b, (((1,), (0,)), ((), ())), preferred_element_type=F32)


def dot_nt(a, b):
    return lax.dot_general(a, b, (((1,), (1,)), ((), ())), preferred_element_type=F32)


def shape(*dims, dtype=BF16):
    return jax.ShapeDtypeStruct(dims, dtype)


def call(kernel, out_shape, args, scratch=(), flops=0, limit=32, copied=0):
    whole = pl.BlockSpec(memory_space=pltpu.VMEM)
    kept = pl.BlockSpec(memory_space=pltpu.HBM)
    moved = sum(x.size * x.dtype.itemsize for x in (*args, *out_shape))
    return pl.pallas_call(
        kernel,
        out_shape=out_shape,
        in_specs=[kept if copied else whole] * len(args),
        out_specs=[kept] * copied + [whole] * (len(out_shape) - copied),
        scratch_shapes=scratch,
        compiler_params=pltpu.CompilerParams(vmem_limit_bytes=limit << 20),
        cost_estimate=pl.CostEstimate(flops=flops, bytes_accessed=moved if flops else 0, transcendentals=0),
    )(*args)


def columns(index):
    return pl.ds(pl.multiple_of(index * HEAD_DIM, HEAD_DIM), HEAD_DIM)


def span(index, size):
    start = index * size
    return pl.ds(start if isinstance(start, int) else pl.multiple_of(start, size), size)


def iota(dims, axis):
    return lax.broadcasted_iota(jnp.int32, dims, axis)


def averaging(level):
    dims = (BLOCK, BLOCK)
    same = (iota(dims, 0) >> level) == (iota(dims, 1) >> level)
    return jnp.where(same, 2.0**-level, 0.0).astype(BF16)


def pooling():
    dims = (BLOCK // 2, BLOCK)
    return jnp.where(iota(dims, 0) == (iota(dims, 1) >> 1), 0.5, 0.0).astype(BF16)


def spreading(level):
    dims = (BLOCK, BLOCK >> level)
    return jnp.where((iota(dims, 0) >> level) == iota(dims, 1), 2.0**-level, 0.0).astype(BF16)


def halves(x):
    high = x.astype(BF16)
    return high, (x - high.astype(F32)).astype(BF16)


def at_block(b):
    return slice(b * BLOCK, (b + 1) * BLOCK)


def sibling(b):
    return (b >> 1) ^ 1


def rim_present(groups):
    group = lax.axis_index("seq") // GROUP
    return group > 0, group < groups - 1


def member():
    return lax.rem(lax.axis_index("seq"), GROUP)


def columns(index):
    return pl.ds(pl.multiple_of(index * HEAD_DIM, HEAD_DIM), HEAD_DIM)


def pack_kernel(q, k, v, *refs):
    *outs, sems = refs
    me = member()
    copies = []
    for step, out in zip(STEPS, outs):
        for part, source in enumerate((k, v, q)):
            piece = source.at[:, columns(me ^ step)]
            copies.append(pltpu.make_async_copy(piece, out.at[part], sems.at[len(copies)]))
    for copy in copies:
        copy.start()
    for copy in copies:
        copy.wait()


def pool_kernel(*refs):
    *chunks, out = refs
    me = member()
    pool = pooling()
    half = BLOCK // 2
    for step, chunk in zip(STEPS, chunks):
        for part in range(2):
            once = dot(pool, chunk[part]).astype(BF16)
            out[me ^ step, part] = dot(pool[: half // 2, :half], once).astype(BF16)


def copy_kernel(*refs):
    count = len(refs) // 2
    for x, out in zip(refs[:count], refs[count:]):
        out[...] = x[...]


def gather_kernel(nb, groups, *refs):
    chunks, (near, queries, level_1, *rims) = refs[:GROUP], refs[GROUP:]
    me = member()
    for step, chunk in zip(STEPS, chunks):
        near[me ^ step] = chunk[:2]
        queries[me ^ step] = chunk[2]
    pool = pooling()
    half = BLOCK // 2
    for part in range(2):
        for b in range(nb):
            level_1[part, b * half : (b + 1) * half] = dot(pool, near[b, part]).astype(BF16)
    if groups == 2:
        upper = lax.axis_index("seq") >= GROUP
        rims[0][...] = jnp.where(upper, near[0], near[nb - 1])
    else:
        rims[0][...] = near[nb - 1]
        rims[1][...] = near[0]


def from_beside(groups, refs):
    if groups == 2:
        return (refs[0], refs[0]), refs[1:]
    return refs[:2], refs[2:]


def from_others(groups, refs):
    if groups == 2:
        return (refs[0].at[: 2 * REST], refs[0].at[2 * REST :], refs[0].at[2 * REST :]), refs[1:]
    return refs[:3], refs[3:]


def odd_group():
    return lax.rem(lax.axis_index("seq") // GROUP, 2)


def near_sides(b, nb):
    return [side for side in range(3) if 0 <= b + side - 1 < nb]


def local_kernel(nb, near, queries, level_1, _, query, k_t, v_t, k1_t, v1_t, weights, stats):
    even_1, even_2 = averaging(1), averaging(2)
    for b in range(nb):
        query[0, b] = queries[b]
        once = dot(even_1, queries[b]).astype(BF16)
        query[1, b] = once
        query[2, b] = dot(even_2, once).astype(BF16)
        for part, transposed in enumerate((k_t, v_t)):
            transposed[:, at_block(b)] = near[b, part].T
    for c in range(nb // 2):
        for part, transposed in enumerate((k1_t, v1_t)):
            transposed[:, at_block(c)] = level_1[part, at_block(c)].T
    for b in range(nb):
        sides = near_sides(b, nb)
        scores = [dot_nt(near[b + side - 1, 0], query[0, b]) * (SCALE * LOG2E) for side in sides]
        coarse = dot_nt(level_1[0, at_block(sibling(b))], query[1, b]) * (SCALE * LOG2E)
        top = coarse.max(0, keepdims=True)
        for score in scores:
            top = jnp.maximum(top, score.max(0, keepdims=True))
        weight = 2.0 * jnp.exp2(coarse - top)
        weights[b, 3] = weight
        total = weight.sum(0, keepdims=True)
        for side, score in zip(sides, scores):
            weight = jnp.exp2(score - top)
            weights[b, side] = weight
            total = total + weight.sum(0, keepdims=True)
        stats[:1, at_block(b)] = top
        stats[1:2, at_block(b)] = total


def rims_of(nb, groups, low, high):
    group = lax.axis_index("seq") // GROUP
    if groups == 2:
        return [(jnp.where(group > 0, 0, nb - 1), low, None)]
    return [(0, low, group > 0), (nb - 1, high, group < groups - 1)]


def forward_kernel(nb, groups, *refs):
    (query, v_t, v1_t, weights, stats), refs = refs[:5], refs[5:]
    (rim_low, rim_high), refs = from_beside(groups, refs)
    chunks, refs = refs[:GROUP], refs[GROUP:]
    (prob, grads, top_2, deltas, far_shift, rim_shift), refs = refs[:6], refs[6:]
    outs, (*rim_outs, attended, far_prob, rim_prob, row, context_t, far_sums) = refs[:GROUP], refs[GROUP:]
    rims = rims_of(nb, groups, rim_low, rim_high)
    me = member()
    quarter = BLOCK // 4
    tokens = nb * BLOCK
    for step, chunk in zip(STEPS, chunks):
        grads[me ^ step] = chunk[:BLOCK]
        for part in range(2):
            level = chunk[BLOCK + part * quarter : BLOCK + (part + 1) * quarter]
            top_2[part, span(me ^ step, quarter), :] = level
    coarse_query = query[2].reshape(tokens, HEAD_DIM)
    coarse = dot_nt(top_2[0], coarse_query) * (SCALE * LOG2E)
    row[:1] = jnp.maximum(stats[:1], coarse.max(0, keepdims=True))
    scores = []
    for b, block, present in rims:
        score = dot_nt(block[0], query[0, b]) * (SCALE * LOG2E)
        if present is not None:
            score = jnp.where(present, score, -jnp.inf)
        at = span(b, BLOCK)
        row[:1, at] = jnp.maximum(row[:1, at], score.max(0, keepdims=True))
        scores.append(score)
    top = row[:1]
    shrink = jnp.exp2(stats[:1] - top)
    far = 4.0 * jnp.exp2(coarse - top)
    row[1:2] = shrink * stats[1:2] + far.sum(0, keepdims=True)
    fresh = []
    for (b, _, _), score in zip(rims, scores):
        at = span(b, BLOCK)
        fresh.append(jnp.exp2(score - row[:1, at]))
        row[1:2, at] += fresh[-1].sum(0, keepdims=True)
    inverse = 1.0 / row[1:2]
    row[2:3] = inverse
    row[3:4] = shrink * inverse
    far_prob[...] = (far * inverse).astype(BF16)
    context_t[...] = dot(top_2[1].T, far_prob[...])
    for i, (b, block, _) in enumerate(rims):
        at = span(b, BLOCK)
        rim_prob[i] = (fresh[i] * row[2:3, at]).astype(BF16)
        context_t[:, at] += dot(block[1].T, rim_prob[i])
    for b in range(nb):
        shrink = row[3:4, at_block(b)]
        prob[b, 3] = (weights[b, 3] * shrink).astype(BF16)
        context = context_t[:, at_block(b)] + dot(v1_t[:, at_block(sibling(b))], prob[b, 3])
        for side in near_sides(b, nb):
            prob[b, side] = (weights[b, side] * shrink).astype(BF16)
            context = context + dot(v_t[:, at_block(b + side - 1)], prob[b, side])
        attended[b] = context.T.astype(BF16)
        deltas[:1, at_block(b)] = (grads[b].T.astype(F32) * context).sum(0, keepdims=True)
    grad = grads[...].reshape(tokens, HEAD_DIM)
    slope = dot_nt(top_2[1], grad)
    far_shift[...] = (far_prob[...].astype(F32) * (slope - deltas[:1])).astype(BF16)
    far_sums[0] = SCALE * dot(far_shift[...], coarse_query)
    far_sums[1] = dot(far_prob[...], grad)
    odd = odd_group()
    spread = spreading(2)
    folded = []
    for part in range(2):
        rest = far_sums[part, pl.ds(pl.multiple_of((1 - odd) * quarter, quarter), REST), :]
        rim_outs[0][part * REST : (part + 1) * REST] = rest.astype(BF16)
        high, low = halves(far_sums[part, pl.ds(pl.multiple_of(odd * REST, quarter), quarter), :])
        folded.append(dot(spread, high) + dot(spread, low))
    pairs = []
    for i, (b, block, _) in enumerate(rims):
        slope = dot_nt(block[1], grads[b])
        rim_shift[i] = (rim_prob[i].astype(F32) * (slope - deltas[:1, span(b, BLOCK)])).astype(BF16)
        pairs.append((SCALE * dot(rim_shift[i], query[0, b]), dot(rim_prob[i], grads[b])))
    for part in range(2):
        at = slice(part * BLOCK, (part + 1) * BLOCK)
        if groups == 2:
            rim_outs[0][2 * REST + part * BLOCK : 2 * REST + (part + 1) * BLOCK] = (
                pairs[0][part] + folded[part]
            ).astype(BF16)
        else:
            rim_outs[1][at] = (pairs[1][part] + jnp.where(odd == 0, folded[part], 0.0)).astype(BF16)
            rim_outs[2][at] = (pairs[0][part] + jnp.where(odd == 1, folded[part], 0.0)).astype(BF16)
    for step, out in zip(STEPS, outs):
        out[...] = attended[me ^ step]


def backward_kernel(nb, groups, *refs):
    (query, near, level_1, k_t, k1_t, prob, grads, top_2, deltas, far_shift, rim_shift), refs = refs[:11], refs[11:]
    (rim_low, rim_high), refs = from_beside(groups, refs)
    grad_q, grad_kv, shift, sums_1, query_t = refs
    even_1, even_2 = averaging(1), averaging(2)
    coarse = dot(top_2[0].T, far_shift[...])
    for b in range(nb):
        high, low = halves(coarse[:, at_block(b)])
        query_t[:, at_block(b)] = dot(high, even_2) + dot(low, even_2)
    for i, (b, block, _) in enumerate(rims_of(nb, groups, rim_low, rim_high)):
        query_t[:, span(b, BLOCK)] += dot(block[0].T, rim_shift[i])
    for b in range(nb):
        grad, delta = grads[b], deltas[:1, at_block(b)]
        grad_t = query_t[:, at_block(b)]
        for side in near_sides(b, nb):
            slope = dot_nt(near[b + side - 1, 1], grad)
            part = (prob[b, side].astype(F32) * (slope - delta)).astype(BF16)
            shift[b, side] = part
            grad_t = grad_t + dot(k_t[:, at_block(b + side - 1)], part)
        slope = dot_nt(level_1[1, at_block(sibling(b))], grad)
        part = (prob[b, 3].astype(F32) * (slope - delta)).astype(BF16)
        shift[b, 3] = part
        high, low = halves(dot(k1_t[:, at_block(sibling(b))], part))
        grad_t = grad_t + (dot(high, even_1) + dot(low, even_1))
        grad_q[b] = (SCALE * grad_t).T.astype(BF16)
    for c in range(nb // 2):
        users = [b for b in range(nb) if sibling(b) == c]
        sums_1[0, at_block(c)] = SCALE * sum(dot(shift[b, 3], query[1, b]) for b in users)
        sums_1[1, at_block(c)] = sum(dot(prob[b, 3], grads[b]) for b in users)
    spread = spreading(1)
    half = BLOCK // 2
    for s in range(nb):
        users = [(s + 1 - side, side) for side in range(3) if 0 <= s + 1 - side < nb]
        key = SCALE * sum(dot(shift[b, side], query[0, b]) for b, side in users)
        value = sum(dot(prob[b, side], grads[b]) for b, side in users)
        for part, total in enumerate((key, value)):
            high, low = halves(sums_1[part, s * half : (s + 1) * half])
            grad_kv[part, s] = total + (dot(spread, high) + dot(spread, low))


def share_kernel(kept, *refs):
    *got, across_0, across_1, here = refs
    half = across_0.shape[0]
    for i, piece in enumerate(got):
        far, at = i // 2, pl.ds(i % 2 * half, half)
        total = kept[far, at, :].astype(F32) + piece[...].astype(F32)
        if far:
            (across_0, across_1)[i % 2][...] = total.astype(BF16)
        else:
            here[at, :] = total


def combine_kernel(nb, groups, grad_q, grad_kv, _, *refs):
    (got_top, got_low, got_high), (*outs, out) = from_others(groups, refs)
    present = rim_present(groups)
    spread = spreading(2)
    quarter = BLOCK // 4
    odd = odd_group()
    for b in range(nb):
        for part in range(2):
            total = grad_kv[part, b]
            place = 0 if b == 0 else 2 if b == nb - 1 else b - odd
            level = dot(spread, got_top[span(part * (REST // quarter) + place, quarter), :])
            rim = slice(part * BLOCK, (part + 1) * BLOCK)
            if b == 0:
                level = jnp.where(odd == 0, level, 0.0)
                total = total + jnp.where(present[0], got_low[rim].astype(F32), 0.0)
            if b == nb - 1:
                level = jnp.where(odd == 1, level, 0.0)
                total = total + jnp.where(present[1], got_high[rim].astype(F32), 0.0)
            total = total + level
            out[b, part] = total.astype(BF16)
    me = member()
    for step, chunk in zip(STEPS, outs):
        chunk[:2] = out[me ^ step]
        chunk[2] = grad_q[me ^ step]


def unpack_kernel(*refs):
    here, across_0, across_1, *refs = refs
    chunks, (*outs, mixed) = refs[:GROUP], refs[GROUP:]
    half = across_0.shape[0]
    for part, across in enumerate((across_0, across_1)):
        at = pl.ds(part * half, half)
        mixed[at, :] = (here[at, :] + across[...].astype(F32)).astype(BF16)
    me = member()
    for step, chunk in zip(STEPS, chunks):
        at = columns(me ^ step)
        for part, out in enumerate(outs):
            out[:, at] = chunk[part]


def share():
    return lax.axis_index("mp")


def grad_kernel(*refs):
    pieces, (out_weight, tops), refs = refs[:N_MP], refs[N_MP : N_MP + 2], refs[N_MP + 2 :]
    *outs, whole, heads = refs
    me = member()
    for step, piece in enumerate(pieces):
        whole[span(share() ^ step, piece.shape[0]), :] = piece[...]
    heads[...] = dot_nt(whole[...], out_weight[...]).astype(BF16)
    quarter = tops.shape[2]
    for step, out in zip(STEPS, outs):
        out[:BLOCK] = heads[:, columns(me ^ step)]
        for part in range(2):
            out[BLOCK + part * quarter : BLOCK + (part + 1) * quarter] = tops[me ^ step, part]


def project_kernel(*refs):
    chunks, out_weight, (kept, *sent, attended, whole) = refs[:GROUP], refs[GROUP], refs[GROUP + 2 :]
    me = member()
    for step, chunk in zip(STEPS, chunks):
        attended[:, columns(me ^ step)] = chunk[...]
    whole[...] = dot(attended[...], out_weight[...]).astype(BF16)
    rows = kept.shape[1]
    for far in range(2):
        kept[far] = whole[span(share() ^ (2 * far), rows), :]
        for part in range(2):
            half = rows // 2
            at = 2 * (share() ^ (2 * far + 1)) + part
            sent[2 * far + part][...] = whole[span(at, half), :]


def swapped(x, axis, step):
    return lax.ppermute(x, axis, [(i, i ^ step) for i in range(lax.axis_size(axis))])


def exchanged(chunks):
    return [chunks[0]] + [swapped(chunk, "seq", step) for step, chunk in zip(STEPS[1:], chunks[1:])]


def beside(arrays):
    count = lax.axis_size("seq")
    if len(arrays) == 1:
        return [swapped(arrays[0], "seq", GROUP)]
    up = [(i, i + GROUP) for i in range(count - GROUP)]
    down = [(j, i) for i, j in up]
    return [lax.ppermute(arrays[0], "seq", up), lax.ppermute(arrays[1], "seq", down)]


def crossed(arrays):
    count = lax.axis_size("seq")
    across = swapped(arrays[0], "seq", GROUP)
    if len(arrays) == 1:
        return [across]
    up = [(i, i + GROUP) for i in range(count - GROUP)]
    down = [(j, i) for i, j in up]
    return [across, lax.ppermute(arrays[1], "seq", up), lax.ppermute(arrays[2], "seq", down)]


def per_device(queries, keys, values, out_weight, out_grad):
    rows, width = queries.shape
    assert width == GROUP * HEAD_DIM and rows == BLOCK and lax.axis_size("mp") == N_MP
    count = lax.axis_size("seq")
    assert count % (2 * GROUP) == 0
    groups = count // GROUP
    nb = GROUP
    tokens = nb * rows
    half, quarter = rows // 2, rows // 4
    model = out_weight.shape[1]
    block = shape(2, rows, HEAD_DIM)
    sent = [shape(2 * REST + 2 * rows, HEAD_DIM)]
    if groups > 2:
        sent = [shape(2 * REST, HEAD_DIM)] + [shape(2 * rows, HEAD_DIM)] * 2
    rims = [block] * (1 if groups == 2 else 2)
    quarter = rows // 4
    in_order = shape(nb, rows, HEAD_DIM)
    score_flops = 2 * tokens * 5 * BLOCK * HEAD_DIM
    weight_flops = 2 * rows * out_weight.size

    chunk = shape(rows, HEAD_DIM)
    triple = shape(3, rows, HEAD_DIM)
    chunks = call(
        pack_kernel,
        [triple] * GROUP,
        (queries, keys, values),
        scratch=[pltpu.SemaphoreType.DMA((3 * GROUP,))],
        copied=GROUP,
        limit=53,
    )
    far = swapped(out_grad, "mp", 2)
    (tops,) = call(pool_kernel, [shape(GROUP, 2, quarter, HEAD_DIM)], chunks)
    chunks = exchanged(chunks)
    tops = swapped(tops, "seq", GROUP)
    arrays = (out_grad, far, out_weight)
    own_grad, far, out_weight = call(copy_kernel, [shape(*x.shape) for x in arrays], arrays)
    near, queries, level_1, *refs = call(
        functools.partial(gather_kernel, nb, groups),
        [
            shape(nb, 2, rows, HEAD_DIM),
            shape(nb, rows, HEAD_DIM),
            shape(2, tokens // 2, HEAD_DIM),
        ]
        + rims,
        chunks,
        flops=20 * score_flops,
    )
    rim_blocks = beside(refs)
    grad_chunks = call(
        grad_kernel,
        [shape(rows + 2 * quarter, HEAD_DIM)] * GROUP,
        (own_grad, swapped(own_grad, "mp", 1), far, swapped(far, "mp", 1), out_weight, tops),
        scratch=[pltpu.VMEM((rows, model), BF16), pltpu.VMEM((rows, width), BF16)],
        flops=weight_flops,
    )
    query, k_t, v_t, k1_t, v1_t, weights, stats = call(
        functools.partial(local_kernel, nb),
        [
            shape(3, nb, rows, HEAD_DIM),
            shape(HEAD_DIM, tokens),
            shape(HEAD_DIM, tokens),
            shape(HEAD_DIM, tokens // 2),
            shape(HEAD_DIM, tokens // 2),
            shape(nb, 4, BLOCK, BLOCK, dtype=F32),
            shape(8, tokens, dtype=F32),
        ],
        (near, queries, level_1, grad_chunks[0]),
        flops=score_flops,
    )
    grad_chunks = exchanged(grad_chunks)
    rim_square = shape(len(rims), BLOCK, BLOCK)
    prob, grads, top_2, deltas, far_shift, rim_shift, *refs = call(
        functools.partial(forward_kernel, nb, groups),
        [
            shape(nb, 4, BLOCK, BLOCK),
            in_order,
            block,
            shape(8, tokens, dtype=F32),
            shape(BLOCK, tokens),
            rim_square,
        ]
        + [chunk] * GROUP
        + sent,
        (query, v_t, v1_t, weights, stats, *rim_blocks, *grad_chunks),
        scratch=[
            pltpu.VMEM((nb, rows, HEAD_DIM), BF16),
            pltpu.VMEM((BLOCK, tokens), BF16),
            pltpu.VMEM(rim_square.shape, BF16),
            pltpu.VMEM((8, tokens), F32),
            pltpu.VMEM((HEAD_DIM, tokens), F32),
            pltpu.VMEM((2, BLOCK, HEAD_DIM), F32),
        ],
        flops=score_flops,
    )
    attended = exchanged(refs[:GROUP])
    rim_grads = refs[GROUP:]
    other_grads = crossed(rim_grads)
    grad_q, grad_kv = call(
        functools.partial(backward_kernel, nb, groups),
        [in_order, shape(2, nb, rows, HEAD_DIM, dtype=F32)],
        (query, near, level_1, k_t, k1_t, prob, grads, top_2, deltas, far_shift, rim_shift, *rim_blocks),
        scratch=[
            pltpu.VMEM((nb, 4, BLOCK, BLOCK), BF16),
            pltpu.VMEM((2, tokens // 2, HEAD_DIM), F32),
            pltpu.VMEM((HEAD_DIM, tokens), F32),
        ],
    )
    local = rows // N_MP
    kept, *given = call(
        project_kernel,
        [shape(2, local, model)] + [shape(local // 2, model)] * 4,
        (*attended, out_weight, grad_q),
        scratch=[pltpu.VMEM((rows, width), BF16), pltpu.VMEM((rows, model), BF16)],
    )
    *across, here = call(
        share_kernel,
        [shape(local // 2, model)] * 2 + [shape(local, model, dtype=F32)],
        (kept, *(swapped(piece, "mp", 1) for piece in given)),
    )
    chunks = call(
        functools.partial(combine_kernel, nb, groups),
        [triple] * GROUP,
        (grad_q, grad_kv, here, *other_grads),
        scratch=[pltpu.VMEM((nb, 2, rows, HEAD_DIM), BF16)],
        flops=20 * score_flops,
    )
    chunks = exchanged(chunks)
    across = [swapped(piece, "mp", 2) for piece in across]
    grad_k, grad_v, grad_q, mixed = call(
        unpack_kernel,
        [shape(rows, width)] * 3 + [shape(local, model)],
        (here, *across, *chunks),
    )
    return mixed, grad_q, grad_k, grad_v


def solution(mesh):
    return jax.shard_map(
        per_device,
        mesh=mesh,
        in_specs=(
            P("seq", "mp"),
            P("seq", "mp"),
            P("seq", "mp"),
            P("mp", None),
            P(("seq", "mp"), None),
        ),
        out_specs=(P(("seq", "mp"), None), P("seq", "mp"), P("seq", "mp"), P("seq", "mp")),
        check_vma=False,
    )
```

```python
import functools

import jax
import jax.numpy as jnp
from jax import lax
from jax.experimental import pallas as pl
from jax.experimental.pallas import tpu as pltpu
from jax.sharding import PartitionSpec as P

HEAD_DIM = 128
BLOCK = 256
REST = 3 * BLOCK // 4
LEVELS = 2
GROUP = 4
STEPS = (0, 3, 2, 1)
N_MP = 4
SCALE = HEAD_DIM**-0.5
LOG2E = 1.4426950408889634
BF16 = jnp.bfloat16
F32 = jnp.float32


def dot(a, b):
    return lax.dot_general(a, b, (((1,), (0,)), ((), ())), preferred_element_type=F32)


def dot_nt(a, b):
    return lax.dot_general(a, b, (((1,), (1,)), ((), ())), preferred_element_type=F32)


def shape(*dims, dtype=BF16):
    return jax.ShapeDtypeStruct(dims, dtype)


def call(kernel, out_shape, args, scratch=(), flops=0, limit=32, copied=0):
    whole = pl.BlockSpec(memory_space=pltpu.VMEM)
    kept = pl.BlockSpec(memory_space=pltpu.HBM)
    moved = sum(x.size * x.dtype.itemsize for x in (*args, *out_shape))
    return pl.pallas_call(
        kernel,
        out_shape=out_shape,
        in_specs=[kept if copied else whole] * len(args),
        out_specs=[kept] * copied + [whole] * (len(out_shape) - copied),
        scratch_shapes=scratch,
        compiler_params=pltpu.CompilerParams(vmem_limit_bytes=limit << 20),
        cost_estimate=pl.CostEstimate(flops=flops, bytes_accessed=moved if flops else 0, transcendentals=0),
    )(*args)


def columns(index):
    return pl.ds(pl.multiple_of(index * HEAD_DIM, HEAD_DIM), HEAD_DIM)


def span(index, size):
    start = index * size
    return pl.ds(start if isinstance(start, int) else pl.multiple_of(start, size), size)


def iota(dims, axis):
    return lax.broadcasted_iota(jnp.int32, dims, axis)


def averaging(level):
    dims = (BLOCK, BLOCK)
    same = (iota(dims, 0) >> level) == (iota(dims, 1) >> level)
    return jnp.where(same, 2.0**-level, 0.0).astype(BF16)


def pooling():
    dims = (BLOCK // 2, BLOCK)
    return jnp.where(iota(dims, 0) == (iota(dims, 1) >> 1), 0.5, 0.0).astype(BF16)


def spreading(level):
    dims = (BLOCK, BLOCK >> level)
    return jnp.where((iota(dims, 0) >> level) == iota(dims, 1), 2.0**-level, 0.0).astype(BF16)


def halves(x):
    high = x.astype(BF16)
    return high, (x - high.astype(F32)).astype(BF16)


def at_block(b):
    return slice(b * BLOCK, (b + 1) * BLOCK)


def sibling(b):
    return (b >> 1) ^ 1


def rim_present(groups):
    group = lax.axis_index("seq") // GROUP
    return group > 0, group < groups - 1


def member():
    return lax.rem(lax.axis_index("seq"), GROUP)


def columns(index):
    return pl.ds(pl.multiple_of(index * HEAD_DIM, HEAD_DIM), HEAD_DIM)


def pack_kernel(q, k, v, *refs):
    *outs, sems = refs
    me = member()
    copies = []
    for step, out in zip(STEPS, outs):
        for part, source in enumerate((k, v, q)):
            piece = source.at[:, columns(me ^ step)]
            copies.append(pltpu.make_async_copy(piece, out.at[part], sems.at[len(copies)]))
    for copy in copies:
        copy.start()
    for copy in copies:
        copy.wait()


def pool_kernel(*refs):
    *chunks, out = refs
    me = member()
    pool = pooling()
    half = BLOCK // 2
    for step, chunk in zip(STEPS, chunks):
        for part in range(2):
            once = dot(pool, chunk[part]).astype(BF16)
            out[me ^ step, part] = dot(pool[: half // 2, :half], once).astype(BF16)


def copy_kernel(*refs):
    count = len(refs) // 2
    for x, out in zip(refs[:count], refs[count:]):
        out[...] = x[...]


def gather_kernel(nb, groups, *refs):
    chunks, (near, queries, level_1, *rims) = refs[:GROUP], refs[GROUP:]
    me = member()
    for step, chunk in zip(STEPS, chunks):
        near[me ^ step] = chunk[:2]
        queries[me ^ step] = chunk[2]
    pool = pooling()
    half = BLOCK // 2
    for part in range(2):
        for b in range(nb):
            level_1[part, b * half : (b + 1) * half] = dot(pool, near[b, part]).astype(BF16)
    if groups == 2:
        upper = lax.axis_index("seq") >= GROUP
        rims[0][...] = jnp.where(upper, near[0], near[nb - 1])
    else:
        rims[0][...] = near[nb - 1]
        rims[1][...] = near[0]


def from_beside(groups, refs):
    if groups == 2:
        return (refs[0], refs[0]), refs[1:]
    return refs[:2], refs[2:]


def from_others(groups, refs):
    if groups == 2:
        return (refs[0].at[: 2 * REST], refs[0].at[2 * REST :], refs[0].at[2 * REST :]), refs[1:]
    return refs[:3], refs[3:]


def odd_group():
    return lax.rem(lax.axis_index("seq") // GROUP, 2)


def near_sides(b, nb):
    return [side for side in range(3) if 0 <= b + side - 1 < nb]


def local_kernel(nb, near, queries, level_1, _, query, k_t, v_t, k1_t, v1_t, weights, stats):
    even_1, even_2 = averaging(1), averaging(2)
    for b in range(nb):
        query[0, b] = queries[b]
        once = dot(even_1, queries[b]).astype(BF16)
        query[1, b] = once
        query[2, b] = dot(even_2, once).astype(BF16)
        for part, transposed in enumerate((k_t, v_t)):
            transposed[:, at_block(b)] = near[b, part].T
    for c in range(nb // 2):
        for part, transposed in enumerate((k1_t, v1_t)):
            transposed[:, at_block(c)] = level_1[part, at_block(c)].T
    for b in range(nb):
        sides = near_sides(b, nb)
        scores = [dot_nt(near[b + side - 1, 0], query[0, b]) * (SCALE * LOG2E) for side in sides]
        coarse = dot_nt(level_1[0, at_block(sibling(b))], query[1, b]) * (SCALE * LOG2E)
        top = coarse.max(0, keepdims=True)
        for score in scores:
            top = jnp.maximum(top, score.max(0, keepdims=True))
        weight = 2.0 * jnp.exp2(coarse - top)
        weights[b, 3] = weight
        total = weight.sum(0, keepdims=True)
        for side, score in zip(sides, scores):
            weight = jnp.exp2(score - top)
            weights[b, side] = weight
            total = total + weight.sum(0, keepdims=True)
        stats[:1, at_block(b)] = top
        stats[1:2, at_block(b)] = total


def rims_of(nb, groups, low, high):
    group = lax.axis_index("seq") // GROUP
    if groups == 2:
        return [(jnp.where(group > 0, 0, nb - 1), low, None)]
    return [(0, low, group > 0), (nb - 1, high, group < groups - 1)]


def forward_kernel(nb, groups, *refs):
    (query, v_t, v1_t, weights, stats), refs = refs[:5], refs[5:]
    (rim_low, rim_high), refs = from_beside(groups, refs)
    chunks, refs = refs[:GROUP], refs[GROUP:]
    (prob, grads, top_2, deltas, far_shift, rim_shift), refs = refs[:6], refs[6:]
    outs, (*rim_outs, attended, far_prob, rim_prob, row, context_t, far_sums) = refs[:GROUP], refs[GROUP:]
    rims = rims_of(nb, groups, rim_low, rim_high)
    me = member()
    quarter = BLOCK // 4
    tokens = nb * BLOCK
    for step, chunk in zip(STEPS, chunks):
        grads[me ^ step] = chunk[:BLOCK]
        for part in range(2):
            level = chunk[BLOCK + part * quarter : BLOCK + (part + 1) * quarter]
            top_2[part, span(me ^ step, quarter), :] = level
    coarse_query = query[2].reshape(tokens, HEAD_DIM)
    coarse = dot_nt(top_2[0], coarse_query) * (SCALE * LOG2E)
    row[:1] = jnp.maximum(stats[:1], coarse.max(0, keepdims=True))
    scores = []
    for b, block, present in rims:
        score = dot_nt(block[0], query[0, b]) * (SCALE * LOG2E)
        if present is not None:
            score = jnp.where(present, score, -jnp.inf)
        at = span(b, BLOCK)
        row[:1, at] = jnp.maximum(row[:1, at], score.max(0, keepdims=True))
        scores.append(score)
    top = row[:1]
    shrink = jnp.exp2(stats[:1] - top)
    far = 4.0 * jnp.exp2(coarse - top)
    row[1:2] = shrink * stats[1:2] + far.sum(0, keepdims=True)
    fresh = []
    for (b, _, _), score in zip(rims, scores):
        at = span(b, BLOCK)
        fresh.append(jnp.exp2(score - row[:1, at]))
        row[1:2, at] += fresh[-1].sum(0, keepdims=True)
    inverse = 1.0 / row[1:2]
    row[2:3] = inverse
    row[3:4] = shrink * inverse
    far_prob[...] = (far * inverse).astype(BF16)
    context_t[...] = dot(top_2[1].T, far_prob[...])
    for i, (b, block, _) in enumerate(rims):
        at = span(b, BLOCK)
        rim_prob[i] = (fresh[i] * row[2:3, at]).astype(BF16)
        context_t[:, at] += dot(block[1].T, rim_prob[i])
    for b in range(nb):
        shrink = row[3:4, at_block(b)]
        prob[b, 3] = (weights[b, 3] * shrink).astype(BF16)
        context = context_t[:, at_block(b)] + dot(v1_t[:, at_block(sibling(b))], prob[b, 3])
        for side in near_sides(b, nb):
            prob[b, side] = (weights[b, side] * shrink).astype(BF16)
            context = context + dot(v_t[:, at_block(b + side - 1)], prob[b, side])
        attended[b] = context.T.astype(BF16)
        deltas[:1, at_block(b)] = (grads[b].T.astype(F32) * context).sum(0, keepdims=True)
    grad = grads[...].reshape(tokens, HEAD_DIM)
    slope = dot_nt(top_2[1], grad)
    far_shift[...] = (far_prob[...].astype(F32) * (slope - deltas[:1])).astype(BF16)
    far_sums[0] = SCALE * dot(far_shift[...], coarse_query)
    far_sums[1] = dot(far_prob[...], grad)
    odd = odd_group()
    spread = spreading(2)
    folded = []
    for part in range(2):
        rest = far_sums[part, pl.ds(pl.multiple_of((1 - odd) * quarter, quarter), REST), :]
        rim_outs[0][part * REST : (part + 1) * REST] = rest.astype(BF16)
        high, low = halves(far_sums[part, pl.ds(pl.multiple_of(odd * REST, quarter), quarter), :])
        folded.append(dot(spread, high) + dot(spread, low))
    pairs = []
    for i, (b, block, _) in enumerate(rims):
        slope = dot_nt(block[1], grads[b])
        rim_shift[i] = (rim_prob[i].astype(F32) * (slope - deltas[:1, span(b, BLOCK)])).astype(BF16)
        pairs.append((SCALE * dot(rim_shift[i], query[0, b]), dot(rim_prob[i], grads[b])))
    for part in range(2):
        at = slice(part * BLOCK, (part + 1) * BLOCK)
        if groups == 2:
            rim_outs[0][2 * REST + part * BLOCK : 2 * REST + (part + 1) * BLOCK] = (
                pairs[0][part] + folded[part]
            ).astype(BF16)
        else:
            rim_outs[1][at] = (pairs[1][part] + jnp.where(odd == 0, folded[part], 0.0)).astype(BF16)
            rim_outs[2][at] = (pairs[0][part] + jnp.where(odd == 1, folded[part], 0.0)).astype(BF16)
    for step, out in zip(STEPS, outs):
        out[...] = attended[me ^ step]


def backward_kernel(nb, groups, *refs):
    (query, near, level_1, k_t, k1_t, prob, grads, top_2, deltas, far_shift, rim_shift), refs = refs[:11], refs[11:]
    (rim_low, rim_high), refs = from_beside(groups, refs)
    grad_q, grad_kv, shift, sums_1, query_t = refs
    even_1, even_2 = averaging(1), averaging(2)
    coarse = dot(top_2[0].T, far_shift[...])
    for b in range(nb):
        high, low = halves(coarse[:, at_block(b)])
        query_t[:, at_block(b)] = dot(high, even_2) + dot(low, even_2)
    for i, (b, block, _) in enumerate(rims_of(nb, groups, rim_low, rim_high)):
        query_t[:, span(b, BLOCK)] += dot(block[0].T, rim_shift[i])
    for b in range(nb):
        grad, delta = grads[b], deltas[:1, at_block(b)]
        grad_t = query_t[:, at_block(b)]
        for side in near_sides(b, nb):
            slope = dot_nt(near[b + side - 1, 1], grad)
            part = (prob[b, side].astype(F32) * (slope - delta)).astype(BF16)
            shift[b, side] = part
            grad_t = grad_t + dot(k_t[:, at_block(b + side - 1)], part)
        slope = dot_nt(level_1[1, at_block(sibling(b))], grad)
        part = (prob[b, 3].astype(F32) * (slope - delta)).astype(BF16)
        shift[b, 3] = part
        high, low = halves(dot(k1_t[:, at_block(sibling(b))], part))
        grad_t = grad_t + (dot(high, even_1) + dot(low, even_1))
        grad_q[b] = (SCALE * grad_t).T.astype(BF16)
    for c in range(nb // 2):
        users = [b for b in range(nb) if sibling(b) == c]
        sums_1[0, at_block(c)] = SCALE * sum(dot(shift[b, 3], query[1, b]) for b in users)
        sums_1[1, at_block(c)] = sum(dot(prob[b, 3], grads[b]) for b in users)
    spread = spreading(1)
    half = BLOCK // 2
    for s in range(nb):
        users = [(s + 1 - side, side) for side in range(3) if 0 <= s + 1 - side < nb]
        key = SCALE * sum(dot(shift[b, side], query[0, b]) for b, side in users)
        value = sum(dot(prob[b, side], grads[b]) for b, side in users)
        for part, total in enumerate((key, value)):
            high, low = halves(sums_1[part, s * half : (s + 1) * half])
            grad_kv[part, s] = total + (dot(spread, high) + dot(spread, low))


def share_kernel(kept, *refs):
    *got, across_0, across_1, here = refs
    half = across_0.shape[0]
    for i, piece in enumerate(got):
        far, at = i // 2, pl.ds(i % 2 * half, half)
        total = kept[far, at, :].astype(F32) + piece[...].astype(F32)
        if far:
            (across_0, across_1)[i % 2][...] = total.astype(BF16)
        else:
            here[at, :] = total


def combine_kernel(nb, groups, grad_q, grad_kv, *refs):
    (got_top, got_low, got_high), (*outs, out) = from_others(groups, refs)
    present = rim_present(groups)
    spread = spreading(2)
    quarter = BLOCK // 4
    odd = odd_group()
    for b in range(nb):
        for part in range(2):
            total = grad_kv[part, b]
            place = 0 if b == 0 else 2 if b == nb - 1 else b - odd
            level = dot(spread, got_top[span(part * (REST // quarter) + place, quarter), :])
            rim = slice(part * BLOCK, (part + 1) * BLOCK)
            if b == 0:
                level = jnp.where(odd == 0, level, 0.0)
                total = total + jnp.where(present[0], got_low[rim].astype(F32), 0.0)
            if b == nb - 1:
                level = jnp.where(odd == 1, level, 0.0)
                total = total + jnp.where(present[1], got_high[rim].astype(F32), 0.0)
            total = total + level
            out[b, part] = total.astype(BF16)
    me = member()
    for step, chunk in zip(STEPS, outs):
        chunk[:2] = out[me ^ step]
        chunk[2] = grad_q[me ^ step]


def unpack_kernel(*refs):
    here, across_0, across_1, *refs = refs
    chunks, (*outs, mixed) = refs[:GROUP], refs[GROUP:]
    half = across_0.shape[0]
    for part, across in enumerate((across_0, across_1)):
        at = pl.ds(part * half, half)
        mixed[at, :] = (here[at, :] + across[...].astype(F32)).astype(BF16)
    me = member()
    for step, chunk in zip(STEPS, chunks):
        at = columns(me ^ step)
        for part, out in enumerate(outs):
            out[:, at] = chunk[part]


def share():
    return lax.axis_index("mp")


def grad_kernel(*refs):
    pieces, (out_weight, tops), refs = refs[:N_MP], refs[N_MP : N_MP + 2], refs[N_MP + 2 :]
    *outs, whole, heads = refs
    me = member()
    for step, piece in enumerate(pieces):
        whole[span(share() ^ step, piece.shape[0]), :] = piece[...]
    heads[...] = dot_nt(whole[...], out_weight[...]).astype(BF16)
    quarter = tops.shape[2]
    for step, out in zip(STEPS, outs):
        out[:BLOCK] = heads[:, columns(me ^ step)]
        for part in range(2):
            out[BLOCK + part * quarter : BLOCK + (part + 1) * quarter] = tops[me ^ step, part]


def project_kernel(*refs):
    chunks, out_weight, (kept, *sent, attended, whole) = refs[:GROUP], refs[GROUP], refs[GROUP + 2 :]
    me = member()
    for step, chunk in zip(STEPS, chunks):
        attended[:, columns(me ^ step)] = chunk[...]
    whole[...] = dot(attended[...], out_weight[...]).astype(BF16)
    rows = kept.shape[1]
    for far in range(2):
        kept[far] = whole[span(share() ^ (2 * far), rows), :]
        for part in range(2):
            half = rows // 2
            at = 2 * (share() ^ (2 * far + 1)) + part
            sent[2 * far + part][...] = whole[span(at, half), :]


def swapped(x, axis, step):
    return lax.ppermute(x, axis, [(i, i ^ step) for i in range(lax.axis_size(axis))])


def exchanged(chunks):
    return [chunks[0]] + [swapped(chunk, "seq", step) for step, chunk in zip(STEPS[1:], chunks[1:])]


def beside(arrays):
    count = lax.axis_size("seq")
    if len(arrays) == 1:
        return [swapped(arrays[0], "seq", GROUP)]
    up = [(i, i + GROUP) for i in range(count - GROUP)]
    down = [(j, i) for i, j in up]
    return [lax.ppermute(arrays[0], "seq", up), lax.ppermute(arrays[1], "seq", down)]


def crossed(arrays):
    count = lax.axis_size("seq")
    across = swapped(arrays[0], "seq", GROUP)
    if len(arrays) == 1:
        return [across]
    up = [(i, i + GROUP) for i in range(count - GROUP)]
    down = [(j, i) for i, j in up]
    return [across, lax.ppermute(arrays[1], "seq", up), lax.ppermute(arrays[2], "seq", down)]


def per_device(queries, keys, values, out_weight, out_grad):
    rows, width = queries.shape
    assert width == GROUP * HEAD_DIM and rows == BLOCK and lax.axis_size("mp") == N_MP
    count = lax.axis_size("seq")
    assert count % (2 * GROUP) == 0
    groups = count // GROUP
    nb = GROUP
    tokens = nb * rows
    half, quarter = rows // 2, rows // 4
    model = out_weight.shape[1]
    block = shape(2, rows, HEAD_DIM)
    sent = [shape(2 * REST + 2 * rows, HEAD_DIM)]
    if groups > 2:
        sent = [shape(2 * REST, HEAD_DIM)] + [shape(2 * rows, HEAD_DIM)] * 2
    rims = [block] * (1 if groups == 2 else 2)
    quarter = rows // 4
    in_order = shape(nb, rows, HEAD_DIM)
    score_flops = 2 * tokens * 5 * BLOCK * HEAD_DIM
    weight_flops = 2 * rows * out_weight.size

    chunk = shape(rows, HEAD_DIM)
    triple = shape(3, rows, HEAD_DIM)
    chunks = call(
        pack_kernel,
        [triple] * GROUP,
        (queries, keys, values),
        scratch=[pltpu.SemaphoreType.DMA((3 * GROUP,))],
        copied=GROUP,
        limit=53,
    )
    far = swapped(out_grad, "mp", 2)
    (tops,) = call(pool_kernel, [shape(GROUP, 2, quarter, HEAD_DIM)], chunks)
    chunks = exchanged(chunks)
    tops = swapped(tops, "seq", GROUP)
    arrays = (out_grad, far, out_weight)
    own_grad, far, out_weight = call(copy_kernel, [shape(*x.shape) for x in arrays], arrays)
    near, queries, level_1, *refs = call(
        functools.partial(gather_kernel, nb, groups),
        [
            shape(nb, 2, rows, HEAD_DIM),
            shape(nb, rows, HEAD_DIM),
            shape(2, tokens // 2, HEAD_DIM),
        ]
        + rims,
        chunks,
        flops=20 * score_flops,
    )
    rim_blocks = beside(refs)
    grad_chunks = call(
        grad_kernel,
        [shape(rows + 2 * quarter, HEAD_DIM)] * GROUP,
        (own_grad, swapped(own_grad, "mp", 1), far, swapped(far, "mp", 1), out_weight, tops),
        scratch=[pltpu.VMEM((rows, model), BF16), pltpu.VMEM((rows, width), BF16)],
        flops=weight_flops,
    )
    query, k_t, v_t, k1_t, v1_t, weights, stats = call(
        functools.partial(local_kernel, nb),
        [
            shape(3, nb, rows, HEAD_DIM),
            shape(HEAD_DIM, tokens),
            shape(HEAD_DIM, tokens),
            shape(HEAD_DIM, tokens // 2),
            shape(HEAD_DIM, tokens // 2),
            shape(nb, 4, BLOCK, BLOCK, dtype=F32),
            shape(8, tokens, dtype=F32),
        ],
        (near, queries, level_1, grad_chunks[0]),
        flops=score_flops,
    )
    grad_chunks = exchanged(grad_chunks)
    rim_square = shape(len(rims), BLOCK, BLOCK)
    prob, grads, top_2, deltas, far_shift, rim_shift, *refs = call(
        functools.partial(forward_kernel, nb, groups),
        [
            shape(nb, 4, BLOCK, BLOCK),
            in_order,
            block,
            shape(8, tokens, dtype=F32),
            shape(BLOCK, tokens),
            rim_square,
        ]
        + [chunk] * GROUP
        + sent,
        (query, v_t, v1_t, weights, stats, *rim_blocks, *grad_chunks),
        scratch=[
            pltpu.VMEM((nb, rows, HEAD_DIM), BF16),
            pltpu.VMEM((BLOCK, tokens), BF16),
            pltpu.VMEM(rim_square.shape, BF16),
            pltpu.VMEM((8, tokens), F32),
            pltpu.VMEM((HEAD_DIM, tokens), F32),
            pltpu.VMEM((2, BLOCK, HEAD_DIM), F32),
        ],
        flops=score_flops,
    )
    attended = exchanged(refs[:GROUP])
    rim_grads = refs[GROUP:]
    other_grads = crossed(rim_grads)
    grad_q, grad_kv = call(
        functools.partial(backward_kernel, nb, groups),
        [in_order, shape(2, nb, rows, HEAD_DIM, dtype=F32)],
        (query, near, level_1, k_t, k1_t, prob, grads, top_2, deltas, far_shift, rim_shift, *rim_blocks),
        scratch=[
            pltpu.VMEM((nb, 4, BLOCK, BLOCK), BF16),
            pltpu.VMEM((2, tokens // 2, HEAD_DIM), F32),
            pltpu.VMEM((HEAD_DIM, tokens), F32),
        ],
    )
    local = rows // N_MP
    kept, *given = call(
        project_kernel,
        [shape(2, local, model)] + [shape(local // 2, model)] * 4,
        (*attended, out_weight, grad_q),
        scratch=[pltpu.VMEM((rows, width), BF16), pltpu.VMEM((rows, model), BF16)],
    )
    *across, here = call(
        share_kernel,
        [shape(local // 2, model)] * 2 + [shape(local, model, dtype=F32)],
        (kept, *(swapped(piece, "mp", 1) for piece in given)),
    )
    chunks = call(
        functools.partial(combine_kernel, nb, groups),
        [triple] * GROUP,
        (grad_q, grad_kv, *other_grads),
        scratch=[pltpu.VMEM((nb, 2, rows, HEAD_DIM), BF16)],
        flops=20 * score_flops,
    )
    chunks = exchanged(chunks)
    across = [swapped(piece, "mp", 2) for piece in across]
    grad_k, grad_v, grad_q, mixed = call(
        unpack_kernel,
        [shape(rows, width)] * 3 + [shape(local, model)],
        (here, *across, *chunks),
    )
    return mixed, grad_q, grad_k, grad_v


def solution(mesh):
    return jax.shard_map(
        per_device,
        mesh=mesh,
        in_specs=(
            P("seq", "mp"),
            P("seq", "mp"),
            P("seq", "mp"),
            P("mp", None),
            P(("seq", "mp"), None),
        ),
        out_specs=(P(("seq", "mp"), None), P("seq", "mp"), P("seq", "mp"), P("seq", "mp")),
        check_vma=False,
    )
```

```python
import functools

import jax
import jax.numpy as jnp
from jax import lax
from jax.experimental import pallas as pl
from jax.experimental.pallas import tpu as pltpu
from jax.sharding import PartitionSpec as P

HEAD_DIM = 128
BLOCK = 256
REST = 3 * BLOCK // 4
LEVELS = 2
GROUP = 4
STEPS = (0, 3, 2, 1)
N_MP = 4
SCALE = HEAD_DIM**-0.5
LOG2E = 1.4426950408889634
BF16 = jnp.bfloat16
F32 = jnp.float32


def dot(a, b):
    return lax.dot_general(a, b, (((1,), (0,)), ((), ())), preferred_element_type=F32)


def dot_nt(a, b):
    return lax.dot_general(a, b, (((1,), (1,)), ((), ())), preferred_element_type=F32)


def shape(*dims, dtype=BF16):
    return jax.ShapeDtypeStruct(dims, dtype)


def call(kernel, out_shape, args, scratch=(), flops=0, limit=32, copied=0):
    whole = pl.BlockSpec(memory_space=pltpu.VMEM)
    kept = pl.BlockSpec(memory_space=pltpu.HBM)
    moved = sum(x.size * x.dtype.itemsize for x in (*args, *out_shape))
    return pl.pallas_call(
        kernel,
        out_shape=out_shape,
        in_specs=[kept if copied else whole] * len(args),
        out_specs=[kept] * copied + [whole] * (len(out_shape) - copied),
        scratch_shapes=scratch,
        compiler_params=pltpu.CompilerParams(vmem_limit_bytes=limit << 20),
        cost_estimate=pl.CostEstimate(flops=flops, bytes_accessed=moved if flops else 0, transcendentals=0),
    )(*args)


def columns(index):
    return pl.ds(pl.multiple_of(index * HEAD_DIM, HEAD_DIM), HEAD_DIM)


def span(index, size):
    start = index * size
    return pl.ds(start if isinstance(start, int) else pl.multiple_of(start, size), size)


def iota(dims, axis):
    return lax.broadcasted_iota(jnp.int32, dims, axis)


def averaging(level):
    dims = (BLOCK, BLOCK)
    same = (iota(dims, 0) >> level) == (iota(dims, 1) >> level)
    return jnp.where(same, 2.0**-level, 0.0).astype(BF16)


def pooling():
    dims = (BLOCK // 2, BLOCK)
    return jnp.where(iota(dims, 0) == (iota(dims, 1) >> 1), 0.5, 0.0).astype(BF16)


def spreading(level):
    dims = (BLOCK, BLOCK >> level)
    return jnp.where((iota(dims, 0) >> level) == iota(dims, 1), 2.0**-level, 0.0).astype(BF16)


def halves(x):
    high = x.astype(BF16)
    return high, (x - high.astype(F32)).astype(BF16)


def at_block(b):
    return slice(b * BLOCK, (b + 1) * BLOCK)


def sibling(b):
    return (b >> 1) ^ 1


def rim_present(groups):
    group = lax.axis_index("seq") // GROUP
    return group > 0, group < groups - 1


def member():
    return lax.rem(lax.axis_index("seq"), GROUP)


def columns(index):
    return pl.ds(pl.multiple_of(index * HEAD_DIM, HEAD_DIM), HEAD_DIM)


def pack_kernel(q, k, v, *refs):
    *outs, sems = refs
    me = member()
    copies = []
    for step, out in zip(STEPS, outs):
        for part, source in enumerate((k, v, q)):
            piece = source.at[:, columns(me ^ step)]
            copies.append(pltpu.make_async_copy(piece, out.at[part], sems.at[len(copies)]))
    for copy in copies:
        copy.start()
    for copy in copies:
        copy.wait()


def pool_kernel(*refs):
    *chunks, out = refs
    me = member()
    pool = pooling()
    half = BLOCK // 2
    for step, chunk in zip(STEPS, chunks):
        for part in range(2):
            once = dot(pool, chunk[part]).astype(BF16)
            out[me ^ step, part] = dot(pool[: half // 2, :half], once).astype(BF16)


def copy_kernel(*refs):
    count = len(refs) // 2
    for x, out in zip(refs[:count], refs[count:]):
        out[...] = x[...]


def gather_kernel(nb, *refs):
    chunks, (near, queries, level_1) = refs[:GROUP], refs[GROUP:]
    me = member()
    for step, chunk in zip(STEPS, chunks):
        near[me ^ step] = chunk[:2]
        queries[me ^ step] = chunk[2]
    pool = pooling()
    half = BLOCK // 2
    for part in range(2):
        for b in range(nb):
            level_1[part, b * half : (b + 1) * half] = dot(pool, near[b, part]).astype(BF16)


def rim_kernel(groups, *refs):
    chunks, outs = refs[:GROUP], refs[GROUP:]
    me = member()
    members = [GROUP - 1, 0]
    if groups == 2:
        members = [jnp.where(lax.axis_index("seq") >= GROUP, 0, GROUP - 1)]
    for wanted, out in zip(members, outs):
        for step, chunk in zip(STEPS, chunks):

            @pl.when(me ^ step == wanted)
            def _():
                out[...] = chunk[:2]


def from_beside(groups, refs):
    if groups == 2:
        return (refs[0], refs[0]), refs[1:]
    return refs[:2], refs[2:]


def from_others(groups, refs):
    if groups == 2:
        return (refs[0].at[: 2 * REST], refs[0].at[2 * REST :], refs[0].at[2 * REST :]), refs[1:]
    return refs[:3], refs[3:]


def odd_group():
    return lax.rem(lax.axis_index("seq") // GROUP, 2)


def near_window(b, nb):
    sides = near_sides(b, nb)
    low, high = sides[0], sides[-1] + 1
    return slice(low, high), slice((b + low - 1) * BLOCK, (b + high - 1) * BLOCK)


def near_sides(b, nb):
    return [side for side in range(3) if 0 <= b + side - 1 < nb]


def local_kernel(nb, near, queries, level_1, _, query, k_t, v_t, k1_t, v1_t, weights, stats):
    even_1, even_2 = averaging(1), averaging(2)
    for b in range(nb):
        query[0, b] = queries[b]
        once = dot(even_1, queries[b]).astype(BF16)
        query[1, b] = once
        query[2, b] = dot(even_2, once).astype(BF16)
        for part, transposed in enumerate((k_t, v_t)):
            transposed[:, at_block(b)] = near[b, part].T
    for c in range(nb // 2):
        for part, transposed in enumerate((k1_t, v1_t)):
            transposed[:, at_block(c)] = level_1[part, at_block(c)].T
    for b in range(nb):
        sides = near_sides(b, nb)
        scores = [dot_nt(near[b + side - 1, 0], query[0, b]) * (SCALE * LOG2E) for side in sides]
        coarse = dot_nt(level_1[0, at_block(sibling(b))], query[1, b]) * (SCALE * LOG2E)
        top = coarse.max(0, keepdims=True)
        for score in scores:
            top = jnp.maximum(top, score.max(0, keepdims=True))
        weight = 2.0 * jnp.exp2(coarse - top)
        weights[b, 3] = weight
        total = weight.sum(0, keepdims=True)
        for side, score in zip(sides, scores):
            weight = jnp.exp2(score - top)
            weights[b, side] = weight
            total = total + weight.sum(0, keepdims=True)
        stats[:1, at_block(b)] = top
        stats[1:2, at_block(b)] = total


def rims_of(nb, groups, low, high):
    group = lax.axis_index("seq") // GROUP
    if groups == 2:
        return [(jnp.where(group > 0, 0, nb - 1), low, None)]
    return [(0, low, group > 0), (nb - 1, high, group < groups - 1)]


def forward_kernel(nb, groups, *refs):
    (query, v_t, v1_t, weights, stats), refs = refs[:5], refs[5:]
    (rim_low, rim_high), refs = from_beside(groups, refs)
    chunks, refs = refs[:GROUP], refs[GROUP:]
    (prob, grads, top_2, deltas, far_shift, rim_shift), refs = refs[:6], refs[6:]
    outs, (*rim_outs, attended, far_prob, rim_prob, row, context_t, far_sums) = refs[:GROUP], refs[GROUP:]
    rims = rims_of(nb, groups, rim_low, rim_high)
    me = member()
    quarter = BLOCK // 4
    tokens = nb * BLOCK
    for step, chunk in zip(STEPS, chunks):
        grads[me ^ step] = chunk[:BLOCK]
        for part in range(2):
            level = chunk[BLOCK + part * quarter : BLOCK + (part + 1) * quarter]
            top_2[part, span(me ^ step, quarter), :] = level
    coarse_query = query[2].reshape(tokens, HEAD_DIM)
    coarse = dot_nt(top_2[0], coarse_query) * (SCALE * LOG2E)
    row[:1] = jnp.maximum(stats[:1], coarse.max(0, keepdims=True))
    scores = []
    for b, block, present in rims:
        score = dot_nt(block[0], query[0, b]) * (SCALE * LOG2E)
        if present is not None:
            score = jnp.where(present, score, -jnp.inf)
        at = span(b, BLOCK)
        row[:1, at] = jnp.maximum(row[:1, at], score.max(0, keepdims=True))
        scores.append(score)
    top = row[:1]
    shrink = jnp.exp2(stats[:1] - top)
    far = 4.0 * jnp.exp2(coarse - top)
    row[1:2] = shrink * stats[1:2] + far.sum(0, keepdims=True)
    fresh = []
    for (b, _, _), score in zip(rims, scores):
        at = span(b, BLOCK)
        fresh.append(jnp.exp2(score - row[:1, at]))
        row[1:2, at] += fresh[-1].sum(0, keepdims=True)
    inverse = 1.0 / row[1:2]
    row[2:3] = inverse
    row[3:4] = shrink * inverse
    far_prob[...] = (far * inverse).astype(BF16)
    context_t[...] = dot(top_2[1].T, far_prob[...])
    for i, (b, block, _) in enumerate(rims):
        at = span(b, BLOCK)
        rim_prob[i] = (fresh[i] * row[2:3, at]).astype(BF16)
        context_t[:, at] += dot(block[1].T, rim_prob[i])
    for b in range(nb):
        shrink = row[3:4, at_block(b)]
        prob[b, 3] = (weights[b, 3] * shrink).astype(BF16)
        context = context_t[:, at_block(b)] + dot(v1_t[:, at_block(sibling(b))], prob[b, 3])
        sides, keys = near_window(b, nb)
        parts = (weights[b, sides] * shrink).astype(BF16)
        prob[b, sides] = parts
        context = context + dot(v_t[:, keys], parts.reshape(-1, BLOCK))
        attended[b] = context.T.astype(BF16)
        deltas[:1, at_block(b)] = (grads[b].T.astype(F32) * context).sum(0, keepdims=True)
    grad = grads[...].reshape(tokens, HEAD_DIM)
    slope = dot_nt(top_2[1], grad)
    far_shift[...] = (far_prob[...].astype(F32) * (slope - deltas[:1])).astype(BF16)
    far_sums[0] = SCALE * dot(far_shift[...], coarse_query)
    far_sums[1] = dot(far_prob[...], grad)
    odd = odd_group()
    spread = spreading(2)
    folded = []
    for part in range(2):
        rest = far_sums[part, pl.ds(pl.multiple_of((1 - odd) * quarter, quarter), REST), :]
        rim_outs[0][part * REST : (part + 1) * REST] = rest.astype(BF16)
        high, low = halves(far_sums[part, pl.ds(pl.multiple_of(odd * REST, quarter), quarter), :])
        folded.append(dot(spread, high) + dot(spread, low))
    pairs = []
    for i, (b, block, _) in enumerate(rims):
        slope = dot_nt(block[1], grads[b])
        rim_shift[i] = (rim_prob[i].astype(F32) * (slope - deltas[:1, span(b, BLOCK)])).astype(BF16)
        pairs.append((SCALE * dot(rim_shift[i], query[0, b]), dot(rim_prob[i], grads[b])))
    for part in range(2):
        at = slice(part * BLOCK, (part + 1) * BLOCK)
        if groups == 2:
            rim_outs[0][2 * REST + part * BLOCK : 2 * REST + (part + 1) * BLOCK] = (
                pairs[0][part] + folded[part]
            ).astype(BF16)
        else:
            rim_outs[1][at] = (pairs[1][part] + jnp.where(odd == 0, folded[part], 0.0)).astype(BF16)
            rim_outs[2][at] = (pairs[0][part] + jnp.where(odd == 1, folded[part], 0.0)).astype(BF16)
    for step, out in zip(STEPS, outs):
        out[...] = attended[me ^ step]


def backward_kernel(nb, groups, *refs):
    (query, near, level_1, k_t, k1_t, prob, grads, top_2, deltas, far_shift, rim_shift), refs = refs[:11], refs[11:]
    (rim_low, rim_high), refs = from_beside(groups, refs)
    grad_q, grad_kv, shift, sums_1, query_t = refs
    even_1, even_2 = averaging(1), averaging(2)
    coarse = dot(top_2[0].T, far_shift[...])
    for b in range(nb):
        high, low = halves(coarse[:, at_block(b)])
        query_t[:, at_block(b)] = dot(high, even_2) + dot(low, even_2)
    for i, (b, block, _) in enumerate(rims_of(nb, groups, rim_low, rim_high)):
        query_t[:, span(b, BLOCK)] += dot(block[0].T, rim_shift[i])
    for b in range(nb):
        grad, delta = grads[b], deltas[:1, at_block(b)]
        sides, keys = near_window(b, nb)
        blocks = slice(keys.start // BLOCK, keys.stop // BLOCK)
        slope = dot_nt(near[blocks, 1].reshape(-1, HEAD_DIM), grad)
        parts = (prob[b, sides].reshape(-1, BLOCK).astype(F32) * (slope - delta)).astype(BF16)
        shift[b, sides] = parts.reshape(-1, BLOCK, BLOCK)
        grad_t = query_t[:, at_block(b)] + dot(k_t[:, keys], parts)
        slope = dot_nt(level_1[1, at_block(sibling(b))], grad)
        part = (prob[b, 3].astype(F32) * (slope - delta)).astype(BF16)
        shift[b, 3] = part
        high, low = halves(dot(k1_t[:, at_block(sibling(b))], part))
        grad_t = grad_t + (dot(high, even_1) + dot(low, even_1))
        grad_q[b] = (SCALE * grad_t).T.astype(BF16)
    for c in range(nb // 2):
        users = [b for b in range(nb) if sibling(b) == c]
        sums_1[0, at_block(c)] = SCALE * sum(dot(shift[b, 3], query[1, b]) for b in users)
        sums_1[1, at_block(c)] = sum(dot(prob[b, 3], grads[b]) for b in users)
    spread = spreading(1)
    half = BLOCK // 2
    for s in range(nb):
        users = [(s + 1 - side, side) for side in range(3) if 0 <= s + 1 - side < nb]
        key = SCALE * sum(dot(shift[b, side], query[0, b]) for b, side in users)
        value = sum(dot(prob[b, side], grads[b]) for b, side in users)
        for part, total in enumerate((key, value)):
            high, low = halves(sums_1[part, s * half : (s + 1) * half])
            grad_kv[part, s] = total + (dot(spread, high) + dot(spread, low))


def share_kernel(kept, *refs):
    *got, across_0, across_1, here = refs
    half = across_0.shape[0]
    for i, piece in enumerate(got):
        far, at = i // 2, pl.ds(i % 2 * half, half)
        total = kept[far, at, :].astype(F32) + piece[...].astype(F32)
        if far:
            (across_0, across_1)[i % 2][...] = total.astype(BF16)
        else:
            here[at, :] = total


def combine_kernel(nb, groups, grad_q, grad_kv, *refs):
    (got_top, got_low, got_high), (*outs, out) = from_others(groups, refs)
    present = rim_present(groups)
    spread = spreading(2)
    quarter = BLOCK // 4
    odd = odd_group()
    for b in range(nb):
        for part in range(2):
            total = grad_kv[part, b]
            place = 0 if b == 0 else 2 if b == nb - 1 else b - odd
            level = dot(spread, got_top[span(part * (REST // quarter) + place, quarter), :])
            rim = slice(part * BLOCK, (part + 1) * BLOCK)
            if b == 0:
                level = jnp.where(odd == 0, level, 0.0)
                total = total + jnp.where(present[0], got_low[rim].astype(F32), 0.0)
            if b == nb - 1:
                level = jnp.where(odd == 1, level, 0.0)
                total = total + jnp.where(present[1], got_high[rim].astype(F32), 0.0)
            total = total + level
            out[b, part] = total.astype(BF16)
    me = member()
    for step, chunk in zip(STEPS, outs):
        chunk[:2] = out[me ^ step]
        chunk[2] = grad_q[me ^ step]


def unpack_kernel(*refs):
    here, across_0, across_1, *refs = refs
    chunks, (*outs, mixed) = refs[:GROUP], refs[GROUP:]
    half = across_0.shape[0]
    for part, across in enumerate((across_0, across_1)):
        at = pl.ds(part * half, half)
        mixed[at, :] = (here[at, :] + across[...].astype(F32)).astype(BF16)
    me = member()
    for step, chunk in zip(STEPS, chunks):
        at = columns(me ^ step)
        for part, out in enumerate(outs):
            out[:, at] = chunk[part]


def share():
    return lax.axis_index("mp")


def grad_kernel(*refs):
    pieces, (out_weight, tops), refs = refs[:N_MP], refs[N_MP : N_MP + 2], refs[N_MP + 2 :]
    *outs, whole, heads = refs
    me = member()
    for step, piece in enumerate(pieces):
        whole[span(share() ^ step, piece.shape[0]), :] = piece[...]
    heads[...] = dot_nt(whole[...], out_weight[...]).astype(BF16)
    quarter = tops.shape[2]
    for step, out in zip(STEPS, outs):
        out[:BLOCK] = heads[:, columns(me ^ step)]
        for part in range(2):
            out[BLOCK + part * quarter : BLOCK + (part + 1) * quarter] = tops[me ^ step, part]


def project_kernel(*refs):
    chunks, out_weight, (kept, *sent, attended, whole) = refs[:GROUP], refs[GROUP], refs[GROUP + 2 :]
    me = member()
    for step, chunk in zip(STEPS, chunks):
        attended[:, columns(me ^ step)] = chunk[...]
    whole[...] = dot(attended[...], out_weight[...]).astype(BF16)
    rows = kept.shape[1]
    for far in range(2):
        kept[far] = whole[span(share() ^ (2 * far), rows), :]
        for part in range(2):
            half = rows // 2
            at = 2 * (share() ^ (2 * far + 1)) + part
            sent[2 * far + part][...] = whole[span(at, half), :]


def swapped(x, axis, step):
    return lax.ppermute(x, axis, [(i, i ^ step) for i in range(lax.axis_size(axis))])


def exchanged(chunks):
    return [chunks[0]] + [swapped(chunk, "seq", step) for step, chunk in zip(STEPS[1:], chunks[1:])]


def beside(arrays):
    count = lax.axis_size("seq")
    if len(arrays) == 1:
        return [swapped(arrays[0], "seq", GROUP)]
    up = [(i, i + GROUP) for i in range(count - GROUP)]
    down = [(j, i) for i, j in up]
    return [lax.ppermute(arrays[0], "seq", up), lax.ppermute(arrays[1], "seq", down)]


def crossed(arrays):
    count = lax.axis_size("seq")
    across = swapped(arrays[0], "seq", GROUP)
    if len(arrays) == 1:
        return [across]
    up = [(i, i + GROUP) for i in range(count - GROUP)]
    down = [(j, i) for i, j in up]
    return [across, lax.ppermute(arrays[1], "seq", up), lax.ppermute(arrays[2], "seq", down)]


def per_device(queries, keys, values, out_weight, out_grad):
    rows, width = queries.shape
    assert width == GROUP * HEAD_DIM and rows == BLOCK and lax.axis_size("mp") == N_MP
    count = lax.axis_size("seq")
    assert count % (2 * GROUP) == 0
    groups = count // GROUP
    nb = GROUP
    tokens = nb * rows
    half, quarter = rows // 2, rows // 4
    model = out_weight.shape[1]
    block = shape(2, rows, HEAD_DIM)
    sent = [shape(2 * REST + 2 * rows, HEAD_DIM)]
    if groups > 2:
        sent = [shape(2 * REST, HEAD_DIM)] + [shape(2 * rows, HEAD_DIM)] * 2
    rims = [block] * (1 if groups == 2 else 2)
    quarter = rows // 4
    in_order = shape(nb, rows, HEAD_DIM)
    score_flops = 2 * tokens * 5 * BLOCK * HEAD_DIM
    weight_flops = 2 * rows * out_weight.size

    chunk = shape(rows, HEAD_DIM)
    triple = shape(3, rows, HEAD_DIM)
    chunks = call(
        pack_kernel,
        [triple] * GROUP,
        (queries, keys, values),
        scratch=[pltpu.SemaphoreType.DMA((3 * GROUP,))],
        copied=GROUP,
        limit=53,
    )
    far = swapped(out_grad, "mp", 2)
    (tops,) = call(pool_kernel, [shape(GROUP, 2, quarter, HEAD_DIM)], chunks)
    chunks = exchanged(chunks)
    tops = swapped(tops, "seq", GROUP)
    arrays = (out_grad, far, out_weight)
    own_grad, far, out_weight = call(copy_kernel, [shape(*x.shape) for x in arrays], arrays)
    rim_blocks = beside(call(functools.partial(rim_kernel, groups), rims, chunks, flops=20 * score_flops))
    near, queries, level_1 = call(
        functools.partial(gather_kernel, nb),
        [
            shape(nb, 2, rows, HEAD_DIM),
            shape(nb, rows, HEAD_DIM),
            shape(2, tokens // 2, HEAD_DIM),
        ],
        chunks,
    )
    grad_chunks = call(
        grad_kernel,
        [shape(rows + 2 * quarter, HEAD_DIM)] * GROUP,
        (own_grad, swapped(own_grad, "mp", 1), far, swapped(far, "mp", 1), out_weight, tops),
        scratch=[pltpu.VMEM((rows, model), BF16), pltpu.VMEM((rows, width), BF16)],
        flops=weight_flops,
    )
    query, k_t, v_t, k1_t, v1_t, weights, stats = call(
        functools.partial(local_kernel, nb),
        [
            shape(3, nb, rows, HEAD_DIM),
            shape(HEAD_DIM, tokens),
            shape(HEAD_DIM, tokens),
            shape(HEAD_DIM, tokens // 2),
            shape(HEAD_DIM, tokens // 2),
            shape(nb, 4, BLOCK, BLOCK, dtype=F32),
            shape(8, tokens, dtype=F32),
        ],
        (near, queries, level_1, grad_chunks[0]),
        flops=score_flops,
    )
    grad_chunks = exchanged(grad_chunks)
    rim_square = shape(len(rims), BLOCK, BLOCK)
    prob, grads, top_2, deltas, far_shift, rim_shift, *refs = call(
        functools.partial(forward_kernel, nb, groups),
        [
            shape(nb, 4, BLOCK, BLOCK),
            in_order,
            block,
            shape(8, tokens, dtype=F32),
            shape(BLOCK, tokens),
            rim_square,
        ]
        + [chunk] * GROUP
        + sent,
        (query, v_t, v1_t, weights, stats, *rim_blocks, *grad_chunks),
        scratch=[
            pltpu.VMEM((nb, rows, HEAD_DIM), BF16),
            pltpu.VMEM((BLOCK, tokens), BF16),
            pltpu.VMEM(rim_square.shape, BF16),
            pltpu.VMEM((8, tokens), F32),
            pltpu.VMEM((HEAD_DIM, tokens), F32),
            pltpu.VMEM((2, BLOCK, HEAD_DIM), F32),
        ],
        flops=score_flops,
    )
    attended = exchanged(refs[:GROUP])
    rim_grads = refs[GROUP:]
    other_grads = crossed(rim_grads)
    grad_q, grad_kv = call(
        functools.partial(backward_kernel, nb, groups),
        [in_order, shape(2, nb, rows, HEAD_DIM, dtype=F32)],
        (query, near, level_1, k_t, k1_t, prob, grads, top_2, deltas, far_shift, rim_shift, *rim_blocks),
        scratch=[
            pltpu.VMEM((nb, 4, BLOCK, BLOCK), BF16),
            pltpu.VMEM((2, tokens // 2, HEAD_DIM), F32),
            pltpu.VMEM((HEAD_DIM, tokens), F32),
        ],
    )
    local = rows // N_MP
    kept, *given = call(
        project_kernel,
        [shape(2, local, model)] + [shape(local // 2, model)] * 4,
        (*attended, out_weight, grad_q),
        scratch=[pltpu.VMEM((rows, width), BF16), pltpu.VMEM((rows, model), BF16)],
    )
    *across, here = call(
        share_kernel,
        [shape(local // 2, model)] * 2 + [shape(local, model, dtype=F32)],
        (kept, *(swapped(piece, "mp", 1) for piece in given)),
    )
    chunks = call(
        functools.partial(combine_kernel, nb, groups),
        [triple] * GROUP,
        (grad_q, grad_kv, *other_grads),
        scratch=[pltpu.VMEM((nb, 2, rows, HEAD_DIM), BF16)],
        flops=20 * score_flops,
    )
    chunks = exchanged(chunks)
    across = [swapped(piece, "mp", 2) for piece in across]
    grad_k, grad_v, grad_q, mixed = call(
        unpack_kernel,
        [shape(rows, width)] * 3 + [shape(local, model)],
        (here, *across, *chunks),
    )
    return mixed, grad_q, grad_k, grad_v


def solution(mesh):
    return jax.shard_map(
        per_device,
        mesh=mesh,
        in_specs=(
            P("seq", "mp"),
            P("seq", "mp"),
            P("seq", "mp"),
            P("mp", None),
            P(("seq", "mp"), None),
        ),
        out_specs=(P(("seq", "mp"), None), P("seq", "mp"), P("seq", "mp"), P("seq", "mp")),
        check_vma=False,
    )
```

```python
import functools

import jax
import jax.numpy as jnp
from jax import lax
from jax.experimental import pallas as pl
from jax.experimental.pallas import tpu as pltpu
from jax.sharding import PartitionSpec as P

HEAD_DIM = 128
BLOCK = 256
REST = 3 * BLOCK // 4
LEVELS = 2
GROUP = 4
STEPS = (0, 3, 2, 1)
N_MP = 4
SCALE = HEAD_DIM**-0.5
LOG2E = 1.4426950408889634
BF16 = jnp.bfloat16
F32 = jnp.float32


def dot(a, b):
    return lax.dot_general(a, b, (((1,), (0,)), ((), ())), preferred_element_type=F32)


def dot_nt(a, b):
    return lax.dot_general(a, b, (((1,), (1,)), ((), ())), preferred_element_type=F32)


def shape(*dims, dtype=BF16):
    return jax.ShapeDtypeStruct(dims, dtype)


def call(kernel, out_shape, args, scratch=(), flops=0, limit=32, copied=0):
    whole = pl.BlockSpec(memory_space=pltpu.VMEM)
    kept = pl.BlockSpec(memory_space=pltpu.HBM)
    moved = sum(x.size * x.dtype.itemsize for x in (*args, *out_shape))
    return pl.pallas_call(
        kernel,
        out_shape=out_shape,
        in_specs=[kept if copied else whole] * len(args),
        out_specs=[kept] * copied + [whole] * (len(out_shape) - copied),
        scratch_shapes=scratch,
        compiler_params=pltpu.CompilerParams(vmem_limit_bytes=limit << 20),
        cost_estimate=pl.CostEstimate(flops=flops, bytes_accessed=moved if flops else 0, transcendentals=0),
    )(*args)


def columns(index):
    return pl.ds(pl.multiple_of(index * HEAD_DIM, HEAD_DIM), HEAD_DIM)


def span(index, size):
    start = index * size
    return pl.ds(start if isinstance(start, int) else pl.multiple_of(start, size), size)


def iota(dims, axis):
    return lax.broadcasted_iota(jnp.int32, dims, axis)


def averaging(level):
    dims = (BLOCK, BLOCK)
    same = (iota(dims, 0) >> level) == (iota(dims, 1) >> level)
    return jnp.where(same, 2.0**-level, 0.0).astype(BF16)


def pooling():
    dims = (BLOCK // 2, BLOCK)
    return jnp.where(iota(dims, 0) == (iota(dims, 1) >> 1), 0.5, 0.0).astype(BF16)


def spreading(level):
    dims = (BLOCK, BLOCK >> level)
    return jnp.where((iota(dims, 0) >> level) == iota(dims, 1), 2.0**-level, 0.0).astype(BF16)


def halves(x):
    high = x.astype(BF16)
    return high, (x - high.astype(F32)).astype(BF16)


def at_block(b):
    return slice(b * BLOCK, (b + 1) * BLOCK)


def sibling(b):
    return (b >> 1) ^ 1


def rim_present(groups):
    group = lax.axis_index("seq") // GROUP
    return group > 0, group < groups - 1


def member():
    return lax.rem(lax.axis_index("seq"), GROUP)


def columns(index):
    return pl.ds(pl.multiple_of(index * HEAD_DIM, HEAD_DIM), HEAD_DIM)


def pack_kernel(q, k, v, *refs):
    *outs, sems = refs
    me = member()
    copies = []
    for step, out in zip(STEPS, outs):
        for part, source in enumerate((k, v, q)):
            piece = source.at[:, columns(me ^ step)]
            copies.append(pltpu.make_async_copy(piece, out.at[part], sems.at[len(copies)]))
    for copy in copies:
        copy.start()
    for copy in copies:
        copy.wait()


def pool_kernel(*refs):
    *chunks, out = refs
    me = member()
    pool = pooling()
    half = BLOCK // 2
    for step, chunk in zip(STEPS, chunks):
        for part in range(2):
            once = dot(pool, chunk[part]).astype(BF16)
            out[me ^ step, part] = dot(pool[: half // 2, :half], once).astype(BF16)


def copy_kernel(*refs):
    count = len(refs) // 2
    for x, out in zip(refs[:count], refs[count:]):
        out[...] = x[...]


def gather_kernel(nb, *refs):
    chunks, (near, queries, level_1) = refs[:GROUP], refs[GROUP:]
    me = member()
    for step, chunk in zip(STEPS, chunks):
        near[me ^ step] = chunk[:2]
        queries[me ^ step] = chunk[2]
    pool = pooling()
    half = BLOCK // 2
    for part in range(2):
        for b in range(nb):
            level_1[part, b * half : (b + 1) * half] = dot(pool, near[b, part]).astype(BF16)


def rim_kernel(groups, *refs):
    chunks, outs = refs[:GROUP], refs[GROUP:]
    me = member()
    members = [GROUP - 1, 0]
    if groups == 2:
        members = [jnp.where(lax.axis_index("seq") >= GROUP, 0, GROUP - 1)]
    for wanted, out in zip(members, outs):
        for step, chunk in zip(STEPS, chunks):

            @pl.when(me ^ step == wanted)
            def _():
                out[...] = chunk[:2]


def from_beside(groups, refs):
    if groups == 2:
        return (refs[0], refs[0]), refs[1:]
    return refs[:2], refs[2:]


def from_others(groups, refs):
    if groups == 2:
        return (refs[0].at[: 2 * REST], refs[0].at[2 * REST :], refs[0].at[2 * REST :]), refs[1:]
    return refs[:3], refs[3:]


def odd_group():
    return lax.rem(lax.axis_index("seq") // GROUP, 2)


def near_window(b, nb):
    sides = near_sides(b, nb)
    low, high = sides[0], sides[-1] + 1
    return slice(low, high), slice((b + low - 1) * BLOCK, (b + high - 1) * BLOCK)


def near_sides(b, nb):
    return [side for side in range(3) if 0 <= b + side - 1 < nb]


def local_kernel(nb, near, queries, level_1, _, query, k_t, v_t, k1_t, v1_t, weights, stats):
    even_1, even_2 = averaging(1), averaging(2)
    for b in range(nb):
        query[0, b] = queries[b]
        once = dot(even_1, queries[b]).astype(BF16)
        query[1, b] = once
        query[2, b] = dot(even_2, once).astype(BF16)
        for part, transposed in enumerate((k_t, v_t)):
            transposed[:, at_block(b)] = near[b, part].T
    for c in range(nb // 2):
        for part, transposed in enumerate((k1_t, v1_t)):
            transposed[:, at_block(c)] = level_1[part, at_block(c)].T
    for b in range(nb):
        sides = near_sides(b, nb)
        scores = [dot_nt(near[b + side - 1, 0], query[0, b]) * (SCALE * LOG2E) for side in sides]
        coarse = dot_nt(level_1[0, at_block(sibling(b))], query[1, b]) * (SCALE * LOG2E)
        top = coarse.max(0, keepdims=True)
        for score in scores:
            top = jnp.maximum(top, score.max(0, keepdims=True))
        weight = 2.0 * jnp.exp2(coarse - top)
        weights[b, 3] = weight
        total = weight.sum(0, keepdims=True)
        for side, score in zip(sides, scores):
            weight = jnp.exp2(score - top)
            weights[b, side] = weight
            total = total + weight.sum(0, keepdims=True)
        stats[:1, at_block(b)] = top
        stats[1:2, at_block(b)] = total


def rims_of(nb, groups, low, high):
    group = lax.axis_index("seq") // GROUP
    if groups == 2:
        return [(jnp.where(group > 0, 0, nb - 1), low, None)]
    return [(0, low, group > 0), (nb - 1, high, group < groups - 1)]


def forward_kernel(nb, groups, *refs):
    (query, v_t, v1_t, weights, stats), refs = refs[:5], refs[5:]
    (rim_low, rim_high), refs = from_beside(groups, refs)
    chunks, refs = refs[:GROUP], refs[GROUP:]
    (prob, grads, top_2, deltas, far_shift, rim_shift), refs = refs[:6], refs[6:]
    outs, (*rim_outs, attended, far_prob, rim_prob, row, context_t, far_sums) = refs[:GROUP], refs[GROUP:]
    rims = rims_of(nb, groups, rim_low, rim_high)
    me = member()
    quarter = BLOCK // 4
    tokens = nb * BLOCK
    for step, chunk in zip(STEPS, chunks):
        grads[me ^ step] = chunk[:BLOCK]
        for part in range(2):
            level = chunk[BLOCK + part * quarter : BLOCK + (part + 1) * quarter]
            top_2[part, span(me ^ step, quarter), :] = level
    coarse_query = query[2].reshape(tokens, HEAD_DIM)
    coarse = dot_nt(top_2[0], coarse_query) * (SCALE * LOG2E)
    row[:1] = jnp.maximum(stats[:1], coarse.max(0, keepdims=True))
    scores = []
    for b, block, present in rims:
        score = dot_nt(block[0], query[0, b]) * (SCALE * LOG2E)
        if present is not None:
            score = jnp.where(present, score, -jnp.inf)
        at = span(b, BLOCK)
        row[:1, at] = jnp.maximum(row[:1, at], score.max(0, keepdims=True))
        scores.append(score)
    top = row[:1]
    shrink = jnp.exp2(stats[:1] - top)
    far = 4.0 * jnp.exp2(coarse - top)
    row[1:2] = shrink * stats[1:2] + far.sum(0, keepdims=True)
    fresh = []
    for (b, _, _), score in zip(rims, scores):
        at = span(b, BLOCK)
        fresh.append(jnp.exp2(score - row[:1, at]))
        row[1:2, at] += fresh[-1].sum(0, keepdims=True)
    inverse = 1.0 / row[1:2]
    row[2:3] = inverse
    row[3:4] = shrink * inverse
    far_prob[...] = (far * inverse).astype(BF16)
    context_t[...] = dot(top_2[1].T, far_prob[...])
    for i, (b, block, _) in enumerate(rims):
        at = span(b, BLOCK)
        rim_prob[i] = (fresh[i] * row[2:3, at]).astype(BF16)
        context_t[:, at] += dot(block[1].T, rim_prob[i])
    for b in range(nb):
        shrink = row[3:4, at_block(b)]
        prob[b, 3] = (weights[b, 3] * shrink).astype(BF16)
        context = context_t[:, at_block(b)] + dot(v1_t[:, at_block(sibling(b))], prob[b, 3])
        sides, keys = near_window(b, nb)
        parts = (weights[b, sides] * shrink).astype(BF16)
        prob[b, sides] = parts
        context = context + dot(v_t[:, keys], parts.reshape(-1, BLOCK))
        attended[b] = context.T.astype(BF16)
        deltas[:1, at_block(b)] = (grads[b].T.astype(F32) * context).sum(0, keepdims=True)
    grad = grads[...].reshape(tokens, HEAD_DIM)
    slope = dot_nt(top_2[1], grad)
    far_shift[...] = (far_prob[...].astype(F32) * (slope - deltas[:1])).astype(BF16)
    far_sums[0] = SCALE * dot(far_shift[...], coarse_query)
    far_sums[1] = dot(far_prob[...], grad)
    odd = odd_group()
    spread = spreading(2)
    folded = []
    for part in range(2):
        rest = far_sums[part, pl.ds(pl.multiple_of((1 - odd) * quarter, quarter), REST), :]
        rim_outs[0][part * REST : (part + 1) * REST] = rest.astype(BF16)
        high, low = halves(far_sums[part, pl.ds(pl.multiple_of(odd * REST, quarter), quarter), :])
        folded.append(dot(spread, high) + dot(spread, low))
    pairs = []
    for i, (b, block, _) in enumerate(rims):
        slope = dot_nt(block[1], grads[b])
        rim_shift[i] = (rim_prob[i].astype(F32) * (slope - deltas[:1, span(b, BLOCK)])).astype(BF16)
        pairs.append((SCALE * dot(rim_shift[i], query[0, b]), dot(rim_prob[i], grads[b])))
    for part in range(2):
        at = slice(part * BLOCK, (part + 1) * BLOCK)
        if groups == 2:
            rim_outs[0][2 * REST + part * BLOCK : 2 * REST + (part + 1) * BLOCK] = (
                pairs[0][part] + folded[part]
            ).astype(BF16)
        else:
            rim_outs[1][at] = (pairs[1][part] + jnp.where(odd == 0, folded[part], 0.0)).astype(BF16)
            rim_outs[2][at] = (pairs[0][part] + jnp.where(odd == 1, folded[part], 0.0)).astype(BF16)
    for step, out in zip(STEPS, outs):
        out[...] = attended[me ^ step]


def backward_kernel(nb, groups, *refs):
    (query, near, level_1, k_t, k1_t, prob, grads, top_2, deltas, far_shift, rim_shift), refs = refs[:11], refs[11:]
    (rim_low, rim_high), refs = from_beside(groups, refs)
    grad_q, grad_kv, shift, sums_1, query_t = refs
    even_1, even_2 = averaging(1), averaging(2)
    coarse = dot(top_2[0].T, far_shift[...])
    for b in range(nb):
        high, low = halves(coarse[:, at_block(b)])
        query_t[:, at_block(b)] = dot(high, even_2) + dot(low, even_2)
    for i, (b, block, _) in enumerate(rims_of(nb, groups, rim_low, rim_high)):
        query_t[:, span(b, BLOCK)] += dot(block[0].T, rim_shift[i])
    for b in range(nb):
        grad, delta = grads[b], deltas[:1, at_block(b)]
        grad_t = query_t[:, at_block(b)]
        for side in near_sides(b, nb):
            slope = dot_nt(near[b + side - 1, 1], grad)
            part = (prob[b, side].astype(F32) * (slope - delta)).astype(BF16)
            shift[b, side] = part
            grad_t = grad_t + dot(k_t[:, at_block(b + side - 1)], part)
        slope = dot_nt(level_1[1, at_block(sibling(b))], grad)
        part = (prob[b, 3].astype(F32) * (slope - delta)).astype(BF16)
        shift[b, 3] = part
        high, low = halves(dot(k1_t[:, at_block(sibling(b))], part))
        grad_t = grad_t + (dot(high, even_1) + dot(low, even_1))
        grad_q[b] = (SCALE * grad_t).T.astype(BF16)
    for c in range(nb // 2):
        users = [b for b in range(nb) if sibling(b) == c]
        sums_1[0, at_block(c)] = SCALE * sum(dot(shift[b, 3], query[1, b]) for b in users)
        sums_1[1, at_block(c)] = sum(dot(prob[b, 3], grads[b]) for b in users)
    spread = spreading(1)
    half = BLOCK // 2
    for s in range(nb):
        users = [(s + 1 - side, side) for side in range(3) if 0 <= s + 1 - side < nb]
        key = SCALE * sum(dot(shift[b, side], query[0, b]) for b, side in users)
        value = sum(dot(prob[b, side], grads[b]) for b, side in users)
        for part, total in enumerate((key, value)):
            high, low = halves(sums_1[part, s * half : (s + 1) * half])
            grad_kv[part, s] = total + (dot(spread, high) + dot(spread, low))


def share_kernel(kept, *refs):
    *got, across_0, across_1, here = refs
    half = across_0.shape[0]
    for i, piece in enumerate(got):
        far, at = i // 2, pl.ds(i % 2 * half, half)
        total = kept[far, at, :].astype(F32) + piece[...].astype(F32)
        if far:
            (across_0, across_1)[i % 2][...] = total.astype(BF16)
        else:
            here[at, :] = total


def combine_kernel(nb, groups, grad_q, grad_kv, *refs):
    (got_top, got_low, got_high), (*outs, out) = from_others(groups, refs)
    present = rim_present(groups)
    spread = spreading(2)
    quarter = BLOCK // 4
    odd = odd_group()
    for b in range(nb):
        for part in range(2):
            total = grad_kv[part, b]
            place = 0 if b == 0 else 2 if b == nb - 1 else b - odd
            level = dot(spread, got_top[span(part * (REST // quarter) + place, quarter), :])
            rim = slice(part * BLOCK, (part + 1) * BLOCK)
            if b == 0:
                level = jnp.where(odd == 0, level, 0.0)
                total = total + jnp.where(present[0], got_low[rim].astype(F32), 0.0)
            if b == nb - 1:
                level = jnp.where(odd == 1, level, 0.0)
                total = total + jnp.where(present[1], got_high[rim].astype(F32), 0.0)
            total = total + level
            out[b, part] = total.astype(BF16)
    me = member()
    for step, chunk in zip(STEPS, outs):
        chunk[:2] = out[me ^ step]
        chunk[2] = grad_q[me ^ step]


def unpack_kernel(*refs):
    here, across_0, across_1, *refs = refs
    chunks, (*outs, mixed) = refs[:GROUP], refs[GROUP:]
    half = across_0.shape[0]
    for part, across in enumerate((across_0, across_1)):
        at = pl.ds(part * half, half)
        mixed[at, :] = (here[at, :] + across[...].astype(F32)).astype(BF16)
    me = member()
    for step, chunk in zip(STEPS, chunks):
        at = columns(me ^ step)
        for part, out in enumerate(outs):
            out[:, at] = chunk[part]


def share():
    return lax.axis_index("mp")


def grad_kernel(*refs):
    pieces, (out_weight, tops), refs = refs[:N_MP], refs[N_MP : N_MP + 2], refs[N_MP + 2 :]
    *outs, whole, heads = refs
    me = member()
    for step, piece in enumerate(pieces):
        whole[span(share() ^ step, piece.shape[0]), :] = piece[...]
    heads[...] = dot_nt(whole[...], out_weight[...]).astype(BF16)
    quarter = tops.shape[2]
    for step, out in zip(STEPS, outs):
        out[:BLOCK] = heads[:, columns(me ^ step)]
        for part in range(2):
            out[BLOCK + part * quarter : BLOCK + (part + 1) * quarter] = tops[me ^ step, part]


def project_kernel(*refs):
    chunks, out_weight, (kept, *sent, attended, whole) = refs[:GROUP], refs[GROUP], refs[GROUP + 2 :]
    me = member()
    for step, chunk in zip(STEPS, chunks):
        attended[:, columns(me ^ step)] = chunk[...]
    whole[...] = dot(attended[...], out_weight[...]).astype(BF16)
    rows = kept.shape[1]
    for far in range(2):
        kept[far] = whole[span(share() ^ (2 * far), rows), :]
        for part in range(2):
            half = rows // 2
            at = 2 * (share() ^ (2 * far + 1)) + part
            sent[2 * far + part][...] = whole[span(at, half), :]


def swapped(x, axis, step):
    return lax.ppermute(x, axis, [(i, i ^ step) for i in range(lax.axis_size(axis))])


def exchanged(chunks):
    return [chunks[0]] + [swapped(chunk, "seq", step) for step, chunk in zip(STEPS[1:], chunks[1:])]


def beside(arrays):
    count = lax.axis_size("seq")
    if len(arrays) == 1:
        return [swapped(arrays[0], "seq", GROUP)]
    up = [(i, i + GROUP) for i in range(count - GROUP)]
    down = [(j, i) for i, j in up]
    return [lax.ppermute(arrays[0], "seq", up), lax.ppermute(arrays[1], "seq", down)]


def crossed(arrays):
    count = lax.axis_size("seq")
    across = swapped(arrays[0], "seq", GROUP)
    if len(arrays) == 1:
        return [across]
    up = [(i, i + GROUP) for i in range(count - GROUP)]
    down = [(j, i) for i, j in up]
    return [across, lax.ppermute(arrays[1], "seq", up), lax.ppermute(arrays[2], "seq", down)]


def per_device(queries, keys, values, out_weight, out_grad):
    rows, width = queries.shape
    assert width == GROUP * HEAD_DIM and rows == BLOCK and lax.axis_size("mp") == N_MP
    count = lax.axis_size("seq")
    assert count % (2 * GROUP) == 0
    groups = count // GROUP
    nb = GROUP
    tokens = nb * rows
    half, quarter = rows // 2, rows // 4
    model = out_weight.shape[1]
    block = shape(2, rows, HEAD_DIM)
    sent = [shape(2 * REST + 2 * rows, HEAD_DIM)]
    if groups > 2:
        sent = [shape(2 * REST, HEAD_DIM)] + [shape(2 * rows, HEAD_DIM)] * 2
    rims = [block] * (1 if groups == 2 else 2)
    quarter = rows // 4
    in_order = shape(nb, rows, HEAD_DIM)
    score_flops = 2 * tokens * 5 * BLOCK * HEAD_DIM
    weight_flops = 2 * rows * out_weight.size

    chunk = shape(rows, HEAD_DIM)
    triple = shape(3, rows, HEAD_DIM)
    chunks = call(
        pack_kernel,
        [triple] * GROUP,
        (queries, keys, values),
        scratch=[pltpu.SemaphoreType.DMA((3 * GROUP,))],
        copied=GROUP,
        limit=53,
    )
    far = swapped(out_grad, "mp", 2)
    (tops,) = call(pool_kernel, [shape(GROUP, 2, quarter, HEAD_DIM)], chunks)
    chunks = exchanged(chunks)
    tops = swapped(tops, "seq", GROUP)
    arrays = (out_grad, far, out_weight)
    own_grad, far, out_weight = call(copy_kernel, [shape(*x.shape) for x in arrays], arrays)
    rim_blocks = beside(call(functools.partial(rim_kernel, groups), rims, chunks, flops=20 * score_flops))
    near, queries, level_1 = call(
        functools.partial(gather_kernel, nb),
        [
            shape(nb, 2, rows, HEAD_DIM),
            shape(nb, rows, HEAD_DIM),
            shape(2, tokens // 2, HEAD_DIM),
        ],
        chunks,
    )
    grad_chunks = call(
        grad_kernel,
        [shape(rows + 2 * quarter, HEAD_DIM)] * GROUP,
        (own_grad, swapped(own_grad, "mp", 1), far, swapped(far, "mp", 1), out_weight, tops),
        scratch=[pltpu.VMEM((rows, model), BF16), pltpu.VMEM((rows, width), BF16)],
        flops=weight_flops,
    )
    query, k_t, v_t, k1_t, v1_t, weights, stats = call(
        functools.partial(local_kernel, nb),
        [
            shape(3, nb, rows, HEAD_DIM),
            shape(HEAD_DIM, tokens),
            shape(HEAD_DIM, tokens),
            shape(HEAD_DIM, tokens // 2),
            shape(HEAD_DIM, tokens // 2),
            shape(nb, 4, BLOCK, BLOCK, dtype=F32),
            shape(8, tokens, dtype=F32),
        ],
        (near, queries, level_1, grad_chunks[0]),
        flops=score_flops,
    )
    grad_chunks = exchanged(grad_chunks)
    rim_square = shape(len(rims), BLOCK, BLOCK)
    prob, grads, top_2, deltas, far_shift, rim_shift, *refs = call(
        functools.partial(forward_kernel, nb, groups),
        [
            shape(nb, 4, BLOCK, BLOCK),
            in_order,
            block,
            shape(8, tokens, dtype=F32),
            shape(BLOCK, tokens),
            rim_square,
        ]
        + [chunk] * GROUP
        + sent,
        (query, v_t, v1_t, weights, stats, *rim_blocks, *grad_chunks),
        scratch=[
            pltpu.VMEM((nb, rows, HEAD_DIM), BF16),
            pltpu.VMEM((BLOCK, tokens), BF16),
            pltpu.VMEM(rim_square.shape, BF16),
            pltpu.VMEM((8, tokens), F32),
            pltpu.VMEM((HEAD_DIM, tokens), F32),
            pltpu.VMEM((2, BLOCK, HEAD_DIM), F32),
        ],
        flops=score_flops,
    )
    attended = exchanged(refs[:GROUP])
    rim_grads = refs[GROUP:]
    other_grads = crossed(rim_grads)
    grad_q, grad_kv = call(
        functools.partial(backward_kernel, nb, groups),
        [in_order, shape(2, nb, rows, HEAD_DIM, dtype=F32)],
        (query, near, level_1, k_t, k1_t, prob, grads, top_2, deltas, far_shift, rim_shift, *rim_blocks),
        scratch=[
            pltpu.VMEM((nb, 4, BLOCK, BLOCK), BF16),
            pltpu.VMEM((2, tokens // 2, HEAD_DIM), F32),
            pltpu.VMEM((HEAD_DIM, tokens), F32),
        ],
    )
    local = rows // N_MP
    kept, *given = call(
        project_kernel,
        [shape(2, local, model)] + [shape(local // 2, model)] * 4,
        (*attended, out_weight, grad_q),
        scratch=[pltpu.VMEM((rows, width), BF16), pltpu.VMEM((rows, model), BF16)],
    )
    *across, here = call(
        share_kernel,
        [shape(local // 2, model)] * 2 + [shape(local, model, dtype=F32)],
        (kept, *(swapped(piece, "mp", 1) for piece in given)),
    )
    chunks = call(
        functools.partial(combine_kernel, nb, groups),
        [triple] * GROUP,
        (grad_q, grad_kv, *other_grads),
        scratch=[pltpu.VMEM((nb, 2, rows, HEAD_DIM), BF16)],
        flops=20 * score_flops,
    )
    chunks = exchanged(chunks)
    across = [swapped(piece, "mp", 2) for piece in across]
    grad_k, grad_v, grad_q, mixed = call(
        unpack_kernel,
        [shape(rows, width)] * 3 + [shape(local, model)],
        (here, *across, *chunks),
    )
    return mixed, grad_q, grad_k, grad_v


def solution(mesh):
    return jax.shard_map(
        per_device,
        mesh=mesh,
        in_specs=(
            P("seq", "mp"),
            P("seq", "mp"),
            P("seq", "mp"),
            P("mp", None),
            P(("seq", "mp"), None),
        ),
        out_specs=(P(("seq", "mp"), None), P("seq", "mp"), P("seq", "mp"), P("seq", "mp")),
        check_vma=False,
    )
```

```python
import functools

import jax
import jax.numpy as jnp
from jax import lax
from jax.experimental import pallas as pl
from jax.experimental.pallas import tpu as pltpu
from jax.sharding import PartitionSpec as P

HEAD_DIM = 128
BLOCK = 256
REST = 3 * BLOCK // 4
LEVELS = 2
GROUP = 4
STEPS = (0, 3, 2, 1)
N_MP = 4
SCALE = HEAD_DIM**-0.5
LOG2E = 1.4426950408889634
BF16 = jnp.bfloat16
F32 = jnp.float32


def dot(a, b):
    return lax.dot_general(a, b, (((1,), (0,)), ((), ())), preferred_element_type=F32)


def dot_nt(a, b):
    return lax.dot_general(a, b, (((1,), (1,)), ((), ())), preferred_element_type=F32)


def shape(*dims, dtype=BF16):
    return jax.ShapeDtypeStruct(dims, dtype)


def call(kernel, out_shape, args, scratch=(), flops=0, limit=32, copied=0):
    whole = pl.BlockSpec(memory_space=pltpu.VMEM)
    kept = pl.BlockSpec(memory_space=pltpu.HBM)
    moved = sum(x.size * x.dtype.itemsize for x in (*args, *out_shape))
    return pl.pallas_call(
        kernel,
        out_shape=out_shape,
        in_specs=[kept if copied else whole] * len(args),
        out_specs=[kept] * copied + [whole] * (len(out_shape) - copied),
        scratch_shapes=scratch,
        compiler_params=pltpu.CompilerParams(vmem_limit_bytes=limit << 20),
        cost_estimate=pl.CostEstimate(flops=flops, bytes_accessed=moved if flops else 0, transcendentals=0),
    )(*args)


def columns(index):
    return pl.ds(pl.multiple_of(index * HEAD_DIM, HEAD_DIM), HEAD_DIM)


def span(index, size):
    start = index * size
    return pl.ds(start if isinstance(start, int) else pl.multiple_of(start, size), size)


def iota(dims, axis):
    return lax.broadcasted_iota(jnp.int32, dims, axis)


def averaging(level):
    dims = (BLOCK, BLOCK)
    same = (iota(dims, 0) >> level) == (iota(dims, 1) >> level)
    return jnp.where(same, 2.0**-level, 0.0).astype(BF16)


def pooling():
    dims = (BLOCK // 2, BLOCK)
    return jnp.where(iota(dims, 0) == (iota(dims, 1) >> 1), 0.5, 0.0).astype(BF16)


def spreading(level):
    dims = (BLOCK, BLOCK >> level)
    return jnp.where((iota(dims, 0) >> level) == iota(dims, 1), 2.0**-level, 0.0).astype(BF16)


def halves(x):
    high = x.astype(BF16)
    return high, (x - high.astype(F32)).astype(BF16)


def at_block(b):
    return slice(b * BLOCK, (b + 1) * BLOCK)


def sibling(b):
    return (b >> 1) ^ 1


def rim_present(groups):
    group = lax.axis_index("seq") // GROUP
    return group > 0, group < groups - 1


def member():
    return lax.rem(lax.axis_index("seq"), GROUP)


def columns(index):
    return pl.ds(pl.multiple_of(index * HEAD_DIM, HEAD_DIM), HEAD_DIM)


def pack_kernel(q, k, v, *refs):
    *outs, sems = refs
    me = member()
    copies = []
    for step, out in zip(STEPS, outs):
        for part, source in enumerate((k, v, q)):
            piece = source.at[:, columns(me ^ step)]
            copies.append(pltpu.make_async_copy(piece, out.at[part], sems.at[len(copies)]))
    for copy in copies:
        copy.start()
    for copy in copies:
        copy.wait()


def pool_kernel(*refs):
    *chunks, out = refs
    me = member()
    pool = pooling()
    half = BLOCK // 2
    for step, chunk in zip(STEPS, chunks):
        for part in range(2):
            once = dot(pool, chunk[part]).astype(BF16)
            out[me ^ step, part] = dot(pool[: half // 2, :half], once).astype(BF16)


def copy_kernel(out_grad, weight, low, high, out_grad_out, weight_out, far):
    out_grad_out[...] = out_grad[...]
    weight_out[...] = weight[...]
    half = low.shape[0]
    far[:half] = low[...]
    far[half:] = high[...]


def gather_kernel(nb, *refs):
    chunks, (near, queries, level_1) = refs[:GROUP], refs[GROUP:]
    me = member()
    for step, chunk in zip(STEPS, chunks):
        near[me ^ step] = chunk[:2]
        queries[me ^ step] = chunk[2]
    pool = pooling()
    half = BLOCK // 2
    for part in range(2):
        for b in range(nb):
            level_1[part, b * half : (b + 1) * half] = dot(pool, near[b, part]).astype(BF16)


def rim_kernel(groups, *refs):
    chunks, outs = refs[:GROUP], refs[GROUP:]
    me = member()
    members = [GROUP - 1, 0]
    if groups == 2:
        members = [jnp.where(lax.axis_index("seq") >= GROUP, 0, GROUP - 1)]
    for wanted, out in zip(members, outs):
        for step, chunk in zip(STEPS, chunks):

            @pl.when(me ^ step == wanted)
            def _():
                out[...] = chunk[:2]


def from_beside(groups, refs):
    if groups == 2:
        return (refs[0], refs[0]), refs[1:]
    return refs[:2], refs[2:]


def from_others(groups, refs):
    if groups == 2:
        return (refs[0].at[: 2 * REST], refs[0].at[2 * REST :], refs[0].at[2 * REST :]), refs[1:]
    return refs[:3], refs[3:]


def odd_group():
    return lax.rem(lax.axis_index("seq") // GROUP, 2)


def near_window(b, nb):
    sides = near_sides(b, nb)
    low, high = sides[0], sides[-1] + 1
    return slice(low, high), slice((b + low - 1) * BLOCK, (b + high - 1) * BLOCK)


def near_sides(b, nb):
    return [side for side in range(3) if 0 <= b + side - 1 < nb]


def local_kernel(nb, near, queries, level_1, _, query, k_t, v_t, k1_t, v1_t, weights, stats):
    even_1, even_2 = averaging(1), averaging(2)
    for b in range(nb):
        query[0, b] = queries[b]
        once = dot(even_1, queries[b]).astype(BF16)
        query[1, b] = once
        query[2, b] = dot(even_2, once).astype(BF16)
        for part, transposed in enumerate((k_t, v_t)):
            transposed[:, at_block(b)] = near[b, part].T
    for c in range(nb // 2):
        for part, transposed in enumerate((k1_t, v1_t)):
            transposed[:, at_block(c)] = level_1[part, at_block(c)].T
    for b in range(nb):
        sides = near_sides(b, nb)
        scores = [dot_nt(near[b + side - 1, 0], query[0, b]) * (SCALE * LOG2E) for side in sides]
        coarse = dot_nt(level_1[0, at_block(sibling(b))], query[1, b]) * (SCALE * LOG2E)
        top = coarse.max(0, keepdims=True)
        for score in scores:
            top = jnp.maximum(top, score.max(0, keepdims=True))
        weight = 2.0 * jnp.exp2(coarse - top)
        weights[b, 3] = weight
        total = weight.sum(0, keepdims=True)
        for side, score in zip(sides, scores):
            weight = jnp.exp2(score - top)
            weights[b, side] = weight
            total = total + weight.sum(0, keepdims=True)
        stats[:1, at_block(b)] = top
        stats[1:2, at_block(b)] = total


def rims_of(nb, groups, low, high):
    group = lax.axis_index("seq") // GROUP
    if groups == 2:
        return [(jnp.where(group > 0, 0, nb - 1), low, None)]
    return [(0, low, group > 0), (nb - 1, high, group < groups - 1)]


def forward_kernel(nb, groups, *refs):
    (query, v_t, v1_t, weights, stats), refs = refs[:5], refs[5:]
    (rim_low, rim_high), refs = from_beside(groups, refs)
    chunks, refs = refs[:GROUP], refs[GROUP:]
    (prob, grads, top_2, deltas, far_shift, rim_shift), refs = refs[:6], refs[6:]
    outs, (*rim_outs, attended, far_prob, rim_prob, row, context_t, far_sums) = refs[:GROUP], refs[GROUP:]
    rims = rims_of(nb, groups, rim_low, rim_high)
    me = member()
    quarter = BLOCK // 4
    tokens = nb * BLOCK
    for step, chunk in zip(STEPS, chunks):
        grads[me ^ step] = chunk[:BLOCK]
        for part in range(2):
            level = chunk[BLOCK + part * quarter : BLOCK + (part + 1) * quarter]
            top_2[part, span(me ^ step, quarter), :] = level
    coarse_query = query[2].reshape(tokens, HEAD_DIM)
    coarse = dot_nt(top_2[0], coarse_query) * (SCALE * LOG2E)
    row[:1] = jnp.maximum(stats[:1], coarse.max(0, keepdims=True))
    scores = []
    for b, block, present in rims:
        score = dot_nt(block[0], query[0, b]) * (SCALE * LOG2E)
        if present is not None:
            score = jnp.where(present, score, -jnp.inf)
        at = span(b, BLOCK)
        row[:1, at] = jnp.maximum(row[:1, at], score.max(0, keepdims=True))
        scores.append(score)
    top = row[:1]
    shrink = jnp.exp2(stats[:1] - top)
    far = 4.0 * jnp.exp2(coarse - top)
    row[1:2] = shrink * stats[1:2] + far.sum(0, keepdims=True)
    fresh = []
    for (b, _, _), score in zip(rims, scores):
        at = span(b, BLOCK)
        fresh.append(jnp.exp2(score - row[:1, at]))
        row[1:2, at] += fresh[-1].sum(0, keepdims=True)
    inverse = 1.0 / row[1:2]
    row[2:3] = inverse
    row[3:4] = shrink * inverse
    far_prob[...] = (far * inverse).astype(BF16)
    context_t[...] = dot(top_2[1].T, far_prob[...])
    for i, (b, block, _) in enumerate(rims):
        at = span(b, BLOCK)
        rim_prob[i] = (fresh[i] * row[2:3, at]).astype(BF16)
        context_t[:, at] += dot(block[1].T, rim_prob[i])
    for b in range(nb):
        shrink = row[3:4, at_block(b)]
        prob[b, 3] = (weights[b, 3] * shrink).astype(BF16)
        context = context_t[:, at_block(b)] + dot(v1_t[:, at_block(sibling(b))], prob[b, 3])
        sides, keys = near_window(b, nb)
        parts = (weights[b, sides] * shrink).astype(BF16)
        prob[b, sides] = parts
        context = context + dot(v_t[:, keys], parts.reshape(-1, BLOCK))
        attended[b] = context.T.astype(BF16)
        deltas[:1, at_block(b)] = (grads[b].T.astype(F32) * context).sum(0, keepdims=True)
    grad = grads[...].reshape(tokens, HEAD_DIM)
    slope = dot_nt(top_2[1], grad)
    far_shift[...] = (far_prob[...].astype(F32) * (slope - deltas[:1])).astype(BF16)
    far_sums[0] = SCALE * dot(far_shift[...], coarse_query)
    far_sums[1] = dot(far_prob[...], grad)
    odd = odd_group()
    spread = spreading(2)
    folded = []
    for part in range(2):
        rest = far_sums[part, pl.ds(pl.multiple_of((1 - odd) * quarter, quarter), REST), :]
        rim_outs[0][part * REST : (part + 1) * REST] = rest.astype(BF16)
        high, low = halves(far_sums[part, pl.ds(pl.multiple_of(odd * REST, quarter), quarter), :])
        folded.append(dot(spread, high) + dot(spread, low))
    pairs = []
    for i, (b, block, _) in enumerate(rims):
        slope = dot_nt(block[1], grads[b])
        rim_shift[i] = (rim_prob[i].astype(F32) * (slope - deltas[:1, span(b, BLOCK)])).astype(BF16)
        pairs.append((SCALE * dot(rim_shift[i], query[0, b]), dot(rim_prob[i], grads[b])))
    for part in range(2):
        at = slice(part * BLOCK, (part + 1) * BLOCK)
        if groups == 2:
            rim_outs[0][2 * REST + part * BLOCK : 2 * REST + (part + 1) * BLOCK] = (
                pairs[0][part] + folded[part]
            ).astype(BF16)
        else:
            rim_outs[1][at] = (pairs[1][part] + jnp.where(odd == 0, folded[part], 0.0)).astype(BF16)
            rim_outs[2][at] = (pairs[0][part] + jnp.where(odd == 1, folded[part], 0.0)).astype(BF16)
    for step, out in zip(STEPS, outs):
        out[...] = attended[me ^ step]


def backward_kernel(nb, groups, *refs):
    (query, near, level_1, k_t, k1_t, prob, grads, top_2, deltas, far_shift, rim_shift), refs = refs[:11], refs[11:]
    (rim_low, rim_high), refs = from_beside(groups, refs)
    grad_q, grad_kv, shift, sums_1, query_t = refs
    even_1, even_2 = averaging(1), averaging(2)
    coarse = dot(top_2[0].T, far_shift[...])
    for b in range(nb):
        high, low = halves(coarse[:, at_block(b)])
        query_t[:, at_block(b)] = dot(high, even_2) + dot(low, even_2)
    for i, (b, block, _) in enumerate(rims_of(nb, groups, rim_low, rim_high)):
        query_t[:, span(b, BLOCK)] += dot(block[0].T, rim_shift[i])
    for b in range(nb):
        grad, delta = grads[b], deltas[:1, at_block(b)]
        grad_t = query_t[:, at_block(b)]
        for side in near_sides(b, nb):
            slope = dot_nt(near[b + side - 1, 1], grad)
            part = (prob[b, side].astype(F32) * (slope - delta)).astype(BF16)
            shift[b, side] = part
            grad_t = grad_t + dot(k_t[:, at_block(b + side - 1)], part)
        slope = dot_nt(level_1[1, at_block(sibling(b))], grad)
        part = (prob[b, 3].astype(F32) * (slope - delta)).astype(BF16)
        shift[b, 3] = part
        high, low = halves(dot(k1_t[:, at_block(sibling(b))], part))
        grad_t = grad_t + (dot(high, even_1) + dot(low, even_1))
        grad_q[b] = (SCALE * grad_t).T.astype(BF16)
    for c in range(nb // 2):
        users = [b for b in range(nb) if sibling(b) == c]
        sums_1[0, at_block(c)] = SCALE * sum(dot(shift[b, 3], query[1, b]) for b in users)
        sums_1[1, at_block(c)] = sum(dot(prob[b, 3], grads[b]) for b in users)
    spread = spreading(1)
    half = BLOCK // 2
    for s in range(nb):
        users = [(s + 1 - side, side) for side in range(3) if 0 <= s + 1 - side < nb]
        key = SCALE * sum(dot(shift[b, side], query[0, b]) for b, side in users)
        value = sum(dot(prob[b, side], grads[b]) for b, side in users)
        for part, total in enumerate((key, value)):
            high, low = halves(sums_1[part, s * half : (s + 1) * half])
            grad_kv[part, s] = total + (dot(spread, high) + dot(spread, low))


def share_kernel(kept, *refs):
    *got, across_0, across_1, here = refs
    half = across_0.shape[0]
    for i, piece in enumerate(got):
        far, at = i // 2, pl.ds(i % 2 * half, half)
        total = kept[far, at, :].astype(F32) + piece[...].astype(F32)
        if far:
            (across_0, across_1)[i % 2][...] = total.astype(BF16)
        else:
            here[at, :] = total


def combine_kernel(nb, groups, grad_q, grad_kv, *refs):
    (got_top, got_low, got_high), (*outs, out) = from_others(groups, refs)
    present = rim_present(groups)
    spread = spreading(2)
    quarter = BLOCK // 4
    odd = odd_group()
    for b in range(nb):
        for part in range(2):
            total = grad_kv[part, b]
            place = 0 if b == 0 else 2 if b == nb - 1 else b - odd
            level = dot(spread, got_top[span(part * (REST // quarter) + place, quarter), :])
            rim = slice(part * BLOCK, (part + 1) * BLOCK)
            if b == 0:
                level = jnp.where(odd == 0, level, 0.0)
                total = total + jnp.where(present[0], got_low[rim].astype(F32), 0.0)
            if b == nb - 1:
                level = jnp.where(odd == 1, level, 0.0)
                total = total + jnp.where(present[1], got_high[rim].astype(F32), 0.0)
            total = total + level
            out[b, part] = total.astype(BF16)
    me = member()
    for step, chunk in zip(STEPS, outs):
        chunk[:2] = out[me ^ step]
        chunk[2] = grad_q[me ^ step]


def unpack_kernel(*refs):
    here, across_0, across_1, *refs = refs
    chunks, (*outs, mixed) = refs[:GROUP], refs[GROUP:]
    half = across_0.shape[0]
    for part, across in enumerate((across_0, across_1)):
        at = pl.ds(part * half, half)
        mixed[at, :] = (here[at, :] + across[...].astype(F32)).astype(BF16)
    me = member()
    for step, chunk in zip(STEPS, chunks):
        at = columns(me ^ step)
        for part, out in enumerate(outs):
            out[:, at] = chunk[part]


def share():
    return lax.axis_index("mp")


def grad_kernel(*refs):
    pieces, (out_weight, tops), refs = refs[:N_MP], refs[N_MP : N_MP + 2], refs[N_MP + 2 :]
    *outs, whole, heads = refs
    me = member()
    for step, piece in enumerate(pieces):
        whole[span(share() ^ step, piece.shape[0]), :] = piece[...]
    heads[...] = dot_nt(whole[...], out_weight[...]).astype(BF16)
    quarter = tops.shape[2]
    for step, out in zip(STEPS, outs):
        out[:BLOCK] = heads[:, columns(me ^ step)]
        for part in range(2):
            out[BLOCK + part * quarter : BLOCK + (part + 1) * quarter] = tops[me ^ step, part]


def project_kernel(*refs):
    chunks, out_weight, (kept, *sent, attended, whole) = refs[:GROUP], refs[GROUP], refs[GROUP + 2 :]
    me = member()
    for step, chunk in zip(STEPS, chunks):
        attended[:, columns(me ^ step)] = chunk[...]
    whole[...] = dot(attended[...], out_weight[...]).astype(BF16)
    rows = kept.shape[1]
    for far in range(2):
        kept[far] = whole[span(share() ^ (2 * far), rows), :]
        for part in range(2):
            half = rows // 2
            at = 2 * (share() ^ (2 * far + 1)) + part
            sent[2 * far + part][...] = whole[span(at, half), :]


def swapped(x, axis, step):
    return lax.ppermute(x, axis, [(i, i ^ step) for i in range(lax.axis_size(axis))])


def exchanged(chunks):
    return [chunks[0]] + [swapped(chunk, "seq", step) for step, chunk in zip(STEPS[1:], chunks[1:])]


def beside(arrays):
    count = lax.axis_size("seq")
    if len(arrays) == 1:
        return [swapped(arrays[0], "seq", GROUP)]
    up = [(i, i + GROUP) for i in range(count - GROUP)]
    down = [(j, i) for i, j in up]
    return [lax.ppermute(arrays[0], "seq", up), lax.ppermute(arrays[1], "seq", down)]


def crossed(arrays):
    count = lax.axis_size("seq")
    across = swapped(arrays[0], "seq", GROUP)
    if len(arrays) == 1:
        return [across]
    up = [(i, i + GROUP) for i in range(count - GROUP)]
    down = [(j, i) for i, j in up]
    return [across, lax.ppermute(arrays[1], "seq", up), lax.ppermute(arrays[2], "seq", down)]


def per_device(queries, keys, values, out_weight, out_grad):
    rows, width = queries.shape
    assert width == GROUP * HEAD_DIM and rows == BLOCK and lax.axis_size("mp") == N_MP
    count = lax.axis_size("seq")
    assert count % (2 * GROUP) == 0
    groups = count // GROUP
    nb = GROUP
    tokens = nb * rows
    half, quarter = rows // 2, rows // 4
    model = out_weight.shape[1]
    block = shape(2, rows, HEAD_DIM)
    sent = [shape(2 * REST + 2 * rows, HEAD_DIM)]
    if groups > 2:
        sent = [shape(2 * REST, HEAD_DIM)] + [shape(2 * rows, HEAD_DIM)] * 2
    rims = [block] * (1 if groups == 2 else 2)
    quarter = rows // 4
    in_order = shape(nb, rows, HEAD_DIM)
    score_flops = 2 * tokens * 5 * BLOCK * HEAD_DIM
    weight_flops = 2 * rows * out_weight.size

    chunk = shape(rows, HEAD_DIM)
    triple = shape(3, rows, HEAD_DIM)
    chunks = call(
        pack_kernel,
        [triple] * GROUP,
        (queries, keys, values),
        scratch=[pltpu.SemaphoreType.DMA((3 * GROUP,))],
        copied=GROUP,
        limit=53,
    )
    half = out_grad.shape[0] // 2
    far = [swapped(piece, "mp", 2) for piece in (out_grad[:half], out_grad[half:])]
    (tops,) = call(pool_kernel, [shape(GROUP, 2, quarter, HEAD_DIM)], chunks)
    chunks = exchanged(chunks)
    tops = swapped(tops, "seq", GROUP)
    arrays = (out_grad, out_weight, *far)
    own_grad, out_weight, far = call(
        copy_kernel, [shape(*x.shape) for x in (out_grad, out_weight, out_grad)], arrays
    )
    rim_blocks = beside(call(functools.partial(rim_kernel, groups), rims, chunks, flops=20 * score_flops))
    near, queries, level_1 = call(
        functools.partial(gather_kernel, nb),
        [
            shape(nb, 2, rows, HEAD_DIM),
            shape(nb, rows, HEAD_DIM),
            shape(2, tokens // 2, HEAD_DIM),
        ],
        chunks,
    )
    grad_chunks = call(
        grad_kernel,
        [shape(rows + 2 * quarter, HEAD_DIM)] * GROUP,
        (own_grad, swapped(own_grad, "mp", 1), far, swapped(far, "mp", 1), out_weight, tops),
        scratch=[pltpu.VMEM((rows, model), BF16), pltpu.VMEM((rows, width), BF16)],
        flops=weight_flops,
    )
    query, k_t, v_t, k1_t, v1_t, weights, stats = call(
        functools.partial(local_kernel, nb),
        [
            shape(3, nb, rows, HEAD_DIM),
            shape(HEAD_DIM, tokens),
            shape(HEAD_DIM, tokens),
            shape(HEAD_DIM, tokens // 2),
            shape(HEAD_DIM, tokens // 2),
            shape(nb, 4, BLOCK, BLOCK, dtype=F32),
            shape(8, tokens, dtype=F32),
        ],
        (near, queries, level_1, grad_chunks[0]),
        flops=score_flops,
    )
    grad_chunks = exchanged(grad_chunks)
    rim_square = shape(len(rims), BLOCK, BLOCK)
    prob, grads, top_2, deltas, far_shift, rim_shift, *refs = call(
        functools.partial(forward_kernel, nb, groups),
        [
            shape(nb, 4, BLOCK, BLOCK),
            in_order,
            block,
            shape(8, tokens, dtype=F32),
            shape(BLOCK, tokens),
            rim_square,
        ]
        + [chunk] * GROUP
        + sent,
        (query, v_t, v1_t, weights, stats, *rim_blocks, *grad_chunks),
        scratch=[
            pltpu.VMEM((nb, rows, HEAD_DIM), BF16),
            pltpu.VMEM((BLOCK, tokens), BF16),
            pltpu.VMEM(rim_square.shape, BF16),
            pltpu.VMEM((8, tokens), F32),
            pltpu.VMEM((HEAD_DIM, tokens), F32),
            pltpu.VMEM((2, BLOCK, HEAD_DIM), F32),
        ],
        flops=score_flops,
    )
    attended = exchanged(refs[:GROUP])
    rim_grads = refs[GROUP:]
    other_grads = crossed(rim_grads)
    grad_q, grad_kv = call(
        functools.partial(backward_kernel, nb, groups),
        [in_order, shape(2, nb, rows, HEAD_DIM, dtype=F32)],
        (query, near, level_1, k_t, k1_t, prob, grads, top_2, deltas, far_shift, rim_shift, *rim_blocks),
        scratch=[
            pltpu.VMEM((nb, 4, BLOCK, BLOCK), BF16),
            pltpu.VMEM((2, tokens // 2, HEAD_DIM), F32),
            pltpu.VMEM((HEAD_DIM, tokens), F32),
        ],
    )
    local = rows // N_MP
    kept, *given = call(
        project_kernel,
        [shape(2, local, model)] + [shape(local // 2, model)] * 4,
        (*attended, out_weight, grad_q),
        scratch=[pltpu.VMEM((rows, width), BF16), pltpu.VMEM((rows, model), BF16)],
    )
    *across, here = call(
        share_kernel,
        [shape(local // 2, model)] * 2 + [shape(local, model, dtype=F32)],
        (kept, *(swapped(piece, "mp", 1) for piece in given)),
    )
    chunks = call(
        functools.partial(combine_kernel, nb, groups),
        [triple] * GROUP,
        (grad_q, grad_kv, *other_grads),
        scratch=[pltpu.VMEM((nb, 2, rows, HEAD_DIM), BF16)],
        flops=20 * score_flops,
    )
    chunks = exchanged(chunks)
    across = [swapped(piece, "mp", 2) for piece in across]
    grad_k, grad_v, grad_q, mixed = call(
        unpack_kernel,
        [shape(rows, width)] * 3 + [shape(local, model)],
        (here, *across, *chunks),
    )
    return mixed, grad_q, grad_k, grad_v


def solution(mesh):
    return jax.shard_map(
        per_device,
        mesh=mesh,
        in_specs=(
            P("seq", "mp"),
            P("seq", "mp"),
            P("seq", "mp"),
            P("mp", None),
            P(("seq", "mp"), None),
        ),
        out_specs=(P(("seq", "mp"), None), P("seq", "mp"), P("seq", "mp"), P("seq", "mp")),
        check_vma=False,
    )
```

```python
import functools

import jax
import jax.numpy as jnp
from jax import lax
from jax.experimental import pallas as pl
from jax.experimental.pallas import tpu as pltpu
from jax.sharding import PartitionSpec as P

HEAD_DIM = 128
BLOCK = 256
REST = 3 * BLOCK // 4
LEVELS = 2
GROUP = 4
STEPS = (0, 3, 2, 1)
N_MP = 4
SCALE = HEAD_DIM**-0.5
LOG2E = 1.4426950408889634
BF16 = jnp.bfloat16
F32 = jnp.float32


def dot(a, b):
    return lax.dot_general(a, b, (((1,), (0,)), ((), ())), preferred_element_type=F32)


def dot_nt(a, b):
    return lax.dot_general(a, b, (((1,), (1,)), ((), ())), preferred_element_type=F32)


def shape(*dims, dtype=BF16):
    return jax.ShapeDtypeStruct(dims, dtype)


def call(kernel, out_shape, args, scratch=(), flops=0, limit=32, copied=0):
    whole = pl.BlockSpec(memory_space=pltpu.VMEM)
    kept = pl.BlockSpec(memory_space=pltpu.HBM)
    moved = sum(x.size * x.dtype.itemsize for x in (*args, *out_shape))
    return pl.pallas_call(
        kernel,
        out_shape=out_shape,
        in_specs=[kept if copied else whole] * len(args),
        out_specs=[kept] * copied + [whole] * (len(out_shape) - copied),
        scratch_shapes=scratch,
        compiler_params=pltpu.CompilerParams(vmem_limit_bytes=limit << 20),
        cost_estimate=pl.CostEstimate(flops=flops, bytes_accessed=moved if flops else 0, transcendentals=0),
    )(*args)


def columns(index):
    return pl.ds(pl.multiple_of(index * HEAD_DIM, HEAD_DIM), HEAD_DIM)


def span(index, size):
    start = index * size
    return pl.ds(start if isinstance(start, int) else pl.multiple_of(start, size), size)


def iota(dims, axis):
    return lax.broadcasted_iota(jnp.int32, dims, axis)


def averaging(level):
    dims = (BLOCK, BLOCK)
    same = (iota(dims, 0) >> level) == (iota(dims, 1) >> level)
    return jnp.where(same, 2.0**-level, 0.0).astype(BF16)


def pooling():
    dims = (BLOCK // 2, BLOCK)
    return jnp.where(iota(dims, 0) == (iota(dims, 1) >> 1), 0.5, 0.0).astype(BF16)


def spreading(level):
    dims = (BLOCK, BLOCK >> level)
    return jnp.where((iota(dims, 0) >> level) == iota(dims, 1), 2.0**-level, 0.0).astype(BF16)


def halves(x):
    high = x.astype(BF16)
    return high, (x - high.astype(F32)).astype(BF16)


def at_block(b):
    return slice(b * BLOCK, (b + 1) * BLOCK)


def sibling(b):
    return (b >> 1) ^ 1


def rim_present(groups):
    group = lax.axis_index("seq") // GROUP
    return group > 0, group < groups - 1


def member():
    return lax.rem(lax.axis_index("seq"), GROUP)


def columns(index):
    return pl.ds(pl.multiple_of(index * HEAD_DIM, HEAD_DIM), HEAD_DIM)


def pack_kernel(q, k, v, *refs):
    *outs, sems = refs
    me = member()
    copies = []
    for step, out in zip(STEPS, outs):
        for part, source in enumerate((k, v, q)):
            piece = source.at[:, columns(me ^ step)]
            copies.append(pltpu.make_async_copy(piece, out.at[part], sems.at[len(copies)]))
    for copy in copies:
        copy.start()
    for copy in copies:
        copy.wait()


def copy_kernel(out_grad, weight, low, high, out_grad_out, weight_out, far):
    out_grad_out[...] = out_grad[...]
    weight_out[...] = weight[...]
    half = low.shape[0]
    far[:half] = low[...]
    far[half:] = high[...]


def gather_kernel(nb, *refs):
    chunks, (near, queries, level_1) = refs[:GROUP], refs[GROUP:]
    me = member()
    for step, chunk in zip(STEPS, chunks):
        near[me ^ step] = chunk[:2]
        queries[me ^ step] = chunk[2]
    pool = pooling()
    half = BLOCK // 2
    for part in range(2):
        for b in range(nb):
            level_1[part, b * half : (b + 1) * half] = dot(pool, near[b, part]).astype(BF16)


def pooled_twice(rows):
    pool = pooling()
    half = BLOCK // 2
    once = dot(pool, rows).astype(BF16)
    return dot(pool[: half // 2, :half], once).astype(BF16)


def cross_kernel(groups, *refs):
    chunks, (top, *outs, levels) = refs[:GROUP], refs[GROUP:]
    me = member()
    quarter = BLOCK // 4
    side_by_side = [chunk[part] for chunk in chunks for part in range(2)]
    pooled = pooled_twice(jnp.concatenate(side_by_side, axis=1))
    for i, step in enumerate(STEPS):
        for part in range(2):
            at = (2 * i + part) * HEAD_DIM
            levels[part, span(me ^ step, quarter), :] = pooled[:, at : at + HEAD_DIM]
    odd = odd_group()
    for part in range(2):
        rest = levels[part, pl.ds(pl.multiple_of(odd * quarter, quarter), REST), :]
        top[part * REST : (part + 1) * REST] = rest
    members = [(GROUP - 1, outs[0], 0), (0, outs[1], 0)] if groups > 2 else [
        (jnp.where(odd == 1, 0, GROUP - 1), top, 2 * REST)
    ]
    for wanted, out, start in members:
        for step, chunk in zip(STEPS, chunks):

            @pl.when(me ^ step == wanted)
            def _():
                for part in range(2):
                    at = start + part * BLOCK
                    out[at : at + BLOCK] = chunk[part]


def from_others(groups, refs):
    if groups == 2:
        return (refs[0].at[: 2 * REST], refs[0].at[2 * REST :], refs[0].at[2 * REST :]), refs[1:]
    return refs[:3], refs[3:]


def odd_group():
    return lax.rem(lax.axis_index("seq") // GROUP, 2)


def near_window(b, nb):
    sides = near_sides(b, nb)
    low, high = sides[0], sides[-1] + 1
    return slice(low, high), slice((b + low - 1) * BLOCK, (b + high - 1) * BLOCK)


def near_sides(b, nb):
    return [side for side in range(3) if 0 <= b + side - 1 < nb]


def local_kernel(nb, near, queries, level_1, _, query, k_t, v_t, k1_t, v1_t, weights, stats):
    even_1, even_2 = averaging(1), averaging(2)
    for b in range(nb):
        query[0, b] = queries[b]
        once = dot(even_1, queries[b]).astype(BF16)
        query[1, b] = once
        query[2, b] = dot(even_2, once).astype(BF16)
        for part, transposed in enumerate((k_t, v_t)):
            transposed[:, at_block(b)] = near[b, part].T
    for c in range(nb // 2):
        for part, transposed in enumerate((k1_t, v1_t)):
            transposed[:, at_block(c)] = level_1[part, at_block(c)].T
    for b in range(nb):
        sides = near_sides(b, nb)
        scores = [dot_nt(near[b + side - 1, 0], query[0, b]) * (SCALE * LOG2E) for side in sides]
        coarse = dot_nt(level_1[0, at_block(sibling(b))], query[1, b]) * (SCALE * LOG2E)
        top = coarse.max(0, keepdims=True)
        for score in scores:
            top = jnp.maximum(top, score.max(0, keepdims=True))
        weight = 2.0 * jnp.exp2(coarse - top)
        weights[b, 3] = weight
        total = weight.sum(0, keepdims=True)
        for side, score in zip(sides, scores):
            weight = jnp.exp2(score - top)
            weights[b, side] = weight
            total = total + weight.sum(0, keepdims=True)
        stats[:1, at_block(b)] = top
        stats[1:2, at_block(b)] = total


def rims_of(nb, groups, low, high):
    group = lax.axis_index("seq") // GROUP
    if groups == 2:
        return [(jnp.where(group > 0, 0, nb - 1), low, None)]
    return [(0, low, group > 0), (nb - 1, high, group < groups - 1)]


def forward_kernel(nb, groups, *refs):
    (query, v_t, v1_t, weights, stats), refs = refs[:5], refs[5:]
    (got_top, rim_low, rim_high), refs = from_others(groups, refs)
    chunks, refs = refs[:GROUP], refs[GROUP:]
    (prob, grads, top_2, deltas, far_shift, rim_shift), refs = refs[:6], refs[6:]
    outs, (*rim_outs, attended, far_prob, rim_prob, row, context_t, far_sums) = refs[:GROUP], refs[GROUP:]
    rims = rims_of(nb, groups, rim_low, rim_high)
    me = member()
    quarter = BLOCK // 4
    tokens = nb * BLOCK
    for step, chunk in zip(STEPS, chunks):
        grads[me ^ step] = chunk[...]
    odd = odd_group()
    for part in range(2):
        at = slice(part * BLOCK, (part + 1) * BLOCK)
        beside_me = jnp.where(odd == 1, rim_low[at], rim_high[at]) if groups > 2 else rim_low[at]
        rest = pl.ds(pl.multiple_of((1 - odd) * quarter, quarter), REST)
        top_2[part, rest, :] = got_top[part * REST : (part + 1) * REST]
        top_2[part, pl.ds(pl.multiple_of(odd * REST, quarter), quarter), :] = pooled_twice(beside_me)
    coarse_query = query[2].reshape(tokens, HEAD_DIM)
    coarse = dot_nt(top_2[0], coarse_query) * (SCALE * LOG2E)
    row[:1] = jnp.maximum(stats[:1], coarse.max(0, keepdims=True))
    scores = []
    for b, block, present in rims:
        score = dot_nt(block[:BLOCK], query[0, b]) * (SCALE * LOG2E)
        if present is not None:
            score = jnp.where(present, score, -jnp.inf)
        at = span(b, BLOCK)
        row[:1, at] = jnp.maximum(row[:1, at], score.max(0, keepdims=True))
        scores.append(score)
    top = row[:1]
    shrink = jnp.exp2(stats[:1] - top)
    far = 4.0 * jnp.exp2(coarse - top)
    row[1:2] = shrink * stats[1:2] + far.sum(0, keepdims=True)
    fresh = []
    for (b, _, _), score in zip(rims, scores):
        at = span(b, BLOCK)
        fresh.append(jnp.exp2(score - row[:1, at]))
        row[1:2, at] += fresh[-1].sum(0, keepdims=True)
    inverse = 1.0 / row[1:2]
    row[2:3] = inverse
    row[3:4] = shrink * inverse
    far_prob[...] = (far * inverse).astype(BF16)
    context_t[...] = dot(top_2[1].T, far_prob[...])
    for i, (b, block, _) in enumerate(rims):
        at = span(b, BLOCK)
        rim_prob[i] = (fresh[i] * row[2:3, at]).astype(BF16)
        context_t[:, at] += dot(block[BLOCK:].T, rim_prob[i])
    for b in range(nb):
        shrink = row[3:4, at_block(b)]
        prob[b, 3] = (weights[b, 3] * shrink).astype(BF16)
        context = context_t[:, at_block(b)] + dot(v1_t[:, at_block(sibling(b))], prob[b, 3])
        sides, keys = near_window(b, nb)
        parts = (weights[b, sides] * shrink).astype(BF16)
        prob[b, sides] = parts
        context = context + dot(v_t[:, keys], parts.reshape(-1, BLOCK))
        attended[b] = context.T.astype(BF16)
        deltas[:1, at_block(b)] = (grads[b].T.astype(F32) * context).sum(0, keepdims=True)
    grad = grads[...].reshape(tokens, HEAD_DIM)
    slope = dot_nt(top_2[1], grad)
    far_shift[...] = (far_prob[...].astype(F32) * (slope - deltas[:1])).astype(BF16)
    far_sums[0] = SCALE * dot(far_shift[...], coarse_query)
    far_sums[1] = dot(far_prob[...], grad)
    spread = spreading(2)
    folded = []
    for part in range(2):
        rest = far_sums[part, pl.ds(pl.multiple_of((1 - odd) * quarter, quarter), REST), :]
        rim_outs[0][part * REST : (part + 1) * REST] = rest.astype(BF16)
        high, low = halves(far_sums[part, pl.ds(pl.multiple_of(odd * REST, quarter), quarter), :])
        folded.append(dot(spread, high) + dot(spread, low))
    pairs = []
    for i, (b, block, _) in enumerate(rims):
        slope = dot_nt(block[BLOCK:], grads[b])
        rim_shift[i] = (rim_prob[i].astype(F32) * (slope - deltas[:1, span(b, BLOCK)])).astype(BF16)
        pairs.append((SCALE * dot(rim_shift[i], query[0, b]), dot(rim_prob[i], grads[b])))
    for part in range(2):
        at = slice(part * BLOCK, (part + 1) * BLOCK)
        if groups == 2:
            rim_outs[0][2 * REST + part * BLOCK : 2 * REST + (part + 1) * BLOCK] = (
                pairs[0][part] + folded[part]
            ).astype(BF16)
        else:
            rim_outs[1][at] = (pairs[1][part] + jnp.where(odd == 0, folded[part], 0.0)).astype(BF16)
            rim_outs[2][at] = (pairs[0][part] + jnp.where(odd == 1, folded[part], 0.0)).astype(BF16)
    for step, out in zip(STEPS, outs):
        out[...] = attended[me ^ step]


def backward_kernel(nb, groups, *refs):
    (query, near, level_1, k_t, k1_t, prob, grads, top_2, deltas, far_shift, rim_shift), refs = refs[:11], refs[11:]
    (_, rim_low, rim_high), refs = from_others(groups, refs)
    grad_q, grad_kv, shift, sums_1, query_t = refs
    even_1, even_2 = averaging(1), averaging(2)
    coarse = dot(top_2[0].T, far_shift[...])
    for b in range(nb):
        high, low = halves(coarse[:, at_block(b)])
        query_t[:, at_block(b)] = dot(high, even_2) + dot(low, even_2)
    for i, (b, block, _) in enumerate(rims_of(nb, groups, rim_low, rim_high)):
        query_t[:, span(b, BLOCK)] += dot(block[:BLOCK].T, rim_shift[i])
    for b in range(nb):
        grad, delta = grads[b], deltas[:1, at_block(b)]
        grad_t = query_t[:, at_block(b)]
        for side in near_sides(b, nb):
            slope = dot_nt(near[b + side - 1, 1], grad)
            part = (prob[b, side].astype(F32) * (slope - delta)).astype(BF16)
            shift[b, side] = part
            grad_t = grad_t + dot(k_t[:, at_block(b + side - 1)], part)
        slope = dot_nt(level_1[1, at_block(sibling(b))], grad)
        part = (prob[b, 3].astype(F32) * (slope - delta)).astype(BF16)
        shift[b, 3] = part
        high, low = halves(dot(k1_t[:, at_block(sibling(b))], part))
        grad_t = grad_t + (dot(high, even_1) + dot(low, even_1))
        grad_q[b] = (SCALE * grad_t).T.astype(BF16)
    for c in range(nb // 2):
        users = [b for b in range(nb) if sibling(b) == c]
        sums_1[0, at_block(c)] = SCALE * sum(dot(shift[b, 3], query[1, b]) for b in users)
        sums_1[1, at_block(c)] = sum(dot(prob[b, 3], grads[b]) for b in users)
    spread = spreading(1)
    half = BLOCK // 2
    for s in range(nb):
        users = [(s + 1 - side, side) for side in range(3) if 0 <= s + 1 - side < nb]
        key = SCALE * sum(dot(shift[b, side], query[0, b]) for b, side in users)
        value = sum(dot(prob[b, side], grads[b]) for b, side in users)
        for part, total in enumerate((key, value)):
            high, low = halves(sums_1[part, s * half : (s + 1) * half])
            grad_kv[part, s] = total + (dot(spread, high) + dot(spread, low))


def share_kernel(kept, *refs):
    *got, across_0, across_1, here = refs
    half = across_0.shape[0]
    for i, piece in enumerate(got):
        far, at = i // 2, pl.ds(i % 2 * half, half)
        total = kept[far, at, :].astype(F32) + piece[...].astype(F32)
        if far:
            (across_0, across_1)[i % 2][...] = total.astype(BF16)
        else:
            here[at, :] = total


def combine_kernel(nb, groups, grad_q, grad_kv, *refs):
    (got_top, got_low, got_high), (*outs, out) = from_others(groups, refs)
    present = rim_present(groups)
    spread = spreading(2)
    quarter = BLOCK // 4
    odd = odd_group()
    for b in range(nb):
        for part in range(2):
            total = grad_kv[part, b]
            place = 0 if b == 0 else 2 if b == nb - 1 else b - odd
            level = dot(spread, got_top[span(part * (REST // quarter) + place, quarter), :])
            rim = slice(part * BLOCK, (part + 1) * BLOCK)
            if b == 0:
                level = jnp.where(odd == 0, level, 0.0)
                total = total + jnp.where(present[0], got_low[rim].astype(F32), 0.0)
            if b == nb - 1:
                level = jnp.where(odd == 1, level, 0.0)
                total = total + jnp.where(present[1], got_high[rim].astype(F32), 0.0)
            total = total + level
            out[b, part] = total.astype(BF16)
    me = member()
    for step, chunk in zip(STEPS, outs):
        chunk[:2] = out[me ^ step]
        chunk[2] = grad_q[me ^ step]


def unpack_kernel(*refs):
    here, across_0, across_1, *refs = refs
    chunks, (*outs, mixed) = refs[:GROUP], refs[GROUP:]
    half = across_0.shape[0]
    for part, across in enumerate((across_0, across_1)):
        at = pl.ds(part * half, half)
        mixed[at, :] = (here[at, :] + across[...].astype(F32)).astype(BF16)
    me = member()
    for step, chunk in zip(STEPS, chunks):
        at = columns(me ^ step)
        for part, out in enumerate(outs):
            out[:, at] = chunk[part]


def share():
    return lax.axis_index("mp")


def grad_kernel(*refs):
    pieces, out_weight, refs = refs[:N_MP], refs[N_MP], refs[N_MP + 1 :]
    *outs, whole, heads = refs
    me = member()
    for step, piece in enumerate(pieces):
        whole[span(share() ^ step, piece.shape[0]), :] = piece[...]
    heads[...] = dot_nt(whole[...], out_weight[...]).astype(BF16)
    for step, out in zip(STEPS, outs):
        out[...] = heads[:, columns(me ^ step)]


def project_kernel(*refs):
    chunks, out_weight, (kept, *sent, attended, whole) = refs[:GROUP], refs[GROUP], refs[GROUP + 2 :]
    me = member()
    for step, chunk in zip(STEPS, chunks):
        attended[:, columns(me ^ step)] = chunk[...]
    whole[...] = dot(attended[...], out_weight[...]).astype(BF16)
    rows = kept.shape[1]
    for far in range(2):
        kept[far] = whole[span(share() ^ (2 * far), rows), :]
        for part in range(2):
            half = rows // 2
            at = 2 * (share() ^ (2 * far + 1)) + part
            sent[2 * far + part][...] = whole[span(at, half), :]


def swapped(x, axis, step):
    return lax.ppermute(x, axis, [(i, i ^ step) for i in range(lax.axis_size(axis))])


def exchanged(chunks):
    return [chunks[0]] + [swapped(chunk, "seq", step) for step, chunk in zip(STEPS[1:], chunks[1:])]


def crossed(arrays):
    count = lax.axis_size("seq")
    across = swapped(arrays[0], "seq", GROUP)
    if len(arrays) == 1:
        return [across]
    up = [(i, i + GROUP) for i in range(count - GROUP)]
    down = [(j, i) for i, j in up]
    return [across, lax.ppermute(arrays[1], "seq", up), lax.ppermute(arrays[2], "seq", down)]


def per_device(queries, keys, values, out_weight, out_grad):
    rows, width = queries.shape
    assert width == GROUP * HEAD_DIM and rows == BLOCK and lax.axis_size("mp") == N_MP
    count = lax.axis_size("seq")
    assert count % (2 * GROUP) == 0
    groups = count // GROUP
    nb = GROUP
    tokens = nb * rows
    half, quarter = rows // 2, rows // 4
    model = out_weight.shape[1]
    block = shape(2, rows, HEAD_DIM)
    sent = [shape(2 * REST + 2 * rows, HEAD_DIM)]
    if groups > 2:
        sent = [shape(2 * REST, HEAD_DIM)] + [shape(2 * rows, HEAD_DIM)] * 2
    rims = [block] * (1 if groups == 2 else 2)
    quarter = rows // 4
    in_order = shape(nb, rows, HEAD_DIM)
    score_flops = 2 * tokens * 5 * BLOCK * HEAD_DIM
    weight_flops = 2 * rows * out_weight.size

    chunk = shape(rows, HEAD_DIM)
    triple = shape(3, rows, HEAD_DIM)
    chunks = call(
        pack_kernel,
        [triple] * GROUP,
        (queries, keys, values),
        scratch=[pltpu.SemaphoreType.DMA((3 * GROUP,))],
        copied=GROUP,
        limit=53,
    )
    half = out_grad.shape[0] // 2
    far = [swapped(piece, "mp", 2) for piece in (out_grad[:half], out_grad[half:])]
    chunks = exchanged(chunks)
    arrays = (out_grad, out_weight, *far)
    own_grad, out_weight, far = call(
        copy_kernel, [shape(*x.shape) for x in (out_grad, out_weight, out_grad)], arrays
    )
    refs = call(
        functools.partial(cross_kernel, groups),
        sent,
        chunks,
        scratch=[pltpu.VMEM((2, rows, HEAD_DIM), BF16)],
        flops=20 * score_flops,
    )
    rim_blocks = crossed(refs)
    near, queries, level_1 = call(
        functools.partial(gather_kernel, nb),
        [
            shape(nb, 2, rows, HEAD_DIM),
            shape(nb, rows, HEAD_DIM),
            shape(2, tokens // 2, HEAD_DIM),
        ],
        chunks,
    )
    grad_chunks = call(
        grad_kernel,
        [chunk] * GROUP,
        (own_grad, swapped(own_grad, "mp", 1), far, swapped(far, "mp", 1), out_weight),
        scratch=[pltpu.VMEM((rows, model), BF16), pltpu.VMEM((rows, width), BF16)],
        flops=weight_flops,
    )
    query, k_t, v_t, k1_t, v1_t, weights, stats = call(
        functools.partial(local_kernel, nb),
        [
            shape(3, nb, rows, HEAD_DIM),
            shape(HEAD_DIM, tokens),
            shape(HEAD_DIM, tokens),
            shape(HEAD_DIM, tokens // 2),
            shape(HEAD_DIM, tokens // 2),
            shape(nb, 4, BLOCK, BLOCK, dtype=F32),
            shape(8, tokens, dtype=F32),
        ],
        (near, queries, level_1, grad_chunks[0]),
        flops=score_flops,
    )
    grad_chunks = exchanged(grad_chunks)
    rim_square = shape(len(rims), BLOCK, BLOCK)
    prob, grads, top_2, deltas, far_shift, rim_shift, *refs = call(
        functools.partial(forward_kernel, nb, groups),
        [
            shape(nb, 4, BLOCK, BLOCK),
            in_order,
            block,
            shape(8, tokens, dtype=F32),
            shape(BLOCK, tokens),
            rim_square,
        ]
        + [chunk] * GROUP
        + sent,
        (query, v_t, v1_t, weights, stats, *rim_blocks, *grad_chunks),
        scratch=[
            pltpu.VMEM((nb, rows, HEAD_DIM), BF16),
            pltpu.VMEM((BLOCK, tokens), BF16),
            pltpu.VMEM(rim_square.shape, BF16),
            pltpu.VMEM((8, tokens), F32),
            pltpu.VMEM((HEAD_DIM, tokens), F32),
            pltpu.VMEM((2, BLOCK, HEAD_DIM), F32),
        ],
        flops=score_flops,
    )
    attended = exchanged(refs[:GROUP])
    rim_grads = refs[GROUP:]
    other_grads = crossed(rim_grads)
    grad_q, grad_kv = call(
        functools.partial(backward_kernel, nb, groups),
        [in_order, shape(2, nb, rows, HEAD_DIM, dtype=F32)],
        (query, near, level_1, k_t, k1_t, prob, grads, top_2, deltas, far_shift, rim_shift, *rim_blocks),
        scratch=[
            pltpu.VMEM((nb, 4, BLOCK, BLOCK), BF16),
            pltpu.VMEM((2, tokens // 2, HEAD_DIM), F32),
            pltpu.VMEM((HEAD_DIM, tokens), F32),
        ],
    )
    local = rows // N_MP
    kept, *given = call(
        project_kernel,
        [shape(2, local, model)] + [shape(local // 2, model)] * 4,
        (*attended, out_weight, grad_q),
        scratch=[pltpu.VMEM((rows, width), BF16), pltpu.VMEM((rows, model), BF16)],
    )
    *across, here = call(
        share_kernel,
        [shape(local // 2, model)] * 2 + [shape(local, model, dtype=F32)],
        (kept, *(swapped(piece, "mp", 1) for piece in given)),
    )
    chunks = call(
        functools.partial(combine_kernel, nb, groups),
        [triple] * GROUP,
        (grad_q, grad_kv, *other_grads),
        scratch=[pltpu.VMEM((nb, 2, rows, HEAD_DIM), BF16)],
        flops=20 * score_flops,
    )
    chunks = exchanged(chunks)
    across = [swapped(piece, "mp", 2) for piece in across]
    grad_k, grad_v, grad_q, mixed = call(
        unpack_kernel,
        [shape(rows, width)] * 3 + [shape(local, model)],
        (here, *across, *chunks),
    )
    return mixed, grad_q, grad_k, grad_v


def solution(mesh):
    return jax.shard_map(
        per_device,
        mesh=mesh,
        in_specs=(
            P("seq", "mp"),
            P("seq", "mp"),
            P("seq", "mp"),
            P("mp", None),
            P(("seq", "mp"), None),
        ),
        out_specs=(P(("seq", "mp"), None), P("seq", "mp"), P("seq", "mp"), P("seq", "mp")),
        check_vma=False,
    )
```

```python
import functools

import jax
import jax.numpy as jnp
from jax import lax
from jax.experimental import pallas as pl
from jax.experimental.pallas import tpu as pltpu
from jax.sharding import PartitionSpec as P

HEAD_DIM = 128
BLOCK = 256
REST = 3 * BLOCK // 4
LEVELS = 2
GROUP = 4
STEPS = (0, 3, 2, 1)
N_MP = 4
SCALE = HEAD_DIM**-0.5
LOG2E = 1.4426950408889634
BF16 = jnp.bfloat16
F32 = jnp.float32


def dot(a, b):
    return lax.dot_general(a, b, (((1,), (0,)), ((), ())), preferred_element_type=F32)


def dot_nt(a, b):
    return lax.dot_general(a, b, (((1,), (1,)), ((), ())), preferred_element_type=F32)


def shape(*dims, dtype=BF16):
    return jax.ShapeDtypeStruct(dims, dtype)


def call(kernel, out_shape, args, scratch=(), flops=0, limit=32, copied=0):
    whole = pl.BlockSpec(memory_space=pltpu.VMEM)
    kept = pl.BlockSpec(memory_space=pltpu.HBM)
    moved = sum(x.size * x.dtype.itemsize for x in (*args, *out_shape))
    return pl.pallas_call(
        kernel,
        out_shape=out_shape,
        in_specs=[kept if copied else whole] * len(args),
        out_specs=[kept] * copied + [whole] * (len(out_shape) - copied),
        scratch_shapes=scratch,
        compiler_params=pltpu.CompilerParams(vmem_limit_bytes=limit << 20),
        cost_estimate=pl.CostEstimate(flops=flops, bytes_accessed=moved if flops else 0, transcendentals=0),
    )(*args)


def columns(index):
    return pl.ds(pl.multiple_of(index * HEAD_DIM, HEAD_DIM), HEAD_DIM)


def span(index, size):
    start = index * size
    return pl.ds(start if isinstance(start, int) else pl.multiple_of(start, size), size)


def iota(dims, axis):
    return lax.broadcasted_iota(jnp.int32, dims, axis)


def averaging(level):
    dims = (BLOCK, BLOCK)
    same = (iota(dims, 0) >> level) == (iota(dims, 1) >> level)
    return jnp.where(same, 2.0**-level, 0.0).astype(BF16)


def pooling():
    dims = (BLOCK // 2, BLOCK)
    return jnp.where(iota(dims, 0) == (iota(dims, 1) >> 1), 0.5, 0.0).astype(BF16)


def spreading(level):
    dims = (BLOCK, BLOCK >> level)
    return jnp.where((iota(dims, 0) >> level) == iota(dims, 1), 2.0**-level, 0.0).astype(BF16)


def halves(x):
    high = x.astype(BF16)
    return high, (x - high.astype(F32)).astype(BF16)


def at_block(b):
    return slice(b * BLOCK, (b + 1) * BLOCK)


def sibling(b):
    return (b >> 1) ^ 1


def rim_present(groups):
    group = lax.axis_index("seq") // GROUP
    return group > 0, group < groups - 1


def member():
    return lax.rem(lax.axis_index("seq"), GROUP)


def columns(index):
    return pl.ds(pl.multiple_of(index * HEAD_DIM, HEAD_DIM), HEAD_DIM)


def pack_kernel(q, k, v, *refs):
    *outs, sems = refs
    me = member()
    copies = []
    for step, out in zip(STEPS, outs):
        for part, source in enumerate((k, v, q)):
            piece = source.at[:, columns(me ^ step)]
            copies.append(pltpu.make_async_copy(piece, out.at[part], sems.at[len(copies)]))
    for copy in copies:
        copy.start()
    for copy in copies:
        copy.wait()


def copy_kernel(out_grad, low, high, _, *outs):
    half = low.shape[0]
    outs[0][...] = out_grad[:half]
    outs[1][...] = out_grad[half:]
    outs[2][...] = low[...]
    outs[3][...] = high[...]


def gather_kernel(nb, *refs):
    chunks, (near, queries, level_1) = refs[:GROUP], refs[GROUP:]
    me = member()
    for step, chunk in zip(STEPS, chunks):
        near[me ^ step] = chunk[:2]
        queries[me ^ step] = chunk[2]
    pool = pooling()
    half = BLOCK // 2
    for part in range(2):
        for b in range(nb):
            level_1[part, b * half : (b + 1) * half] = dot(pool, near[b, part]).astype(BF16)


def pooled_twice(rows):
    pool = pooling()
    half = BLOCK // 2
    once = dot(pool, rows).astype(BF16)
    return dot(pool[: half // 2, :half], once).astype(BF16)


def cross_kernel(groups, *refs):
    chunks, (top, *outs, levels) = refs[:GROUP], refs[GROUP:]
    me = member()
    quarter = BLOCK // 4
    side_by_side = [chunk[part] for chunk in chunks for part in range(2)]
    pooled = pooled_twice(jnp.concatenate(side_by_side, axis=1))
    for i, step in enumerate(STEPS):
        for part in range(2):
            at = (2 * i + part) * HEAD_DIM
            levels[part, span(me ^ step, quarter), :] = pooled[:, at : at + HEAD_DIM]
    odd = odd_group()
    for part in range(2):
        rest = levels[part, pl.ds(pl.multiple_of(odd * quarter, quarter), REST), :]
        top[part * REST : (part + 1) * REST] = rest
    members = [(GROUP - 1, outs[0], 0), (0, outs[1], 0)] if groups > 2 else [
        (jnp.where(odd == 1, 0, GROUP - 1), top, 2 * REST)
    ]
    for wanted, out, start in members:
        for step, chunk in zip(STEPS, chunks):

            @pl.when(me ^ step == wanted)
            def _():
                for part in range(2):
                    at = start + part * BLOCK
                    out[at : at + BLOCK] = chunk[part]


def from_others(groups, refs):
    if groups == 2:
        return (refs[0].at[: 2 * REST], refs[0].at[2 * REST :], refs[0].at[2 * REST :]), refs[1:]
    return refs[:3], refs[3:]


def odd_group():
    return lax.rem(lax.axis_index("seq") // GROUP, 2)


def near_window(b, nb):
    sides = near_sides(b, nb)
    low, high = sides[0], sides[-1] + 1
    return slice(low, high), slice((b + low - 1) * BLOCK, (b + high - 1) * BLOCK)


def near_sides(b, nb):
    return [side for side in range(3) if 0 <= b + side - 1 < nb]


def local_kernel(nb, near, queries, level_1, _, query, k_t, v_t, k1_t, v1_t, weights, stats):
    even_1, even_2 = averaging(1), averaging(2)
    for b in range(nb):
        query[0, b] = queries[b]
        once = dot(even_1, queries[b]).astype(BF16)
        query[1, b] = once
        query[2, b] = dot(even_2, once).astype(BF16)
        for part, transposed in enumerate((k_t, v_t)):
            transposed[:, at_block(b)] = near[b, part].T
    for c in range(nb // 2):
        for part, transposed in enumerate((k1_t, v1_t)):
            transposed[:, at_block(c)] = level_1[part, at_block(c)].T
    for b in range(nb):
        sides = near_sides(b, nb)
        scores = [dot_nt(near[b + side - 1, 0], query[0, b]) * (SCALE * LOG2E) for side in sides]
        coarse = dot_nt(level_1[0, at_block(sibling(b))], query[1, b]) * (SCALE * LOG2E)
        top = coarse.max(0, keepdims=True)
        for score in scores:
            top = jnp.maximum(top, score.max(0, keepdims=True))
        weight = 2.0 * jnp.exp2(coarse - top)
        weights[b, 3] = weight
        total = weight.sum(0, keepdims=True)
        for side, score in zip(sides, scores):
            weight = jnp.exp2(score - top)
            weights[b, side] = weight
            total = total + weight.sum(0, keepdims=True)
        stats[:1, at_block(b)] = top
        stats[1:2, at_block(b)] = total


def rims_of(nb, groups, low, high):
    group = lax.axis_index("seq") // GROUP
    if groups == 2:
        return [(jnp.where(group > 0, 0, nb - 1), low, None)]
    return [(0, low, group > 0), (nb - 1, high, group < groups - 1)]


def forward_kernel(nb, groups, *refs):
    (query, v_t, v1_t, weights, stats), refs = refs[:5], refs[5:]
    (got_top, rim_low, rim_high), refs = from_others(groups, refs)
    chunks, refs = refs[:GROUP], refs[GROUP:]
    (prob, grads, top_2, deltas, far_shift, rim_shift), refs = refs[:6], refs[6:]
    outs, (*rim_outs, attended, far_prob, rim_prob, row, context_t, far_sums) = refs[:GROUP], refs[GROUP:]
    rims = rims_of(nb, groups, rim_low, rim_high)
    me = member()
    quarter = BLOCK // 4
    tokens = nb * BLOCK
    for step, chunk in zip(STEPS, chunks):
        grads[me ^ step] = chunk[...]
    odd = odd_group()
    for part in range(2):
        at = slice(part * BLOCK, (part + 1) * BLOCK)
        beside_me = jnp.where(odd == 1, rim_low[at], rim_high[at]) if groups > 2 else rim_low[at]
        rest = pl.ds(pl.multiple_of((1 - odd) * quarter, quarter), REST)
        top_2[part, rest, :] = got_top[part * REST : (part + 1) * REST]
        top_2[part, pl.ds(pl.multiple_of(odd * REST, quarter), quarter), :] = pooled_twice(beside_me)
    coarse_query = query[2].reshape(tokens, HEAD_DIM)
    coarse = dot_nt(top_2[0], coarse_query) * (SCALE * LOG2E)
    row[:1] = jnp.maximum(stats[:1], coarse.max(0, keepdims=True))
    scores = []
    for b, block, present in rims:
        score = dot_nt(block[:BLOCK], query[0, b]) * (SCALE * LOG2E)
        if present is not None:
            score = jnp.where(present, score, -jnp.inf)
        at = span(b, BLOCK)
        row[:1, at] = jnp.maximum(row[:1, at], score.max(0, keepdims=True))
        scores.append(score)
    top = row[:1]
    shrink = jnp.exp2(stats[:1] - top)
    far = 4.0 * jnp.exp2(coarse - top)
    row[1:2] = shrink * stats[1:2] + far.sum(0, keepdims=True)
    fresh = []
    for (b, _, _), score in zip(rims, scores):
        at = span(b, BLOCK)
        fresh.append(jnp.exp2(score - row[:1, at]))
        row[1:2, at] += fresh[-1].sum(0, keepdims=True)
    inverse = 1.0 / row[1:2]
    row[2:3] = inverse
    row[3:4] = shrink * inverse
    far_prob[...] = (far * inverse).astype(BF16)
    context_t[...] = dot(top_2[1].T, far_prob[...])
    for i, (b, block, _) in enumerate(rims):
        at = span(b, BLOCK)
        rim_prob[i] = (fresh[i] * row[2:3, at]).astype(BF16)
        context_t[:, at] += dot(block[BLOCK:].T, rim_prob[i])
    for b in range(nb):
        shrink = row[3:4, at_block(b)]
        prob[b, 3] = (weights[b, 3] * shrink).astype(BF16)
        context = context_t[:, at_block(b)] + dot(v1_t[:, at_block(sibling(b))], prob[b, 3])
        sides, keys = near_window(b, nb)
        parts = (weights[b, sides] * shrink).astype(BF16)
        prob[b, sides] = parts
        context = context + dot(v_t[:, keys], parts.reshape(-1, BLOCK))
        attended[b] = context.T.astype(BF16)
        deltas[:1, at_block(b)] = (grads[b].T.astype(F32) * context).sum(0, keepdims=True)
    grad = grads[...].reshape(tokens, HEAD_DIM)
    slope = dot_nt(top_2[1], grad)
    far_shift[...] = (far_prob[...].astype(F32) * (slope - deltas[:1])).astype(BF16)
    far_sums[0] = SCALE * dot(far_shift[...], coarse_query)
    far_sums[1] = dot(far_prob[...], grad)
    spread = spreading(2)
    folded = []
    for part in range(2):
        rest = far_sums[part, pl.ds(pl.multiple_of((1 - odd) * quarter, quarter), REST), :]
        rim_outs[0][part * REST : (part + 1) * REST] = rest.astype(BF16)
        high, low = halves(far_sums[part, pl.ds(pl.multiple_of(odd * REST, quarter), quarter), :])
        folded.append(dot(spread, high) + dot(spread, low))
    pairs = []
    for i, (b, block, _) in enumerate(rims):
        slope = dot_nt(block[BLOCK:], grads[b])
        rim_shift[i] = (rim_prob[i].astype(F32) * (slope - deltas[:1, span(b, BLOCK)])).astype(BF16)
        pairs.append((SCALE * dot(rim_shift[i], query[0, b]), dot(rim_prob[i], grads[b])))
    for part in range(2):
        at = slice(part * BLOCK, (part + 1) * BLOCK)
        if groups == 2:
            rim_outs[0][2 * REST + part * BLOCK : 2 * REST + (part + 1) * BLOCK] = (
                pairs[0][part] + folded[part]
            ).astype(BF16)
        else:
            rim_outs[1][at] = (pairs[1][part] + jnp.where(odd == 0, folded[part], 0.0)).astype(BF16)
            rim_outs[2][at] = (pairs[0][part] + jnp.where(odd == 1, folded[part], 0.0)).astype(BF16)
    for step, out in zip(STEPS, outs):
        out[...] = attended[me ^ step]


def backward_kernel(nb, groups, *refs):
    (query, near, level_1, k_t, k1_t, prob, grads, top_2, deltas, far_shift, rim_shift), refs = refs[:11], refs[11:]
    (_, rim_low, rim_high), refs = from_others(groups, refs)
    grad_q, grad_kv, shift, sums_1, query_t = refs
    even_1, even_2 = averaging(1), averaging(2)
    coarse = dot(top_2[0].T, far_shift[...])
    for b in range(nb):
        high, low = halves(coarse[:, at_block(b)])
        query_t[:, at_block(b)] = dot(high, even_2) + dot(low, even_2)
    for i, (b, block, _) in enumerate(rims_of(nb, groups, rim_low, rim_high)):
        query_t[:, span(b, BLOCK)] += dot(block[:BLOCK].T, rim_shift[i])
    for b in range(nb):
        grad, delta = grads[b], deltas[:1, at_block(b)]
        grad_t = query_t[:, at_block(b)]
        for side in near_sides(b, nb):
            slope = dot_nt(near[b + side - 1, 1], grad)
            part = (prob[b, side].astype(F32) * (slope - delta)).astype(BF16)
            shift[b, side] = part
            grad_t = grad_t + dot(k_t[:, at_block(b + side - 1)], part)
        slope = dot_nt(level_1[1, at_block(sibling(b))], grad)
        part = (prob[b, 3].astype(F32) * (slope - delta)).astype(BF16)
        shift[b, 3] = part
        high, low = halves(dot(k1_t[:, at_block(sibling(b))], part))
        grad_t = grad_t + (dot(high, even_1) + dot(low, even_1))
        grad_q[b] = (SCALE * grad_t).T.astype(BF16)
    for c in range(nb // 2):
        users = [b for b in range(nb) if sibling(b) == c]
        sums_1[0, at_block(c)] = SCALE * sum(dot(shift[b, 3], query[1, b]) for b in users)
        sums_1[1, at_block(c)] = sum(dot(prob[b, 3], grads[b]) for b in users)
    spread = spreading(1)
    half = BLOCK // 2
    for s in range(nb):
        users = [(s + 1 - side, side) for side in range(3) if 0 <= s + 1 - side < nb]
        key = SCALE * sum(dot(shift[b, side], query[0, b]) for b, side in users)
        value = sum(dot(prob[b, side], grads[b]) for b, side in users)
        for part, total in enumerate((key, value)):
            high, low = halves(sums_1[part, s * half : (s + 1) * half])
            grad_kv[part, s] = total + (dot(spread, high) + dot(spread, low))


def share_kernel(kept, *refs):
    *got, across_0, across_1, here = refs
    half = across_0.shape[0]
    for i, piece in enumerate(got):
        far, at = i // 2, pl.ds(i % 2 * half, half)
        total = kept[far, at, :].astype(F32) + piece[...].astype(F32)
        if far:
            (across_0, across_1)[i % 2][...] = total.astype(BF16)
        else:
            here[at, :] = total


def combine_kernel(nb, groups, grad_q, grad_kv, *refs):
    (got_top, got_low, got_high), (*outs, out) = from_others(groups, refs)
    present = rim_present(groups)
    spread = spreading(2)
    quarter = BLOCK // 4
    odd = odd_group()
    for b in range(nb):
        for part in range(2):
            total = grad_kv[part, b]
            place = 0 if b == 0 else 2 if b == nb - 1 else b - odd
            level = dot(spread, got_top[span(part * (REST // quarter) + place, quarter), :])
            rim = slice(part * BLOCK, (part + 1) * BLOCK)
            if b == 0:
                level = jnp.where(odd == 0, level, 0.0)
                total = total + jnp.where(present[0], got_low[rim].astype(F32), 0.0)
            if b == nb - 1:
                level = jnp.where(odd == 1, level, 0.0)
                total = total + jnp.where(present[1], got_high[rim].astype(F32), 0.0)
            total = total + level
            out[b, part] = total.astype(BF16)
    me = member()
    for step, chunk in zip(STEPS, outs):
        chunk[:2] = out[me ^ step]
        chunk[2] = grad_q[me ^ step]


def unpack_kernel(*refs):
    here, across_0, across_1, *refs = refs
    chunks, (*outs, mixed) = refs[:GROUP], refs[GROUP:]
    half = across_0.shape[0]
    for part, across in enumerate((across_0, across_1)):
        at = pl.ds(part * half, half)
        mixed[at, :] = (here[at, :] + across[...].astype(F32)).astype(BF16)
    me = member()
    for step, chunk in zip(STEPS, chunks):
        at = columns(me ^ step)
        for part, out in enumerate(outs):
            out[:, at] = chunk[part]


def share():
    return lax.axis_index("mp")


def grad_kernel(*refs):
    pieces, out_weight, refs = refs[: 2 * N_MP], refs[2 * N_MP], refs[2 * N_MP + 1 :]
    *outs, whole, heads = refs
    me = member()
    for i, piece in enumerate(pieces):
        whole[span(2 * (share() ^ (i // 2)) + i % 2, piece.shape[0]), :] = piece[...]
    heads[...] = dot_nt(whole[...], out_weight[...]).astype(BF16)
    for step, out in zip(STEPS, outs):
        out[...] = heads[:, columns(me ^ step)]


def project_kernel(*refs):
    chunks, out_weight, (kept, *sent, attended, whole) = refs[:GROUP], refs[GROUP], refs[GROUP + 2 :]
    me = member()
    for step, chunk in zip(STEPS, chunks):
        attended[:, columns(me ^ step)] = chunk[...]
    whole[...] = dot(attended[...], out_weight[...]).astype(BF16)
    rows = kept.shape[1]
    for far in range(2):
        kept[far] = whole[span(share() ^ (2 * far), rows), :]
        for part in range(2):
            half = rows // 2
            at = 2 * (share() ^ (2 * far + 1)) + part
            sent[2 * far + part][...] = whole[span(at, half), :]


def swapped(x, axis, step):
    return lax.ppermute(x, axis, [(i, i ^ step) for i in range(lax.axis_size(axis))])


def exchanged(chunks):
    return [chunks[0]] + [swapped(chunk, "seq", step) for step, chunk in zip(STEPS[1:], chunks[1:])]


def crossed(arrays):
    count = lax.axis_size("seq")
    across = swapped(arrays[0], "seq", GROUP)
    if len(arrays) == 1:
        return [across]
    up = [(i, i + GROUP) for i in range(count - GROUP)]
    down = [(j, i) for i, j in up]
    return [across, lax.ppermute(arrays[1], "seq", up), lax.ppermute(arrays[2], "seq", down)]


def per_device(queries, keys, values, out_weight, out_grad):
    rows, width = queries.shape
    assert width == GROUP * HEAD_DIM and rows == BLOCK and lax.axis_size("mp") == N_MP
    count = lax.axis_size("seq")
    assert count % (2 * GROUP) == 0
    groups = count // GROUP
    nb = GROUP
    tokens = nb * rows
    half, quarter = rows // 2, rows // 4
    model = out_weight.shape[1]
    block = shape(2, rows, HEAD_DIM)
    sent = [shape(2 * REST + 2 * rows, HEAD_DIM)]
    if groups > 2:
        sent = [shape(2 * REST, HEAD_DIM)] + [shape(2 * rows, HEAD_DIM)] * 2
    rims = [block] * (1 if groups == 2 else 2)
    quarter = rows // 4
    in_order = shape(nb, rows, HEAD_DIM)
    score_flops = 2 * tokens * 5 * BLOCK * HEAD_DIM
    weight_flops = 2 * rows * out_weight.size

    chunk = shape(rows, HEAD_DIM)
    triple = shape(3, rows, HEAD_DIM)
    chunks = call(
        pack_kernel,
        [triple] * GROUP,
        (queries, keys, values),
        scratch=[pltpu.SemaphoreType.DMA((3 * GROUP,))],
        copied=GROUP,
        limit=53,
    )
    half = out_grad.shape[0] // 2
    far = [swapped(piece, "mp", 2) for piece in (out_grad[:half], out_grad[half:])]
    chunks = exchanged(chunks)
    refs = call(
        functools.partial(cross_kernel, groups),
        sent,
        chunks,
        scratch=[pltpu.VMEM((2, rows, HEAD_DIM), BF16)],
        flops=20 * score_flops,
    )
    rim_blocks = crossed(refs)
    pieces = call(copy_kernel, [shape(half, model)] * N_MP, (out_grad, *far, refs[0]))
    beside_us = [swapped(piece, "mp", 1) for piece in pieces]
    pieces = [*pieces[:2], *beside_us[:2], *pieces[2:], *beside_us[2:]]
    near, queries, level_1 = call(
        functools.partial(gather_kernel, nb),
        [
            shape(nb, 2, rows, HEAD_DIM),
            shape(nb, rows, HEAD_DIM),
            shape(2, tokens // 2, HEAD_DIM),
        ],
        chunks,
    )
    grad_chunks = call(
        grad_kernel,
        [chunk] * GROUP,
        (*pieces, out_weight),
        scratch=[pltpu.VMEM((rows, model), BF16), pltpu.VMEM((rows, width), BF16)],
    )
    query, k_t, v_t, k1_t, v1_t, weights, stats = call(
        functools.partial(local_kernel, nb),
        [
            shape(3, nb, rows, HEAD_DIM),
            shape(HEAD_DIM, tokens),
            shape(HEAD_DIM, tokens),
            shape(HEAD_DIM, tokens // 2),
            shape(HEAD_DIM, tokens // 2),
            shape(nb, 4, BLOCK, BLOCK, dtype=F32),
            shape(8, tokens, dtype=F32),
        ],
        (near, queries, level_1, grad_chunks[0]),
    )
    grad_chunks = exchanged(grad_chunks)
    rim_square = shape(len(rims), BLOCK, BLOCK)
    prob, grads, top_2, deltas, far_shift, rim_shift, *refs = call(
        functools.partial(forward_kernel, nb, groups),
        [
            shape(nb, 4, BLOCK, BLOCK),
            in_order,
            block,
            shape(8, tokens, dtype=F32),
            shape(BLOCK, tokens),
            rim_square,
        ]
        + [chunk] * GROUP
        + sent,
        (query, v_t, v1_t, weights, stats, *rim_blocks, *grad_chunks),
        scratch=[
            pltpu.VMEM((nb, rows, HEAD_DIM), BF16),
            pltpu.VMEM((BLOCK, tokens), BF16),
            pltpu.VMEM(rim_square.shape, BF16),
            pltpu.VMEM((8, tokens), F32),
            pltpu.VMEM((HEAD_DIM, tokens), F32),
            pltpu.VMEM((2, BLOCK, HEAD_DIM), F32),
        ],
        flops=score_flops,
    )
    attended = exchanged(refs[:GROUP])
    rim_grads = refs[GROUP:]
    other_grads = crossed(rim_grads)
    grad_q, grad_kv = call(
        functools.partial(backward_kernel, nb, groups),
        [in_order, shape(2, nb, rows, HEAD_DIM, dtype=F32)],
        (query, near, level_1, k_t, k1_t, prob, grads, top_2, deltas, far_shift, rim_shift, *rim_blocks),
        scratch=[
            pltpu.VMEM((nb, 4, BLOCK, BLOCK), BF16),
            pltpu.VMEM((2, tokens // 2, HEAD_DIM), F32),
            pltpu.VMEM((HEAD_DIM, tokens), F32),
        ],
    )
    local = rows // N_MP
    kept, *given = call(
        project_kernel,
        [shape(2, local, model)] + [shape(local // 2, model)] * 4,
        (*attended, out_weight, grad_q),
        scratch=[pltpu.VMEM((rows, width), BF16), pltpu.VMEM((rows, model), BF16)],
    )
    *across, here = call(
        share_kernel,
        [shape(local // 2, model)] * 2 + [shape(local, model, dtype=F32)],
        (kept, *(swapped(piece, "mp", 1) for piece in given)),
    )
    chunks = call(
        functools.partial(combine_kernel, nb, groups),
        [triple] * GROUP,
        (grad_q, grad_kv, *other_grads),
        scratch=[pltpu.VMEM((nb, 2, rows, HEAD_DIM), BF16)],
        flops=20 * score_flops,
    )
    chunks = exchanged(chunks)
    across = [swapped(piece, "mp", 2) for piece in across]
    grad_k, grad_v, grad_q, mixed = call(
        unpack_kernel,
        [shape(rows, width)] * 3 + [shape(local, model)],
        (here, *across, *chunks),
    )
    return mixed, grad_q, grad_k, grad_v


def solution(mesh):
    return jax.shard_map(
        per_device,
        mesh=mesh,
        in_specs=(
            P("seq", "mp"),
            P("seq", "mp"),
            P("seq", "mp"),
            P("mp", None),
            P(("seq", "mp"), None),
        ),
        out_specs=(P(("seq", "mp"), None), P("seq", "mp"), P("seq", "mp"), P("seq", "mp")),
        check_vma=False,
    )
```
